128 devices in a mesh: ctx: 8 (over x, y_hi), fsdp: 16 (over y_lo, z, core).
Axes of the slice: x: 4, y: 4 (y_hi: 2, y_lo: 2; y = y_hi * 2 + y_lo), z: 4, core: 2. Of those that a mesh axis runs over, the one named last changes fastest.
Arguments:
- layer_hidden_input: bfloat16 [16, 1024, 2048], P('fsdp', 'ctx'), may hold values from -6 to 6
- output_cotangent: bfloat16 [16, 1024, 2048], P('fsdp', 'ctx'), may hold values from -6 to 6
- sequence_pair_lengths: int32 [16, 2], P('fsdp'), may hold values from 1 to 896, 1024 in all within a row
- block_placement_order: int32 [16, 16], P('fsdp'), may hold values from 0 to 15, as said below
- sequence_adapter_index: int32 [16, 2], P('fsdp'), may hold values from 0 to 7
- token_expert_choices: int32 [16, 1024, 4], P('fsdp', 'ctx'), may hold values from 0 to 15, all different within a row; in each aligned block of 128 rows (0 to 127, 128 to 255, ..., all dimensions but the last counted through in order) at most 36 rows name the same one
- attention_norm_gain: bfloat16 [2048], replicated, may hold values from 0.5 to 1.5
- feedforward_norm_gain: bfloat16 [2048], replicated, may hold values from 0.5 to 1.5
- query_key_value_weight: bfloat16 [3, 2048, 2048], P(None, 'fsdp'), may hold values from -0.125 to 0.125
- output_projection_weight: bfloat16 [2048, 2048], P('fsdp'), may hold values from -0.5 to 0.5
- query_key_value_bias: bfloat16 [3, 2048], replicated, may hold values from -0.59765625 to 0.59765625
- router_weight_matrix: bfloat16 [2048, 16], replicated, may hold values from -0.0625 to 0.0625
- shared_gate_up_weight: bfloat16 [2, 2048, 5632], P(None, None, 'fsdp'), may hold values from -0.125 to 0.125
- shared_down_weight: bfloat16 [5632, 2048], P('fsdp'), may hold values from -0.15625 to 0.15625
- shared_sigmoid_gate: bfloat16 [2048], replicated, may hold values from -0.125 to 0.125
- routed_gate_up_weight: bfloat16 [16, 2, 2048, 1408], P('fsdp'), may hold values from -0.125 to 0.125
- routed_down_weight: bfloat16 [16, 1408, 2048], P('fsdp'), may hold values from -0.3125 to 0.3125
- attention_adapter_first: bfloat16 [4, 8, 16, 2048], replicated, may hold values from -0.125 to 0.125
- attention_adapter_second: bfloat16 [4, 8, 16, 2048], replicated, may hold values from -0.75 to 0.75
- feedforward_adapter_first: bfloat16 [5, 8, 16, 2048], replicated, may hold values from -0.125 to 0.125
- router_adapter_second: bfloat16 [8, 16, 16], replicated, may hold values from -0.375 to 0.375
- shared_gate_adapter_second: bfloat16 [2, 8, 16, 5632], replicated, may hold values from -0.75 to 0.75
- shared_down_adapter_first: bfloat16 [8, 16, 5632], replicated, may hold values from -0.078125 to 0.078125
- routed_gate_adapter_second: bfloat16 [2, 8, 16, 1408], replicated, may hold values from -0.75 to 0.75
- routed_down_adapter_first: bfloat16 [8, 16, 1408], replicated, may hold values from -0.15625 to 0.15625
- down_adapter_second: bfloat16 [2, 8, 16, 2048], replicated, may hold values from -0.75 to 0.75
Outputs:
- output: bfloat16 [16, 1024, 2048], P('fsdp', 'ctx')
- input_grad: bfloat16 [16, 1024, 2048], P('fsdp', 'ctx')
- grad_attn_in: float32 [4, 8, 16, 2048], P(None, None, None, 'fsdp')
- grad_attn_out: float32 [4, 8, 16, 2048], P(None, None, None, 'fsdp')
- grad_ffn_in: float32 [5, 8, 16, 2048], P(None, None, None, 'fsdp')
- grad_router_out: float32 [8, 16, 16], P(None, None, 'fsdp')
- grad_shared_out: float32 [2, 8, 16, 5632], P(None, None, None, 'fsdp')
- grad_shared_down_in: float32 [8, 16, 5632], P(None, None, 'fsdp')
- grad_expert_out: float32 [2, 8, 16, 1408], P(None, None, None, 'fsdp')
- grad_expert_down_in: float32 [8, 16, 1408], P(None, None, 'fsdp')
- grad_down_out: float32 [2, 8, 16, 2048], P(None, None, None, 'fsdp')
The draws below stay inside these ranges and needn't reach their ends.
Inputs may be any that keep to these rules, and one draw needn't show every extreme that they name: `sequence_pair_lengths`: each length is 128 to 896, and the two lengths of a group sum to 1024. `block_placement_order`: each row is a permutation of the 16 blocks; entry 2 c is below 8 and entry 2 c + 1 is not. `token_expert_choices`: each token names 4 different experts; among the tokens of one device no expert is named more than 36 times, a bound that some block reaches.
All inputs are finite; a program needn't handle non-finite values.
Results may differ from the reference program's by a relative error of at most 0.025.
Values may be sent and summed in bfloat16 or wider, within the bound.
A program may use at most 448 MiB of HBM per device.

```python
import math
import jax
import jax.numpy as jnp
import numpy as np
from jax import lax

MODEL_WIDTH = 2048
HEADS = 16
HEAD_DIM = 128
EXPERT_HIDDEN = 1408
SHARED_HIDDEN = 5632
TOP = 4
ADAPTER_COUNT = 8
ADAPTER_RANK = 16
TOK_DEV = 128
ROUTED_EXPERTS = 16
GROUPS = 16
GROUP_TOK = 1024
BLOCKS = 16
LONGEST = 896
CAP = 36
EXPERT_ROWS = 4608


def draw_block_placement_order(key, part):
    key = jax.random.fold_in(key, 11)
    half_count = BLOCKS // 2
    group_keys = jax.random.split(key, 2 * GROUPS)

    def shuffled(one_key):
        return jax.random.permutation(one_key, half_count)
    earlier_half = jax.vmap(shuffled)(group_keys[:GROUPS])
    later_half = jax.vmap(shuffled)(group_keys[GROUPS:]) + half_count
    return jnp.stack([earlier_half, later_half], axis=-1).reshape(GROUPS, BLOCKS).astype(jnp.int32)


def plant(values, key, least, top_value):
    shape = values.shape
    spot = [jax.random.randint(jax.random.fold_in(key, axis), (), 0, shape[axis]) for axis in range(len(shape))]
    values = values.at[tuple(spot)].set(least)
    longest = shape.index(max(shape))
    spot[longest] = (spot[longest] + 1) % shape[longest]
    return values.at[tuple(spot)].set(top_value)


def block_levels(key, extent, pieces, least, largest):
    level = 1.0
    for dim, shards_of in pieces:
        steps = jax.random.uniform(jax.random.fold_in(jax.random.fold_in(key, 6), dim), (shards_of,), jnp.float32, least / len(pieces), largest / len(pieces))
        level = level * jnp.repeat(jnp.exp(steps), extent[dim] // shards_of).reshape((-1,) + (1,) * (len(extent) - 1 - dim))
    return level


def profile(amount, total, bound, lean):
    portions = [(1 << 20) // math.isqrt(standing ** lean) + 1 for standing in range(2, amount + 1)]
    rest, given = total - bound - (amount - 1), [1] * (amount - 1)
    while rest > 0:
        candidates = [i for i in range(amount - 1) if given[i] < bound]
        pool, left = sum([portions[i] for i in candidates]), rest
        for i in candidates:
            extra = min(bound - given[i], max(1, left * portions[i] // pool), rest)
            given[i] = given[i] + extra
            rest = rest - extra
    return np.array([bound] + given)


def ragged_sizes(own_key, amount, total, limit, skew):
    if amount == 2:
        one = jax.random.randint(own_key, (), max(1, total - limit), min(limit, total - 1) + 1)
        return jnp.stack([one, total - one])
    sizes = jnp.asarray(profile(amount, total, limit, skew), jnp.int32)
    pairs = (amount - 1) // 2
    donor, sink = sizes[1:1 + 2 * pairs:2], sizes[2:2 + 2 * pairs:2]
    margin = jnp.minimum(donor - 1, limit - sink)
    passed = jax.random.randint(jax.random.fold_in(own_key, 1), (pairs,), 0, 1 << 20) % (margin + 1)
    sizes = sizes.at[1:1 + 2 * pairs:2].set(donor - passed).at[2:2 + 2 * pairs:2].set(sink + passed)
    return sizes[jax.random.permutation(jax.random.fold_in(own_key, 2), amount)]


def routed_block(rng, own, number, rows, amount, top, reach, slope):
    order = jax.random.permutation(rng, amount)
    packed, common = portions_of(amount, rows * top, reach, slope, True), portions_of(amount, rows * top, reach, slope, False)
    places = jnp.arange(amount)

    def named(tallies, rotation):
        used = int((tallies > 0).sum())
        fixed = max(1, used // 4)
        shifted = fixed + (places - fixed + rotation * (used - fixed)) % max(1, amount - fixed)
        return jnp.zeros((amount,), jnp.int32).at[order[jnp.where(places < fixed, places, shifted)]].set(jnp.asarray(tallies, jnp.int32))

    tallies = jnp.where(number % 4 == 0, named(packed, number // 4), named(common, number - number // 4 - 1))
    mixed = jax.random.permutation(jax.random.fold_in(own, 3), amount)
    donor, sink = mixed[0:amount // 2 * 2:2], mixed[1:amount // 2 * 2:2]
    room = jnp.minimum(tallies[donor] - 1, reach - tallies[sink]) // 2
    room = jnp.where((donor == order[0]) | (sink == order[0]) | (tallies[sink] == 0), 0, jnp.maximum(room, 0))
    shifted = jax.random.randint(jax.random.fold_in(own, 4), (amount // 2,), 0, 1 << 20) % (room + 1)
    tallies = tallies.at[donor].add(-shifted).at[sink].add(shifted)
    items = jnp.searchsorted(jnp.cumsum(tallies), jnp.arange(rows * top), side="right").astype(jnp.int32)
    grid = items.reshape(top, rows).T
    grid = grid[jax.random.permutation(jax.random.fold_in(own, 1), rows)]
    rotation = jax.random.randint(jax.random.fold_in(own, 2), (rows, 1), 0, top)
    return jnp.take_along_axis(grid, (jnp.arange(top)[None, :] + rotation) % top, axis=1)


def portions_of(amount, total, limit, lean, full):
    portions = [(1 << 20) // math.isqrt(rank ** lean) + 1 for rank in range(1, amount + 1)]
    largest = limit if full else min(limit, max(-(-total // amount), total * portions[0] // sum(portions)))
    least = 1 if total - largest >= amount - 1 else 0
    given, rest = [largest] + [least] * (amount - 1), total - largest - least * (amount - 1)
    while rest > 0:
        candidates = [i for i in range(1, amount) if given[i] < largest] or [i for i in range(1, amount) if given[i] < limit]
        whole, left = sum([portions[i] for i in candidates]), rest
        for i in candidates:
            more = min(limit - given[i], max(1, left * portions[i] // whole), rest)
            given[i] = given[i] + more
            rest = rest - more
    return np.array(given)


def gaussian(key, shape, deviation, most, shards=(), kind=jnp.bfloat16):
    array = deviation * jax.random.normal(key, shape, jnp.float32)
    if shards:
        array = array * block_levels(key, shape, shards, -0.22, 0.18)
    return jnp.clip(array, -most, most).astype(kind)


def setup_inputs(seed: int = 0) -> dict:
    arg_keys = jax.random.split(jax.random.key(seed), 27)
    layer_hidden_input = gaussian(arg_keys[0], (GROUPS, GROUP_TOK, MODEL_WIDTH), 1.0, 6.0, ((0, 16), (1, 8)))
    output_cotangent = gaussian(arg_keys[1], (GROUPS, GROUP_TOK, MODEL_WIDTH), 1.0, 6.0, ((0, 16), (1, 8)))
    sequence_pair_lengths = jax.vmap(lambda own: ragged_sizes(own, 2, GROUP_TOK, LONGEST, 0))(jax.random.split(arg_keys[2], GROUPS)).reshape((GROUPS, 2)).astype(jnp.int32)
    block_placement_order = draw_block_placement_order(jax.random.fold_in(arg_keys[26], 71), 0)
    sequence_adapter_index = plant(jax.random.randint(arg_keys[4], (GROUPS, 2), 0, ADAPTER_COUNT), jax.random.fold_in(arg_keys[4], 1), 0, ADAPTER_COUNT - 1).astype(jnp.int32)
    token_expert_choices_keys = jax.random.split(jax.random.fold_in(arg_keys[5], 1), GROUPS * GROUP_TOK // TOK_DEV)
    token_expert_choices_turns = jax.random.permutation(jax.random.fold_in(arg_keys[5], 3), GROUPS * GROUP_TOK // TOK_DEV)
    token_expert_choices = jax.vmap(lambda own, number: routed_block(jax.random.fold_in(arg_keys[5], 2), own, number, TOK_DEV, ROUTED_EXPERTS, TOP, CAP, 1))(token_expert_choices_keys, token_expert_choices_turns).reshape((GROUPS, GROUP_TOK, TOP))
    attention_norm_gain = jnp.clip(1.0 + 0.1 * jax.random.normal(arg_keys[6], (MODEL_WIDTH,), jnp.float32), 0.5, 1.5).astype(jnp.bfloat16)
    feedforward_norm_gain = jnp.clip(1.0 + 0.1 * jax.random.normal(arg_keys[7], (MODEL_WIDTH,), jnp.float32), 0.5, 1.5).astype(jnp.bfloat16)
    query_key_value_weight = gaussian(arg_keys[8], (3, MODEL_WIDTH, MODEL_WIDTH), MODEL_WIDTH ** -0.5, 0.125, ((1, 16),))
    output_projection_weight = gaussian(arg_keys[9], (MODEL_WIDTH, MODEL_WIDTH), (MODEL_WIDTH // 16) ** -0.5, 0.5, ((0, 16),))
    query_key_value_bias = gaussian(arg_keys[10], (3, MODEL_WIDTH), 0.1, 0.59765625)
    router_weight_matrix = gaussian(arg_keys[11], (MODEL_WIDTH, ROUTED_EXPERTS), (4 * MODEL_WIDTH) ** -0.5, 0.0625)
    shared_gate_up_weight = gaussian(arg_keys[12], (2, MODEL_WIDTH, SHARED_HIDDEN), MODEL_WIDTH ** -0.5, 0.125, ((2, 16),))
    shared_down_weight = gaussian(arg_keys[13], (SHARED_HIDDEN, MODEL_WIDTH), (SHARED_HIDDEN // 4) ** -0.5, 0.15625, ((0, 16),))
    shared_sigmoid_gate = gaussian(arg_keys[14], (MODEL_WIDTH,), MODEL_WIDTH ** -0.5, 0.125)
    routed_gate_up_weight = gaussian(arg_keys[15], (ROUTED_EXPERTS, 2, MODEL_WIDTH, EXPERT_HIDDEN), MODEL_WIDTH ** -0.5, 0.125, ((0, 16),))
    routed_down_weight = gaussian(arg_keys[16], (ROUTED_EXPERTS, EXPERT_HIDDEN, MODEL_WIDTH), (EXPERT_HIDDEN // 4) ** -0.5, 0.3125, ((0, 16),))
    attention_adapter_first = gaussian(arg_keys[17], (4, ADAPTER_COUNT, ADAPTER_RANK, MODEL_WIDTH), MODEL_WIDTH ** -0.5, 0.125)
    attention_adapter_second = gaussian(arg_keys[18], (4, ADAPTER_COUNT, ADAPTER_RANK, MODEL_WIDTH), (4 * ADAPTER_RANK) ** -0.5, 0.75)
    feedforward_adapter_first = gaussian(arg_keys[19], (5, ADAPTER_COUNT, ADAPTER_RANK, MODEL_WIDTH), MODEL_WIDTH ** -0.5, 0.125)
    router_adapter_second = gaussian(arg_keys[20], (ADAPTER_COUNT, ADAPTER_RANK, ROUTED_EXPERTS), (16 * ADAPTER_RANK) ** -0.5, 0.375)
    shared_gate_adapter_second = gaussian(arg_keys[21], (2, ADAPTER_COUNT, ADAPTER_RANK, SHARED_HIDDEN), (4 * ADAPTER_RANK) ** -0.5, 0.75)
    shared_down_adapter_first = gaussian(arg_keys[22], (ADAPTER_COUNT, ADAPTER_RANK, SHARED_HIDDEN), SHARED_HIDDEN ** -0.5, 0.078125)
    routed_gate_adapter_second = gaussian(arg_keys[23], (2, ADAPTER_COUNT, ADAPTER_RANK, EXPERT_HIDDEN), (4 * ADAPTER_RANK) ** -0.5, 0.75)
    routed_down_adapter_first = gaussian(arg_keys[24], (ADAPTER_COUNT, ADAPTER_RANK, EXPERT_HIDDEN), EXPERT_HIDDEN ** -0.5, 0.15625)
    down_adapter_second = gaussian(arg_keys[25], (2, ADAPTER_COUNT, ADAPTER_RANK, MODEL_WIDTH), (4 * ADAPTER_RANK) ** -0.5, 0.75)
    return dict(layer_hidden_input=layer_hidden_input, output_cotangent=output_cotangent, sequence_pair_lengths=sequence_pair_lengths, block_placement_order=block_placement_order, sequence_adapter_index=sequence_adapter_index, token_expert_choices=token_expert_choices, attention_norm_gain=attention_norm_gain, feedforward_norm_gain=feedforward_norm_gain, query_key_value_weight=query_key_value_weight, output_projection_weight=output_projection_weight, query_key_value_bias=query_key_value_bias, router_weight_matrix=router_weight_matrix, shared_gate_up_weight=shared_gate_up_weight, shared_down_weight=shared_down_weight, shared_sigmoid_gate=shared_sigmoid_gate, routed_gate_up_weight=routed_gate_up_weight, routed_down_weight=routed_down_weight, attention_adapter_first=attention_adapter_first, attention_adapter_second=attention_adapter_second, feedforward_adapter_first=feedforward_adapter_first, router_adapter_second=router_adapter_second, shared_gate_adapter_second=shared_gate_adapter_second, shared_down_adapter_first=shared_down_adapter_first, routed_gate_adapter_second=routed_gate_adapter_second, routed_down_adapter_first=routed_down_adapter_first, down_adapter_second=down_adapter_second)


@jax.custom_vjp
def low(v):
    return lax.optimization_barrier(v.astype(jnp.bfloat16)).astype(jnp.float32)

@jax.custom_vjp
def low_back(v):
    return v

def low_keep(v):
    return (low(v), None)

def low_pass(kept, grad):
    return (grad,)

def back_keep(v):
    return (v, None)

def back_low(kept, grad):
    return (low(grad),)
low.defvjp(low_keep, low_pass)
low_back.defvjp(back_keep, back_low)
norm_eps = 1e-06
rope_theta = 1000000.0
masked_score = -1e+30
highest = lax.Precision.HIGHEST

def product(left, right):
    return jnp.dot(left, right, precision=highest)

def flattened_adapter_factor(factor):
    return factor.reshape(-1, factor.shape[-1])

def rms_scale(values, gain):
    mean_square = lax.optimization_barrier(jnp.mean(values * values, axis=-1, keepdims=True))
    return values * lax.rsqrt(mean_square + norm_eps) * gain

def low_rank(inputs, factor, select_adapter_rows):
    flat = flattened_adapter_factor(factor)
    lanes_all = low_back(product(inputs, flat.T))
    copies = flat.shape[0] // select_adapter_rows.shape[1]
    return low(lanes_all * jnp.tile(select_adapter_rows, (1, copies)))

def rotary_parts(offsets, lane_width):
    fractions = jnp.arange(0, lane_width, 2).astype(jnp.float32) / lane_width
    angles = offsets.astype(jnp.float32)[:, None] * (rope_theta ** (-fractions))[None, :]
    return (jnp.cos(angles), jnp.sin(angles))

def rotate(values, cosine, sine):
    half_width = values.shape[-1] // 2
    front_half = values[..., :half_width]
    back_half = values[..., half_width:]
    cos_part = cosine[:, None, :]
    sin_part = sine[:, None, :]
    return jnp.concatenate([front_half * cos_part - back_half * sin_part, back_half * cos_part + front_half * sin_part], axis=-1)

def attention_core(inputs):
    query_g, key_g, value_g, place_g, second_g = inputs
    scores = jnp.einsum('qhd,khd->hqk', query_g, key_g, precision=highest) * HEAD_DIM ** (-0.5)
    allowed = (second_g[:, None] == second_g[None, :]) & (place_g[None, :] <= place_g[:, None])
    scores = low_back(jnp.where(allowed[None], scores, masked_score))
    weights = low(jax.nn.softmax(scores, axis=-1))
    return jnp.einsum('hqk,khd->qhd', weights, value_g, precision=highest)

def reference(layer_hidden_input, output_cotangent, sequence_pair_lengths, block_placement_order, sequence_adapter_index, token_expert_choices, attention_norm_gain, feedforward_norm_gain, query_key_value_weight, output_projection_weight, query_key_value_bias, router_weight_matrix, shared_gate_up_weight, shared_down_weight, shared_sigmoid_gate, routed_gate_up_weight, routed_down_weight, attention_adapter_first, attention_adapter_second, feedforward_adapter_first, router_adapter_second, shared_gate_adapter_second, shared_down_adapter_first, routed_gate_adapter_second, routed_down_adapter_first, down_adapter_second):
    groups, group_rows, lane_width = layer_hidden_input.shape
    adapter_lanes = ADAPTER_COUNT * ADAPTER_RANK

    def layout(lengths, order):
        positions = jnp.arange(group_rows, dtype=jnp.int32)
        block_size = group_rows // order.shape[0]
        places_g = order[positions // block_size] * block_size + positions % block_size
        second_g = (places_g >= lengths[0]).astype(jnp.int32)
        return (places_g, second_g, places_g - lengths[0] * second_g)
    places, second, offsets = jax.vmap(layout)(sequence_pair_lengths, block_placement_order)
    chosen = jnp.take_along_axis(sequence_adapter_index, second, axis=1).reshape(-1)
    select_adapter_rows = (chosen[:, None] == (jnp.arange(adapter_lanes, dtype=jnp.int32) // ADAPTER_RANK)[None, :]).astype(jnp.float32)
    cosine, sine = rotary_parts(offsets.reshape(-1), HEAD_DIM)
    routes = token_expert_choices.reshape(-1, TOP)
    route_ids = routes.reshape(-1)
    count_routes = route_ids.shape[0]
    sort_order = jnp.argsort(route_ids, stable=True).astype(jnp.int32)
    sorted_ids = route_ids[sort_order]
    per_expert = lax.optimization_barrier(jnp.sum((route_ids[:, None] == jnp.arange(ROUTED_EXPERTS, dtype=jnp.int32)[None, :]).astype(jnp.int32), axis=0)).astype(jnp.int32)
    starts = (jnp.cumsum(per_expert) - per_expert).astype(jnp.int32)
    ranks = jnp.arange(count_routes, dtype=jnp.int32) - starts[sorted_ids]
    table = jnp.full((ROUTED_EXPERTS, EXPERT_ROWS), count_routes, jnp.int32).at[sorted_ids, ranks].set(sort_order)
    owner_table = table // TOP
    attn_norm_f = attention_norm_gain.astype(jnp.float32)
    ffn_norm_f = feedforward_norm_gain.astype(jnp.float32)
    w_qkv_f = query_key_value_weight.astype(jnp.float32)
    w_out_f = output_projection_weight.astype(jnp.float32)
    bias_f = query_key_value_bias.astype(jnp.float32)
    w_router_f = router_weight_matrix.astype(jnp.float32)
    shared_gate_up_f = shared_gate_up_weight.astype(jnp.float32)
    shared_down_f = shared_down_weight.astype(jnp.float32)
    shared_mix_f = shared_sigmoid_gate.astype(jnp.float32)
    expert_gate_up_f = routed_gate_up_weight.astype(jnp.float32)
    expert_down_f = routed_down_weight.astype(jnp.float32)

    def forward_pass(hidden, attn_in, attn_out, ffn_in, router_out, shared_out, shared_down_in, expert_out, expert_down_in, down_out):
        tokens_all = hidden.reshape(-1, lane_width)
        normed_one = low(rms_scale(tokens_all, attn_norm_f))
        query_key_value_lanes = low_rank(normed_one, attn_in[:3], select_adapter_rows)
        projected = []
        for which in range(3):
            lane_block = query_key_value_lanes[:, which * adapter_lanes:(which + 1) * adapter_lanes]
            value_pre = product(normed_one, w_qkv_f[which]) + bias_f[which] + product(lane_block, flattened_adapter_factor(attn_out[which]))
            projected.append(low_back(value_pre))
        heads_shape = (groups, group_rows, HEADS, HEAD_DIM)
        query = low(rotate(projected[0].reshape(-1, HEADS, HEAD_DIM), cosine, sine)).reshape(heads_shape)
        key_rows = low(rotate(projected[1].reshape(-1, HEADS, HEAD_DIM), cosine, sine)).reshape(heads_shape)
        value_rows = low(projected[2]).reshape(heads_shape)
        mixed = lax.map(jax.checkpoint(attention_core), (query, key_rows, value_rows, places, second))
        mixed = low(low_back(mixed.reshape(-1, lane_width)))
        out_lanes = low_rank(mixed, attn_in[3:], select_adapter_rows)
        attended = low_back(product(mixed, w_out_f) + product(out_lanes, flattened_adapter_factor(attn_out[3])))
        residual = tokens_all + attended
        normed_two = low(rms_scale(residual, ffn_norm_f))
        ffn_lanes = low_rank(normed_two, ffn_in, select_adapter_rows)
        logits = product(normed_two, w_router_f) + product(ffn_lanes[:, :adapter_lanes], flattened_adapter_factor(router_out))
        gates = jax.nn.softmax(jnp.take_along_axis(logits, routes, axis=1), axis=-1)
        padded_rows = jnp.concatenate([normed_two, jnp.zeros((1, lane_width), jnp.float32)], axis=0)
        padded_lanes = jnp.concatenate([ffn_lanes[:, 3 * adapter_lanes:], jnp.zeros((1, 2 * adapter_lanes), jnp.float32)], axis=0)
        routed_output_flattened = expert_out.reshape(2, adapter_lanes, -1)
        routed_down_flattened = flattened_adapter_factor(expert_down_in)

        def expert_core(inputs):
            gate_up, down, owners = inputs
            rows_in = low_back(padded_rows[owners])
            lanes_in = low_back(padded_lanes[owners])
            gate = low_back(product(rows_in, gate_up[0]) + product(lanes_in[:, :adapter_lanes], routed_output_flattened[0]))
            upper = low_back(product(rows_in, gate_up[1]) + product(lanes_in[:, adapter_lanes:], routed_output_flattened[1]))
            hidden_units = low(jax.nn.silu(gate) * upper)
            result = low(low_back(product(hidden_units, down)))
            side = low(low_back(product(hidden_units, routed_down_flattened.T)))
            return (result, side)
        results, sides = lax.map(jax.checkpoint(expert_core), (expert_gate_up_f, expert_down_f, owner_table))
        slots_flat = table.reshape(-1)
        routed = jnp.zeros((count_routes + 1, lane_width), jnp.float32).at[slots_flat].add(results.reshape(-1, lane_width))[:count_routes]
        routed_side = jnp.zeros((count_routes + 1, adapter_lanes), jnp.float32).at[slots_flat].add(sides.reshape(-1, adapter_lanes))[:count_routes]
        routed = routed.reshape(-1, TOP, lane_width)
        routed_side = routed_side.reshape(-1, TOP, adapter_lanes) * select_adapter_rows[:, None, :]
        side_out = jnp.einsum('tkr,rd->tkd', routed_side, flattened_adapter_factor(down_out[1]), precision=highest)
        mixture = lax.optimization_barrier(jnp.sum(gates[:, :, None] * (routed + side_out), axis=1))
        shared_flattened = shared_out.reshape(2, adapter_lanes, -1)
        shared_down_flattened = flattened_adapter_factor(shared_down_in)

        def shared_core(inputs):
            rows_in, lanes_in, pick_g = inputs
            gate = low_back(product(rows_in, shared_gate_up_f[0]) + product(lanes_in[:, :adapter_lanes], shared_flattened[0]))
            upper = low_back(product(rows_in, shared_gate_up_f[1]) + product(lanes_in[:, adapter_lanes:], shared_flattened[1]))
            hidden_units = low(jax.nn.silu(gate) * upper)
            side = low(low_back(product(hidden_units, shared_down_flattened.T)) * pick_g)
            return low_back(product(hidden_units, shared_down_f) + product(side, flattened_adapter_factor(down_out[0])))
        shared_value = lax.map(jax.checkpoint(shared_core), (normed_two.reshape(groups, group_rows, lane_width), ffn_lanes[:, adapter_lanes:3 * adapter_lanes].reshape(groups, group_rows, 2 * adapter_lanes), select_adapter_rows.reshape(groups, group_rows, adapter_lanes))).reshape(-1, lane_width)
        mix_gate = jax.nn.sigmoid(product(normed_two, shared_mix_f))
        result_all = residual + mixture + mix_gate[:, None] * shared_value
        return result_all.reshape(groups, group_rows, lane_width)
    layer_result_value, backward_pullback = jax.vjp(forward_pass, layer_hidden_input.astype(jnp.float32), attention_adapter_first.astype(jnp.float32), attention_adapter_second.astype(jnp.float32), feedforward_adapter_first.astype(jnp.float32), router_adapter_second.astype(jnp.float32), shared_gate_adapter_second.astype(jnp.float32), shared_down_adapter_first.astype(jnp.float32), routed_gate_adapter_second.astype(jnp.float32), routed_down_adapter_first.astype(jnp.float32), down_adapter_second.astype(jnp.float32))
    grads = backward_pullback(output_cotangent.astype(jnp.float32))
    return (layer_result_value.astype(jnp.bfloat16), grads[0].astype(jnp.bfloat16), grads[1], grads[2], grads[3], grads[4], grads[5], grads[6], grads[7], grads[8], grads[9])
```

```python
import functools

import jax
import jax.numpy as jnp
from jax import lax
from jax.experimental import pallas as pl
from jax.experimental.pallas import tpu as pltpu
from jax.sharding import PartitionSpec as P

HEADS = 16
HEAD_DIM = 128
TOP = 4
ADAPTER_COUNT = 8
RANK = 16
LANES = ADAPTER_COUNT * RANK
PAIR = 2 * RANK
MAIN = 32

norm_eps = 1e-06
rope_theta = 1000000.0
masked_score = -1e30
highest = lax.Precision.HIGHEST
MESH = pl.DeviceIdType.MESH
BF = jnp.bfloat16
F32 = jnp.float32
VMEM_LIMIT = 56 * 2**20


def dot(left, right):
    return jnp.dot(left, right, preferred_element_type=F32)


def dot_nt(left, right):
    return lax.dot_general(left, right, (((1,), (1,)), ((), ())), preferred_element_type=F32)


def dot_tn(left, right):
    return lax.dot_general(left, right, (((0,), (0,)), ((), ())), preferred_element_type=F32)


GROUP_SIZE = {"x": 4, "y": 2, "c": 8, "f": 16}


def place_in(group):
    ctx, fsdp = lax.axis_index("ctx"), lax.axis_index("fsdp")
    return {"x": ctx // 2, "y": ctx % 2, "c": ctx, "f": fsdp}[group]


def device_of(group, index):
    ctx, fsdp = lax.axis_index("ctx"), lax.axis_index("fsdp")
    if group == "x":
        return (index * 2 + ctx % 2, fsdp)
    if group == "y":
        return ((ctx // 2) * 2 + index, fsdp)
    if group == "c":
        return (index, fsdp)
    return (ctx, index)


def exchanged_shape(kind, group, shape):
    count = GROUP_SIZE[group]
    if kind == "gather":
        return (count,) + shape
    if kind == "swap":
        return shape
    if kind == "from_columns":
        return (count, shape[0], shape[1] // count)
    return (shape[1], count * shape[2])


def exchange_kernel(plan, *refs):
    amount = len(plan)
    inputs, outputs = refs[:amount], refs[amount : 2 * amount]
    send_sem, recv_sem, local_sem = refs[2 * amount :]
    groups = []
    for kind, group in plan:
        if group not in groups:
            groups.append(group)
    barrier = pltpu.get_barrier_semaphore()
    for group in groups:
        for offset in range(1, GROUP_SIZE[group]):
            peer = lax.rem(place_in(group) + offset, GROUP_SIZE[group])
            pl.semaphore_signal(
                barrier, inc=1, device_id=device_of(group, peer), device_id_type=MESH
            )
    pl.semaphore_wait(barrier, sum(GROUP_SIZE[group] - 1 for group in groups))

    def source(item, index):
        kind, group = plan[item]
        if kind == "gather":
            return inputs[item]
        if kind == "from_columns":
            width = inputs[item].shape[1] // GROUP_SIZE[group]
            return inputs[item].at[:, pl.ds(pl.multiple_of(index * width, width), width)]
        return inputs[item].at[index]

    def target(item, index):
        kind, group = plan[item]
        if kind == "to_columns":
            width = inputs[item].shape[2]
            return outputs[item].at[:, pl.ds(pl.multiple_of(index * width, width), width)]
        return outputs[item].at[index]

    copies = []
    slot = 0
    for item, (kind, group) in enumerate(plan):
        count = GROUP_SIZE[group]
        mine = place_in(group)
        for offset in range(1, count):
            peer = lax.rem(mine + offset, count)
            copy = pltpu.make_async_remote_copy(
                src_ref=source(item, peer),
                dst_ref=target(item, mine),
                send_sem=send_sem.at[slot],
                recv_sem=recv_sem.at[slot],
                device_id=device_of(group, peer),
                device_id_type=MESH,
            )
            copy.start()
            copies.append(copy)
            slot += 1
    for item, (kind, group) in enumerate(plan):
        mine = place_in(group)
        copy = pltpu.make_async_copy(source(item, mine), target(item, mine), local_sem.at[item])
        copy.start()
        copies.append(copy)
    for copy in copies:
        copy.wait()


def exchange(name, number, *items):
    plan = tuple((kind, group) for kind, group, array in items)
    arrays = [array for kind, group, array in items]
    slots = sum(GROUP_SIZE[group] - 1 for kind, group in plan)
    return pl.pallas_call(
        functools.partial(exchange_kernel, plan),
        out_shape=[
            jax.ShapeDtypeStruct(exchanged_shape(kind, group, array.shape), array.dtype)
            for kind, group, array in items
        ],
        in_specs=[pl.BlockSpec(memory_space=pl.ANY)] * len(items),
        out_specs=[pl.BlockSpec(memory_space=pl.ANY)] * len(items),
        scratch_shapes=[
            pltpu.SemaphoreType.DMA((slots,)),
            pltpu.SemaphoreType.DMA((slots,)),
            pltpu.SemaphoreType.DMA((len(items),)),
        ],
        compiler_params=pltpu.CompilerParams(collective_id=number, has_side_effects=True),
        name=name,
    )(*arrays)


def half_turn(values):
    parts = []
    for head in range(values.shape[1] // HEAD_DIM):
        part = values[:, head * HEAD_DIM : (head + 1) * HEAD_DIM]
        parts.append(jnp.concatenate([part[:, 64:], part[:, :64]], axis=1))
    return jnp.concatenate(parts, axis=1) if len(parts) > 1 else parts[0]


def project_kernel(rows_ref, weight_ref, lanes_ref, second_ref, bias_ref, cos_ref, sin_ref, out_ref):
    weight = weight_ref[...].reshape(rows_ref.shape[1], weight_ref.shape[3])
    value = dot(rows_ref[...], weight) + bias_ref[0].astype(F32) + dot(lanes_ref[0], second_ref[0])
    copies = value.shape[1] // HEAD_DIM
    cosine = jnp.concatenate([cos_ref[...]] * copies, axis=1)
    sine = jnp.concatenate([sin_ref[...]] * copies, axis=1)
    turned = value * cosine + half_turn(value) * sine
    out_ref[0] = jnp.where(pl.program_id(0) < 2, turned, value).astype(BF)


def project(rows, weight, lanes, second, bias, cosine, sine):
    tokens, width = rows.shape
    columns = weight.shape[3]
    step = 256
    return pl.pallas_call(
        project_kernel,
        grid=(3, columns // step),
        out_shape=jax.ShapeDtypeStruct((3, tokens, columns), BF),
        in_specs=[
            pl.BlockSpec((tokens, width), lambda j, n: (0, 0)),
            pl.BlockSpec((weight.shape[0], 1, weight.shape[2], step), lambda j, n: (0, j, 0, n)),
            pl.BlockSpec((1, tokens, PAIR), lambda j, n: (j, 0, 0)),
            pl.BlockSpec((1, PAIR, step), lambda j, n: (j, 0, n)),
            pl.BlockSpec((1, 1, step), lambda j, n: (j, 0, n)),
            pl.BlockSpec((tokens, HEAD_DIM), lambda j, n: (0, 0)),
            pl.BlockSpec((tokens, HEAD_DIM), lambda j, n: (0, 0)),
        ],
        out_specs=pl.BlockSpec((1, tokens, step), lambda j, n: (j, 0, n)),
        compiler_params=pltpu.CompilerParams(vmem_limit_bytes=VMEM_LIMIT),
        name="project",
    )(rows, weight, lanes, second, bias, cosine, sine)


def back_project_kernel(grads_ref, weight_ref, out_ref):
    total = None
    for j in range(3):
        weight = weight_ref[:, j].reshape(-1, weight_ref.shape[3])
        part = dot_nt(grads_ref[j], weight)
        total = part if total is None else total + part
    out_ref[...] = total.astype(BF)


def back_project(grads, weight):
    tokens = grads.shape[1]
    shards, unused, depth, columns = weight.shape
    step = 4
    return pl.pallas_call(
        back_project_kernel,
        grid=(shards // step,),
        out_shape=jax.ShapeDtypeStruct((tokens, shards * depth), BF),
        in_specs=[
            pl.BlockSpec((3, tokens, columns), lambda n: (0, 0, 0)),
            pl.BlockSpec((step, 3, depth, columns), lambda n: (n, 0, 0, 0)),
        ],
        out_specs=pl.BlockSpec((tokens, step * depth), lambda n: (0, n)),
        compiler_params=pltpu.CompilerParams(vmem_limit_bytes=VMEM_LIMIT),
        name="back_project",
    )(grads, weight)


def probabilities(query, keys, query_place, query_start, key_place):
    scores = dot_nt(query, keys) * (HEAD_DIM**-0.5)
    allowed = (key_place <= query_place) & (key_place >= query_start)
    scores = jnp.where(allowed, scores, masked_score)
    top = jnp.max(scores, axis=1, keepdims=True)
    raised = jnp.exp(scores - top)
    return raised * (1.0 / jnp.sum(raised, axis=1, keepdims=True))


def attend_kernel(query_ref, key_ref, value_ref, place_ref, start_ref, key_place_ref, out_ref):
    keys = key_ref[...].reshape(-1, HEAD_DIM)
    values = value_ref[...].reshape(-1, HEAD_DIM)
    probs = probabilities(query_ref[0], keys, place_ref[...], start_ref[...], key_place_ref[...])
    out_ref[...] = dot(probs.astype(BF), values).astype(BF)


def attend(projected, pairs, place, start, key_place):
    tokens, columns = projected.shape[1:]
    step = 256
    keys = pairs.shape[0] * pairs.shape[2]
    half = pairs.shape[2]
    return pl.pallas_call(
        attend_kernel,
        grid=(columns // HEAD_DIM, tokens // step),
        out_shape=jax.ShapeDtypeStruct((tokens, columns), BF),
        in_specs=[
            pl.BlockSpec((1, step, HEAD_DIM), lambda h, i: (0, i, h)),
            pl.BlockSpec((2, 1, half, HEAD_DIM), lambda h, i: (0, 0, 0, h)),
            pl.BlockSpec((2, 1, half, HEAD_DIM), lambda h, i: (0, 1, 0, h)),
            pl.BlockSpec((step, 1), lambda h, i: (i, 0)),
            pl.BlockSpec((step, 1), lambda h, i: (i, 0)),
            pl.BlockSpec((1, keys), lambda h, i: (0, 0)),
        ],
        out_specs=pl.BlockSpec((step, HEAD_DIM), lambda h, i: (i, h)),
        compiler_params=pltpu.CompilerParams(vmem_limit_bytes=VMEM_LIMIT),
        name="attend",
    )(projected, pairs, pairs, place, start, key_place)


def attend_back_kernel(
    query_ref,
    key_ref,
    value_ref,
    grad_ref,
    place_ref,
    start_ref,
    key_place_ref,
    cos_ref,
    sin_ref,
    query_out,
    pair_out,
    key_total,
    value_total,
):
    step = pl.program_id(1)
    query = query_ref[0]
    grad = grad_ref[...]
    keys = key_ref[...].reshape(-1, HEAD_DIM)
    values = value_ref[...].reshape(-1, HEAD_DIM)
    probs = probabilities(query, keys, place_ref[...], start_ref[...], key_place_ref[...])
    grad_probs = dot_nt(grad, values)
    mean = jnp.sum(probs * grad_probs, axis=1, keepdims=True)
    grad_scores = (probs * (grad_probs - mean)).astype(BF)
    grad_query = dot(grad_scores, keys) * (HEAD_DIM**-0.5)
    query_out[...] = (grad_query * cos_ref[...] - half_turn(grad_query) * sin_ref[...]).astype(BF)
    grad_keys = dot_tn(grad_scores, query) * (HEAD_DIM**-0.5)
    grad_values = dot_tn(probs.astype(BF), grad)

    @pl.when(step == 0)
    def first():
        key_total[...] = grad_keys
        value_total[...] = grad_values

    @pl.when(step > 0)
    def later():
        key_total[...] += grad_keys
        value_total[...] += grad_values

    half = pair_out.shape[2]
    for side in range(2):
        pair_out[side, 0] = key_total[side * half : (side + 1) * half, :].astype(BF)
        pair_out[side, 1] = value_total[side * half : (side + 1) * half, :].astype(BF)


def attend_back(projected, pairs, grads, place, start, key_place, cosine, sine):
    tokens, columns = projected.shape[1:]
    step = 256
    keys = pairs.shape[0] * pairs.shape[2]
    half = pairs.shape[2]
    return pl.pallas_call(
        attend_back_kernel,
        grid=(columns // HEAD_DIM, tokens // step),
        out_shape=[
            jax.ShapeDtypeStruct((tokens, columns), BF),
            jax.ShapeDtypeStruct(pairs.shape, BF),
        ],
        in_specs=[
            pl.BlockSpec((1, step, HEAD_DIM), lambda h, i: (0, i, h)),
            pl.BlockSpec((2, 1, half, HEAD_DIM), lambda h, i: (0, 0, 0, h)),
            pl.BlockSpec((2, 1, half, HEAD_DIM), lambda h, i: (0, 1, 0, h)),
            pl.BlockSpec((step, HEAD_DIM), lambda h, i: (i, h)),
            pl.BlockSpec((step, 1), lambda h, i: (i, 0)),
            pl.BlockSpec((step, 1), lambda h, i: (i, 0)),
            pl.BlockSpec((1, keys), lambda h, i: (0, 0)),
            pl.BlockSpec((step, HEAD_DIM), lambda h, i: (i, 0)),
            pl.BlockSpec((step, HEAD_DIM), lambda h, i: (i, 0)),
        ],
        out_specs=[
            pl.BlockSpec((step, HEAD_DIM), lambda h, i: (i, h)),
            pl.BlockSpec((2, 2, half, HEAD_DIM), lambda h, i: (0, 0, 0, h)),
        ],
        scratch_shapes=[pltpu.VMEM((keys, HEAD_DIM), F32), pltpu.VMEM((keys, HEAD_DIM), F32)],
        compiler_params=pltpu.CompilerParams(vmem_limit_bytes=VMEM_LIMIT),
        name="attend_back",
    )(projected, pairs, pairs, grads, place, start, key_place, cosine, sine)


def rms_forward(values, gain):
    mean_square = jnp.mean(values * values, axis=-1, keepdims=True)
    return values * lax.rsqrt(mean_square + norm_eps) * gain.astype(F32)


def rms_backward(values, gain, grad_result):
    scale = lax.rsqrt(jnp.mean(values * values, axis=-1, keepdims=True) + norm_eps)
    scaled = gain.astype(F32) * grad_result
    inner = jnp.mean(values * scaled, axis=-1, keepdims=True)
    return scale * scaled - values * (scale * scale * scale) * inner


def swiglu_backward(gate, upper, grad_hidden):
    sigma = jax.nn.sigmoid(gate)
    grad_gate = grad_hidden * upper * sigma * (1.0 + gate * (1.0 - sigma))
    grad_upper = grad_hidden * gate * sigma
    return (grad_gate.astype(BF), grad_upper.astype(BF))


def two_parts(values):
    high = values.astype(BF)
    return high, (values - high.astype(F32)).astype(BF)


def shards(
    layer_hidden_input,
    output_cotangent,
    sequence_pair_lengths,
    block_placement_order,
    sequence_adapter_index,
    token_expert_choices,
    attention_norm_gain,
    feedforward_norm_gain,
    query_key_value_weight,
    output_projection_weight,
    query_key_value_bias,
    router_weight_matrix,
    shared_gate_up_weight,
    shared_down_weight,
    shared_sigmoid_gate,
    routed_gate_up_weight,
    routed_down_weight,
    attention_adapter_first,
    attention_adapter_second,
    feedforward_adapter_first,
    router_adapter_second,
    shared_gate_adapter_second,
    shared_down_adapter_first,
    routed_gate_adapter_second,
    routed_down_adapter_first,
    down_adapter_second,
):
    tokens, width = layer_hidden_input.shape[1:]
    experts = router_weight_matrix.shape[1]
    capacity = tokens * TOP // experts * 9 // 8
    tail = capacity - MAIN
    ctx_count = lax.axis_size("ctx")
    group_rows = tokens * ctx_count
    along = ctx_count // 2
    rows_shared = tokens * along
    x_index = lax.axis_index("ctx") // 2
    y_index = lax.axis_index("ctx") % 2
    head_columns = width // along
    hidden = shared_down_weight.shape[0]
    quarter = hidden // along
    shards_of = lax.axis_size("fsdp")
    lengths = sequence_pair_lengths[0]
    order = block_placement_order[0]
    adapters = sequence_adapter_index[0]
    block_size = group_rows // order.shape[0]

    qkv = lax.all_gather(
        lax.dynamic_slice_in_dim(query_key_value_weight, x_index * head_columns, head_columns, 2),
        "fsdp",
    )
    out_weight = lax.all_gather(output_projection_weight, "fsdp", tiled=True)
    gate_up_part = lax.dynamic_slice_in_dim(shared_gate_up_weight, x_index * quarter, quarter, 2)
    gate_up_part = jnp.swapaxes(gate_up_part, 1, 2)
    gate_weight = lax.all_gather(gate_up_part[0], "fsdp", tiled=True)
    up_weight = lax.all_gather(gate_up_part[1], "fsdp", tiled=True)
    down_weight = lax.all_gather(
        lax.dynamic_slice_in_dim(shared_down_weight, x_index * quarter, quarter, 0),
        "fsdp",
        tiled=True,
    )

    def of_group(factor):
        parts = [lax.dynamic_index_in_dim(factor, adapters[s], -3, keepdims=True) for s in range(2)]
        both = jnp.concatenate(parts, axis=-3)
        return both.reshape(both.shape[:-3] + (PAIR, both.shape[-1]))

    def own_quarter(factor):
        parts = factor.reshape(factor.shape[:-1] + (shards_of, along, quarter))
        part = lax.dynamic_index_in_dim(parts, x_index, parts.ndim - 2, keepdims=False)
        return part.reshape(factor.shape[:-1] + (shards_of * quarter,))

    attn_first = of_group(attention_adapter_first)
    attn_second = of_group(attention_adapter_second)
    ffn_first = of_group(feedforward_adapter_first)
    router_second = of_group(router_adapter_second)
    shared_second = own_quarter(of_group(shared_gate_adapter_second))
    shared_first = own_quarter(of_group(shared_down_adapter_first))
    down_second_shared = of_group(down_adapter_second[0])

    def layout(positions):
        places = order[positions // block_size] * block_size + positions % block_size
        second = (places >= lengths[0]).astype(jnp.int32)
        return (places, second, places - lengths[0] * second)

    rows_of = jnp.arange(rows_shared, dtype=jnp.int32)

    def positions_of(side):
        return (2 * (rows_of // tokens) + side) * tokens + rows_of % tokens

    places, second, offsets = layout(positions_of(y_index))
    key_places = jnp.concatenate([layout(positions_of(side))[0] for side in range(2)])
    own_second = lax.dynamic_slice_in_dim(second, x_index * tokens, tokens)
    pair_lane = jnp.arange(PAIR, dtype=jnp.int32) // RANK
    pick_shared = (second[:, None] == pair_lane[None, :]).astype(F32)
    pick = (own_second[:, None] == pair_lane[None, :]).astype(F32)
    fractions = jnp.arange(0, HEAD_DIM, 2).astype(F32) / HEAD_DIM
    angles = offsets.astype(F32)[:, None] * (rope_theta ** (-fractions))[None, :]
    cosine, sine = jnp.cos(angles), jnp.sin(angles)
    cosine = jnp.concatenate([cosine, cosine], axis=1)
    sine = jnp.concatenate([-sine, sine], axis=1)
    place_column = places[:, None]
    start_column = (second * lengths[0])[:, None]
    key_row = key_places[None, :]

    tokens_f = layer_hidden_input[0].astype(F32)
    normed_one = rms_forward(tokens_f, attention_norm_gain).astype(BF)
    (normed_shared,) = exchange("gather_first", 0, ("gather", "x", normed_one))
    normed_shared = normed_shared.reshape(rows_shared, width)
    qkv_lanes = (
        dot_nt(normed_shared, attn_first[:3].reshape(3 * PAIR, width)) * jnp.tile(pick_shared, (1, 3))
    ).astype(BF)
    qkv_lanes = qkv_lanes.reshape(rows_shared, 3, PAIR).transpose(1, 0, 2)
    head_second = lax.dynamic_slice_in_dim(
        attn_second[:3], x_index * head_columns, head_columns, 2
    )
    head_bias = lax.dynamic_slice_in_dim(
        query_key_value_bias, x_index * head_columns, head_columns, 1
    )
    projected = project(
        normed_shared, qkv, qkv_lanes, head_second, head_bias[:, None, :], cosine, sine
    )
    (pairs,) = exchange("keys", 1, ("gather", "y", projected[1:]))
    mixed_heads = attend(projected, pairs, place_column, start_column, key_row)

    routes = token_expert_choices[0]
    route_hot = (routes[:, :, None] == jnp.arange(experts)[None, None, :]).astype(F32)
    route_flat = routes.reshape(-1)
    route_count = (route_flat[:, None] == jnp.arange(experts)[None, :]).astype(jnp.int32)
    earlier = jnp.cumsum(route_count, axis=0) - route_count
    rank = jnp.sum(earlier * route_count, axis=1)
    slots = jnp.where(
        rank < MAIN,
        route_flat * MAIN + rank,
        experts * MAIN + route_flat * tail + (rank - MAIN),
    )
    slot_count = experts * capacity
    main_count = experts * MAIN
    by_choice = slots.reshape(tokens, TOP)
    hot = (by_choice[:, :, None] == jnp.arange(slot_count)[None, None, :]).astype(BF)
    gather_rows = jnp.sum(hot, axis=1)

    def to_slots(rows):
        return dot_tn(gather_rows, rows)

    def split_rows(rows):
        main = rows[:main_count].reshape(experts, MAIN, width)
        rest = rows[main_count:].reshape(experts, 16, tail * width // 16)
        return main, rest

    def join_rows(main, rest):
        return jnp.concatenate(
            [main.reshape(main_count, width), rest.reshape(experts * tail, width)], axis=0
        )

    def split_lanes(lanes):
        main = lanes[:main_count].reshape(experts, MAIN, -1)
        rest = lanes[main_count:].reshape(experts, tail, -1)
        rest = jnp.pad(rest, ((0, 0), (0, 16 - tail), (0, 0)))
        return jnp.concatenate([main, rest], axis=1)

    def join_lanes(lanes):
        return jnp.concatenate(
            [
                lanes[:, :MAIN].reshape(main_count, -1),
                lanes[:, MAIN:capacity].reshape(experts * tail, -1),
            ],
            axis=0,
        )

    grad_out = output_cotangent[0]
    grad_out_f = grad_out.astype(F32)
    sent_grads = split_rows(to_slots(grad_out).astype(BF))
    mixed, grads_shared, got_main, got_rest = exchange(
        "mixed",
        2,
        ("to_columns", "x", mixed_heads.reshape(along, tokens, head_columns)),
        ("gather", "x", grad_out),
        ("swap", "f", sent_grads[0]),
        ("swap", "f", sent_grads[1]),
    )
    grads_shared = grads_shared.reshape(rows_shared, width)
    expert_grads = join_rows(got_main, got_rest)

    out_lanes = (dot_nt(mixed, attn_first[3]) * pick).astype(BF)
    residual = tokens_f + (dot(mixed, out_weight) + dot(out_lanes, attn_second[3]))
    normed_two = rms_forward(residual, feedforward_norm_gain).astype(BF)
    router_lanes = (dot_nt(normed_two, ffn_first[0]) * pick).astype(BF)
    logits = dot(normed_two, router_weight_matrix) + dot(router_lanes, router_second)
    gates = jax.nn.softmax(jnp.sum(route_hot * logits[:, None, :], axis=-1), axis=-1)
    hot_f = hot.astype(F32)
    slot_gates = jnp.sum(hot_f * gates[:, :, None], axis=(0, 1))
    own_adapter = adapters[own_second]
    adapter_hot = (own_adapter[:, None] == jnp.arange(ADAPTER_COUNT)[None, :]).astype(BF)
    slot_adapters = to_slots(adapter_hot).astype(BF)
    gate_high, gate_low = two_parts(slot_gates[:, None])
    notes = jnp.concatenate([slot_adapters, gate_high, gate_low], axis=1)
    notes = jnp.pad(notes, ((0, 0), (0, 128 - notes.shape[1])))
    sent_main, sent_rest = split_rows(to_slots(normed_two).astype(BF))
    second_shared, got_main, got_rest, got_notes = exchange(
        "dispatch",
        3,
        ("gather", "x", normed_two),
        ("swap", "f", sent_main),
        ("swap", "f", sent_rest),
        ("swap", "f", split_lanes(notes)),
    )
    second_shared = second_shared.reshape(rows_shared, width)
    expert_rows = join_rows(got_main, got_rest)
    expert_notes = join_lanes(got_notes)

    shared_lanes = (
        dot_nt(second_shared, ffn_first[1:3].reshape(2 * PAIR, width))
        * jnp.tile(pick_shared, (1, 2))
    ).astype(BF)
    shared_gate = dot_nt(second_shared, gate_weight) + dot(shared_lanes[:, :PAIR], shared_second[0])
    shared_upper = dot_nt(second_shared, up_weight) + dot(shared_lanes[:, PAIR:], shared_second[1])
    shared_hidden = (jax.nn.silu(shared_gate) * shared_upper).astype(BF)
    shared_part = dot(shared_hidden, down_weight)
    shared_side = dot_nt(shared_hidden, shared_first) * pick_shared
    shared_mix = jax.nn.sigmoid(dot(second_shared, shared_sigmoid_gate))
    grads_shared_f = grads_shared.astype(F32)
    grad_shared = (shared_mix[:, None] * grads_shared_f).astype(BF)
    grad_side_shared = (dot_nt(grad_shared, down_second_shared) * pick_shared).astype(BF)
    grad_hidden = dot_nt(grad_shared, down_weight) + dot(grad_side_shared, shared_first)
    grad_gate, grad_upper = swiglu_backward(shared_gate, shared_upper, grad_hidden)
    grad_second_part = dot(grad_gate, gate_weight) + dot(grad_upper, up_weight)
    grad_lanes_part = jnp.concatenate(
        [
            dot_nt(grad_gate, shared_second[0]) * pick_shared,
            dot_nt(grad_upper, shared_second[1]) * pick_shared,
        ],
        axis=1,
    )
    mix_sum = jnp.sum(grads_shared_f * shared_part, axis=1, keepdims=True)
    lanes_part = jnp.concatenate(
        [shared_side.astype(BF), grad_lanes_part.astype(BF), *two_parts(mix_sum)], axis=1
    )
    lanes_part = jnp.pad(lanes_part, ((0, 0), (0, 128 - lanes_part.shape[1])))
    grad_shared_rows = jnp.concatenate(
        [
            dot_tn(shared_lanes[:, :PAIR], grad_gate),
            dot_tn(shared_lanes[:, PAIR:], grad_upper),
            dot_tn(grad_side_shared, shared_hidden),
        ],
        axis=0,
    )

    spread = (
        jnp.arange(128)[:, None] == (jnp.arange(LANES) // RANK)[None, :]
    ).astype(BF)
    expert_pick = dot(expert_notes, spread)
    expert_gate_of = (
        expert_notes[:, ADAPTER_COUNT : ADAPTER_COUNT + 1].astype(F32)
        + expert_notes[:, ADAPTER_COUNT + 1 : ADAPTER_COUNT + 2].astype(F32)
    )
    routed_second = routed_gate_adapter_second.reshape(2, LANES, -1)
    routed_first = routed_down_adapter_first.reshape(LANES, -1)
    expert_down_second = down_adapter_second[1].reshape(LANES, width)
    expert_lanes = (
        dot_nt(expert_rows, feedforward_adapter_first[3:].reshape(2 * LANES, width))
        * jnp.tile(expert_pick, (1, 2))
    ).astype(BF)
    weight_gate = routed_gate_up_weight[0, 0]
    weight_upper = routed_gate_up_weight[0, 1]
    weight_down = routed_down_weight[0]
    expert_gate = dot(expert_rows, weight_gate) + dot(expert_lanes[:, :LANES], routed_second[0])
    expert_upper = dot(expert_rows, weight_upper) + dot(expert_lanes[:, LANES:], routed_second[1])
    expert_hidden = (jax.nn.silu(expert_gate) * expert_upper).astype(BF)
    expert_side = (
        dot_nt(expert_hidden, routed_first).astype(BF).astype(F32) * expert_pick
    ).astype(BF)
    expert_value = dot(expert_hidden, weight_down) + dot(expert_side, expert_down_second)
    expert_grads_f = expert_grads.astype(F32)
    expert_result = (expert_gate_of * expert_value).astype(BF)
    expert_gate_grad = jnp.sum(expert_grads_f * expert_value, axis=1, keepdims=True)
    grad_routed = (expert_gate_of * expert_grads_f).astype(BF)
    grad_side_routed = (
        dot_nt(expert_grads, expert_down_second) * expert_gate_of * expert_pick
    ).astype(BF)
    grad_expert_hidden = dot_nt(grad_routed, weight_down) + dot(grad_side_routed, routed_first)
    grad_expert_gate, grad_expert_upper = swiglu_backward(
        expert_gate, expert_upper, grad_expert_hidden
    )
    back_rows = (
        dot_nt(grad_expert_gate, weight_gate) + dot_nt(grad_expert_upper, weight_upper)
    ).astype(BF)
    fold = ((jnp.arange(LANES) % RANK)[:, None] == jnp.arange(RANK)[None, :]).astype(BF)
    back_lanes = [
        dot((dot_nt(grad, second) * expert_pick).astype(BF), fold).astype(BF)
        for grad, second in (
            (grad_expert_gate, routed_second[0]),
            (grad_expert_upper, routed_second[1]),
        )
    ]
    back_notes = jnp.concatenate([*back_lanes, *two_parts(expert_gate_grad)], axis=1)
    back_notes = jnp.pad(back_notes, ((0, 0), (0, 128 - back_notes.shape[1])))
    grad_expert_rows = jnp.concatenate(
        [
            dot_tn(expert_lanes[:, :LANES], grad_expert_gate),
            dot_tn(expert_lanes[:, LANES:], grad_expert_upper),
            dot_tn(grad_side_routed, expert_hidden),
        ],
        axis=0,
    )
    grad_down_expert = dot_tn(expert_side, grad_routed)

    back_main, back_rest = split_rows(back_rows)
    parts_rows, parts_lanes, got_main, got_rest, got_notes = exchange(
        "collect",
        4,
        ("swap", "x", grad_second_part.astype(BF).reshape(along, tokens, width)),
        ("swap", "x", lanes_part.reshape(along, tokens, 128)),
        ("swap", "f", back_main),
        ("swap", "f", back_rest),
        ("swap", "f", split_lanes(back_notes)),
    )
    returned_rows = join_rows(got_main, got_rest)
    returned_notes = join_lanes(got_notes)

    lanes_sum = jnp.sum(parts_lanes.astype(F32), axis=0)
    side_shared = lanes_sum[:, :PAIR].astype(BF)
    mix_gate = jax.nn.sigmoid(dot(normed_two, shared_sigmoid_gate))
    mix_total = (
        lanes_sum[:, 3 * PAIR]
        + lanes_sum[:, 3 * PAIR + 1]
        + jnp.sum(side_shared.astype(F32) * dot_nt(grad_out, down_second_shared), axis=1)
    )
    grad_mix = mix_total * mix_gate * (1.0 - mix_gate)
    grad_shared_own = (mix_gate[:, None] * grad_out_f).astype(BF)
    grad_down_shared = dot_tn(side_shared, grad_shared_own)
    gate_notes = returned_notes[:, 2 * RANK : 2 * RANK + 2].astype(F32)
    slot_gate_grads = gate_notes[:, 0] + gate_notes[:, 1]
    grad_gates = jnp.sum(hot_f * slot_gate_grads[None, None, :], axis=2)
    grad_chosen = gates * (grad_gates - jnp.sum(gates * grad_gates, axis=-1, keepdims=True))
    grad_logits = jnp.sum(grad_chosen[:, :, None] * route_hot, axis=1)
    grad_router_lanes = jnp.dot(grad_logits, router_second.astype(F32).T, precision=highest)
    grad_router_out = jnp.dot(router_lanes.astype(F32).T, grad_logits, precision=highest)
    token_notes = dot(gather_rows, returned_notes)
    grad_expert_lanes = jnp.concatenate(
        [
            token_notes[:, :RANK],
            token_notes[:, :RANK],
            token_notes[:, RANK : 2 * RANK],
            token_notes[:, RANK : 2 * RANK],
        ],
        axis=1,
    )
    ffn_lane_grads = (
        jnp.concatenate(
            [grad_router_lanes, lanes_sum[:, PAIR : 3 * PAIR], grad_expert_lanes], axis=1
        )
        * jnp.tile(pick, (1, 5))
    ).astype(BF)
    grad_second = (
        grad_mix[:, None] * shared_sigmoid_gate.astype(F32)[None, :]
        + jnp.dot(grad_logits, router_weight_matrix.astype(F32).T, precision=highest)
        + jnp.sum(parts_rows.astype(F32), axis=0)
        + dot(gather_rows, returned_rows)
        + dot(ffn_lane_grads, ffn_first.reshape(5 * PAIR, width))
    )
    grad_ffn_rows = dot_tn(ffn_lane_grads, normed_two)
    grad_residual = grad_out_f + rms_backward(residual, feedforward_norm_gain, grad_second)
    grad_attended = grad_residual.astype(BF)
    grad_attn_out_last = dot_tn(out_lanes, grad_attended)
    grad_out_lanes = (dot_nt(grad_attended, attn_second[3]) * pick).astype(BF)
    grad_attn_in_last = dot_tn(grad_out_lanes, mixed)
    grad_mixed = (dot_nt(grad_attended, out_weight) + dot(grad_out_lanes, attn_first[3])).astype(BF)

    result_main, result_rest = split_rows(expert_result)
    grad_heads, value_parts, got_main, got_rest = exchange(
        "results",
        5,
        ("from_columns", "x", grad_mixed),
        ("swap", "x", shared_part.astype(BF).reshape(along, tokens, width)),
        ("swap", "f", result_main),
        ("swap", "f", result_rest),
    )
    mixture = dot(gather_rows, join_rows(got_main, got_rest))
    shared_value = jnp.sum(value_parts.astype(F32), axis=0) + dot(side_shared, down_second_shared)
    output_value = residual + mixture + mix_gate[:, None] * shared_value

    grad_query, grad_pairs = attend_back(
        projected,
        pairs,
        grad_heads.reshape(rows_shared, head_columns),
        place_column,
        start_column,
        key_row,
        cosine,
        sine,
    )
    (pair_parts,) = exchange("key_grads", 6, ("swap", "y", grad_pairs))
    pair_sum = jnp.sum(pair_parts.astype(F32), axis=0)
    key_sum = pair_sum[0].reshape(rows_shared, -1, HEAD_DIM)
    key_turned = jnp.concatenate([key_sum[..., 64:], key_sum[..., :64]], axis=-1)
    grad_key = key_sum * cosine[:, None, :] - key_turned * sine[:, None, :]
    grad_projected = jnp.stack(
        [grad_query, grad_key.reshape(rows_shared, head_columns).astype(BF), pair_sum[1].astype(BF)]
    )
    first_part = back_project(grad_projected, qkv)
    lanes_first_part = jnp.einsum(
        "jte,jre->tjr", grad_projected, head_second, preferred_element_type=F32
    )
    lanes_first_part = (lanes_first_part * pick_shared[:, None, :]).astype(BF)
    lanes_first_part = jnp.pad(
        lanes_first_part.reshape(rows_shared, 3 * PAIR), ((0, 0), (0, 128 - 3 * PAIR))
    )
    grad_attn_out_heads = jnp.einsum(
        "jtr,jte->jre", qkv_lanes, grad_projected, preferred_element_type=F32
    ).reshape(3 * PAIR, head_columns)

    def by_shard(rows):
        blocks = rows.astype(BF).reshape(rows.shape[0], shards_of, -1)
        blocks = blocks.transpose(1, 0, 2)
        return jnp.pad(blocks, ((0, 0), (0, 0), (0, 128 - blocks.shape[2])))

    early_columns = jnp.concatenate(
        [
            grad_ffn_rows,
            grad_attn_in_last,
            grad_attn_out_last,
            grad_down_shared,
            grad_down_expert,
        ],
        axis=0,
    ).astype(BF)
    early_blocks = by_shard(jnp.concatenate([grad_expert_rows, grad_shared_rows], axis=0))
    router_blocks = by_shard(grad_router_out)
    adapters_row = jnp.broadcast_to(adapters.astype(BF)[None, :, None], (shards_of, 2, RANK))
    adapters_row = adapters_row.reshape(shards_of, PAIR)
    router_blocks = router_blocks.at[:, :, 1].set(adapters_row)
    first_parts, first_lanes, early_got, blocks_got, router_got = exchange(
        "first_grads",
        7,
        ("swap", "x", first_part.reshape(along, tokens, width)),
        ("swap", "x", lanes_first_part.reshape(along, tokens, 128)),
        ("from_columns", "f", early_columns),
        ("swap", "f", early_blocks),
        ("swap", "f", router_blocks),
    )
    first_lane_grads = jnp.sum(first_lanes.astype(F32), axis=0)[:, : 3 * PAIR].astype(BF)
    grad_normed_one = jnp.sum(first_parts.astype(F32), axis=0) + dot(
        first_lane_grads, attn_first[:3].reshape(3 * PAIR, width)
    )
    grad_attn_in_first = dot_tn(first_lane_grads, normed_one)
    grad_tokens = grad_residual + rms_backward(tokens_f, attention_norm_gain, grad_normed_one)

    head_rows = lax.dynamic_update_slice(
        jnp.zeros((3 * PAIR, width), BF),
        grad_attn_out_heads.astype(BF),
        (0, x_index * head_columns),
    )
    late_columns = jnp.concatenate([grad_attn_in_first.astype(BF), head_rows], axis=0)
    (late_got,) = exchange("late_grads", 8, ("from_columns", "f", late_columns))

    group_adapters = router_got[:, :, 1].astype(jnp.int32)
    lane_rank = jnp.tile(jnp.arange(RANK, dtype=jnp.int32), 2)
    lane_of = group_adapters * RANK + lane_rank[None, :]
    expand = (
        jnp.arange(LANES, dtype=jnp.int32)[:, None, None] == lane_of[None, :, :]
    ).astype(BF)
    expand = expand.reshape(LANES, shards_of * PAIR)

    def spread_rows(got):
        factors = got.shape[1] // PAIR
        blocks = got.reshape(shards_of, factors, PAIR, got.shape[2])
        blocks = blocks.transpose(1, 0, 2, 3).reshape(factors, shards_of * PAIR, got.shape[2])
        return [dot(expand, blocks[i]) for i in range(factors)]

    early_sums = spread_rows(early_got[:, : 8 * PAIR])
    down_expert_sum = jnp.sum(early_got[:, 8 * PAIR :].astype(F32), axis=0)
    expert_sum = jnp.sum(blocks_got[:, : 3 * LANES].astype(F32), axis=0)
    shared_sums = spread_rows(blocks_got[:, 3 * LANES :])
    router_sum = spread_rows(router_got)[0]
    late_sums = spread_rows(late_got)
    all_rows = jnp.concatenate(
        [
            *late_sums[:3],
            early_sums[5],
            *late_sums[3:],
            early_sums[6],
            *early_sums[:5],
            early_sums[7],
            down_expert_sum,
            expert_sum,
            router_sum,
        ],
        axis=0,
    ).astype(BF)
    shared_rows = jnp.concatenate(shared_sums, axis=0).astype(BF)
    row_parts, shared_parts = exchange(
        "ctx_parts",
        9,
        ("swap", "c", all_rows.reshape(ctx_count, -1, 128)),
        ("gather", "c", shared_rows),
    )
    row_sum = jnp.sum(row_parts.astype(F32), axis=0).astype(BF)
    (totals,) = exchange("ctx_sums", 10, ("gather", "c", row_sum))
    totals = totals.reshape(-1, 128).astype(F32)
    shared_total = jnp.sum(
        shared_parts.astype(F32).reshape(along, 2, 3 * LANES, 128), axis=1
    )[:, :, :quarter]
    shared_total = shared_total.transpose(1, 0, 2).reshape(3 * LANES, along * quarter)
    expert_width = weight_gate.shape[1] // shards_of

    def rows(first, factors, columns=128):
        part = totals[first * LANES : (first + factors) * LANES, :columns]
        return part.reshape(factors, ADAPTER_COUNT, RANK, columns)

    return (
        output_value.astype(BF)[None],
        grad_tokens.astype(BF)[None],
        rows(0, 4),
        rows(4, 4),
        rows(8, 5),
        rows(18, 1, 1)[0],
        shared_total[: 2 * LANES].reshape(2, ADAPTER_COUNT, RANK, -1),
        shared_total[2 * LANES :].reshape(ADAPTER_COUNT, RANK, -1),
        rows(15, 2, expert_width),
        rows(17, 1, expert_width)[0],
        rows(13, 2),
    )


def solution(mesh):
    return jax.shard_map(
        shards,
        mesh=mesh,
        in_specs=(
            P("fsdp", "ctx", None),
            P("fsdp", "ctx", None),
            P("fsdp", None),
            P("fsdp", None),
            P("fsdp", None),
            P("fsdp", "ctx", None),
            P(),
            P(),
            P(None, "fsdp", None),
            P("fsdp", None),
            P(),
            P(),
            P(None, None, "fsdp"),
            P("fsdp", None),
            P(),
            P("fsdp", None, None, None),
            P("fsdp", None, None),
            P(),
            P(),
            P(),
            P(),
            P(),
            P(),
            P(),
            P(),
            P(),
        ),
        out_specs=(
            P("fsdp", "ctx", None),
            P("fsdp", "ctx", None),
            P(None, None, None, "fsdp"),
            P(None, None, None, "fsdp"),
            P(None, None, None, "fsdp"),
            P(None, None, "fsdp"),
            P(None, None, None, "fsdp"),
            P(None, None, "fsdp"),
            P(None, None, None, "fsdp"),
            P(None, None, "fsdp"),
            P(None, None, None, "fsdp"),
        ),
        check_vma=False,
    )
```

```python
import functools

import jax
import jax.numpy as jnp
from jax import lax
from jax.experimental import pallas as pl
from jax.experimental.pallas import tpu as pltpu
from jax.sharding import PartitionSpec as P

HEADS = 16
HEAD_DIM = 128
TOP = 4
ADAPTER_COUNT = 8
RANK = 16
LANES = ADAPTER_COUNT * RANK
PAIR = 2 * RANK
MAIN = 32

norm_eps = 1e-06
rope_theta = 1000000.0
masked_score = -1e30
highest = lax.Precision.HIGHEST
MESH = pl.DeviceIdType.MESH
BF = jnp.bfloat16
F32 = jnp.float32
VMEM_LIMIT = 56 * 2**20


def dot(left, right):
    return jnp.dot(left, right, preferred_element_type=F32)


def dot_nt(left, right):
    return lax.dot_general(left, right, (((1,), (1,)), ((), ())), preferred_element_type=F32)


def dot_tn(left, right):
    return lax.dot_general(left, right, (((0,), (0,)), ((), ())), preferred_element_type=F32)


GROUP_SIZE = {"x": 4, "y": 2, "c": 8, "f": 16}


def place_in(group):
    ctx, fsdp = lax.axis_index("ctx"), lax.axis_index("fsdp")
    return {"x": ctx // 2, "y": ctx % 2, "c": ctx, "f": fsdp}[group]


def device_of(group, index):
    ctx, fsdp = lax.axis_index("ctx"), lax.axis_index("fsdp")
    if group == "x":
        return (index * 2 + ctx % 2, fsdp)
    if group == "y":
        return ((ctx // 2) * 2 + index, fsdp)
    if group == "c":
        return (index, fsdp)
    return (ctx, index)


def chip():
    ctx, fsdp = lax.axis_index("ctx"), lax.axis_index("fsdp")
    return ctx % 2 * 2 + fsdp // 8, fsdp // 2 % 4, fsdp % 2


def device_at(y, z, core):
    return (lax.axis_index("ctx") // 2 * 2 + y // 2, y % 2 * 8 + z * 2 + core)


def shard_at(y, z, core):
    return y % 2 * 8 + z * 2 + core


def exchanged_shape(kind, group, shape):
    if kind == "share":
        return (GROUP_SIZE["f"],) + shape
    count = GROUP_SIZE[group]
    if kind == "gather":
        return (count,) + shape
    if kind in ("swap", "rows"):
        return shape
    if kind == "from_columns":
        return (count, shape[0], shape[1] // count)
    return (shape[1], count * shape[2])


def own_shape(kind, group, shape):
    if kind in ("gather", "share"):
        return shape
    count = GROUP_SIZE[group]
    if kind == "rows":
        return (shape[0] // count,) + shape[1:]
    if kind == "from_columns":
        return (shape[0], shape[1] // count)
    return shape[1:]


def copies_of(kind, group):
    return 23 if kind == "share" else GROUP_SIZE[group] - 1


def block_of(ref, kind, count, index):
    if kind == "rows":
        depth = ref.shape[0] // count
        return ref.at[pl.ds(pl.multiple_of(index * depth, depth), depth)]
    if kind == "columns":
        width = ref.shape[1] // count
        return ref.at[:, pl.ds(pl.multiple_of(index * width, width), width)]
    return ref.at[index]


def source_of(kind, group, ref, index):
    if kind in ("gather", "share"):
        return ref
    cut = {"rows": "rows", "from_columns": "columns"}.get(kind, "first")
    return block_of(ref, cut, GROUP_SIZE[group], index)


def target_of(kind, group, ref, index):
    cut = {"rows": "rows", "to_columns": "columns"}.get(kind, "first")
    return block_of(ref, cut, GROUP_SIZE["f" if kind == "share" else group], index)


def remote(source, target, send, recv, device):
    return pltpu.make_async_remote_copy(
        src_ref=source,
        dst_ref=target,
        send_sem=send,
        recv_sem=recv,
        device_id=device,
        device_id_type=MESH,
    )


def greet(plan):
    barrier = pltpu.get_barrier_semaphore()
    count = 0
    for group in sorted({group for kind, group in plan}):
        if group == "s":
            y, z, core = chip()
            peers = [device_at(y, lax.rem(z + d, 4), core) for d in (1, 2, 3)]
            peers += [device_at(lax.rem(y + d, 4), z, core) for d in (1, 3)]
            peers += [device_at(y, z, 1 - core)]
        else:
            size = GROUP_SIZE[group]
            mine = place_in(group)
            peers = [device_of(group, lax.rem(mine + d, size)) for d in range(1, size)]
        for peer in peers:
            pl.semaphore_signal(barrier, inc=1, device_id=peer, device_id_type=MESH)
        count += len(peers)
    pl.semaphore_wait(barrier, count)


class Share:
    def __init__(self, source, target, send, recv, first):
        self.target = target
        self.sems = (send, recv, first)
        y, z, core = self.place = chip()
        self.order = (1, 3, 2)
        self.source = source
        self.along_z = [
            self.copy(source, shard_at(y, z, core), None, i, device_at(y, lax.rem(z + d, 4), core))
            for i, d in enumerate(self.order)
        ]
        self.along_y, self.across = [], []

    def copy(self, source, shard, half, number, device):
        send, recv, first = self.sems
        target = self.target.at[shard]
        if half is not None:
            target = target.at[half]
        return remote(source, target, send.at[first + number], recv.at[first + number], device)

    def halves(self):
        half = self.target.shape[1] // 2
        return pl.ds(0, half), pl.ds(half, half)

    def forward(self, number, source, z):
        y, unused, core = self.place
        unused, my_z, unused = self.place
        shard = shard_at(y, z, core)
        for i, (half, d) in enumerate(zip(self.halves(), (3, 1))):
            copy = self.copy(
                source.at[half], shard, half, 3 + 2 * number + i, device_at(lax.rem(y + d, 4), my_z, core)
            )
            copy.start()
            self.along_y.append(copy)
        copy = self.copy(source, shard, None, 11 + number, device_at(y, my_z, 1 - core))
        copy.start()
        self.across.append(copy)

    def start(self):
        for copy in self.along_z:
            copy.start()
        self.forward(0, self.source, self.place[1])

    def finish(self):
        y, z, core = self.place
        for i, d in enumerate(self.order):
            self.along_z[i].wait_recv()
            from_z = lax.rem(z + 4 - d, 4)
            self.forward(i + 1, self.target.at[shard_at(y, from_z, core)], from_z)
        for number in range(4):
            from_z = z if number == 0 else lax.rem(z + 4 - self.order[number - 1], 4)
            shard = shard_at(y + 1, from_z, core)
            for i, half in enumerate(self.halves()):
                self.along_y[2 * number + i].wait_recv()
                block = self.target.at[shard].at[half]
                copy = self.copy(block, shard, half, 15 + 2 * number + i, device_at(y, z, 1 - core))
                copy.start()
                self.across.append(copy)
        for copy in self.along_z + self.along_y:
            copy.wait_send()
        for copy in self.across:
            copy.wait()


def exchange_kernel(plan, *refs):
    amount = len(plan)
    inputs, outputs, own = refs[:amount], refs[amount : 2 * amount], refs[2 * amount : 3 * amount]
    send_sem, recv_sem, in_sem, out_sem = refs[3 * amount :]

    def own_place(item):
        kind, group = plan[item]
        return shard_at(*chip()) if kind == "share" else place_in(group)

    taken = []
    for item, (kind, group) in enumerate(plan):
        copy = pltpu.make_async_copy(
            source_of(kind, group, inputs[item], own_place(item)), own[item], in_sem.at[item]
        )
        copy.start()
        taken.append(copy)
    greet(plan)
    copies, shares = [], []
    slot = 0
    for item, (kind, group) in enumerate(plan):
        if kind == "share":
            share = Share(inputs[item], outputs[item], send_sem, recv_sem, slot)
            share.start()
            shares.append(share)
        else:
            count = GROUP_SIZE[group]
            mine = place_in(group)
            for offset in range(1, count):
                peer = lax.rem(mine + offset, count)
                copy = remote(
                    source_of(kind, group, inputs[item], peer),
                    target_of(kind, group, outputs[item], mine),
                    send_sem.at[slot + offset - 1],
                    recv_sem.at[slot + offset - 1],
                    device_of(group, peer),
                )
                copy.start()
                copies.append(copy)
        slot += copies_of(kind, group)
    for item, (kind, group) in enumerate(plan):
        taken[item].wait()
        copy = pltpu.make_async_copy(
            own[item], target_of(kind, group, outputs[item], own_place(item)), out_sem.at[item]
        )
        copy.start()
        copies.append(copy)
    for share in shares:
        share.finish()
    for copy in copies:
        copy.wait()


def exchange(name, number, *items):
    plan = tuple((kind, group) for kind, group, array in items)
    arrays = [array for kind, group, array in items]
    slots = sum(copies_of(kind, group) for kind, group in plan)
    return pl.pallas_call(
        functools.partial(exchange_kernel, plan),
        out_shape=[
            jax.ShapeDtypeStruct(exchanged_shape(kind, group, array.shape), array.dtype)
            for kind, group, array in items
        ],
        in_specs=[pl.BlockSpec(memory_space=pl.ANY)] * len(items),
        out_specs=[pl.BlockSpec(memory_space=pl.ANY)] * len(items),
        scratch_shapes=[
            pltpu.VMEM(own_shape(kind, group, array.shape), array.dtype)
            for kind, group, array in items
        ]
        + [
            pltpu.SemaphoreType.DMA((slots,)),
            pltpu.SemaphoreType.DMA((slots,)),
            pltpu.SemaphoreType.DMA((len(items),)),
            pltpu.SemaphoreType.DMA((len(items),)),
        ],
        compiler_params=pltpu.CompilerParams(
            collective_id=number, has_side_effects=True, vmem_limit_bytes=16 * 2**20
        ),
        name=name,
    )(*arrays)


def rms_forward(values, gain):
    mean_square = jnp.mean(values * values, axis=-1, keepdims=True)
    return values * lax.rsqrt(mean_square + norm_eps) * gain.astype(F32)


def rms_backward(values, gain, grad_result):
    scale = lax.rsqrt(jnp.mean(values * values, axis=-1, keepdims=True) + norm_eps)
    scaled = gain.astype(F32) * grad_result
    inner = jnp.mean(values * scaled, axis=-1, keepdims=True)
    return scale * scaled - values * (scale * scale * scale) * inner


def logistic(values):
    return 1.0 / (1.0 + jnp.exp(-values))


def swiglu_backward(gate, upper, grad_hidden):
    sigma = logistic(gate)
    grad_gate = grad_hidden * upper * sigma * (1.0 + gate * (1.0 - sigma))
    grad_upper = grad_hidden * gate * sigma
    return (grad_gate.astype(BF), grad_upper.astype(BF))


def two_parts(values):
    high = values.astype(BF)
    return high, (values - high.astype(F32)).astype(BF)


def lane_index(shape):
    return lax.broadcasted_iota(jnp.int32, shape, 1)


def row_index(shape):
    return lax.broadcasted_iota(jnp.int32, shape, 0)


def pair_pick(second, copies):
    shape = (second.shape[0], PAIR * copies)
    of_lane = (lane_index(shape) % PAIR >= RANK).astype(F32)
    return (of_lane == second).astype(F32)


def pair_of(first_ref, last_ref, index):
    return jnp.concatenate([first_ref[index, 0], last_ref[index, 0]], axis=0)


def padded(values):
    rest = 128 - values.shape[1]
    return jnp.concatenate([values, jnp.zeros((values.shape[0], rest), values.dtype)], axis=1)


def routing(routes, experts):
    tokens = routes.shape[0]
    expert_lane = lane_index((tokens, experts))
    expert_hot = [(routes[:, k : k + 1] == expert_lane).astype(F32) for k in range(TOP)]
    count = sum(expert_hot)
    below = (row_index((tokens, tokens)) > lane_index((tokens, tokens))).astype(BF)
    earlier = dot(below, count.astype(BF))
    rank = [jnp.sum(hot * earlier, axis=1, keepdims=True).astype(jnp.int32) for hot in expert_hot]
    main_lane = lane_index((tokens, experts * MAIN))
    rest_lane = lane_index((tokens, experts * 16))
    rest_code = (rest_lane // 16) * 4 + rest_lane % 4
    main_hot, rest_hot = [], []
    for k in range(TOP):
        expert = routes[:, k : k + 1]
        main_slot = jnp.where(rank[k] < MAIN, expert * MAIN + rank[k], -1)
        rest_slot = jnp.where(rank[k] < MAIN, -1, expert * 4 + rank[k] - MAIN)
        main_hot.append((main_lane == main_slot).astype(F32))
        rest_hot.append((rest_code == rest_slot).astype(F32))
    return expert_hot, main_hot, rest_hot


def quarter_mask(shape, quarter):
    return (lane_index(shape) % 16 // 4 == quarter).astype(F32)


def rows_to_slots(main_hot, rest_hot, rows):
    main = dot_tn(sum(main_hot).astype(BF), rows).astype(BF)
    rest_sum = sum(rest_hot)
    width = rows.shape[1] // 4
    rest = None
    for quarter in range(4):
        hot = (rest_sum * quarter_mask(rest_sum.shape, quarter)).astype(BF)
        part = dot_tn(hot, rows[:, quarter * width : (quarter + 1) * width])
        rest = part if rest is None else rest + part
    return main, rest.astype(BF)


def slots_to_rows(main_hot, rest_hot, main, rest):
    rest_sum = sum(rest_hot)
    parts = [
        dot((rest_sum * quarter_mask(rest_sum.shape, quarter)).astype(BF), rest)
        for quarter in range(4)
    ]
    return dot(sum(main_hot).astype(BF), main) + jnp.concatenate(parts, axis=1)


def rest_selectors():
    row, lane = row_index((16, 64)), lane_index((16, 64))
    same = (lane // 16 == row // 4) & (lane % 4 == row % 4)
    return [(same & (lane % 16 // 4 == quarter)).astype(BF) for quarter in range(4)]


def rest_to_rows(selectors, rest):
    return jnp.concatenate([dot(selector, rest) for selector in selectors], axis=1).astype(BF)


def rows_to_rest(selectors, rows):
    width = rows.shape[1] // 4
    total = None
    for quarter in range(4):
        part = dot_tn(selectors[quarter], rows[:, quarter * width : (quarter + 1) * width])
        total = part if total is None else total + part
    return total.astype(BF)


def stage(kernel, name, out_shape, in_specs, out_specs, grid=(1,), scratch=(), prefetch=0):
    return pl.pallas_call(
        kernel,
        out_shape=out_shape,
        grid_spec=pltpu.PrefetchScalarGridSpec(
            num_scalar_prefetch=prefetch,
            grid=grid,
            in_specs=in_specs,
            out_specs=out_specs,
            scratch_shapes=list(scratch),
        ),
        compiler_params=pltpu.CompilerParams(vmem_limit_bytes=VMEM_LIMIT),
        name=name,
    )


def whole(array):
    zeros = (0,) * len(array.shape)
    return pl.BlockSpec(array.shape, lambda *unused: zeros)


def of_sequence(which, block):
    return pl.BlockSpec(block, lambda *at: (0, at[-1][which], 0, 0))


def shape_of(shape, kind):
    return jax.ShapeDtypeStruct(shape, kind)


ANY = pl.BlockSpec(memory_space=pl.ANY)


def prologue_kernel(rows_ref, grads_ref, gain_ref, routes_ref, normed_ref, main_ref, rest_ref):
    normed_ref[...] = rms_forward(rows_ref[0].astype(F32), gain_ref[...]).astype(BF)
    experts = main_ref.shape[0] // MAIN
    unused, main_hot, rest_hot = routing(routes_ref[0], experts)
    main, rest = rows_to_slots(main_hot, rest_hot, grads_ref[0])
    main_ref[...] = main
    rest_ref[...] = rest


def prologue(rows, grads, gain, routes, experts):
    tokens, width = rows.shape[1:]
    return stage(
        prologue_kernel,
        "prologue",
        [
            shape_of((tokens, width), BF),
            shape_of((experts * MAIN, width), BF),
            shape_of((experts * 16, width // 4), BF),
        ],
        [whole(rows), whole(grads), whole(gain), whole(routes)],
        [
            pl.BlockSpec((tokens, width), lambda n: (0, 0)),
            pl.BlockSpec((experts * MAIN, width), lambda n: (0, 0)),
            pl.BlockSpec((experts * 16, width // 4), lambda n: (0, 0)),
        ],
    )(rows, grads, gain, routes)


def half_turn(values):
    parts = []
    for head in range(values.shape[1] // HEAD_DIM):
        part = values[:, head * HEAD_DIM : (head + 1) * HEAD_DIM]
        parts.append(jnp.concatenate([part[:, 64:], part[:, :64]], axis=1))
    return jnp.concatenate(parts, axis=1) if len(parts) > 1 else parts[0]


def project_kernel(
    numbers_ref,
    rows_ref,
    weight_ref,
    first_a_ref,
    first_b_ref,
    second_a_ref,
    second_b_ref,
    bias_ref,
    side_ref,
    cos_ref,
    sin_ref,
    out_ref,
    lanes_ref,
):
    which = pl.program_id(0)

    @pl.when(pl.program_id(1) == 0)
    def lanes():
        first = pair_of(first_a_ref, first_b_ref, 0)
        picked = dot_nt(rows_ref[...], first) * pair_pick(side_ref[...], 1)
        lanes_ref[0] = picked.astype(BF)

    weight = weight_ref[...].reshape(rows_ref.shape[1], weight_ref.shape[3])
    bias = bias_ref[...].astype(F32)
    bias = jnp.sum(jnp.where(row_index(bias.shape) == which, bias, 0.0), axis=0, keepdims=True)
    second = pair_of(second_a_ref, second_b_ref, 0)
    value = dot(rows_ref[...], weight) + bias + dot(lanes_ref[0], second)
    copies = value.shape[1] // HEAD_DIM
    cosine = jnp.concatenate([cos_ref[...]] * copies, axis=1)
    sine = jnp.concatenate([sin_ref[...]] * copies, axis=1)
    turned = value * cosine + half_turn(value) * sine
    out_ref[0] = jnp.where(which < 2, turned, value).astype(BF)


def project(numbers, rows, weight, first, second, bias, side, cosine, sine):
    tokens, width = rows.shape
    columns = weight.shape[3]
    step = 256
    steps = columns // step
    return stage(
        project_kernel,
        "project",
        [shape_of((3, tokens, columns), BF), shape_of((3, tokens, PAIR), BF)],
        [
            whole(rows),
            pl.BlockSpec((weight.shape[0], 1, weight.shape[2], step), lambda j, n, a: (0, j, 0, n)),
            pl.BlockSpec((1, 1, RANK, width), lambda j, n, a: (j, a[0], 0, 0)),
            pl.BlockSpec((1, 1, RANK, width), lambda j, n, a: (j, a[1], 0, 0)),
            pl.BlockSpec((1, 1, RANK, step), lambda j, n, a: (j, a[0], 0, a[2] * steps + n)),
            pl.BlockSpec((1, 1, RANK, step), lambda j, n, a: (j, a[1], 0, a[2] * steps + n)),
            pl.BlockSpec((3, step), lambda j, n, a: (0, a[2] * steps + n)),
            whole(side),
            whole(cosine),
            whole(sine),
        ],
        [
            pl.BlockSpec((1, tokens, step), lambda j, n, a: (j, 0, n)),
            pl.BlockSpec((1, tokens, PAIR), lambda j, n, a: (j, 0, 0)),
        ],
        grid=(3, steps),
        prefetch=1,
    )(numbers, rows, weight, first, first, second, second, bias, side, cosine, sine)


def probabilities(query, keys, query_place, query_start, key_place):
    scores = dot_nt(query, keys) * (HEAD_DIM**-0.5)
    allowed = (key_place <= query_place) & (key_place >= query_start)
    scores = jnp.where(allowed, scores, masked_score)
    top = jnp.max(scores, axis=1, keepdims=True)
    raised = jnp.exp(scores - top)
    return raised * (1.0 / jnp.sum(raised, axis=1, keepdims=True))


def attend_kernel(query_ref, key_ref, value_ref, place_ref, start_ref, key_place_ref, out_ref):
    keys = key_ref[...].reshape(-1, HEAD_DIM)
    values = value_ref[...].reshape(-1, HEAD_DIM)
    probs = probabilities(query_ref[0], keys, place_ref[...], start_ref[...], key_place_ref[...])
    out_ref[...] = dot(probs.astype(BF), values).astype(BF)


def attend(projected, pairs, place, start, key_place):
    tokens, columns = projected.shape[1:]
    step = 256
    keys = pairs.shape[0] * pairs.shape[2]
    half = pairs.shape[2]
    return pl.pallas_call(
        attend_kernel,
        grid=(columns // HEAD_DIM, tokens // step),
        out_shape=jax.ShapeDtypeStruct((tokens, columns), BF),
        in_specs=[
            pl.BlockSpec((1, step, HEAD_DIM), lambda h, i: (0, i, h)),
            pl.BlockSpec((2, 1, half, HEAD_DIM), lambda h, i: (0, 0, 0, h)),
            pl.BlockSpec((2, 1, half, HEAD_DIM), lambda h, i: (0, 1, 0, h)),
            pl.BlockSpec((step, 1), lambda h, i: (i, 0)),
            pl.BlockSpec((step, 1), lambda h, i: (i, 0)),
            pl.BlockSpec((1, keys), lambda h, i: (0, 0)),
        ],
        out_specs=pl.BlockSpec((step, HEAD_DIM), lambda h, i: (i, h)),
        compiler_params=pltpu.CompilerParams(vmem_limit_bytes=VMEM_LIMIT),
        name="attend",
    )(projected, pairs, pairs, place, start, key_place)


def attend_back_kernel(
    query_ref,
    key_ref,
    value_ref,
    grad_ref,
    place_ref,
    start_ref,
    key_place_ref,
    cos_ref,
    sin_ref,
    query_out,
    pair_out,
    key_total,
    value_total,
):
    step = pl.program_id(1)
    query = query_ref[0]
    grad = grad_ref[...]
    keys = key_ref[...].reshape(-1, HEAD_DIM)
    values = value_ref[...].reshape(-1, HEAD_DIM)
    probs = probabilities(query, keys, place_ref[...], start_ref[...], key_place_ref[...])
    grad_probs = dot_nt(grad, values)
    mean = jnp.sum(probs * grad_probs, axis=1, keepdims=True)
    grad_scores = (probs * (grad_probs - mean)).astype(BF)
    grad_query = dot(grad_scores, keys) * (HEAD_DIM**-0.5)
    query_out[...] = (grad_query * cos_ref[...] - half_turn(grad_query) * sin_ref[...]).astype(BF)
    grad_keys = dot_tn(grad_scores, query) * (HEAD_DIM**-0.5)
    grad_values = dot_tn(probs.astype(BF), grad)

    @pl.when(step == 0)
    def first():
        key_total[...] = grad_keys
        value_total[...] = grad_values

    @pl.when(step > 0)
    def later():
        key_total[...] += grad_keys
        value_total[...] += grad_values

    half = pair_out.shape[2]
    for side in range(2):
        pair_out[side, 0] = key_total[side * half : (side + 1) * half, :].astype(BF)
        pair_out[side, 1] = value_total[side * half : (side + 1) * half, :].astype(BF)


def attend_back(projected, pairs, grads, place, start, key_place, cosine, sine):
    tokens, columns = projected.shape[1:]
    step = 256
    keys = pairs.shape[0] * pairs.shape[2]
    half = pairs.shape[2]
    return pl.pallas_call(
        attend_back_kernel,
        grid=(columns // HEAD_DIM, tokens // step),
        out_shape=[
            jax.ShapeDtypeStruct((tokens, columns), BF),
            jax.ShapeDtypeStruct(pairs.shape, BF),
        ],
        in_specs=[
            pl.BlockSpec((1, step, HEAD_DIM), lambda h, i: (0, i, h)),
            pl.BlockSpec((2, 1, half, HEAD_DIM), lambda h, i: (0, 0, 0, h)),
            pl.BlockSpec((2, 1, half, HEAD_DIM), lambda h, i: (0, 1, 0, h)),
            pl.BlockSpec((step, HEAD_DIM), lambda h, i: (i, h)),
            pl.BlockSpec((step, 1), lambda h, i: (i, 0)),
            pl.BlockSpec((step, 1), lambda h, i: (i, 0)),
            pl.BlockSpec((1, keys), lambda h, i: (0, 0)),
            pl.BlockSpec((step, HEAD_DIM), lambda h, i: (i, 0)),
            pl.BlockSpec((step, HEAD_DIM), lambda h, i: (i, 0)),
        ],
        out_specs=[
            pl.BlockSpec((step, HEAD_DIM), lambda h, i: (i, h)),
            pl.BlockSpec((2, 2, half, HEAD_DIM), lambda h, i: (0, 0, 0, h)),
        ],
        scratch_shapes=[pltpu.VMEM((keys, HEAD_DIM), F32), pltpu.VMEM((keys, HEAD_DIM), F32)],
        compiler_params=pltpu.CompilerParams(vmem_limit_bytes=VMEM_LIMIT),
        name="attend_back",
    )(projected, pairs, pairs, grads, place, start, key_place, cosine, sine)


def after_attention_kernel(
    numbers_ref,
    mixed_ref,
    weight_ref,
    rows_ref,
    first_a_ref,
    first_b_ref,
    second_a_ref,
    second_b_ref,
    gain_ref,
    ffn_a_ref,
    ffn_b_ref,
    router_ref,
    router_a_ref,
    router_b_ref,
    mix_ref,
    routes_ref,
    side_ref,
    residual_ref,
    normed_ref,
    small_ref,
    main_ref,
    rest_ref,
    main_notes_ref,
    rest_notes_ref,
    lanes_ref,
):
    step = pl.program_id(0)
    side = side_ref[...]
    pick = pair_pick(side, 1)

    @pl.when(step == 0)
    def lanes():
        first = pair_of(first_a_ref, first_b_ref, 0)
        lanes_ref[...] = (dot_nt(mixed_ref[...], first) * pick).astype(BF)

    columns = weight_ref.shape[1]
    here = pl.ds(pl.multiple_of(step * columns, columns), columns)
    second = pair_of(second_a_ref, second_b_ref, 0)
    residual_ref[:, here] = rows_ref[0].astype(F32) + (
        dot(mixed_ref[...], weight_ref[...]) + dot(lanes_ref[...], second)
    )

    @pl.when(step == pl.num_programs(0) - 1)
    def last():
        tokens = residual_ref.shape[0]
        experts = router_ref.shape[1]
        normed = rms_forward(residual_ref[...], gain_ref[...]).astype(BF)
        normed_ref[...] = normed
        router_lanes = (dot_nt(normed, pair_of(ffn_a_ref, ffn_b_ref, 0)) * pick).astype(BF)
        router_second = jnp.concatenate([router_a_ref[0], router_b_ref[0]], axis=0)
        logits = dot(normed, router_ref[...]) + dot(router_lanes, router_second)
        expert_hot, main_hot, rest_hot = routing(routes_ref[0], experts)
        chosen = [jnp.sum(hot * logits, axis=1, keepdims=True) for hot in expert_hot]
        top = jnp.maximum(jnp.maximum(chosen[0], chosen[1]), jnp.maximum(chosen[2], chosen[3]))
        raised = [jnp.exp(value - top) for value in chosen]
        total = sum(raised)
        gates = [value / total for value in raised]
        mix = logistic(
            jnp.sum(normed.astype(F32) * mix_ref[...].astype(F32), axis=1, keepdims=True)
        )
        small_ref[...] = padded(
            jnp.concatenate(
                [lanes_ref[...].astype(F32), router_lanes.astype(F32), *gates, mix], axis=1
            )
        )
        main, rest = rows_to_slots(main_hot, rest_hot, normed)
        main_ref[...] = main
        rest_ref[...] = rest
        adapter = jnp.where(side > 0.5, numbers_ref[1], numbers_ref[0])
        lane = lane_index((tokens, 128))
        adapter_hot = (lane == adapter).astype(F32)
        main_notes, rest_notes = None, None
        for k in range(TOP):
            high, low = two_parts(gates[k])
            notes = jnp.where(
                lane == ADAPTER_COUNT,
                high.astype(F32),
                jnp.where(lane == ADAPTER_COUNT + 1, low.astype(F32), adapter_hot),
            ).astype(BF)
            main_part = dot_tn(main_hot[k].astype(BF), notes)
            rest_part = dot_tn(rest_hot[k].astype(BF), notes)
            main_notes = main_part if k == 0 else main_notes + main_part
            rest_notes = rest_part if k == 0 else rest_notes + rest_part
        main_notes_ref[...] = main_notes.astype(BF)
        rest_notes_ref[...] = rest_notes.astype(BF)


def after_attention(
    numbers, mixed, weight, rows, first, second, gain, ffn_first, router, router_second, mix, routes, side
):
    tokens, width = mixed.shape
    experts = router.shape[1]
    step = 512
    kept = lambda *shape: pl.BlockSpec(shape, lambda n, a: (0,) * len(shape))
    outs = [
        ((tokens, width), F32),
        ((tokens, width), BF),
        ((tokens, 128), F32),
        ((experts * MAIN, width), BF),
        ((experts * 16, width // 4), BF),
        ((experts * MAIN, 128), BF),
        ((experts * 16, 128), BF),
    ]
    return stage(
        after_attention_kernel,
        "after_attention",
        [shape_of(*out) for out in outs],
        [
            whole(mixed),
            pl.BlockSpec((width, step), lambda n, a: (0, n)),
            pl.BlockSpec((1, tokens, step), lambda n, a: (0, 0, n)),
            pl.BlockSpec((1, 1, RANK, width), lambda n, a: (3, a[0], 0, 0)),
            pl.BlockSpec((1, 1, RANK, width), lambda n, a: (3, a[1], 0, 0)),
            pl.BlockSpec((1, 1, RANK, step), lambda n, a: (3, a[0], 0, n)),
            pl.BlockSpec((1, 1, RANK, step), lambda n, a: (3, a[1], 0, n)),
            whole(gain),
            pl.BlockSpec((1, 1, RANK, width), lambda n, a: (0, a[0], 0, 0)),
            pl.BlockSpec((1, 1, RANK, width), lambda n, a: (0, a[1], 0, 0)),
            whole(router),
            pl.BlockSpec((1, RANK, experts), lambda n, a: (a[0], 0, 0)),
            pl.BlockSpec((1, RANK, experts), lambda n, a: (a[1], 0, 0)),
            whole(mix),
            whole(routes),
            whole(side),
        ],
        [kept(*shape) for shape, kind in outs],
        grid=(width // step,),
        scratch=[pltpu.VMEM((tokens, PAIR), BF)],
        prefetch=1,
    )(
        numbers, mixed, weight, rows, first, first, second, second, gain, ffn_first, ffn_first, router,
        router_second, router_second, mix, routes, side,
    )


def shared_kernel(
    numbers_ref,
    rows_ref,
    grads_ref,
    side_ref,
    ffn_a_ref,
    ffn_b_ref,
    second_ref,
    down_a_ref,
    down_b_ref,
    mix_ref,
    weights_hbm,
    grad_rows_ref,
    value_ref,
    notes_ref,
    adapter_ref,
    gate_ref,
    up_ref,
    down_ref,
    sems,
):
    step = pl.program_id(0)
    units, width = gate_ref.shape[1:]
    loads = [
        pltpu.make_async_copy(
            weights_hbm.at[:, pl.ds(i * units, units)], target, sems.at[i]
        )
        for i, target in enumerate((gate_ref, up_ref, down_ref))
    ]

    @pl.when(step == 0)
    def start():
        for load in loads:
            load.start()

    rows, grads = rows_ref[...], grads_ref[...]
    grads_f = grads.astype(F32)
    pick = pair_pick(side_ref[...], 1)
    second = second_ref[...]
    second_gate, second_up, down_first = second[:PAIR], second[PAIR : 2 * PAIR], second[2 * PAIR :]
    down_second = pair_of(down_a_ref, down_b_ref, 0)
    lanes_gate = (dot_nt(rows, pair_of(ffn_a_ref, ffn_b_ref, 1)) * pick).astype(BF)
    lanes_up = (dot_nt(rows, pair_of(ffn_a_ref, ffn_b_ref, 2)) * pick).astype(BF)
    mix = logistic(jnp.sum(rows.astype(F32) * mix_ref[...].astype(F32), axis=1, keepdims=True))
    grad_shared = (mix * grads_f).astype(BF)
    grad_side = (dot_nt(grad_shared, down_second) * pick).astype(BF)

    @pl.when(step == 0)
    def ready():
        for load in loads:
            load.wait()

    weight_gate = gate_ref[...].reshape(-1, width)
    weight_up = up_ref[...].reshape(-1, width)
    weight_down = down_ref[...].reshape(-1, width)
    gate = dot_nt(rows, weight_gate) + dot(lanes_gate, second_gate)
    upper = dot_nt(rows, weight_up) + dot(lanes_up, second_up)
    hidden = (gate * logistic(gate) * upper).astype(BF)
    grad_hidden = dot_nt(grad_shared, weight_down) + dot(grad_side, down_first)
    grad_gate, grad_upper = swiglu_backward(gate, upper, grad_hidden)
    value = dot(hidden, weight_down)
    value_ref[...] = value.astype(BF)
    mix_sum = jnp.sum(grads_f * value, axis=1, keepdims=True)
    grad_rows_ref[...] = (dot(grad_gate, weight_gate) + dot(grad_upper, weight_up)).astype(BF)
    side = (dot_nt(hidden, down_first) * pick).astype(BF)
    grad_lanes_gate = (dot_nt(grad_gate, second_gate) * pick).astype(BF)
    grad_lanes_up = (dot_nt(grad_upper, second_up) * pick).astype(BF)
    notes_ref[...] = padded(
        jnp.concatenate([side, grad_lanes_gate, grad_lanes_up, *two_parts(mix_sum)], axis=1)
    )
    adapter = jnp.concatenate(
        [dot_tn(lanes_gate, grad_gate), dot_tn(lanes_up, grad_upper), dot_tn(grad_side, hidden)],
        axis=0,
    )

    @pl.when(step == 0)
    def first():
        adapter_ref[...] = adapter

    @pl.when(step > 0)
    def later():
        adapter_ref[...] += adapter


def shared_expert(numbers, rows, grads, side, ffn_first, second, down_second, mix, weights):
    tokens, width = rows.shape
    shards_of, units = weights.shape[0], weights.shape[1] // 3
    hidden = shards_of * units
    step = 256
    block = pl.BlockSpec((step, width), lambda n, a: (n, 0))
    factors = ffn_first.shape[0]
    return stage(
        shared_kernel,
        "shared_expert",
        [
            shape_of((tokens, width), BF),
            shape_of((tokens, width), BF),
            shape_of((tokens, 128), BF),
            shape_of((3 * PAIR, hidden), F32),
        ],
        [
            block,
            block,
            pl.BlockSpec((step, 1), lambda n, a: (n, 0)),
            of_sequence(0, (factors, 1, RANK, width)),
            of_sequence(1, (factors, 1, RANK, width)),
            whole(second),
            of_sequence(0, (1, 1, RANK, width)),
            of_sequence(1, (1, 1, RANK, width)),
            whole(mix),
            ANY,
        ],
        [
            block,
            block,
            pl.BlockSpec((step, 128), lambda n, a: (n, 0)),
            pl.BlockSpec((3 * PAIR, hidden), lambda n, a: (0, 0)),
        ],
        grid=(tokens // step,),
        scratch=[pltpu.VMEM((shards_of, units, width), BF)] * 3 + [pltpu.SemaphoreType.DMA((3,))],
        prefetch=1,
    )(
        numbers, rows, grads, side, ffn_first, ffn_first, second, down_second, down_second, mix,
        weights,
    )


def routed_kernel(
    main_ref,
    rest_ref,
    main_grads_ref,
    rest_grads_ref,
    main_notes_ref,
    rest_notes_ref,
    first_ref,
    second_ref,
    down_first_ref,
    down_second_ref,
    gate_up_hbm,
    down_hbm,
    back_main_ref,
    back_rest_ref,
    result_main_ref,
    result_rest_ref,
    notes_main_ref,
    notes_rest_ref,
    adapter_ref,
    adapter_down_ref,
    gate_up_ref,
    weight_down_ref,
    sems,
):
    step = pl.program_id(0)
    loads = [
        pltpu.make_async_copy(gate_up_hbm.at[0, 0], gate_up_ref.at[0], sems.at[0]),
        pltpu.make_async_copy(gate_up_hbm.at[0, 1], gate_up_ref.at[1], sems.at[1]),
        pltpu.make_async_copy(down_hbm.at[0], weight_down_ref, sems.at[2]),
    ]

    @pl.when(step == 0)
    def start():
        for load in loads:
            load.start()

    selectors = rest_selectors()
    rows = jnp.concatenate([main_ref[...], rest_to_rows(selectors, rest_ref[...])], axis=0)
    grads = jnp.concatenate(
        [main_grads_ref[...], rest_to_rows(selectors, rest_grads_ref[...])], axis=0
    )
    notes = jnp.concatenate(
        [main_notes_ref[...], dot(selectors[0], rest_notes_ref[...]).astype(BF)], axis=0
    )
    spread = (row_index((128, LANES)) == lane_index((128, LANES)) // RANK).astype(BF)
    pick = dot(notes, spread)
    gate_of = (
        notes[:, ADAPTER_COUNT : ADAPTER_COUNT + 1].astype(F32)
        + notes[:, ADAPTER_COUNT + 1 : ADAPTER_COUNT + 2].astype(F32)
    )
    grads_f = grads.astype(F32)
    lanes_gate = (dot_nt(rows, first_ref[0]) * pick).astype(BF)
    lanes_up = (dot_nt(rows, first_ref[1]) * pick).astype(BF)
    grad_routed = (gate_of * grads_f).astype(BF)
    grad_side = (dot_nt(grads, down_second_ref[0]) * gate_of * pick).astype(BF)

    @pl.when(step == 0)
    def ready():
        for load in loads:
            load.wait()

    gate = dot(rows, gate_up_ref[0]) + dot(lanes_gate, second_ref[0])
    upper = dot(rows, gate_up_ref[1]) + dot(lanes_up, second_ref[1])
    hidden = (gate * logistic(gate) * upper).astype(BF)
    grad_hidden = dot_nt(grad_routed, weight_down_ref[...]) + dot(grad_side, down_first_ref[...])
    grad_gate, grad_upper = swiglu_backward(gate, upper, grad_hidden)
    side = (dot_nt(hidden, down_first_ref[...]).astype(BF).astype(F32) * pick).astype(BF)
    value = dot(hidden, weight_down_ref[...]) + dot(side, down_second_ref[0])
    gate_grad = jnp.sum(grads_f * value, axis=1, keepdims=True)
    result = (gate_of * value).astype(BF)
    back = (dot_nt(grad_gate, gate_up_ref[0]) + dot_nt(grad_upper, gate_up_ref[1])).astype(BF)
    fold = (row_index((LANES, 128)) % RANK == lane_index((LANES, 128))).astype(BF)
    fold_later = (row_index((LANES, 128)) % RANK == lane_index((LANES, 128)) - RANK).astype(BF)
    back_gate = (dot_nt(grad_gate, second_ref[0]) * pick).astype(BF)
    back_up = (dot_nt(grad_upper, second_ref[1]) * pick).astype(BF)
    high, low = two_parts(gate_grad)
    lane = lane_index((rows.shape[0], 128))
    back_notes = jnp.where(
        lane == PAIR,
        high.astype(F32),
        jnp.where(
            lane == PAIR + 1, low.astype(F32), dot(back_gate, fold) + dot(back_up, fold_later)
        ),
    ).astype(BF)
    count = main_ref.shape[0]
    back_main_ref[...] = back[:count]
    back_rest_ref[...] = rows_to_rest(selectors, back[count:])
    result_main_ref[...] = result[:count]
    result_rest_ref[...] = rows_to_rest(selectors, result[count:])
    notes_main_ref[...] = back_notes[:count]
    notes_rest_ref[...] = dot_tn(selectors[0], back_notes[count:]).astype(BF)
    adapter = jnp.concatenate(
        [dot_tn(lanes_gate, grad_gate), dot_tn(lanes_up, grad_upper), dot_tn(grad_side, hidden)],
        axis=0,
    )
    adapter_down = dot_tn(side, grad_routed)

    @pl.when(step == 0)
    def first():
        adapter_ref[...] = adapter
        adapter_down_ref[...] = adapter_down

    @pl.when(step > 0)
    def later():
        adapter_ref[...] += adapter
        adapter_down_ref[...] += adapter_down


def routed_expert(rows, grads, notes, first, second, down_first, down_second, gate_up, down):
    slots, width = rows[0].shape
    hidden = down.shape[1]
    steps = 4
    main = pl.BlockSpec((slots // steps, width), lambda n: (n, 0))
    rest = pl.BlockSpec((rows[1].shape[0] // steps, width // 4), lambda n: (n, 0))
    main_notes = pl.BlockSpec((slots // steps, 128), lambda n: (n, 0))
    rest_notes = pl.BlockSpec((rows[1].shape[0] // steps, 128), lambda n: (n, 0))
    down_second_spec = pl.BlockSpec((1, LANES, width), lambda n: (1, 0, 0))
    return stage(
        routed_kernel,
        "routed_expert",
        [shape_of(array.shape, BF) for array in (*rows, *rows, *notes)]
        + [shape_of((3 * LANES, hidden), F32), shape_of((LANES, width), F32)],
        [
            main,
            rest,
            main,
            rest,
            main_notes,
            rest_notes,
            whole(first),
            whole(second),
            whole(down_first),
            down_second_spec,
            ANY,
            ANY,
        ],
        [
            main,
            rest,
            main,
            rest,
            main_notes,
            rest_notes,
            pl.BlockSpec((3 * LANES, hidden), lambda n: (0, 0)),
            pl.BlockSpec((LANES, width), lambda n: (0, 0)),
        ],
        grid=(steps,),
        scratch=[
            pltpu.VMEM((2, width, hidden), BF),
            pltpu.VMEM((hidden, width), BF),
            pltpu.SemaphoreType.DMA((3,)),
        ],
    )(*rows, *grads, *notes, first, second, down_first, down_second, gate_up, down)


def after_experts_kernel(
    numbers_ref,
    parts_ref,
    part_notes_ref,
    main_ref,
    rest_ref,
    main_notes_ref,
    rest_notes_ref,
    grads_ref,
    normed_ref,
    residual_ref,
    small_ref,
    mixed_ref,
    routes_ref,
    side_ref,
    ffn_a_ref,
    ffn_b_ref,
    router_ref,
    router_a_ref,
    router_b_ref,
    mix_ref,
    gain_ref,
    down_a_ref,
    down_b_ref,
    first_a_ref,
    first_b_ref,
    second_a_ref,
    second_b_ref,
    weight_hbm,
    grad_residual_ref,
    grad_mixed_ref,
    adapter_ref,
    router_grad_ref,
    shared_side_ref,
    weight_ref,
    sem,
):
    load = pltpu.make_async_copy(weight_hbm, weight_ref, sem)
    load.start()
    experts = router_ref.shape[1]
    side = side_ref[...]
    pick = pair_pick(side, 1)
    grads = grads_ref[0]
    grads_f = grads.astype(F32)
    normed = normed_ref[...]
    out_lanes = small_ref[:, :PAIR].astype(BF)
    router_lanes = small_ref[:, PAIR : 2 * PAIR].astype(BF)
    gates = [small_ref[:, 2 * PAIR + k : 2 * PAIR + k + 1] for k in range(TOP)]
    mix = small_ref[:, 2 * PAIR + TOP : 2 * PAIR + TOP + 1]
    notes = sum(part_notes_ref[i].astype(F32) for i in range(part_notes_ref.shape[0]))
    shared_side = notes[:, :PAIR].astype(BF)
    shared_side_ref[...] = padded(shared_side)
    down_second = pair_of(down_a_ref, down_b_ref, 0)
    mix_total = (
        notes[:, 3 * PAIR : 3 * PAIR + 1]
        + notes[:, 3 * PAIR + 1 : 3 * PAIR + 2]
        + jnp.sum(shared_side.astype(F32) * dot_nt(grads, down_second), axis=1, keepdims=True)
    )
    grad_mix = mix_total * mix * (1.0 - mix)
    grad_shared = (mix * grads_f).astype(BF)
    expert_hot, main_hot, rest_hot = routing(routes_ref[0], experts)
    grad_gates = []
    mask = quarter_mask(rest_hot[0].shape, 0)
    token_notes = None
    for k in range(TOP):
        mine = dot(main_hot[k].astype(BF), main_notes_ref[...]) + dot(
            (rest_hot[k] * mask).astype(BF), rest_notes_ref[...]
        )
        grad_gates.append(mine[:, PAIR : PAIR + 1] + mine[:, PAIR + 1 : PAIR + 2])
        token_notes = mine if k == 0 else token_notes + mine
    inner = sum(gate * grad for gate, grad in zip(gates, grad_gates))
    grad_logits = sum(
        hot * (gate * (grad - inner)) for hot, gate, grad in zip(expert_hot, gates, grad_gates)
    )
    logits_high, logits_low = two_parts(grad_logits)
    router_second = jnp.concatenate([router_a_ref[0], router_b_ref[0]], axis=0)
    grad_router_lanes = dot_nt(logits_high, router_second) + dot_nt(logits_low, router_second)
    router_grad = dot_tn(router_lanes, logits_high) + dot_tn(router_lanes, logits_low)
    of_row = jnp.where(row_index((PAIR, 128)) < RANK, numbers_ref[0], numbers_ref[1]).astype(F32)
    router_grad_ref[...] = jnp.where(
        lane_index((PAIR, 128)) == experts, of_row, padded(router_grad)
    ).astype(BF)
    lane_grads = (
        jnp.concatenate(
            [
                grad_router_lanes,
                notes[:, PAIR : 3 * PAIR],
                token_notes[:, :RANK],
                token_notes[:, :RANK],
                token_notes[:, RANK:PAIR],
                token_notes[:, RANK:PAIR],
            ],
            axis=1,
        )
        * pair_pick(side, 5)
    ).astype(BF)
    factors = ffn_a_ref.shape[0]
    ffn_first = jnp.concatenate([pair_of(ffn_a_ref, ffn_b_ref, i) for i in range(factors)], axis=0)
    grad_second = (
        grad_mix * mix_ref[...].astype(F32)
        + dot_nt(logits_high, router_ref[...])
        + dot_nt(logits_low, router_ref[...])
        + sum(parts_ref[i].astype(F32) for i in range(parts_ref.shape[0]))
        + slots_to_rows(main_hot, rest_hot, main_ref[...], rest_ref[...])
        + dot(lane_grads, ffn_first)
    )
    grad_residual = grads_f + rms_backward(residual_ref[...], gain_ref[...], grad_second)
    grad_residual_ref[...] = grad_residual
    grad_attended = grad_residual.astype(BF)
    first, second = pair_of(first_a_ref, first_b_ref, 0), pair_of(second_a_ref, second_b_ref, 0)
    grad_out_lanes = (dot_nt(grad_attended, second) * pick).astype(BF)
    adapter_ref[...] = jnp.concatenate(
        [
            dot_tn(lane_grads, normed),
            dot_tn(grad_out_lanes, mixed_ref[...]),
            dot_tn(out_lanes, grad_attended),
            dot_tn(shared_side, grad_shared),
        ],
        axis=0,
    ).astype(BF)
    load.wait()
    grad_mixed_ref[...] = (
        dot_nt(grad_attended, weight_ref[...]) + dot(grad_out_lanes, first)
    ).astype(BF)


def after_experts(
    numbers, parts, part_notes, main, rest, main_notes, rest_notes, grads, normed, residual, small, mixed,
    routes, side, ffn_first, router, router_second, mix, gain, down_second, first, second, weight,
):
    tokens, width = normed.shape
    experts = router.shape[1]
    factors = ffn_first.shape[0]
    last = lambda which: pl.BlockSpec((1, 1, RANK, width), lambda n, a: (3, a[which], 0, 0))
    outs = [
        ((tokens, width), F32),
        ((tokens, width), BF),
        (((factors + 3) * PAIR, width), BF),
        ((PAIR, 128), BF),
        ((tokens, 128), BF),
    ]
    plain = (
        parts, part_notes, main, rest, main_notes, rest_notes, grads, normed, residual, small, mixed, routes,
        side,
    )
    return stage(
        after_experts_kernel,
        "after_experts",
        [shape_of(*out) for out in outs],
        [whole(array) for array in plain]
        + [
            of_sequence(0, (factors, 1, RANK, width)),
            of_sequence(1, (factors, 1, RANK, width)),
            whole(router),
            pl.BlockSpec((1, RANK, experts), lambda n, a: (a[0], 0, 0)),
            pl.BlockSpec((1, RANK, experts), lambda n, a: (a[1], 0, 0)),
            whole(mix),
            whole(gain),
            of_sequence(0, (1, 1, RANK, width)),
            of_sequence(1, (1, 1, RANK, width)),
            last(0),
            last(1),
            last(0),
            last(1),
            ANY,
        ],
        [pl.BlockSpec(shape, lambda n, a: (0, 0)) for shape, kind in outs],
        scratch=[pltpu.VMEM(weight.shape, BF), pltpu.SemaphoreType.DMA],
        prefetch=1,
    )(
        numbers, *plain, ffn_first, ffn_first, router, router_second, router_second, mix, gain, down_second,
        down_second, first, first, second, second, weight,
    )


def back_project_kernel(
    numbers_ref,
    query_ref,
    pairs_ref,
    cos_ref,
    sin_ref,
    side_ref,
    lanes_ref,
    second_a_ref,
    second_b_ref,
    weight_ref,
    out_ref,
    notes_ref,
    adapter_ref,
    grads_ref,
):
    columns = grads_ref.shape[2]

    @pl.when(pl.program_id(0) == 0)
    def prepare():
        grads_ref[0] = query_ref[...]
        key = pairs_ref[0, 0].astype(F32) + pairs_ref[1, 0].astype(F32)
        copies = columns // HEAD_DIM
        cosine = jnp.concatenate([cos_ref[...]] * copies, axis=1)
        sine = jnp.concatenate([sin_ref[...]] * copies, axis=1)
        grads_ref[1] = (key * cosine - half_turn(key) * sine).astype(BF)
        grads_ref[2] = (pairs_ref[0, 1].astype(F32) + pairs_ref[1, 1].astype(F32)).astype(BF)
        pick = pair_pick(side_ref[...], 1)
        notes = []
        for j in range(3):
            second = pair_of(second_a_ref, second_b_ref, j)
            notes.append((dot_nt(grads_ref[j], second) * pick).astype(BF))
            adapter_ref[j * PAIR : (j + 1) * PAIR, :] = dot_tn(lanes_ref[j], grads_ref[j]).astype(BF)
        notes_ref[...] = padded(jnp.concatenate(notes, axis=1))

    total = None
    for j in range(3):
        weight = weight_ref[:, j].reshape(-1, columns)
        part = dot_nt(grads_ref[j], weight)
        total = part if total is None else total + part
    out_ref[...] = total.astype(BF)


def back_project(numbers, query, pairs, cosine, sine, side, lanes, second, weight):
    tokens, columns = query.shape
    shards, unused, depth, unused = weight.shape
    step = 4
    sequence = lambda which: pl.BlockSpec(
        (3, 1, RANK, columns), lambda n, a: (0, a[which], 0, a[2])
    )
    return stage(
        back_project_kernel,
        "back_project",
        [
            shape_of((tokens, shards * depth), BF),
            shape_of((tokens, 128), BF),
            shape_of((3 * PAIR, columns), BF),
        ],
        [
            whole(query),
            whole(pairs),
            whole(cosine),
            whole(sine),
            whole(side),
            whole(lanes),
            sequence(0),
            sequence(1),
            pl.BlockSpec((step, 3, depth, columns), lambda n, a: (n, 0, 0, 0)),
        ],
        [
            pl.BlockSpec((tokens, step * depth), lambda n, a: (0, n)),
            pl.BlockSpec((tokens, 128), lambda n, a: (0, 0)),
            pl.BlockSpec((3 * PAIR, columns), lambda n, a: (0, 0)),
        ],
        grid=(shards // step,),
        scratch=[pltpu.VMEM((3, tokens, columns), BF)],
        prefetch=1,
    )(numbers, query, pairs, cosine, sine, side, lanes, second, second, weight)


def last_kernel(
    numbers_ref,
    parts_ref,
    notes_ref,
    rows_ref,
    normed_ref,
    residual_ref,
    gain_ref,
    first_a_ref,
    first_b_ref,
    out_ref,
    adapter_ref,
):
    lanes = sum(notes_ref[i].astype(F32) for i in range(notes_ref.shape[0]))[:, : 3 * PAIR]
    lanes = lanes.astype(BF)
    first = jnp.concatenate([pair_of(first_a_ref, first_b_ref, j) for j in range(3)], axis=0)
    grad = sum(parts_ref[i].astype(F32) for i in range(parts_ref.shape[0])) + dot(lanes, first)
    adapter_ref[...] = dot_tn(lanes, normed_ref[...]).astype(BF)
    total = residual_ref[...] + rms_backward(rows_ref[0].astype(F32), gain_ref[...], grad)
    out_ref[0] = total.astype(BF)


def last_stage(numbers, parts, notes, rows, normed, residual, gain, first):
    width = rows.shape[2]
    plain = (parts, notes, rows, normed, residual, gain)
    return stage(
        last_kernel,
        "last_stage",
        [shape_of(rows.shape, BF), shape_of((3 * PAIR, width), BF)],
        [whole(array) for array in plain]
        + [of_sequence(0, (3, 1, RANK, width)), of_sequence(1, (3, 1, RANK, width))],
        [
            pl.BlockSpec(rows.shape, lambda n, a: (0, 0, 0)),
            pl.BlockSpec((3 * PAIR, width), lambda n, a: (0, 0)),
        ],
        prefetch=1,
    )(numbers, *plain, first, first)


def combine_kernel(
    numbers_ref, main_ref, rest_ref, routes_ref, residual_ref, parts_ref, side_ref, small_ref, down_a_ref,
    down_b_ref, out_ref,
):
    experts = main_ref.shape[0] // MAIN
    unused, main_hot, rest_hot = routing(routes_ref[0], experts)
    mixture = slots_to_rows(main_hot, rest_hot, main_ref[...], rest_ref[...])
    shared = sum(parts_ref[i].astype(F32) for i in range(parts_ref.shape[0]))
    shared = shared + dot(side_ref[:, :PAIR], pair_of(down_a_ref, down_b_ref, 0))
    mix = small_ref[:, 2 * PAIR + TOP : 2 * PAIR + TOP + 1]
    out_ref[0] = (residual_ref[...] + mixture + mix * shared).astype(BF)


def combine(results, routes, residual, parts, side, small, down_second, numbers):
    tokens, width = residual.shape
    plain = (*results, routes, residual, parts, side, small)
    return stage(
        combine_kernel,
        "combine",
        shape_of((1, tokens, width), BF),
        [whole(array) for array in plain]
        + [of_sequence(0, (1, 1, RANK, width)), of_sequence(1, (1, 1, RANK, width))],
        pl.BlockSpec((1, tokens, width), lambda n, a: (0, 0, 0)),
        prefetch=1,
    )(numbers, *plain, down_second, down_second)


def shards(
    layer_hidden_input,
    output_cotangent,
    sequence_pair_lengths,
    block_placement_order,
    sequence_adapter_index,
    token_expert_choices,
    attention_norm_gain,
    feedforward_norm_gain,
    query_key_value_weight,
    output_projection_weight,
    query_key_value_bias,
    router_weight_matrix,
    shared_gate_up_weight,
    shared_down_weight,
    shared_sigmoid_gate,
    routed_gate_up_weight,
    routed_down_weight,
    attention_adapter_first,
    attention_adapter_second,
    feedforward_adapter_first,
    router_adapter_second,
    shared_gate_adapter_second,
    shared_down_adapter_first,
    routed_gate_adapter_second,
    routed_down_adapter_first,
    down_adapter_second,
):
    tokens, width = layer_hidden_input.shape[1:]
    experts = router_weight_matrix.shape[1]
    capacity = tokens * TOP // experts * 9 // 8
    tail = capacity - MAIN
    ctx_count = lax.axis_size("ctx")
    group_rows = tokens * ctx_count
    along = ctx_count // 2
    rows_shared = tokens * along
    x_index = lax.axis_index("ctx") // 2
    y_index = lax.axis_index("ctx") % 2
    head_columns = width // along
    hidden = shared_down_weight.shape[0]
    quarter = hidden // along
    shards_of = lax.axis_size("fsdp")
    lengths = sequence_pair_lengths[0]
    order = block_placement_order[0]
    adapters = sequence_adapter_index[0]
    block_size = group_rows // order.shape[0]

    qkv_own = lax.dynamic_slice_in_dim(
        query_key_value_weight, x_index * head_columns, head_columns, 2
    ).reshape(-1, head_columns)
    out_weight = lax.all_gather(output_projection_weight, "fsdp", tiled=True)
    units = -(-quarter // 32) * 32
    own_up = jnp.swapaxes(
        lax.dynamic_slice_in_dim(shared_gate_up_weight, x_index * quarter, quarter, 2), 1, 2
    )
    own_down = lax.dynamic_slice_in_dim(shared_down_weight, x_index * quarter, quarter, 0)
    own_shared = jnp.pad(
        jnp.concatenate([own_up, own_down[None]]), ((0, 0), (0, units - quarter), (0, 0))
    ).reshape(3 * units, width)

    def of_group(factor):
        parts = [lax.dynamic_index_in_dim(factor, adapters[s], -3, keepdims=True) for s in range(2)]
        both = jnp.concatenate(parts, axis=-3)
        return both.reshape(both.shape[:-3] + (PAIR, both.shape[-1]))

    shared_second = jnp.concatenate(
        [
            of_group(shared_gate_adapter_second).reshape(2 * PAIR, hidden * shards_of),
            of_group(shared_down_adapter_first),
        ],
        axis=0,
    )
    shared_second = lax.dynamic_index_in_dim(
        shared_second.reshape(3 * PAIR, shards_of, along, quarter), x_index, 2, keepdims=False
    )
    shared_second = jnp.pad(shared_second, ((0, 0), (0, 0), (0, units - quarter)))
    shared_second = shared_second.reshape(3 * PAIR, shards_of * units)
    numbers = jnp.concatenate([adapters, x_index[None].astype(jnp.int32)])

    start = lengths[0]
    block_rows = jnp.arange(block_size, dtype=jnp.int32)
    blocks = order.reshape(along, 2, -1)
    key_places = (jnp.swapaxes(blocks, 0, 1).reshape(-1)[:, None] * block_size + block_rows).reshape(
        1, group_rows
    )
    own_blocks = lax.dynamic_index_in_dim(blocks, y_index, 1, keepdims=False).reshape(-1)
    places = own_blocks[:, None] * block_size + block_rows
    second = places >= start
    fractions = jnp.arange(0, HEAD_DIM, 2).astype(F32) / HEAD_DIM
    speeds = rope_theta ** (-fractions)
    bases = jnp.stack([own_blocks * block_size, own_blocks * block_size - start])
    base_angles = bases.astype(F32)[:, :, None, None] * speeds
    base_angles = jnp.concatenate([base_angles, base_angles], axis=3)
    base_cos, base_sin = jnp.cos(base_angles), jnp.sin(base_angles)
    base_cos = jnp.where(second[:, :, None], base_cos[1], base_cos[0])
    base_sin = jnp.where(second[:, :, None], base_sin[1], base_sin[0])
    row_angles = block_rows.astype(F32)[:, None] * speeds[None, :]
    row_angles = jnp.concatenate([row_angles, row_angles], axis=1)
    row_cos, row_sin = jnp.cos(row_angles), jnp.sin(row_angles)
    cosine = base_cos * row_cos - base_sin * row_sin
    sine = base_sin * row_cos + base_cos * row_sin
    sine = jnp.where(jnp.arange(HEAD_DIM) < HEAD_DIM // 2, -sine, sine)
    cosine, sine = cosine.reshape(rows_shared, HEAD_DIM), sine.reshape(rows_shared, HEAD_DIM)
    place_column = places.reshape(rows_shared, 1)
    start_column = jnp.where(second, start, 0).reshape(rows_shared, 1)
    side_shared = second.astype(F32).reshape(rows_shared, 1)
    side = lax.dynamic_slice_in_dim(side_shared, x_index * tokens, tokens)

    attention_gain = attention_norm_gain[None, :]
    feedforward_gain = feedforward_norm_gain[None, :]
    mix_weight = shared_sigmoid_gate[None, :]
    routed_second = routed_gate_adapter_second.reshape(2, LANES, -1)
    routed_first = routed_down_adapter_first.reshape(LANES, -1)
    ffn_flat = feedforward_adapter_first.reshape(-1, LANES, width)[3:]
    down_flat = down_adapter_second.reshape(2, LANES, width)

    normed_one, grads_main, grads_rest = prologue(
        layer_hidden_input, output_cotangent, attention_gain, token_expert_choices, experts
    )
    own_shared, normed_one = lax.optimization_barrier((own_shared, normed_one))
    shared_weight = lax.all_gather(own_shared, "fsdp")
    qkv, normed_shared = exchange(
        "gather_first", 0, ("share", "s", qkv_own), ("gather", "x", normed_one)
    )
    qkv = qkv.reshape(shards_of, 3, tokens, head_columns)
    projected, qkv_lanes = project(
        numbers,
        normed_shared.reshape(rows_shared, width),
        qkv,
        attention_adapter_first,
        attention_adapter_second,
        query_key_value_bias,
        side_shared,
        cosine,
        sine,
    )
    pairs, grads_main, grads_rest, grads_shared = exchange(
        "keys",
        1,
        ("gather", "y", projected[1:]),
        ("rows", "f", grads_main),
        ("rows", "f", grads_rest),
        ("gather", "x", output_cotangent[0]),
    )
    expert_grads = (grads_main, grads_rest)
    mixed_heads = attend(projected, pairs, place_column, start_column, key_places)
    (mixed,) = exchange(
        "mixed", 2, ("to_columns", "x", mixed_heads.reshape(along, tokens, head_columns))
    )
    residual, normed_two, small, sent_main, sent_rest, notes_main, notes_rest = after_attention(
        numbers,
        mixed,
        out_weight,
        layer_hidden_input,
        attention_adapter_first,
        attention_adapter_second,
        feedforward_gain,
        feedforward_adapter_first,
        router_weight_matrix,
        router_adapter_second,
        mix_weight,
        token_expert_choices,
        side,
    )
    second_shared, got_main, got_rest, got_notes_main, got_notes_rest = exchange(
        "dispatch",
        3,
        ("gather", "x", normed_two),
        ("rows", "f", sent_main),
        ("rows", "f", sent_rest),
        ("rows", "f", notes_main),
        ("rows", "f", notes_rest),
    )
    (
        back_main,
        back_rest,
        result_main,
        result_rest,
        back_notes_main,
        back_notes_rest,
        grad_expert_rows,
        grad_down_expert,
    ) = routed_expert(
        (got_main, got_rest),
        expert_grads,
        (got_notes_main, got_notes_rest),
        ffn_flat,
        routed_second,
        routed_first,
        down_flat,
        routed_gate_up_weight,
        routed_down_weight,
    )
    grad_second_part, value_part, lanes_part, grad_shared_rows = shared_expert(
        numbers,
        second_shared.reshape(rows_shared, width),
        grads_shared.reshape(rows_shared, width),
        side_shared,
        feedforward_adapter_first,
        shared_second,
        down_adapter_second,
        mix_weight,
        shared_weight,
    )
    parts_rows, parts_lanes, got_main, got_rest, got_notes_main, got_notes_rest = exchange(
        "collect",
        4,
        ("swap", "x", grad_second_part.reshape(along, tokens, width)),
        ("swap", "x", lanes_part.reshape(along, tokens, 128)),
        ("rows", "f", back_main),
        ("rows", "f", back_rest),
        ("rows", "f", back_notes_main),
        ("rows", "f", back_notes_rest),
    )
    grad_residual, grad_mixed, early_columns, router_rows, shared_side = after_experts(
        numbers,
        parts_rows,
        parts_lanes,
        got_main,
        got_rest,
        got_notes_main,
        got_notes_rest,
        output_cotangent,
        normed_two,
        residual,
        small,
        mixed,
        token_expert_choices,
        side,
        feedforward_adapter_first,
        router_weight_matrix,
        router_adapter_second,
        mix_weight,
        feedforward_gain,
        down_adapter_second,
        attention_adapter_first,
        attention_adapter_second,
        out_weight,
    )

    grad_heads, result_main, result_rest = exchange(
        "heads",
        5,
        ("from_columns", "x", grad_mixed),
        ("rows", "f", result_main),
        ("rows", "f", result_rest),
    )
    results = (result_main, result_rest)
    grad_query, grad_pairs = attend_back(
        projected,
        pairs,
        grad_heads.reshape(rows_shared, head_columns),
        place_column,
        start_column,
        key_places,
        cosine,
        sine,
    )
    pair_parts, value_parts = exchange(
        "key_grads",
        6,
        ("swap", "y", grad_pairs),
        ("swap", "x", value_part.reshape(along, tokens, width)),
    )
    first_part, lanes_first_part, head_rows = back_project(
        numbers,
        grad_query,
        pair_parts,
        cosine,
        sine,
        side_shared,
        qkv_lanes,
        attention_adapter_second,
        qkv,
    )

    def by_shard(rows):
        blocks = rows.astype(BF).reshape(rows.shape[0], shards_of, -1)
        blocks = blocks.transpose(1, 0, 2)
        return jnp.pad(blocks, ((0, 0), (0, 0), (0, 128 - blocks.shape[2])))

    early_blocks = jnp.concatenate(
        [by_shard(grad_expert_rows), by_shard(grad_shared_rows)], axis=1
    )
    head_rows = lax.dynamic_update_slice(
        jnp.zeros((3 * PAIR, width), BF), head_rows, (0, x_index * head_columns)
    )
    early_columns = jnp.concatenate(
        [early_columns, head_rows, grad_down_expert.astype(BF)], axis=0
    )
    first_parts, first_lanes, early_got, blocks_got, router_got = exchange(
        "first_grads",
        7,
        ("swap", "x", first_part.reshape(along, tokens, width)),
        ("swap", "x", lanes_first_part.reshape(along, tokens, 128)),
        ("from_columns", "f", early_columns),
        ("swap", "f", early_blocks),
        ("gather", "f", router_rows),
    )
    grad_tokens, late_columns = last_stage(
        numbers,
        first_parts,
        first_lanes,
        layer_hidden_input,
        normed_one,
        grad_residual,
        attention_gain,
        attention_adapter_first,
    )

    (late_got,) = exchange("late_grads", 8, ("from_columns", "f", late_columns))

    group_adapters = router_got[:, :, experts].astype(jnp.int32)
    lane_of = group_adapters * RANK + jnp.arange(PAIR, dtype=jnp.int32)[None, :] % RANK
    expand = (
        jnp.arange(LANES, dtype=jnp.int32)[:, None, None] == lane_of[None, :, :]
    ).astype(BF)
    expand = expand.reshape(LANES, shards_of * PAIR)

    def spread_rows(got):
        factors = got.shape[1] // PAIR
        blocks = got.reshape(shards_of, factors, PAIR, got.shape[2])
        blocks = blocks.transpose(1, 0, 2, 3).reshape(factors, shards_of * PAIR, got.shape[2])
        return [dot(expand, blocks[i]) for i in range(factors)]

    early_sums = spread_rows(early_got[:, : 11 * PAIR])
    down_expert_sum = jnp.sum(early_got[:, 11 * PAIR :].astype(F32), axis=0)
    expert_sum = jnp.sum(blocks_got[:, : 3 * LANES].astype(F32), axis=0)
    shared_sums = spread_rows(blocks_got[:, 3 * LANES :])
    own_column = (jnp.arange(128) == lax.axis_index("fsdp")).astype(BF)
    router_sum = spread_rows(router_got * own_column)[0]
    late_sums = spread_rows(late_got)
    all_rows = jnp.concatenate(
        [
            *late_sums,
            early_sums[5],
            *early_sums[8:11],
            early_sums[6],
            *early_sums[:5],
            early_sums[7],
            down_expert_sum,
            expert_sum,
            router_sum,
        ],
        axis=0,
    ).astype(BF)
    shared_rows = jnp.concatenate(shared_sums, axis=0).astype(BF)
    row_parts, shared_parts = exchange(
        "ctx_parts",
        9,
        ("swap", "c", all_rows.reshape(ctx_count, -1, 128)),
        ("gather", "c", shared_rows),
    )
    row_sum = jnp.sum(row_parts.astype(F32), axis=0).astype(BF)
    (totals,) = exchange("ctx_sums", 10, ("gather", "c", row_sum))
    totals = totals.reshape(-1, 128).astype(F32)
    shared_total = jnp.sum(
        shared_parts.astype(F32).reshape(along, 2, 3 * LANES, 128), axis=1
    )[:, :, :quarter]
    shared_total = shared_total.transpose(1, 0, 2).reshape(3 * LANES, along * quarter)
    expert_width = routed_down_weight.shape[1] // shards_of

    def rows(first, factors, columns=128):
        part = totals[first * LANES : (first + factors) * LANES, :columns]
        return part.reshape(factors, ADAPTER_COUNT, RANK, columns)

    mixture = combine(results, token_expert_choices, residual, value_parts, shared_side, small, down_adapter_second, numbers)

    return (
        mixture,
        grad_tokens,
        rows(0, 4),
        rows(4, 4),
        rows(8, 5),
        jnp.sum(totals[18 * LANES : 19 * LANES], axis=1).reshape(ADAPTER_COUNT, RANK, 1),
        shared_total[: 2 * LANES].reshape(2, ADAPTER_COUNT, RANK, -1),
        shared_total[2 * LANES :].reshape(ADAPTER_COUNT, RANK, -1),
        rows(15, 2, expert_width),
        rows(17, 1, expert_width)[0],
        rows(13, 2),
    )


def solution(mesh):
    return jax.shard_map(
        shards,
        mesh=mesh,
        in_specs=(
            P("fsdp", "ctx", None),
            P("fsdp", "ctx", None),
            P("fsdp", None),
            P("fsdp", None),
            P("fsdp", None),
            P("fsdp", "ctx", None),
            P(),
            P(),
            P(None, "fsdp", None),
            P("fsdp", None),
            P(),
            P(),
            P(None, None, "fsdp"),
            P("fsdp", None),
            P(),
            P("fsdp", None, None, None),
            P("fsdp", None, None),
            P(),
            P(),
            P(),
            P(),
            P(),
            P(),
            P(),
            P(),
            P(),
        ),
        out_specs=(
            P("fsdp", "ctx", None),
            P("fsdp", "ctx", None),
            P(None, None, None, "fsdp"),
            P(None, None, None, "fsdp"),
            P(None, None, None, "fsdp"),
            P(None, None, "fsdp"),
            P(None, None, None, "fsdp"),
            P(None, None, "fsdp"),
            P(None, None, None, "fsdp"),
            P(None, None, "fsdp"),
            P(None, None, None, "fsdp"),
        ),
        check_vma=False,
    )
```

```python
import functools

import jax
import jax.numpy as jnp
from jax import lax
from jax.experimental import pallas as pl
from jax.experimental.pallas import tpu as pltpu
from jax.sharding import PartitionSpec as P

HEADS = 16
HEAD_DIM = 128
TOP = 4
ADAPTER_COUNT = 8
RANK = 16
LANES = ADAPTER_COUNT * RANK
PAIR = 2 * RANK
MAIN = 32

norm_eps = 1e-06
rope_theta = 1000000.0
masked_score = -1e30
highest = lax.Precision.HIGHEST
MESH = pl.DeviceIdType.MESH
BF = jnp.bfloat16
F32 = jnp.float32
VMEM_LIMIT = 56 * 2**20


def dot(left, right):
    return jnp.dot(left, right, preferred_element_type=F32)


def dot_nt(left, right):
    return lax.dot_general(left, right, (((1,), (1,)), ((), ())), preferred_element_type=F32)


def dot_tn(left, right):
    return lax.dot_general(left, right, (((0,), (0,)), ((), ())), preferred_element_type=F32)


GROUP_SIZE = {"x": 4, "y": 2, "c": 8, "f": 16}


def place_in(group):
    ctx, fsdp = lax.axis_index("ctx"), lax.axis_index("fsdp")
    return {"x": ctx // 2, "y": ctx % 2, "c": ctx, "f": fsdp}[group]


def device_of(group, index):
    ctx, fsdp = lax.axis_index("ctx"), lax.axis_index("fsdp")
    if group == "x":
        return (index * 2 + ctx % 2, fsdp)
    if group == "y":
        return ((ctx // 2) * 2 + index, fsdp)
    if group == "c":
        return (index, fsdp)
    return (ctx, index)


def chip():
    ctx, fsdp = lax.axis_index("ctx"), lax.axis_index("fsdp")
    return ctx % 2 * 2 + fsdp // 8, fsdp // 2 % 4, fsdp % 2


def device_at(y, z, core):
    return (lax.axis_index("ctx") // 2 * 2 + y // 2, y % 2 * 8 + z * 2 + core)


def shard_at(y, z, core):
    return y % 2 * 8 + z * 2 + core


def exchanged_shape(kind, group, shape):
    if kind == "share":
        return (GROUP_SIZE["f"],) + shape
    count = GROUP_SIZE[group]
    if kind == "gather":
        return (count,) + shape
    if kind in ("swap", "rows"):
        return shape
    if kind == "from_columns":
        return (count, shape[0], shape[1] // count)
    return (shape[1], count * shape[2])


def own_shape(kind, group, shape):
    if kind in ("gather", "share"):
        return shape
    count = GROUP_SIZE[group]
    if kind == "rows":
        return (shape[0] // count,) + shape[1:]
    if kind == "from_columns":
        return (shape[0], shape[1] // count)
    return shape[1:]


def copies_of(kind, group):
    return 23 if kind == "share" else GROUP_SIZE[group] - 1


def block_of(ref, kind, count, index):
    if kind == "rows":
        depth = ref.shape[0] // count
        return ref.at[pl.ds(pl.multiple_of(index * depth, depth), depth)]
    if kind == "columns":
        width = ref.shape[1] // count
        return ref.at[:, pl.ds(pl.multiple_of(index * width, width), width)]
    return ref.at[index]


def source_of(kind, group, ref, index):
    if kind in ("gather", "share"):
        return ref
    cut = {"rows": "rows", "from_columns": "columns"}.get(kind, "first")
    return block_of(ref, cut, GROUP_SIZE[group], index)


def target_of(kind, group, ref, index):
    cut = {"rows": "rows", "to_columns": "columns"}.get(kind, "first")
    return block_of(ref, cut, GROUP_SIZE["f" if kind == "share" else group], index)


def remote(source, target, send, recv, device):
    return pltpu.make_async_remote_copy(
        src_ref=source,
        dst_ref=target,
        send_sem=send,
        recv_sem=recv,
        device_id=device,
        device_id_type=MESH,
    )


def greet(plan):
    barrier = pltpu.get_barrier_semaphore()
    count = 0
    for group in sorted({group for kind, group in plan}):
        if group == "s":
            y, z, core = chip()
            peers = [device_at(y, lax.rem(z + d, 4), core) for d in (1, 2, 3)]
            peers += [device_at(lax.rem(y + d, 4), z, core) for d in (1, 3)]
            peers += [device_at(y, z, 1 - core)]
        else:
            size = GROUP_SIZE[group]
            mine = place_in(group)
            peers = [device_of(group, lax.rem(mine + d, size)) for d in range(1, size)]
        for peer in peers:
            pl.semaphore_signal(barrier, inc=1, device_id=peer, device_id_type=MESH)
        count += len(peers)
    pl.semaphore_wait(barrier, count)


class Share:
    def __init__(self, source, target, send, recv, first):
        self.target = target
        self.sems = (send, recv, first)
        y, z, core = self.place = chip()
        self.order = (1, 3, 2)
        self.source = source
        self.along_z = [
            self.copy(source, shard_at(y, z, core), None, i, device_at(y, lax.rem(z + d, 4), core))
            for i, d in enumerate(self.order)
        ]
        self.along_y, self.across = [], []

    def copy(self, source, shard, half, number, device):
        send, recv, first = self.sems
        target = self.target.at[shard]
        if half is not None:
            target = target.at[half]
        return remote(source, target, send.at[first + number], recv.at[first + number], device)

    def halves(self):
        half = self.target.shape[1] // 2
        return pl.ds(0, half), pl.ds(half, half)

    def forward(self, number, source, z):
        y, unused, core = self.place
        unused, my_z, unused = self.place
        shard = shard_at(y, z, core)
        for i, (half, d) in enumerate(zip(self.halves(), (3, 1))):
            copy = self.copy(
                source.at[half], shard, half, 3 + 2 * number + i, device_at(lax.rem(y + d, 4), my_z, core)
            )
            copy.start()
            self.along_y.append(copy)
        copy = self.copy(source, shard, None, 11 + number, device_at(y, my_z, 1 - core))
        copy.start()
        self.across.append(copy)

    def start(self):
        for copy in self.along_z:
            copy.start()
        self.forward(0, self.source, self.place[1])

    def finish(self):
        y, z, core = self.place
        for i, d in enumerate(self.order):
            self.along_z[i].wait_recv()
            from_z = lax.rem(z + 4 - d, 4)
            self.forward(i + 1, self.target.at[shard_at(y, from_z, core)], from_z)
        for number in range(4):
            from_z = z if number == 0 else lax.rem(z + 4 - self.order[number - 1], 4)
            shard = shard_at(y + 1, from_z, core)
            for i, half in enumerate(self.halves()):
                self.along_y[2 * number + i].wait_recv()
                block = self.target.at[shard].at[half]
                copy = self.copy(block, shard, half, 15 + 2 * number + i, device_at(y, z, 1 - core))
                copy.start()
                self.across.append(copy)
        for copy in self.along_z + self.along_y:
            copy.wait_send()
        for copy in self.across:
            copy.wait()


class Mover:
    def __init__(self, plan, inputs, outputs, own, send, recv, in_sem, out_sem):
        self.plan, self.inputs, self.outputs, self.own = plan, inputs, outputs, own
        self.send, self.recv, self.in_sem, self.out_sem = send, recv, in_sem, out_sem
        self.taken, self.copies, self.shares = [], [], []

    def own_place(self, item):
        kind, group = self.plan[item]
        return shard_at(*chip()) if kind == "share" else place_in(group)

    def take(self):
        for item, (kind, group) in enumerate(self.plan):
            block = source_of(kind, group, self.inputs[item], self.own_place(item))
            copy = pltpu.make_async_copy(block, self.own[item], self.in_sem.at[item])
            copy.start()
            self.taken.append(copy)

    def start(self):
        slot = 0
        for item, (kind, group) in enumerate(self.plan):
            source, target = self.inputs[item], self.outputs[item]
            if kind == "share":
                share = Share(source, target, self.send, self.recv, slot)
                share.start()
                self.shares.append(share)
            else:
                count = GROUP_SIZE[group]
                mine = place_in(group)
                for offset in range(1, count):
                    peer = lax.rem(mine + offset, count)
                    copy = remote(
                        source_of(kind, group, source, peer),
                        target_of(kind, group, target, mine),
                        self.send.at[slot + offset - 1],
                        self.recv.at[slot + offset - 1],
                        device_of(group, peer),
                    )
                    copy.start()
                    self.copies.append(copy)
            slot += copies_of(kind, group)
        for item, (kind, group) in enumerate(self.plan):
            self.taken[item].wait()
            block = target_of(kind, group, self.outputs[item], self.own_place(item))
            copy = pltpu.make_async_copy(self.own[item], block, self.out_sem.at[item])
            copy.start()
            self.copies.append(copy)

    def finish(self):
        for share in self.shares:
            share.finish()
        for copy in self.copies:
            copy.wait()


def exchange_kernel(plan, *refs):
    amount = len(plan)
    mover = Mover(
        plan, refs[:amount], refs[amount : 2 * amount], refs[2 * amount : 3 * amount], *refs[3 * amount :]
    )
    mover.take()
    greet(plan)
    mover.start()
    mover.finish()


def mover_scratch(items):
    plan = tuple((kind, group) for kind, group, array in items)
    slots = sum(copies_of(kind, group) for kind, group in plan)
    return [
        pltpu.VMEM(own_shape(kind, group, array.shape), array.dtype) for kind, group, array in items
    ] + [
        pltpu.SemaphoreType.DMA((slots,)),
        pltpu.SemaphoreType.DMA((slots,)),
        pltpu.SemaphoreType.DMA((len(items),)),
        pltpu.SemaphoreType.DMA((len(items),)),
    ]


def exchange(name, number, *items):
    plan = tuple((kind, group) for kind, group, array in items)
    arrays = [array for kind, group, array in items]
    return pl.pallas_call(
        functools.partial(exchange_kernel, plan),
        out_shape=[
            jax.ShapeDtypeStruct(exchanged_shape(kind, group, array.shape), array.dtype)
            for kind, group, array in items
        ],
        in_specs=[pl.BlockSpec(memory_space=pltpu.HBM)] * len(items),
        out_specs=[pl.BlockSpec(memory_space=pltpu.HBM)] * len(items),
        scratch_shapes=mover_scratch(items),
        compiler_params=pltpu.CompilerParams(
            collective_id=number, has_side_effects=True, vmem_limit_bytes=16 * 2**20
        ),
        name=name,
    )(*arrays)


def rms_forward(values, gain):
    mean_square = jnp.mean(values * values, axis=-1, keepdims=True)
    return values * lax.rsqrt(mean_square + norm_eps) * gain.astype(F32)


def rms_backward(values, gain, grad_result):
    scale = lax.rsqrt(jnp.mean(values * values, axis=-1, keepdims=True) + norm_eps)
    scaled = gain.astype(F32) * grad_result
    inner = jnp.mean(values * scaled, axis=-1, keepdims=True)
    return scale * scaled - values * (scale * scale * scale) * inner


def logistic(values):
    return 1.0 / (1.0 + jnp.exp(-values))


def swiglu_backward(gate, upper, grad_hidden):
    sigma = logistic(gate)
    grad_gate = grad_hidden * upper * sigma * (1.0 + gate * (1.0 - sigma))
    grad_upper = grad_hidden * gate * sigma
    return (grad_gate.astype(BF), grad_upper.astype(BF))


def two_parts(values):
    high = values.astype(BF)
    return high, (values - high.astype(F32)).astype(BF)


def lane_index(shape):
    return lax.broadcasted_iota(jnp.int32, shape, 1)


def row_index(shape):
    return lax.broadcasted_iota(jnp.int32, shape, 0)


def pair_pick(second, copies):
    shape = (second.shape[0], PAIR * copies)
    of_lane = (lane_index(shape) % PAIR >= RANK).astype(F32)
    return (of_lane == second).astype(F32)


def pair_of(first_ref, last_ref, index):
    return jnp.concatenate([first_ref[index, 0], last_ref[index, 0]], axis=0)


def padded(values):
    rest = 128 - values.shape[1]
    return jnp.concatenate([values, jnp.zeros((values.shape[0], rest), values.dtype)], axis=1)


def routing(routes, experts):
    tokens = routes.shape[0]
    expert_lane = lane_index((tokens, experts))
    expert_hot = [(routes[:, k : k + 1] == expert_lane).astype(F32) for k in range(TOP)]
    count = sum(expert_hot)
    below = (row_index((tokens, tokens)) > lane_index((tokens, tokens))).astype(BF)
    earlier = dot(below, count.astype(BF))
    rank = [jnp.sum(hot * earlier, axis=1, keepdims=True).astype(jnp.int32) for hot in expert_hot]
    main_lane = lane_index((tokens, experts * MAIN))
    rest_lane = lane_index((tokens, experts * 16))
    rest_code = (rest_lane // 16) * 4 + rest_lane % 4
    main_hot, rest_hot = [], []
    for k in range(TOP):
        expert = routes[:, k : k + 1]
        main_slot = jnp.where(rank[k] < MAIN, expert * MAIN + rank[k], -1)
        rest_slot = jnp.where(rank[k] < MAIN, -1, expert * 4 + rank[k] - MAIN)
        main_hot.append((main_lane == main_slot).astype(F32))
        rest_hot.append((rest_code == rest_slot).astype(F32))
    return expert_hot, main_hot, rest_hot


def quarter_mask(shape, quarter):
    return (lane_index(shape) % 16 // 4 == quarter).astype(F32)


def rows_to_slots(main_hot, rest_hot, rows):
    main = dot_tn(sum(main_hot).astype(BF), rows).astype(BF)
    rest_sum = sum(rest_hot)
    width = rows.shape[1] // 4
    rest = None
    for quarter in range(4):
        hot = (rest_sum * quarter_mask(rest_sum.shape, quarter)).astype(BF)
        part = dot_tn(hot, rows[:, quarter * width : (quarter + 1) * width])
        rest = part if rest is None else rest + part
    return main, rest.astype(BF)


def slots_to_rows(main_hot, rest_hot, main, rest):
    rest_sum = sum(rest_hot)
    parts = [
        dot((rest_sum * quarter_mask(rest_sum.shape, quarter)).astype(BF), rest)
        for quarter in range(4)
    ]
    return dot(sum(main_hot).astype(BF), main) + jnp.concatenate(parts, axis=1)


def rest_selectors(sources):
    shape = (4 * sources, 16 * sources)
    row, lane = row_index(shape), lane_index(shape)
    same = (lane // 16 == row // 4) & (lane % 4 == row % 4)
    return [(same & (lane % 16 // 4 == quarter)).astype(BF) for quarter in range(4)]


def rest_to_rows(selectors, rest):
    return jnp.concatenate([dot(selector, rest) for selector in selectors], axis=1).astype(BF)


def rows_to_rest(selectors, rows):
    width = rows.shape[1] // 4
    total = None
    for quarter in range(4):
        part = dot_tn(selectors[quarter], rows[:, quarter * width : (quarter + 1) * width])
        total = part if total is None else total + part
    return total.astype(BF)


def stage(kernel, name, out_shape, in_specs, out_specs, grid=(1,), scratch=(), prefetch=0):
    return pl.pallas_call(
        kernel,
        out_shape=out_shape,
        grid_spec=pltpu.PrefetchScalarGridSpec(
            num_scalar_prefetch=prefetch,
            grid=grid,
            in_specs=in_specs,
            out_specs=out_specs,
            scratch_shapes=list(scratch),
        ),
        compiler_params=pltpu.CompilerParams(vmem_limit_bytes=VMEM_LIMIT),
        name=name,
    )


def whole(array):
    zeros = (0,) * len(array.shape)
    return pl.BlockSpec(array.shape, lambda *unused: zeros)


def of_sequence(which, block):
    return pl.BlockSpec(block, lambda *at: (0, at[-1][which], 0, 0))


def shape_of(shape, kind):
    return jax.ShapeDtypeStruct(shape, kind)


HBM = pl.BlockSpec(memory_space=pltpu.HBM)


def prologue_kernel(
    numbers_ref,
    rows_ref,
    grads_ref,
    gain_ref,
    routes_ref,
    ffn_a_ref,
    ffn_b_ref,
    down_a_ref,
    down_b_ref,
    normed_ref,
    main_ref,
    rest_ref,
    picked_ref,
):
    normed_ref[...] = rms_forward(rows_ref[0].astype(F32), gain_ref[...]).astype(BF)
    experts = main_ref.shape[0] // MAIN
    unused, main_hot, rest_hot = routing(routes_ref[0], experts)
    main, rest = rows_to_slots(main_hot, rest_hot, grads_ref[0])
    main_ref[...] = main
    rest_ref[...] = rest
    picked_ref[...] = jnp.concatenate(
        [
            pair_of(ffn_a_ref, ffn_b_ref, 1),
            pair_of(ffn_a_ref, ffn_b_ref, 2),
            pair_of(down_a_ref, down_b_ref, 0),
        ],
        axis=0,
    )


def prologue(numbers, rows, grads, gain, routes, ffn_first, down_second, experts):
    tokens, width = rows.shape[1:]
    outs = [
        (tokens, width),
        (experts * MAIN, width),
        (experts * 16, width // 4),
        (3 * PAIR, width),
    ]
    return stage(
        prologue_kernel,
        "prologue",
        [shape_of(shape, BF) for shape in outs],
        [
            whole(rows),
            whole(grads),
            whole(gain),
            whole(routes),
            of_sequence(0, (3, 1, RANK, width)),
            of_sequence(1, (3, 1, RANK, width)),
            of_sequence(0, (1, 1, RANK, width)),
            of_sequence(1, (1, 1, RANK, width)),
        ],
        [pl.BlockSpec(shape, lambda n, a: (0, 0)) for shape in outs],
        prefetch=1,
    )(numbers, rows, grads, gain, routes, ffn_first, ffn_first, down_second, down_second)


def half_turn(values):
    parts = []
    for head in range(values.shape[1] // HEAD_DIM):
        part = values[:, head * HEAD_DIM : (head + 1) * HEAD_DIM]
        parts.append(jnp.concatenate([part[:, 64:], part[:, :64]], axis=1))
    return jnp.concatenate(parts, axis=1) if len(parts) > 1 else parts[0]


def project_kernel(
    numbers_ref,
    rows_ref,
    weight_ref,
    first_a_ref,
    first_b_ref,
    second_a_ref,
    second_b_ref,
    bias_ref,
    side_ref,
    cos_ref,
    sin_ref,
    out_ref,
    lanes_ref,
):
    which = pl.program_id(0)

    @pl.when(pl.program_id(1) == 0)
    def lanes():
        first = pair_of(first_a_ref, first_b_ref, 0)
        picked = dot_nt(rows_ref[...], first) * pair_pick(side_ref[...], 1)
        lanes_ref[0] = picked.astype(BF)

    weight = weight_ref[...].reshape(rows_ref.shape[1], weight_ref.shape[3])
    bias = bias_ref[...].astype(F32)
    bias = jnp.sum(jnp.where(row_index(bias.shape) == which, bias, 0.0), axis=0, keepdims=True)
    second = pair_of(second_a_ref, second_b_ref, 0)
    value = dot(rows_ref[...], weight) + bias + dot(lanes_ref[0], second)
    copies = value.shape[1] // HEAD_DIM
    cosine = jnp.concatenate([cos_ref[...]] * copies, axis=1)
    sine = jnp.concatenate([sin_ref[...]] * copies, axis=1)
    turned = value * cosine + half_turn(value) * sine
    out_ref[0] = jnp.where(which < 2, turned, value).astype(BF)


def project(numbers, rows, weight, first, second, bias, side, cosine, sine):
    tokens, width = rows.shape
    columns = weight.shape[3]
    step = 256
    steps = columns // step
    return stage(
        project_kernel,
        "project",
        [shape_of((3, tokens, columns), BF), shape_of((3, tokens, PAIR), BF)],
        [
            whole(rows),
            pl.BlockSpec((weight.shape[0], 1, weight.shape[2], step), lambda j, n, a: (0, j, 0, n)),
            pl.BlockSpec((1, 1, RANK, width), lambda j, n, a: (j, a[0], 0, 0)),
            pl.BlockSpec((1, 1, RANK, width), lambda j, n, a: (j, a[1], 0, 0)),
            pl.BlockSpec((1, 1, RANK, step), lambda j, n, a: (j, a[0], 0, a[2] * steps + n)),
            pl.BlockSpec((1, 1, RANK, step), lambda j, n, a: (j, a[1], 0, a[2] * steps + n)),
            pl.BlockSpec((3, step), lambda j, n, a: (0, a[2] * steps + n)),
            whole(side),
            whole(cosine),
            whole(sine),
        ],
        [
            pl.BlockSpec((1, tokens, step), lambda j, n, a: (j, 0, n)),
            pl.BlockSpec((1, tokens, PAIR), lambda j, n, a: (j, 0, 0)),
        ],
        grid=(3, steps),
        prefetch=1,
    )(numbers, rows, weight, first, first, second, second, bias, side, cosine, sine)


def probabilities(query, keys, query_place, query_start, key_place):
    scores = dot_nt(query, keys) * (HEAD_DIM**-0.5)
    allowed = (key_place <= query_place) & (key_place >= query_start)
    scores = jnp.where(allowed, scores, masked_score)
    top = jnp.max(scores, axis=1, keepdims=True)
    raised = jnp.exp(scores - top)
    return raised * (1.0 / jnp.sum(raised, axis=1, keepdims=True))


def attend_kernel(query_ref, key_ref, value_ref, place_ref, start_ref, key_place_ref, out_ref):
    keys = key_ref[...].reshape(-1, HEAD_DIM)
    values = value_ref[...].reshape(-1, HEAD_DIM)
    probs = probabilities(query_ref[0], keys, place_ref[...], start_ref[...], key_place_ref[...])
    out_ref[...] = dot(probs.astype(BF), values).astype(BF)


def attend(projected, pairs, place, start, key_place):
    tokens, columns = projected.shape[1:]
    step = 256
    keys = pairs.shape[0] * pairs.shape[2]
    half = pairs.shape[2]
    return pl.pallas_call(
        attend_kernel,
        grid=(columns // HEAD_DIM, tokens // step),
        out_shape=jax.ShapeDtypeStruct((tokens, columns), BF),
        in_specs=[
            pl.BlockSpec((1, step, HEAD_DIM), lambda h, i: (0, i, h)),
            pl.BlockSpec((2, 1, half, HEAD_DIM), lambda h, i: (0, 0, 0, h)),
            pl.BlockSpec((2, 1, half, HEAD_DIM), lambda h, i: (0, 1, 0, h)),
            pl.BlockSpec((step, 1), lambda h, i: (i, 0)),
            pl.BlockSpec((step, 1), lambda h, i: (i, 0)),
            pl.BlockSpec((1, keys), lambda h, i: (0, 0)),
        ],
        out_specs=pl.BlockSpec((step, HEAD_DIM), lambda h, i: (i, h)),
        compiler_params=pltpu.CompilerParams(vmem_limit_bytes=VMEM_LIMIT),
        name="attend",
    )(projected, pairs, pairs, place, start, key_place)


def attend_back_kernel(
    query_ref,
    key_ref,
    value_ref,
    grad_ref,
    place_ref,
    start_ref,
    key_place_ref,
    cos_ref,
    sin_ref,
    query_out,
    pair_out,
    key_total,
    value_total,
):
    step = pl.program_id(1)
    query = query_ref[0]
    grad = grad_ref[...]
    keys = key_ref[...].reshape(-1, HEAD_DIM)
    values = value_ref[...].reshape(-1, HEAD_DIM)
    probs = probabilities(query, keys, place_ref[...], start_ref[...], key_place_ref[...])
    grad_probs = dot_nt(grad, values)
    mean = jnp.sum(probs * grad_probs, axis=1, keepdims=True)
    grad_scores = (probs * (grad_probs - mean)).astype(BF)
    grad_query = dot(grad_scores, keys) * (HEAD_DIM**-0.5)
    query_out[...] = (grad_query * cos_ref[...] - half_turn(grad_query) * sin_ref[...]).astype(BF)
    grad_keys = dot_tn(grad_scores, query) * (HEAD_DIM**-0.5)
    grad_values = dot_tn(probs.astype(BF), grad)

    @pl.when(step == 0)
    def first():
        key_total[...] = grad_keys
        value_total[...] = grad_values

    @pl.when(step > 0)
    def later():
        key_total[...] += grad_keys
        value_total[...] += grad_values

    half = pair_out.shape[2]
    for side in range(2):
        pair_out[side, 0] = key_total[side * half : (side + 1) * half, :].astype(BF)
        pair_out[side, 1] = value_total[side * half : (side + 1) * half, :].astype(BF)


def attend_back(projected, pairs, grads, place, start, key_place, cosine, sine):
    tokens, columns = projected.shape[1:]
    step = 256
    keys = pairs.shape[0] * pairs.shape[2]
    half = pairs.shape[2]
    return pl.pallas_call(
        attend_back_kernel,
        grid=(columns // HEAD_DIM, tokens // step),
        out_shape=[
            jax.ShapeDtypeStruct((tokens, columns), BF),
            jax.ShapeDtypeStruct(pairs.shape, BF),
        ],
        in_specs=[
            pl.BlockSpec((1, step, HEAD_DIM), lambda h, i: (0, i, h)),
            pl.BlockSpec((2, 1, half, HEAD_DIM), lambda h, i: (0, 0, 0, h)),
            pl.BlockSpec((2, 1, half, HEAD_DIM), lambda h, i: (0, 1, 0, h)),
            pl.BlockSpec((step, HEAD_DIM), lambda h, i: (i, h)),
            pl.BlockSpec((step, 1), lambda h, i: (i, 0)),
            pl.BlockSpec((step, 1), lambda h, i: (i, 0)),
            pl.BlockSpec((1, keys), lambda h, i: (0, 0)),
            pl.BlockSpec((step, HEAD_DIM), lambda h, i: (i, 0)),
            pl.BlockSpec((step, HEAD_DIM), lambda h, i: (i, 0)),
        ],
        out_specs=[
            pl.BlockSpec((step, HEAD_DIM), lambda h, i: (i, h)),
            pl.BlockSpec((2, 2, half, HEAD_DIM), lambda h, i: (0, 0, 0, h)),
        ],
        scratch_shapes=[pltpu.VMEM((keys, HEAD_DIM), F32), pltpu.VMEM((keys, HEAD_DIM), F32)],
        compiler_params=pltpu.CompilerParams(vmem_limit_bytes=VMEM_LIMIT),
        name="attend_back",
    )(projected, pairs, pairs, grads, place, start, key_place, cosine, sine)


def after_attention_kernel(
    numbers_ref,
    mixed_ref,
    weight_ref,
    rows_ref,
    first_a_ref,
    first_b_ref,
    second_a_ref,
    second_b_ref,
    gain_ref,
    ffn_a_ref,
    ffn_b_ref,
    router_ref,
    router_a_ref,
    router_b_ref,
    mix_ref,
    routes_ref,
    side_ref,
    residual_ref,
    normed_ref,
    small_ref,
    main_ref,
    rest_ref,
    main_notes_ref,
    rest_notes_ref,
    lanes_ref,
):
    step = pl.program_id(0)
    side = side_ref[...]
    pick = pair_pick(side, 1)

    @pl.when(step == 0)
    def lanes():
        first = pair_of(first_a_ref, first_b_ref, 0)
        lanes_ref[...] = (dot_nt(mixed_ref[...], first) * pick).astype(BF)

    columns = weight_ref.shape[1]
    here = pl.ds(pl.multiple_of(step * columns, columns), columns)
    second = pair_of(second_a_ref, second_b_ref, 0)
    residual_ref[:, here] = rows_ref[0].astype(F32) + (
        dot(mixed_ref[...], weight_ref[...]) + dot(lanes_ref[...], second)
    )

    @pl.when(step == pl.num_programs(0) - 1)
    def last():
        tokens = residual_ref.shape[0]
        experts = router_ref.shape[1]
        normed = rms_forward(residual_ref[...], gain_ref[...]).astype(BF)
        normed_ref[...] = normed
        router_lanes = (dot_nt(normed, pair_of(ffn_a_ref, ffn_b_ref, 0)) * pick).astype(BF)
        router_second = jnp.concatenate([router_a_ref[0], router_b_ref[0]], axis=0)
        logits = dot(normed, router_ref[...]) + dot(router_lanes, router_second)
        expert_hot, main_hot, rest_hot = routing(routes_ref[0], experts)
        chosen = [jnp.sum(hot * logits, axis=1, keepdims=True) for hot in expert_hot]
        top = jnp.maximum(jnp.maximum(chosen[0], chosen[1]), jnp.maximum(chosen[2], chosen[3]))
        raised = [jnp.exp(value - top) for value in chosen]
        total = sum(raised)
        gates = [value / total for value in raised]
        mix = logistic(
            jnp.sum(normed.astype(F32) * mix_ref[...].astype(F32), axis=1, keepdims=True)
        )
        small_ref[...] = padded(
            jnp.concatenate(
                [lanes_ref[...].astype(F32), router_lanes.astype(F32), *gates, mix], axis=1
            )
        )
        main, rest = rows_to_slots(main_hot, rest_hot, normed)
        main_ref[...] = main
        rest_ref[...] = rest
        adapter = jnp.where(side > 0.5, numbers_ref[1], numbers_ref[0])
        lane = lane_index((tokens, 128))
        adapter_hot = (lane == adapter).astype(F32)
        main_notes, rest_notes = None, None
        for k in range(TOP):
            high, low = two_parts(gates[k])
            notes = jnp.where(
                lane == ADAPTER_COUNT,
                high.astype(F32),
                jnp.where(lane == ADAPTER_COUNT + 1, low.astype(F32), adapter_hot),
            ).astype(BF)
            main_part = dot_tn(main_hot[k].astype(BF), notes)
            rest_part = dot_tn(rest_hot[k].astype(BF), notes)
            main_notes = main_part if k == 0 else main_notes + main_part
            rest_notes = rest_part if k == 0 else rest_notes + rest_part
        main_notes_ref[...] = main_notes.astype(BF)
        rest_notes_ref[...] = rest_notes.astype(BF)


def after_attention(
    numbers, mixed, weight, rows, first, second, gain, ffn_first, router, router_second, mix, routes, side
):
    tokens, width = mixed.shape
    experts = router.shape[1]
    step = 512
    kept = lambda *shape: pl.BlockSpec(shape, lambda n, a: (0,) * len(shape))
    outs = [
        ((tokens, width), F32),
        ((tokens, width), BF),
        ((tokens, 128), F32),
        ((experts * MAIN, width), BF),
        ((experts * 16, width // 4), BF),
        ((experts * MAIN, 128), BF),
        ((experts * 16, 128), BF),
    ]
    return stage(
        after_attention_kernel,
        "after_attention",
        [shape_of(*out) for out in outs],
        [
            whole(mixed),
            pl.BlockSpec((width, step), lambda n, a: (0, n)),
            pl.BlockSpec((1, tokens, step), lambda n, a: (0, 0, n)),
            pl.BlockSpec((1, 1, RANK, width), lambda n, a: (3, a[0], 0, 0)),
            pl.BlockSpec((1, 1, RANK, width), lambda n, a: (3, a[1], 0, 0)),
            pl.BlockSpec((1, 1, RANK, step), lambda n, a: (3, a[0], 0, n)),
            pl.BlockSpec((1, 1, RANK, step), lambda n, a: (3, a[1], 0, n)),
            whole(gain),
            pl.BlockSpec((1, 1, RANK, width), lambda n, a: (0, a[0], 0, 0)),
            pl.BlockSpec((1, 1, RANK, width), lambda n, a: (0, a[1], 0, 0)),
            whole(router),
            pl.BlockSpec((1, RANK, experts), lambda n, a: (a[0], 0, 0)),
            pl.BlockSpec((1, RANK, experts), lambda n, a: (a[1], 0, 0)),
            whole(mix),
            whole(routes),
            whole(side),
        ],
        [kept(*shape) for shape, kind in outs],
        grid=(width // step,),
        scratch=[pltpu.VMEM((tokens, PAIR), BF)],
        prefetch=1,
    )(
        numbers, mixed, weight, rows, first, first, second, second, gain, ffn_first, ffn_first, router,
        router_second, router_second, mix, routes, side,
    )


def x_step(step):
    return step + step // 2 * (1 - 2 * (step % 2))


def shared_kernel(plan, *refs):
    amount = len(plan)
    inputs, refs = refs[:amount], refs[amount:]
    normed_ref, grads_hbm, weights_hbm, side_ref, picked_ref, second_ref, mix_ref = refs[:7]
    outputs, refs = refs[7 : 7 + amount], refs[7 + amount :]
    parts_refs, values_ref, adapter_ref, refs = refs[:2], refs[2], refs[3], refs[4:]
    own, move_sems, refs = refs[:amount], refs[amount : amount + 4], refs[amount + 4 :]
    rows_buf, grads_buf, gate_buf, up_buf, down_buf = refs[:5]
    parts_buf, values_buf, total, refs = refs[5:7], refs[7], refs[8], refs[9:]
    rows_send, rows_recv, parts_send, parts_recv, load_sem, parts_sem = refs

    units, width = gate_buf.shape[1:]
    along, tokens = rows_buf.shape[:2]
    me = place_in("x")
    loads = [
        pltpu.make_async_copy(normed_ref, rows_buf.at[me], load_sem.at[0]),
        pltpu.make_async_copy(grads_hbm, grads_buf, load_sem.at[1]),
    ]
    loads += [
        pltpu.make_async_copy(weights_hbm.at[:, pl.ds(i * units, units)], target, load_sem.at[2 + i])
        for i, target in enumerate((gate_buf, up_buf, down_buf))
    ]
    for load in loads:
        load.start()
    mover = Mover(plan, inputs, outputs, own, *move_sems)
    mover.take()
    greet(plan + (("gather", "x"),))

    def rows_copy(offset):
        return remote(
            normed_ref,
            rows_buf.at[me],
            rows_send.at[offset],
            rows_recv.at[offset],
            device_of("x", lax.rem(me + offset, along)),
        )

    def parts_copy(kind, offset):
        peer = lax.rem(me + along - offset, along)
        return remote(
            parts_buf[kind].at[peer],
            parts_refs[kind].at[me],
            parts_send.at[kind, offset],
            parts_recv.at[kind, offset],
            device_of("x", peer),
        )

    def own_parts(kind):
        return pltpu.make_async_copy(
            parts_buf[kind].at[me], parts_refs[kind].at[me], parts_sem.at[kind]
        )

    for offset in (1, 3, 2):
        rows_copy(offset).start()
    mover.start()
    for load in loads:
        load.wait()
    total[...] = jnp.zeros_like(total)

    def block(step, carry):
        offset = x_step(step)
        source = lax.rem(me + along - offset, along)

        @pl.when(step > 0)
        def arrived():
            rows_copy(offset).wait_recv()

        rows, grads = rows_buf[source], grads_buf[source]
        grads_f = grads.astype(F32)
        pick = pair_pick(side_ref[source], 1)
        second_gate, second_up = second_ref[:PAIR], second_ref[PAIR : 2 * PAIR]
        down_first = second_ref[2 * PAIR :]
        weight_gate = gate_buf[...].reshape(-1, width)
        weight_up = up_buf[...].reshape(-1, width)
        weight_down = down_buf[...].reshape(-1, width)
        lanes_gate = (dot_nt(rows, picked_ref[:PAIR]) * pick).astype(BF)
        lanes_up = (dot_nt(rows, picked_ref[PAIR : 2 * PAIR]) * pick).astype(BF)
        mix = logistic(jnp.sum(rows.astype(F32) * mix_ref[...].astype(F32), axis=1, keepdims=True))
        grad_shared = (mix * grads_f).astype(BF)
        grad_side = (dot_nt(grad_shared, picked_ref[2 * PAIR :]) * pick).astype(BF)
        gate = dot_nt(rows, weight_gate) + dot(lanes_gate, second_gate)
        upper = dot_nt(rows, weight_up) + dot(lanes_up, second_up)
        hidden = (gate * logistic(gate) * upper).astype(BF)
        grad_hidden = dot_nt(grad_shared, weight_down) + dot(grad_side, down_first)
        grad_gate, grad_upper = swiglu_backward(gate, upper, grad_hidden)
        grad_rows = dot(grad_gate, weight_gate) + dot(grad_upper, weight_up)
        parts_buf[0][source] = grad_rows.astype(BF)
        value = dot(hidden, weight_down)
        values_buf[source] = value.astype(BF)
        mix_sum = jnp.sum(grads_f * value, axis=1, keepdims=True)
        side = (dot_nt(hidden, down_first) * pick).astype(BF)
        grad_lanes_gate = (dot_nt(grad_gate, second_gate) * pick).astype(BF)
        grad_lanes_up = (dot_nt(grad_upper, second_up) * pick).astype(BF)
        parts_buf[1][source] = padded(
            jnp.concatenate([side, grad_lanes_gate, grad_lanes_up, *two_parts(mix_sum)], axis=1)
        )
        total[:PAIR] += dot_tn(lanes_gate, grad_gate)
        total[PAIR : 2 * PAIR] += dot_tn(lanes_up, grad_upper)
        total[2 * PAIR :] += dot_tn(grad_side, hidden)

        @pl.when(step == 0)
        def keep():
            for kind in range(2):
                own_parts(kind).start()

        @pl.when(step > 0)
        def send():
            for kind in range(2):
                parts_copy(kind, offset).start()

        return carry

    lax.fori_loop(0, along, block, 0)
    values_out = pltpu.make_async_copy(values_buf, values_ref, parts_sem.at[2])
    values_out.start()
    adapter_ref[...] = total[...].astype(BF)
    mover.finish()
    for kind in range(2):
        own_parts(kind).wait()
    for offset in range(1, along):
        rows_copy(offset).wait_send()
        for kind in range(2):
            parts_copy(kind, offset).wait()
    values_out.wait()


def shared_expert(number, normed, items, grads, weights, side, picked, second, mix):
    tokens, width = normed.shape
    plan = tuple((kind, group) for kind, group, array in items)
    arrays = [array for kind, group, array in items]
    along = GROUP_SIZE["x"]
    shards_of, units = weights.shape[0], weights.shape[1] // 3
    hidden = shards_of * units
    vmem = pl.BlockSpec(memory_space=pltpu.VMEM)
    parts = [(along, tokens, width), (along, tokens, 128), (along, tokens, width)]
    return pl.pallas_call(
        functools.partial(shared_kernel, plan),
        out_shape=[shape_of(array.shape, BF) for array in arrays]
        + [shape_of(part, BF) for part in parts]
        + [shape_of((3 * PAIR, hidden), BF)],
        in_specs=[HBM] * (len(items) + 3) + [vmem] * 4,
        out_specs=[HBM] * (len(items) + 3) + [vmem],
        scratch_shapes=mover_scratch(items)
        + [pltpu.VMEM((along, tokens, width), BF)] * 2
        + [pltpu.VMEM((shards_of, units, width), BF)] * 3
        + [pltpu.VMEM(part, BF) for part in parts]
        + [pltpu.VMEM((3 * PAIR, hidden), F32)]
        + [
            pltpu.SemaphoreType.DMA((along,)),
            pltpu.SemaphoreType.DMA((along,)),
            pltpu.SemaphoreType.DMA((2, along)),
            pltpu.SemaphoreType.DMA((2, along)),
            pltpu.SemaphoreType.DMA((5,)),
            pltpu.SemaphoreType.DMA((3,)),
        ],
        compiler_params=pltpu.CompilerParams(
            collective_id=number, has_side_effects=True, vmem_limit_bytes=VMEM_LIMIT
        ),
        name="shared_expert",
    )(*arrays, normed, grads, weights, side, picked, second, mix)


BACK = 6
ROUTED_STEPS = 4


def routed_kernel(*refs):
    held_hbm, gate_up_hbm, down_hbm, values_hbm = refs[:6], refs[6], refs[7], refs[8]
    first_ref, second_ref, down_first_ref, down_second_ref = refs[9:13]
    back_refs, values_ref, refs = refs[13 : 13 + BACK], refs[13 + BACK], refs[14 + BACK :]
    adapter_ref, adapter_down_ref = refs[:2]
    own, move_sems, refs = refs[2:3], refs[3:7], refs[7:]
    held, back_buf, refs = refs[:6], refs[6 : 6 + BACK], refs[6 + BACK :]
    gate_up_buf, down_buf, total, total_down = refs[:4]
    send_sem, recv_sem, load_sem, own_sem = refs[4:]

    me = place_in("f")
    experts = GROUP_SIZE["f"]
    loads = [
        pltpu.make_async_copy(source, target, load_sem.at[i])
        for i, (source, target) in enumerate(zip(held_hbm, held))
    ]
    loads += [
        pltpu.make_async_copy(gate_up_hbm.at[0, 0], gate_up_buf.at[0], load_sem.at[6]),
        pltpu.make_async_copy(gate_up_hbm.at[0, 1], gate_up_buf.at[1], load_sem.at[7]),
        pltpu.make_async_copy(down_hbm.at[0], down_buf, load_sem.at[8]),
    ]
    for load in loads:
        load.start()
    mover = Mover((("swap", "x"),), (values_hbm,), (values_ref,), own, *move_sems)
    mover.take()
    greet((("rows", "f"), ("swap", "x")))
    mover.start()
    total[...] = jnp.zeros_like(total)
    total_down[...] = jnp.zeros_like(total_down)

    def back_copy(kind, peer, landing):
        return remote(
            block_of(back_buf[kind], "rows", experts, peer),
            block_of(back_refs[kind], "rows", experts, me),
            send_sem.at[kind, peer],
            recv_sem.at[kind, landing],
            device_of("f", peer),
        )

    def own_copy(kind):
        return pltpu.make_async_copy(
            block_of(back_buf[kind], "rows", experts, me),
            block_of(back_refs[kind], "rows", experts, me),
            own_sem.at[kind],
        )

    steps = ROUTED_STEPS
    selectors = rest_selectors(experts // steps)
    spread = (row_index((128, LANES)) == lane_index((128, LANES)) // RANK).astype(BF)
    fold = (row_index((LANES, 128)) % RANK == lane_index((LANES, 128))).astype(BF)
    fold_later = (row_index((LANES, 128)) % RANK == lane_index((LANES, 128)) - RANK).astype(BF)
    for load in loads:
        load.wait()
    count, rest_count = held[0].shape[0] // steps, held[1].shape[0] // steps

    def block(step, carry):
        number = lax.rem(me + 1 + step, steps)
        peers = [number + steps * turn for turn in range(experts // steps)]

        def read(ref):
            depth = ref.shape[0] // experts
            blocks = [ref[pl.ds(pl.multiple_of(peer * depth, depth), depth)] for peer in peers]
            return jnp.concatenate(blocks, axis=0)

        def write(ref, value):
            depth = ref.shape[0] // experts
            for turn, peer in enumerate(peers):
                part = value[turn * depth : (turn + 1) * depth]
                ref[pl.ds(pl.multiple_of(peer * depth, depth), depth)] = part

        rows = jnp.concatenate([read(held[0]), rest_to_rows(selectors, read(held[1]))], axis=0)
        grads = jnp.concatenate([read(held[2]), rest_to_rows(selectors, read(held[3]))], axis=0)
        notes = jnp.concatenate(
            [read(held[4]), dot(selectors[0], read(held[5])).astype(BF)], axis=0
        )
        pick = dot(notes, spread)
        gate_of = (
            notes[:, ADAPTER_COUNT : ADAPTER_COUNT + 1].astype(F32)
            + notes[:, ADAPTER_COUNT + 1 : ADAPTER_COUNT + 2].astype(F32)
        )
        grads_f = grads.astype(F32)
        lanes_gate = (dot_nt(rows, first_ref[0]) * pick).astype(BF)
        lanes_up = (dot_nt(rows, first_ref[1]) * pick).astype(BF)
        grad_routed = (gate_of * grads_f).astype(BF)
        grad_side = (dot_nt(grads, down_second_ref[1]) * gate_of * pick).astype(BF)
        gate = dot(rows, gate_up_buf[0]) + dot(lanes_gate, second_ref[0])
        upper = dot(rows, gate_up_buf[1]) + dot(lanes_up, second_ref[1])
        hidden = (gate * logistic(gate) * upper).astype(BF)
        grad_hidden = dot_nt(grad_routed, down_buf[...]) + dot(grad_side, down_first_ref[...])
        grad_gate, grad_upper = swiglu_backward(gate, upper, grad_hidden)
        side = (dot_nt(hidden, down_first_ref[...]).astype(BF).astype(F32) * pick).astype(BF)
        value = dot(hidden, down_buf[...]) + dot(side, down_second_ref[1])
        gate_grad = jnp.sum(grads_f * value, axis=1, keepdims=True)
        result = (gate_of * value).astype(BF)
        write(back_buf[4], result[:count])
        write(back_buf[5], rows_to_rest(selectors, result[count:]))
        back = (dot_nt(grad_gate, gate_up_buf[0]) + dot_nt(grad_upper, gate_up_buf[1])).astype(BF)
        back_gate = (dot_nt(grad_gate, second_ref[0]) * pick).astype(BF)
        back_up = (dot_nt(grad_upper, second_ref[1]) * pick).astype(BF)
        high, low = two_parts(gate_grad)
        lane = lane_index((count + rest_count // 4, 128))
        back_notes = jnp.where(
            lane == PAIR,
            high.astype(F32),
            jnp.where(
                lane == PAIR + 1, low.astype(F32), dot(back_gate, fold) + dot(back_up, fold_later)
            ),
        ).astype(BF)
        write(back_buf[0], back[:count])
        write(back_buf[1], rows_to_rest(selectors, back[count:]))
        write(back_buf[2], back_notes[:count])
        write(back_buf[3], dot_tn(selectors[0], back_notes[count:]).astype(BF))
        for peer in peers:

            @pl.when(peer == me)
            def keep():
                for kind in range(BACK):
                    own_copy(kind).start()

            @pl.when(peer != me)
            def send():
                for kind in range(BACK):
                    back_copy(kind, peer, me).start()

        total[:LANES] += dot_tn(lanes_gate, grad_gate)
        total[LANES : 2 * LANES] += dot_tn(lanes_up, grad_upper)
        total[2 * LANES :] += dot_tn(grad_side, hidden)
        total_down[...] += dot_tn(side, grad_routed)
        return carry

    lax.fori_loop(0, steps, block, 0)
    adapter_ref[...] = total[...].astype(BF)
    adapter_down_ref[...] = total_down[...].astype(BF)
    mover.finish()
    for kind in range(BACK):
        own_copy(kind).wait()

    def settle(offset, carry):
        peer = lax.rem(me + offset, experts)
        for kind in range(BACK):
            copy = back_copy(kind, peer, peer)
            copy.wait_send()
            copy.wait_recv()
        return carry

    lax.fori_loop(1, experts, settle, 0)


def routed_expert(number, held, values, first, second, down_first, down_second, gate_up, down):
    width, hidden = gate_up.shape[2:]
    experts = GROUP_SIZE["f"]
    vmem = pl.BlockSpec(memory_space=pltpu.VMEM)
    back = [held[0], held[1], held[4], held[5], held[0], held[1]]
    items = [("swap", "x", values)]
    return pl.pallas_call(
        routed_kernel,
        out_shape=[shape_of(array.shape, BF) for array in (*back, values)]
        + [shape_of((3 * LANES, hidden), BF), shape_of((LANES, width), BF)],
        in_specs=[HBM] * 9 + [vmem] * 4,
        out_specs=[HBM] * (BACK + 1) + [vmem] * 2,
        scratch_shapes=mover_scratch(items)
        + [pltpu.VMEM(array.shape, BF) for array in held]
        + [pltpu.VMEM(array.shape, BF) for array in back]
        + [
            pltpu.VMEM((2, width, hidden), BF),
            pltpu.VMEM((hidden, width), BF),
            pltpu.VMEM((3 * LANES, hidden), F32),
            pltpu.VMEM((LANES, width), F32),
            pltpu.SemaphoreType.DMA((BACK, experts)),
            pltpu.SemaphoreType.DMA((BACK, experts)),
            pltpu.SemaphoreType.DMA((9,)),
            pltpu.SemaphoreType.DMA((BACK,)),
        ],
        compiler_params=pltpu.CompilerParams(
            collective_id=number, has_side_effects=True, vmem_limit_bytes=VMEM_LIMIT
        ),
        name="routed_expert",
    )(*held, gate_up, down, values, first, second, down_first, down_second)


def after_experts_kernel(
    numbers_ref,
    parts_ref,
    part_notes_ref,
    main_ref,
    rest_ref,
    main_notes_ref,
    rest_notes_ref,
    grads_ref,
    normed_ref,
    residual_ref,
    small_ref,
    mixed_ref,
    routes_ref,
    side_ref,
    ffn_a_ref,
    ffn_b_ref,
    router_ref,
    router_a_ref,
    router_b_ref,
    mix_ref,
    gain_ref,
    down_a_ref,
    down_b_ref,
    first_a_ref,
    first_b_ref,
    second_a_ref,
    second_b_ref,
    weight_hbm,
    grad_residual_ref,
    grad_mixed_ref,
    adapter_ref,
    router_grad_ref,
    shared_side_ref,
    weight_ref,
    sem,
):
    load = pltpu.make_async_copy(weight_hbm, weight_ref, sem)
    load.start()
    experts = router_ref.shape[1]
    side = side_ref[...]
    pick = pair_pick(side, 1)
    grads = grads_ref[0]
    grads_f = grads.astype(F32)
    normed = normed_ref[...]
    out_lanes = small_ref[:, :PAIR].astype(BF)
    router_lanes = small_ref[:, PAIR : 2 * PAIR].astype(BF)
    gates = [small_ref[:, 2 * PAIR + k : 2 * PAIR + k + 1] for k in range(TOP)]
    mix = small_ref[:, 2 * PAIR + TOP : 2 * PAIR + TOP + 1]
    notes = sum(part_notes_ref[i].astype(F32) for i in range(part_notes_ref.shape[0]))
    shared_side = notes[:, :PAIR].astype(BF)
    shared_side_ref[...] = padded(shared_side)
    down_second = pair_of(down_a_ref, down_b_ref, 0)
    mix_total = (
        notes[:, 3 * PAIR : 3 * PAIR + 1]
        + notes[:, 3 * PAIR + 1 : 3 * PAIR + 2]
        + jnp.sum(shared_side.astype(F32) * dot_nt(grads, down_second), axis=1, keepdims=True)
    )
    grad_mix = mix_total * mix * (1.0 - mix)
    grad_shared = (mix * grads_f).astype(BF)
    expert_hot, main_hot, rest_hot = routing(routes_ref[0], experts)
    grad_gates = []
    mask = quarter_mask(rest_hot[0].shape, 0)
    token_notes = None
    for k in range(TOP):
        mine = dot(main_hot[k].astype(BF), main_notes_ref[...]) + dot(
            (rest_hot[k] * mask).astype(BF), rest_notes_ref[...]
        )
        grad_gates.append(mine[:, PAIR : PAIR + 1] + mine[:, PAIR + 1 : PAIR + 2])
        token_notes = mine if k == 0 else token_notes + mine
    inner = sum(gate * grad for gate, grad in zip(gates, grad_gates))
    grad_logits = sum(
        hot * (gate * (grad - inner)) for hot, gate, grad in zip(expert_hot, gates, grad_gates)
    )
    logits_high, logits_low = two_parts(grad_logits)
    router_second = jnp.concatenate([router_a_ref[0], router_b_ref[0]], axis=0)
    grad_router_lanes = dot_nt(logits_high, router_second) + dot_nt(logits_low, router_second)
    router_grad = dot_tn(router_lanes, logits_high) + dot_tn(router_lanes, logits_low)
    of_row = jnp.where(row_index((PAIR, 128)) < RANK, numbers_ref[0], numbers_ref[1]).astype(F32)
    router_grad_ref[...] = jnp.where(
        lane_index((PAIR, 128)) == experts, of_row, padded(router_grad)
    ).astype(BF)
    lane_grads = (
        jnp.concatenate(
            [
                grad_router_lanes,
                notes[:, PAIR : 3 * PAIR],
                token_notes[:, :RANK],
                token_notes[:, :RANK],
                token_notes[:, RANK:PAIR],
                token_notes[:, RANK:PAIR],
            ],
            axis=1,
        )
        * pair_pick(side, 5)
    ).astype(BF)
    factors = ffn_a_ref.shape[0]
    ffn_first = jnp.concatenate([pair_of(ffn_a_ref, ffn_b_ref, i) for i in range(factors)], axis=0)
    grad_second = (
        grad_mix * mix_ref[...].astype(F32)
        + dot_nt(logits_high, router_ref[...])
        + dot_nt(logits_low, router_ref[...])
        + sum(parts_ref[i].astype(F32) for i in range(parts_ref.shape[0]))
        + slots_to_rows(main_hot, rest_hot, main_ref[...], rest_ref[...])
        + dot(lane_grads, ffn_first)
    )
    grad_residual = grads_f + rms_backward(residual_ref[...], gain_ref[...], grad_second)
    grad_residual_ref[...] = grad_residual
    grad_attended = grad_residual.astype(BF)
    first, second = pair_of(first_a_ref, first_b_ref, 0), pair_of(second_a_ref, second_b_ref, 0)
    grad_out_lanes = (dot_nt(grad_attended, second) * pick).astype(BF)
    adapter_ref[...] = jnp.concatenate(
        [
            dot_tn(lane_grads, normed),
            dot_tn(grad_out_lanes, mixed_ref[...]),
            dot_tn(out_lanes, grad_attended),
            dot_tn(shared_side, grad_shared),
        ],
        axis=0,
    ).astype(BF)
    load.wait()
    grad_mixed_ref[...] = (
        dot_nt(grad_attended, weight_ref[...]) + dot(grad_out_lanes, first)
    ).astype(BF)


def after_experts(
    numbers, parts, part_notes, main, rest, main_notes, rest_notes, grads, normed, residual, small, mixed,
    routes, side, ffn_first, router, router_second, mix, gain, down_second, first, second, weight,
):
    tokens, width = normed.shape
    experts = router.shape[1]
    factors = ffn_first.shape[0]
    last = lambda which: pl.BlockSpec((1, 1, RANK, width), lambda n, a: (3, a[which], 0, 0))
    outs = [
        ((tokens, width), F32),
        ((tokens, width), BF),
        (((factors + 3) * PAIR, width), BF),
        ((PAIR, 128), BF),
        ((tokens, 128), BF),
    ]
    plain = (
        parts, part_notes, main, rest, main_notes, rest_notes, grads, normed, residual, small, mixed, routes,
        side,
    )
    return stage(
        after_experts_kernel,
        "after_experts",
        [shape_of(*out) for out in outs],
        [whole(array) for array in plain]
        + [
            of_sequence(0, (factors, 1, RANK, width)),
            of_sequence(1, (factors, 1, RANK, width)),
            whole(router),
            pl.BlockSpec((1, RANK, experts), lambda n, a: (a[0], 0, 0)),
            pl.BlockSpec((1, RANK, experts), lambda n, a: (a[1], 0, 0)),
            whole(mix),
            whole(gain),
            of_sequence(0, (1, 1, RANK, width)),
            of_sequence(1, (1, 1, RANK, width)),
            last(0),
            last(1),
            last(0),
            last(1),
            HBM,
        ],
        [pl.BlockSpec(shape, lambda n, a: (0, 0)) for shape, kind in outs],
        scratch=[pltpu.VMEM(weight.shape, BF), pltpu.SemaphoreType.DMA],
        prefetch=1,
    )(
        numbers, *plain, ffn_first, ffn_first, router, router_second, router_second, mix, gain, down_second,
        down_second, first, first, second, second, weight,
    )


def back_project_kernel(
    numbers_ref,
    query_ref,
    pairs_ref,
    cos_ref,
    sin_ref,
    side_ref,
    lanes_ref,
    second_a_ref,
    second_b_ref,
    weight_ref,
    out_ref,
    notes_ref,
    adapter_ref,
    grads_ref,
):
    columns = grads_ref.shape[2]

    @pl.when(pl.program_id(0) == 0)
    def prepare():
        grads_ref[0] = query_ref[...]
        key = pairs_ref[0, 0].astype(F32) + pairs_ref[1, 0].astype(F32)
        copies = columns // HEAD_DIM
        cosine = jnp.concatenate([cos_ref[...]] * copies, axis=1)
        sine = jnp.concatenate([sin_ref[...]] * copies, axis=1)
        grads_ref[1] = (key * cosine - half_turn(key) * sine).astype(BF)
        grads_ref[2] = (pairs_ref[0, 1].astype(F32) + pairs_ref[1, 1].astype(F32)).astype(BF)
        pick = pair_pick(side_ref[...], 1)
        notes = []
        for j in range(3):
            second = pair_of(second_a_ref, second_b_ref, j)
            notes.append((dot_nt(grads_ref[j], second) * pick).astype(BF))
            adapter_ref[j * PAIR : (j + 1) * PAIR, :] = dot_tn(lanes_ref[j], grads_ref[j]).astype(BF)
        notes_ref[...] = padded(jnp.concatenate(notes, axis=1))

    total = None
    for j in range(3):
        weight = weight_ref[:, j].reshape(-1, columns)
        part = dot_nt(grads_ref[j], weight)
        total = part if total is None else total + part
    out_ref[...] = total.astype(BF)


def back_project(numbers, query, pairs, cosine, sine, side, lanes, second, weight):
    tokens, columns = query.shape
    shards, unused, depth, unused = weight.shape
    step = 4
    sequence = lambda which: pl.BlockSpec(
        (3, 1, RANK, columns), lambda n, a: (0, a[which], 0, a[2])
    )
    return stage(
        back_project_kernel,
        "back_project",
        [
            shape_of((tokens, shards * depth), BF),
            shape_of((tokens, 128), BF),
            shape_of((3 * PAIR, columns), BF),
        ],
        [
            whole(query),
            whole(pairs),
            whole(cosine),
            whole(sine),
            whole(side),
            whole(lanes),
            sequence(0),
            sequence(1),
            pl.BlockSpec((step, 3, depth, columns), lambda n, a: (n, 0, 0, 0)),
        ],
        [
            pl.BlockSpec((tokens, step * depth), lambda n, a: (0, n)),
            pl.BlockSpec((tokens, 128), lambda n, a: (0, 0)),
            pl.BlockSpec((3 * PAIR, columns), lambda n, a: (0, 0)),
        ],
        grid=(shards // step,),
        scratch=[pltpu.VMEM((3, tokens, columns), BF)],
        prefetch=1,
    )(numbers, query, pairs, cosine, sine, side, lanes, second, second, weight)


def last_kernel(
    numbers_ref,
    parts_ref,
    notes_ref,
    rows_ref,
    normed_ref,
    residual_ref,
    gain_ref,
    first_a_ref,
    first_b_ref,
    out_ref,
    adapter_ref,
):
    lanes = sum(notes_ref[i].astype(F32) for i in range(notes_ref.shape[0]))[:, : 3 * PAIR]
    lanes = lanes.astype(BF)
    first = jnp.concatenate([pair_of(first_a_ref, first_b_ref, j) for j in range(3)], axis=0)
    grad = sum(parts_ref[i].astype(F32) for i in range(parts_ref.shape[0])) + dot(lanes, first)
    adapter_ref[...] = dot_tn(lanes, normed_ref[...]).astype(BF)
    total = residual_ref[...] + rms_backward(rows_ref[0].astype(F32), gain_ref[...], grad)
    out_ref[0] = total.astype(BF)


def last_stage(numbers, parts, notes, rows, normed, residual, gain, first):
    width = rows.shape[2]
    plain = (parts, notes, rows, normed, residual, gain)
    return stage(
        last_kernel,
        "last_stage",
        [shape_of(rows.shape, BF), shape_of((3 * PAIR, width), BF)],
        [whole(array) for array in plain]
        + [of_sequence(0, (3, 1, RANK, width)), of_sequence(1, (3, 1, RANK, width))],
        [
            pl.BlockSpec(rows.shape, lambda n, a: (0, 0, 0)),
            pl.BlockSpec((3 * PAIR, width), lambda n, a: (0, 0)),
        ],
        prefetch=1,
    )(numbers, *plain, first, first)


def lane_expansion(ids_ref, group):
    ids = ids_ref[group][:, GROUP_SIZE["f"] : GROUP_SIZE["f"] + 1].astype(F32)
    lane = lane_index((PAIR, LANES))
    same = (lane // RANK).astype(F32) == ids
    return (same & (lane % RANK == row_index((PAIR, LANES)) % RANK)).astype(BF)


def expanded(expansions, got_ref, factor):
    total = None
    for group, expansion in enumerate(expansions):
        part = dot_tn(expansion, got_ref[group, factor * PAIR : (factor + 1) * PAIR, :])
        total = part if total is None else total + part
    return total.astype(BF)


def expand_early_kernel(
    ids_ref, early_ref, shared_ref, heads_ref, expert_ref, column_ref, early_out, shared_out, expert_out
):
    groups = ids_ref.shape[0]
    expansions = [lane_expansion(ids_ref, group) for group in range(groups)]
    row = 0
    for got in (early_ref, heads_ref):
        for factor in range(got.shape[1] // PAIR):
            early_out[row : row + LANES, :] = expanded(expansions, got, factor)
            row += LANES
    router = None
    for group in range(groups):
        part = dot_tn(expansions[group], ids_ref[group])
        router = part if router is None else router + part
    router = jnp.sum(router * column_ref[...].astype(F32), axis=1, keepdims=True)
    early_out[row : row + LANES, :] = jnp.broadcast_to(router, (LANES, 128)).astype(BF)
    for factor in range(shared_ref.shape[1] // PAIR):
        shared_out[factor * LANES : (factor + 1) * LANES, :] = expanded(
            expansions, shared_ref, factor
        )
    expert_out[...] = sum(expert_ref[group].astype(F32) for group in range(groups)).astype(BF)


def expand_early(ids, early, shared, heads, expert, column):
    arrays = (ids, early, shared, heads, expert, column)
    factors = (early.shape[1] + heads.shape[1]) // PAIR + 1
    outs = [
        (factors * LANES, 128),
        (shared.shape[1] // PAIR * LANES, 128),
        expert.shape[1:],
    ]
    return stage(
        expand_early_kernel,
        "expand_early",
        [shape_of(shape, BF) for shape in outs],
        [whole(array) for array in arrays],
        [pl.BlockSpec(shape, lambda n: (0, 0)) for shape in outs],
    )(*arrays)


def expand_late_kernel(ids_ref, late_ref, early_ref, shared_ref, late_out, early_out, shared_out):
    groups = ids_ref.shape[0]
    expansions = [lane_expansion(ids_ref, group) for group in range(groups)]
    for factor in range(late_ref.shape[1] // PAIR):
        late_out[factor * LANES : (factor + 1) * LANES, :] = expanded(expansions, late_ref, factor)
    early_out[...] = sum(early_ref[i].astype(F32) for i in range(early_ref.shape[0])).astype(BF)
    shared_out[...] = (shared_ref[0].astype(F32) + shared_ref[1].astype(F32)).astype(BF)


def expand_late(ids, late, early, shared):
    arrays = (ids, late, early, shared)
    outs = [(late.shape[1] // PAIR * LANES, 128), early.shape[1:], shared.shape[1:]]
    return stage(
        expand_late_kernel,
        "expand_late",
        [shape_of(shape, BF) for shape in outs],
        [whole(array) for array in arrays],
        [pl.BlockSpec(shape, lambda n: (0, 0)) for shape in outs],
    )(*arrays)


def combine_kernel(
    numbers_ref, main_ref, rest_ref, routes_ref, residual_ref, parts_ref, side_ref, small_ref, down_a_ref,
    down_b_ref, out_ref,
):
    experts = main_ref.shape[0] // MAIN
    unused, main_hot, rest_hot = routing(routes_ref[0], experts)
    mixture = slots_to_rows(main_hot, rest_hot, main_ref[...], rest_ref[...])
    shared = sum(parts_ref[i].astype(F32) for i in range(parts_ref.shape[0]))
    shared = shared + dot(side_ref[:, :PAIR], pair_of(down_a_ref, down_b_ref, 0))
    mix = small_ref[:, 2 * PAIR + TOP : 2 * PAIR + TOP + 1]
    out_ref[0] = (residual_ref[...] + mixture + mix * shared).astype(BF)


def combine(results, routes, residual, parts, side, small, down_second, numbers):
    tokens, width = residual.shape
    plain = (*results, routes, residual, parts, side, small)
    return stage(
        combine_kernel,
        "combine",
        shape_of((1, tokens, width), BF),
        [whole(array) for array in plain]
        + [of_sequence(0, (1, 1, RANK, width)), of_sequence(1, (1, 1, RANK, width))],
        pl.BlockSpec((1, tokens, width), lambda n, a: (0, 0, 0)),
        prefetch=1,
    )(numbers, *plain, down_second, down_second)


def shards(
    layer_hidden_input,
    output_cotangent,
    sequence_pair_lengths,
    block_placement_order,
    sequence_adapter_index,
    token_expert_choices,
    attention_norm_gain,
    feedforward_norm_gain,
    query_key_value_weight,
    output_projection_weight,
    query_key_value_bias,
    router_weight_matrix,
    shared_gate_up_weight,
    shared_down_weight,
    shared_sigmoid_gate,
    routed_gate_up_weight,
    routed_down_weight,
    attention_adapter_first,
    attention_adapter_second,
    feedforward_adapter_first,
    router_adapter_second,
    shared_gate_adapter_second,
    shared_down_adapter_first,
    routed_gate_adapter_second,
    routed_down_adapter_first,
    down_adapter_second,
):
    tokens, width = layer_hidden_input.shape[1:]
    experts = router_weight_matrix.shape[1]
    capacity = tokens * TOP // experts * 9 // 8
    tail = capacity - MAIN
    ctx_count = lax.axis_size("ctx")
    group_rows = tokens * ctx_count
    along = ctx_count // 2
    rows_shared = tokens * along
    x_index = lax.axis_index("ctx") // 2
    y_index = lax.axis_index("ctx") % 2
    head_columns = width // along
    hidden = shared_down_weight.shape[0]
    quarter = hidden // along
    shards_of = lax.axis_size("fsdp")
    lengths = sequence_pair_lengths[0]
    order = block_placement_order[0]
    adapters = sequence_adapter_index[0]
    block_size = group_rows // order.shape[0]

    qkv_own = lax.dynamic_slice_in_dim(
        query_key_value_weight, x_index * head_columns, head_columns, 2
    ).reshape(-1, head_columns)
    out_weight = lax.all_gather(output_projection_weight, "fsdp", tiled=True)
    units = -(-quarter // 32) * 32
    own_up = jnp.swapaxes(
        lax.dynamic_slice_in_dim(shared_gate_up_weight, x_index * quarter, quarter, 2), 1, 2
    )
    own_down = lax.dynamic_slice_in_dim(shared_down_weight, x_index * quarter, quarter, 0)
    own_shared = jnp.pad(
        jnp.concatenate([own_up, own_down[None]]), ((0, 0), (0, units - quarter), (0, 0))
    ).reshape(3 * units, width)

    def of_group(factor):
        parts = [lax.dynamic_index_in_dim(factor, adapters[s], -3, keepdims=True) for s in range(2)]
        both = jnp.concatenate(parts, axis=-3)
        return both.reshape(both.shape[:-3] + (PAIR, both.shape[-1]))

    shared_second = jnp.concatenate(
        [
            of_group(shared_gate_adapter_second).reshape(2 * PAIR, hidden * shards_of),
            of_group(shared_down_adapter_first),
        ],
        axis=0,
    )
    shared_second = lax.dynamic_index_in_dim(
        shared_second.reshape(3 * PAIR, shards_of, along, quarter), x_index, 2, keepdims=False
    )
    shared_second = jnp.pad(shared_second, ((0, 0), (0, 0), (0, units - quarter)))
    shared_second = shared_second.reshape(3 * PAIR, shards_of * units)
    numbers = jnp.concatenate([adapters, x_index[None].astype(jnp.int32)])

    start = lengths[0]
    block_rows = jnp.arange(block_size, dtype=jnp.int32)
    blocks = order.reshape(along, 2, -1)
    key_places = (jnp.swapaxes(blocks, 0, 1).reshape(-1)[:, None] * block_size + block_rows).reshape(
        1, group_rows
    )
    own_blocks = lax.dynamic_index_in_dim(blocks, y_index, 1, keepdims=False).reshape(-1)
    places = own_blocks[:, None] * block_size + block_rows
    second = places >= start
    fractions = jnp.arange(0, HEAD_DIM, 2).astype(F32) / HEAD_DIM
    speeds = rope_theta ** (-fractions)
    bases = jnp.stack([own_blocks * block_size, own_blocks * block_size - start])
    base_angles = bases.astype(F32)[:, :, None, None] * speeds
    base_angles = jnp.concatenate([base_angles, base_angles], axis=3)
    base_cos, base_sin = jnp.cos(base_angles), jnp.sin(base_angles)
    base_cos = jnp.where(second[:, :, None], base_cos[1], base_cos[0])
    base_sin = jnp.where(second[:, :, None], base_sin[1], base_sin[0])
    row_angles = block_rows.astype(F32)[:, None] * speeds[None, :]
    row_angles = jnp.concatenate([row_angles, row_angles], axis=1)
    row_cos, row_sin = jnp.cos(row_angles), jnp.sin(row_angles)
    cosine = base_cos * row_cos - base_sin * row_sin
    sine = base_sin * row_cos + base_cos * row_sin
    sine = jnp.where(jnp.arange(HEAD_DIM) < HEAD_DIM // 2, -sine, sine)
    cosine, sine = cosine.reshape(rows_shared, HEAD_DIM), sine.reshape(rows_shared, HEAD_DIM)
    place_column = places.reshape(rows_shared, 1)
    start_column = jnp.where(second, start, 0).reshape(rows_shared, 1)
    side_shared = second.astype(F32).reshape(rows_shared, 1)
    side = lax.dynamic_slice_in_dim(side_shared, x_index * tokens, tokens)

    attention_gain = attention_norm_gain[None, :]
    feedforward_gain = feedforward_norm_gain[None, :]
    mix_weight = shared_sigmoid_gate[None, :]
    routed_second = routed_gate_adapter_second.reshape(2, LANES, -1)
    routed_first = routed_down_adapter_first.reshape(LANES, -1)
    ffn_flat = feedforward_adapter_first.reshape(-1, LANES, width)[3:]
    down_flat = down_adapter_second.reshape(2, LANES, width)

    normed_one, sent_grads_main, sent_grads_rest, picked = prologue(
        numbers,
        layer_hidden_input,
        output_cotangent,
        attention_gain,
        token_expert_choices,
        feedforward_adapter_first,
        down_adapter_second,
        experts,
    )
    own_shared, normed_one = lax.optimization_barrier((own_shared, normed_one))
    shared_weight = lax.all_gather(own_shared, "fsdp")
    qkv, normed_shared = exchange(
        "gather_first", 0, ("share", "s", qkv_own), ("gather", "x", normed_one)
    )
    qkv = qkv.reshape(shards_of, 3, tokens, head_columns)
    projected, qkv_lanes = project(
        numbers,
        normed_shared.reshape(rows_shared, width),
        qkv,
        attention_adapter_first,
        attention_adapter_second,
        query_key_value_bias,
        side_shared,
        cosine,
        sine,
    )
    pairs, grads_shared = exchange(
        "keys", 1, ("gather", "y", projected[1:]), ("gather", "x", output_cotangent[0])
    )
    mixed_heads = attend(projected, pairs, place_column, start_column, key_places)
    (mixed,) = exchange(
        "mixed", 2, ("to_columns", "x", mixed_heads.reshape(along, tokens, head_columns))
    )
    residual, normed_two, small, sent_main, sent_rest, notes_main, notes_rest = after_attention(
        numbers,
        mixed,
        out_weight,
        layer_hidden_input,
        attention_adapter_first,
        attention_adapter_second,
        feedforward_gain,
        feedforward_adapter_first,
        router_weight_matrix,
        router_adapter_second,
        mix_weight,
        token_expert_choices,
        side,
    )
    *held, parts_rows, parts_lanes, value_part, grad_shared_rows = shared_expert(
        3,
        normed_two,
        [
            ("rows", "f", array)
            for array in (
                sent_main,
                sent_rest,
                sent_grads_main,
                sent_grads_rest,
                notes_main,
                notes_rest,
            )
        ],
        grads_shared,
        shared_weight,
        side_shared.reshape(along, tokens, 1),
        picked,
        shared_second,
        mix_weight,
    )
    (
        got_main,
        got_rest,
        got_notes_main,
        got_notes_rest,
        result_main,
        result_rest,
        value_parts,
        grad_expert_rows,
        grad_down_expert,
    ) = routed_expert(
        4,
        held,
        value_part,
        ffn_flat,
        routed_second,
        routed_first,
        down_flat,
        routed_gate_up_weight,
        routed_down_weight,
    )
    def wide(rows):
        blocks = rows.reshape(rows.shape[0], shards_of, -1)
        blocks = jnp.pad(blocks, ((0, 0), (0, 0), (0, 128 - blocks.shape[2])))
        return blocks.reshape(rows.shape[0], shards_of * 128)

    expert_rows = lax.psum_scatter(
        jnp.concatenate([wide(grad_expert_rows), grad_down_expert], axis=0), "ctx", tiled=True
    )
    grad_residual, grad_mixed, early_columns, router_rows, shared_side = after_experts(
        numbers,
        parts_rows,
        parts_lanes,
        got_main,
        got_rest,
        got_notes_main,
        got_notes_rest,
        output_cotangent,
        normed_two,
        residual,
        small,
        mixed,
        token_expert_choices,
        side,
        feedforward_adapter_first,
        router_weight_matrix,
        router_adapter_second,
        mix_weight,
        feedforward_gain,
        down_adapter_second,
        attention_adapter_first,
        attention_adapter_second,
        out_weight,
    )

    (grad_heads,) = exchange("heads", 5, ("from_columns", "x", grad_mixed))
    grad_query, grad_pairs = attend_back(
        projected,
        pairs,
        grad_heads.reshape(rows_shared, head_columns),
        place_column,
        start_column,
        key_places,
        cosine,
        sine,
    )
    (pair_parts,) = exchange("key_grads", 6, ("swap", "y", grad_pairs))
    first_part, lanes_first_part, head_rows = back_project(
        numbers,
        grad_query,
        pair_parts,
        cosine,
        sine,
        side_shared,
        qkv_lanes,
        attention_adapter_second,
        qkv,
    )

    early_blocks = wide(grad_shared_rows)
    head_rows = lax.dynamic_update_slice(
        jnp.zeros((3 * PAIR, width), BF), head_rows, (0, x_index * head_columns)
    )
    first_parts, first_lanes, early_got, shared_got, heads_got, expert_got, router_got = exchange(
        "first_grads",
        7,
        ("swap", "x", first_part.reshape(along, tokens, width)),
        ("swap", "x", lanes_first_part.reshape(along, tokens, 128)),
        ("from_columns", "f", early_columns),
        ("from_columns", "f", early_blocks),
        ("from_columns", "f", head_rows),
        ("from_columns", "f", expert_rows),
        ("gather", "f", router_rows),
    )
    grad_tokens, late_columns = last_stage(
        numbers,
        first_parts,
        first_lanes,
        layer_hidden_input,
        normed_one,
        grad_residual,
        attention_gain,
        attention_adapter_first,
    )

    own_column = (jnp.arange(128) == lax.axis_index("fsdp")).astype(BF)[None, :]
    early_sum, shared_sum, expert_sum = expand_early(
        router_got, early_got, shared_got, heads_got, expert_got, own_column
    )
    late_got, early_parts, shared_parts = exchange(
        "late_grads",
        8,
        ("from_columns", "f", late_columns),
        ("swap", "c", early_sum.reshape(ctx_count, -1, 128)),
        ("swap", "y", shared_sum.reshape(2, -1, 128)),
    )
    late_sum, early_row, shared_row = expand_late(router_got, late_got, early_parts, shared_parts)
    late_all, early_all, shared_all, expert_all = exchange(
        "ctx_sums",
        9,
        ("gather", "c", late_sum),
        ("gather", "c", early_row),
        ("gather", "c", shared_row),
        ("gather", "c", expert_sum),
    )
    late_total = jnp.sum(late_all.astype(F32), axis=0)
    early_total = early_all.reshape(-1, 128).astype(F32)
    expert_total = expert_all.reshape(-1, 128).astype(F32)
    shared_total = shared_all.reshape(along, 3 * LANES, 128)[:, :, :quarter].astype(F32)
    shared_total = shared_total.transpose(1, 0, 2).reshape(3 * LANES, along * quarter)
    expert_width = routed_down_weight.shape[1] // shards_of

    def rows(total, first, factors, columns=128):
        part = total[first * LANES : (first + factors) * LANES, :columns]
        return part.reshape(factors, ADAPTER_COUNT, RANK, columns)

    def joined(*parts):
        return jnp.concatenate(parts, axis=0)

    attn_in = joined(rows(late_total, 0, 3), rows(early_total, 5, 1))
    attn_out = joined(rows(early_total, 8, 3), rows(early_total, 6, 1))
    down_out = joined(rows(early_total, 7, 1), rows(expert_total, 3, 1))

    mixture = combine((result_main, result_rest), token_expert_choices, residual, value_parts, shared_side, small, down_adapter_second, numbers)

    return (
        mixture,
        grad_tokens,
        attn_in,
        attn_out,
        rows(early_total, 0, 5),
        rows(early_total, 11, 1, 1)[0],
        shared_total[: 2 * LANES].reshape(2, ADAPTER_COUNT, RANK, -1),
        shared_total[2 * LANES :].reshape(ADAPTER_COUNT, RANK, -1),
        rows(expert_total, 0, 2, expert_width),
        rows(expert_total, 2, 1, expert_width)[0],
        down_out,
    )


def solution(mesh):
    return jax.shard_map(
        shards,
        mesh=mesh,
        in_specs=(
            P("fsdp", "ctx", None),
            P("fsdp", "ctx", None),
            P("fsdp", None),
            P("fsdp", None),
            P("fsdp", None),
            P("fsdp", "ctx", None),
            P(),
            P(),
            P(None, "fsdp", None),
            P("fsdp", None),
            P(),
            P(),
            P(None, None, "fsdp"),
            P("fsdp", None),
            P(),
            P("fsdp", None, None, None),
            P("fsdp", None, None),
            P(),
            P(),
            P(),
            P(),
            P(),
            P(),
            P(),
            P(),
            P(),
        ),
        out_specs=(
            P("fsdp", "ctx", None),
            P("fsdp", "ctx", None),
            P(None, None, None, "fsdp"),
            P(None, None, None, "fsdp"),
            P(None, None, None, "fsdp"),
            P(None, None, "fsdp"),
            P(None, None, None, "fsdp"),
            P(None, None, "fsdp"),
            P(None, None, None, "fsdp"),
            P(None, None, "fsdp"),
            P(None, None, None, "fsdp"),
        ),
        check_vma=False,
    )
```

```python
import functools

import jax
import jax.numpy as jnp
from jax import lax
from jax.experimental import pallas as pl
from jax.experimental.pallas import tpu as pltpu
from jax.sharding import PartitionSpec as P

HEADS = 16
HEAD_DIM = 128
TOP = 4
ADAPTER_COUNT = 8
RANK = 16
LANES = ADAPTER_COUNT * RANK
PAIR = 2 * RANK
MAIN = 32

norm_eps = 1e-06
rope_theta = 1000000.0
masked_score = -1e30
highest = lax.Precision.HIGHEST
MESH = pl.DeviceIdType.MESH
BF = jnp.bfloat16
F32 = jnp.float32
VMEM_LIMIT = 56 * 2**20


def dot(left, right):
    return jnp.dot(left, right, preferred_element_type=F32)


def dot_nt(left, right):
    return lax.dot_general(left, right, (((1,), (1,)), ((), ())), preferred_element_type=F32)


def dot_tn(left, right):
    return lax.dot_general(left, right, (((0,), (0,)), ((), ())), preferred_element_type=F32)


GROUP_SIZE = {"x": 4, "y": 2, "c": 8, "f": 16}


def place_in(group):
    ctx, fsdp = lax.axis_index("ctx"), lax.axis_index("fsdp")
    return {"x": ctx // 2, "y": ctx % 2, "c": ctx, "f": fsdp}[group]


def device_of(group, index):
    ctx, fsdp = lax.axis_index("ctx"), lax.axis_index("fsdp")
    if group == "x":
        return (index * 2 + ctx % 2, fsdp)
    if group == "y":
        return ((ctx // 2) * 2 + index, fsdp)
    if group == "c":
        return (index, fsdp)
    return (ctx, index)


def chip():
    ctx, fsdp = lax.axis_index("ctx"), lax.axis_index("fsdp")
    return ctx % 2 * 2 + fsdp // 8, fsdp // 2 % 4, fsdp % 2


def device_at(y, z, core):
    return (lax.axis_index("ctx") // 2 * 2 + y // 2, y % 2 * 8 + z * 2 + core)


def shard_at(y, z, core):
    return y % 2 * 8 + z * 2 + core


def exchanged_shape(kind, group, shape):
    if kind == "share":
        return (GROUP_SIZE["f"],) + shape
    count = GROUP_SIZE[group]
    if kind == "gather":
        return (count,) + shape
    if kind in ("swap", "rows"):
        return shape
    if kind == "from_columns":
        return (count, shape[0], shape[1] // count)
    return (shape[1], count * shape[2])


def own_shape(kind, group, shape):
    if kind in ("gather", "share"):
        return shape
    count = GROUP_SIZE[group]
    if kind == "rows":
        return (shape[0] // count,) + shape[1:]
    if kind == "from_columns":
        return (shape[0], shape[1] // count)
    return shape[1:]


def copies_of(kind, group):
    return 23 if kind == "share" else GROUP_SIZE[group] - 1


def block_of(ref, kind, count, index):
    if kind == "rows":
        depth = ref.shape[0] // count
        return ref.at[pl.ds(pl.multiple_of(index * depth, depth), depth)]
    if kind == "columns":
        width = ref.shape[1] // count
        return ref.at[:, pl.ds(pl.multiple_of(index * width, width), width)]
    return ref.at[index]


def source_of(kind, group, ref, index):
    if kind in ("gather", "share"):
        return ref
    cut = {"rows": "rows", "from_columns": "columns"}.get(kind, "first")
    return block_of(ref, cut, GROUP_SIZE[group], index)


def target_of(kind, group, ref, index):
    cut = {"rows": "rows", "to_columns": "columns"}.get(kind, "first")
    return block_of(ref, cut, GROUP_SIZE["f" if kind == "share" else group], index)


def remote(source, target, send, recv, device):
    return pltpu.make_async_remote_copy(
        src_ref=source,
        dst_ref=target,
        send_sem=send,
        recv_sem=recv,
        device_id=device,
        device_id_type=MESH,
    )


def greet(plan):
    barrier = pltpu.get_barrier_semaphore()
    count = 0
    for group in sorted({group for kind, group in plan}):
        if group == "s":
            y, z, core = chip()
            peers = [device_at(y, lax.rem(z + d, 4), core) for d in (1, 2, 3)]
            peers += [device_at(lax.rem(y + d, 4), z, core) for d in (1, 3)]
            peers += [device_at(y, z, 1 - core)]
        else:
            size = GROUP_SIZE[group]
            mine = place_in(group)
            peers = [device_of(group, lax.rem(mine + d, size)) for d in range(1, size)]
        for peer in peers:
            pl.semaphore_signal(barrier, inc=1, device_id=peer, device_id_type=MESH)
        count += len(peers)
    pl.semaphore_wait(barrier, count)


class Share:
    def __init__(self, source, target, send, recv, first):
        self.target = target
        self.sems = (send, recv, first)
        y, z, core = self.place = chip()
        self.order = (1, 3, 2)
        self.source = source
        self.along_z = [
            self.copy(source, shard_at(y, z, core), None, i, device_at(y, lax.rem(z + d, 4), core))
            for i, d in enumerate(self.order)
        ]
        self.along_y, self.across = [], []

    def copy(self, source, shard, half, number, device):
        send, recv, first = self.sems
        target = self.target.at[shard]
        if half is not None:
            target = target.at[half]
        return remote(source, target, send.at[first + number], recv.at[first + number], device)

    def halves(self):
        half = self.target.shape[1] // 2
        return pl.ds(0, half), pl.ds(half, half)

    def forward(self, number, source, z):
        y, unused, core = self.place
        unused, my_z, unused = self.place
        shard = shard_at(y, z, core)
        for i, (half, d) in enumerate(zip(self.halves(), (3, 1))):
            copy = self.copy(
                source.at[half], shard, half, 3 + 2 * number + i, device_at(lax.rem(y + d, 4), my_z, core)
            )
            copy.start()
            self.along_y.append(copy)
        copy = self.copy(source, shard, None, 11 + number, device_at(y, my_z, 1 - core))
        copy.start()
        self.across.append(copy)

    def start(self):
        for copy in self.along_z:
            copy.start()
        self.forward(0, self.source, self.place[1])

    def finish(self):
        y, z, core = self.place
        for i, d in enumerate(self.order):
            self.along_z[i].wait_recv()
            from_z = lax.rem(z + 4 - d, 4)
            self.forward(i + 1, self.target.at[shard_at(y, from_z, core)], from_z)
        for number in range(4):
            from_z = z if number == 0 else lax.rem(z + 4 - self.order[number - 1], 4)
            shard = shard_at(y + 1, from_z, core)
            for i, half in enumerate(self.halves()):
                self.along_y[2 * number + i].wait_recv()
                block = self.target.at[shard].at[half]
                copy = self.copy(block, shard, half, 15 + 2 * number + i, device_at(y, z, 1 - core))
                copy.start()
                self.across.append(copy)
        for copy in self.along_z + self.along_y:
            copy.wait_send()
        for copy in self.across:
            copy.wait()


class Mover:
    def __init__(self, plan, inputs, outputs, own, send, recv, in_sem, out_sem):
        self.plan, self.inputs, self.outputs, self.own = plan, inputs, outputs, own
        self.send, self.recv, self.in_sem, self.out_sem = send, recv, in_sem, out_sem
        self.taken, self.copies, self.shares = [], [], []

    def own_place(self, item):
        kind, group = self.plan[item]
        return shard_at(*chip()) if kind == "share" else place_in(group)

    def take(self):
        for item, (kind, group) in enumerate(self.plan):
            block = source_of(kind, group, self.inputs[item], self.own_place(item))
            copy = pltpu.make_async_copy(block, self.own[item], self.in_sem.at[item])
            copy.start()
            self.taken.append(copy)

    def start(self):
        slot = 0
        for item, (kind, group) in enumerate(self.plan):
            source, target = self.inputs[item], self.outputs[item]
            if kind == "share":
                share = Share(source, target, self.send, self.recv, slot)
                share.start()
                self.shares.append(share)
            else:
                count = GROUP_SIZE[group]
                mine = place_in(group)
                for offset in range(1, count):
                    peer = lax.rem(mine + offset, count)
                    copy = remote(
                        source_of(kind, group, source, peer),
                        target_of(kind, group, target, mine),
                        self.send.at[slot + offset - 1],
                        self.recv.at[slot + offset - 1],
                        device_of(group, peer),
                    )
                    copy.start()
                    self.copies.append(copy)
            slot += copies_of(kind, group)
        for item, (kind, group) in enumerate(self.plan):
            self.taken[item].wait()
            block = target_of(kind, group, self.outputs[item], self.own_place(item))
            copy = pltpu.make_async_copy(self.own[item], block, self.out_sem.at[item])
            copy.start()
            self.copies.append(copy)

    def finish(self):
        for share in self.shares:
            share.finish()
        for copy in self.copies:
            copy.wait()


def exchange_kernel(plan, *refs):
    amount = len(plan)
    mover = Mover(
        plan, refs[:amount], refs[amount : 2 * amount], refs[2 * amount : 3 * amount], *refs[3 * amount :]
    )
    mover.take()
    greet(plan)
    mover.start()
    mover.finish()


def mover_scratch(items):
    plan = tuple((kind, group) for kind, group, array in items)
    slots = sum(copies_of(kind, group) for kind, group in plan)
    return [
        pltpu.VMEM(own_shape(kind, group, array.shape), array.dtype) for kind, group, array in items
    ] + [
        pltpu.SemaphoreType.DMA((slots,)),
        pltpu.SemaphoreType.DMA((slots,)),
        pltpu.SemaphoreType.DMA((len(items),)),
        pltpu.SemaphoreType.DMA((len(items),)),
    ]


def exchange(name, number, *items):
    plan = tuple((kind, group) for kind, group, array in items)
    arrays = [array for kind, group, array in items]
    return pl.pallas_call(
        functools.partial(exchange_kernel, plan),
        out_shape=[
            jax.ShapeDtypeStruct(exchanged_shape(kind, group, array.shape), array.dtype)
            for kind, group, array in items
        ],
        in_specs=[pl.BlockSpec(memory_space=pltpu.HBM)] * len(items),
        out_specs=[pl.BlockSpec(memory_space=pltpu.HBM)] * len(items),
        scratch_shapes=mover_scratch(items),
        compiler_params=pltpu.CompilerParams(
            collective_id=number, has_side_effects=True, vmem_limit_bytes=16 * 2**20
        ),
        name=name,
    )(*arrays)


def rms_forward(values, gain):
    mean_square = jnp.mean(values * values, axis=-1, keepdims=True)
    return values * lax.rsqrt(mean_square + norm_eps) * gain.astype(F32)


def rms_backward(values, gain, grad_result):
    scale = lax.rsqrt(jnp.mean(values * values, axis=-1, keepdims=True) + norm_eps)
    scaled = gain.astype(F32) * grad_result
    inner = jnp.mean(values * scaled, axis=-1, keepdims=True)
    return scale * scaled - values * (scale * scale * scale) * inner


def logistic(values):
    return 1.0 / (1.0 + jnp.exp(-values))


def swiglu_backward(gate, upper, grad_hidden):
    sigma = logistic(gate)
    grad_gate = grad_hidden * upper * sigma * (1.0 + gate * (1.0 - sigma))
    grad_upper = grad_hidden * gate * sigma
    return (grad_gate.astype(BF), grad_upper.astype(BF))


def two_parts(values):
    high = values.astype(BF)
    return high, (values - high.astype(F32)).astype(BF)


def lane_index(shape):
    return lax.broadcasted_iota(jnp.int32, shape, 1)


def row_index(shape):
    return lax.broadcasted_iota(jnp.int32, shape, 0)


def pair_pick(second, copies):
    shape = (second.shape[0], PAIR * copies)
    of_lane = (lane_index(shape) % PAIR >= RANK).astype(F32)
    return (of_lane == second).astype(F32)


def pair_of(first_ref, last_ref, index):
    return jnp.concatenate([first_ref[index, 0], last_ref[index, 0]], axis=0)


def padded(values):
    rest = 128 - values.shape[1]
    return jnp.concatenate([values, jnp.zeros((values.shape[0], rest), values.dtype)], axis=1)


def routing(routes, experts):
    tokens = routes.shape[0]
    expert_lane = lane_index((tokens, experts))
    expert_hot = [(routes[:, k : k + 1] == expert_lane).astype(F32) for k in range(TOP)]
    count = sum(expert_hot)
    below = (row_index((tokens, tokens)) > lane_index((tokens, tokens))).astype(BF)
    earlier = dot(below, count.astype(BF))
    rank = [jnp.sum(hot * earlier, axis=1, keepdims=True).astype(jnp.int32) for hot in expert_hot]
    main_lane = lane_index((tokens, experts * MAIN))
    rest_lane = lane_index((tokens, experts * 16))
    rest_code = (rest_lane // 16) * 4 + rest_lane % 4
    main_hot, rest_hot = [], []
    for k in range(TOP):
        expert = routes[:, k : k + 1]
        main_slot = jnp.where(rank[k] < MAIN, expert * MAIN + rank[k], -1)
        rest_slot = jnp.where(rank[k] < MAIN, -1, expert * 4 + rank[k] - MAIN)
        main_hot.append((main_lane == main_slot).astype(F32))
        rest_hot.append((rest_code == rest_slot).astype(F32))
    return expert_hot, main_hot, rest_hot


def quarter_mask(shape, quarter):
    return (lane_index(shape) % 16 // 4 == quarter).astype(F32)


def rows_to_slots(main_hot, rest_hot, rows):
    main = dot_tn(sum(main_hot).astype(BF), rows).astype(BF)
    rest_sum = sum(rest_hot)
    width = rows.shape[1] // 4
    rest = None
    for quarter in range(4):
        hot = (rest_sum * quarter_mask(rest_sum.shape, quarter)).astype(BF)
        part = dot_tn(hot, rows[:, quarter * width : (quarter + 1) * width])
        rest = part if rest is None else rest + part
    return main, rest.astype(BF)


def slots_to_rows(main_hot, rest_hot, main, rest):
    rest_sum = sum(rest_hot)
    parts = [
        dot((rest_sum * quarter_mask(rest_sum.shape, quarter)).astype(BF), rest)
        for quarter in range(4)
    ]
    return dot(sum(main_hot).astype(BF), main) + jnp.concatenate(parts, axis=1)


def rest_selectors(sources):
    shape = (4 * sources, 16 * sources)
    row, lane = row_index(shape), lane_index(shape)
    same = (lane // 16 == row // 4) & (lane % 4 == row % 4)
    return [(same & (lane % 16 // 4 == quarter)).astype(BF) for quarter in range(4)]


def rest_to_rows(selectors, rest):
    return jnp.concatenate([dot(selector, rest) for selector in selectors], axis=1).astype(BF)


def rows_to_rest(selectors, rows):
    width = rows.shape[1] // 4
    total = None
    for quarter in range(4):
        part = dot_tn(selectors[quarter], rows[:, quarter * width : (quarter + 1) * width])
        total = part if total is None else total + part
    return total.astype(BF)


def stage(kernel, name, out_shape, in_specs, out_specs, grid=(1,), scratch=(), prefetch=0):
    return pl.pallas_call(
        kernel,
        out_shape=out_shape,
        grid_spec=pltpu.PrefetchScalarGridSpec(
            num_scalar_prefetch=prefetch,
            grid=grid,
            in_specs=in_specs,
            out_specs=out_specs,
            scratch_shapes=list(scratch),
        ),
        compiler_params=pltpu.CompilerParams(vmem_limit_bytes=VMEM_LIMIT),
        name=name,
    )


def whole(array):
    zeros = (0,) * len(array.shape)
    return pl.BlockSpec(array.shape, lambda *unused: zeros)


def of_sequence(which, block):
    return pl.BlockSpec(block, lambda *at: (0, at[-1][which], 0, 0))


def shape_of(shape, kind):
    return jax.ShapeDtypeStruct(shape, kind)


HBM = pl.BlockSpec(memory_space=pltpu.HBM)


def prologue_kernel(
    numbers_ref,
    rows_ref,
    grads_ref,
    gain_ref,
    routes_ref,
    ffn_a_ref,
    ffn_b_ref,
    down_a_ref,
    down_b_ref,
    first_a_ref,
    first_b_ref,
    second_a_ref,
    second_b_ref,
    normed_ref,
    main_ref,
    rest_ref,
    picked_ref,
    first_ref,
    second_ref,
):
    normed_ref[...] = rms_forward(rows_ref[0].astype(F32), gain_ref[...]).astype(BF)
    experts = main_ref.shape[0] // MAIN
    unused, main_hot, rest_hot = routing(routes_ref[0], experts)
    main, rest = rows_to_slots(main_hot, rest_hot, grads_ref[0])
    main_ref[...] = main
    rest_ref[...] = rest
    picked_ref[...] = jnp.concatenate(
        [
            pair_of(ffn_a_ref, ffn_b_ref, 1),
            pair_of(ffn_a_ref, ffn_b_ref, 2),
            pair_of(down_a_ref, down_b_ref, 0),
        ],
        axis=0,
    )
    for j in range(3):
        first_ref[j * PAIR : (j + 1) * PAIR, :] = pair_of(first_a_ref, first_b_ref, j)
        second_ref[j * PAIR : (j + 1) * PAIR, :] = pair_of(second_a_ref, second_b_ref, j)


def prologue(
    numbers, rows, grads, gain, routes, ffn_first, down_second, first, second, experts, columns
):
    tokens, width = rows.shape[1:]
    heads = lambda which: pl.BlockSpec(
        (3, 1, RANK, columns), lambda n, a: (0, a[which], 0, a[2])
    )
    outs = [
        (tokens, width),
        (experts * MAIN, width),
        (experts * 16, width // 4),
        (3 * PAIR, width),
        (3 * PAIR, width),
        (3 * PAIR, columns),
    ]
    return stage(
        prologue_kernel,
        "prologue",
        [shape_of(shape, BF) for shape in outs],
        [
            whole(rows),
            whole(grads),
            whole(gain),
            whole(routes),
            of_sequence(0, (3, 1, RANK, width)),
            of_sequence(1, (3, 1, RANK, width)),
            of_sequence(0, (1, 1, RANK, width)),
            of_sequence(1, (1, 1, RANK, width)),
            of_sequence(0, (3, 1, RANK, width)),
            of_sequence(1, (3, 1, RANK, width)),
            heads(0),
            heads(1),
        ],
        [pl.BlockSpec(shape, lambda n, a: (0, 0)) for shape in outs],
        prefetch=1,
    )(
        numbers, rows, grads, gain, routes, ffn_first, ffn_first, down_second, down_second, first, first,
        second, second,
    )


def half_turn(values):
    parts = []
    for head in range(values.shape[1] // HEAD_DIM):
        part = values[:, head * HEAD_DIM : (head + 1) * HEAD_DIM]
        parts.append(jnp.concatenate([part[:, 64:], part[:, :64]], axis=1))
    return jnp.concatenate(parts, axis=1) if len(parts) > 1 else parts[0]


def project_kernel(
    numbers_ref,
    rows_ref,
    weight_ref,
    first_a_ref,
    first_b_ref,
    second_a_ref,
    second_b_ref,
    bias_ref,
    side_ref,
    cos_ref,
    sin_ref,
    out_ref,
    lanes_ref,
):
    which = pl.program_id(0)

    @pl.when(pl.program_id(1) == 0)
    def lanes():
        first = pair_of(first_a_ref, first_b_ref, 0)
        picked = dot_nt(rows_ref[...], first) * pair_pick(side_ref[...], 1)
        lanes_ref[0] = picked.astype(BF)

    weight = weight_ref[...].reshape(rows_ref.shape[1], weight_ref.shape[3])
    bias = bias_ref[...].astype(F32)
    bias = jnp.sum(jnp.where(row_index(bias.shape) == which, bias, 0.0), axis=0, keepdims=True)
    second = pair_of(second_a_ref, second_b_ref, 0)
    value = dot(rows_ref[...], weight) + bias + dot(lanes_ref[0], second)
    copies = value.shape[1] // HEAD_DIM
    cosine = jnp.concatenate([cos_ref[...]] * copies, axis=1)
    sine = jnp.concatenate([sin_ref[...]] * copies, axis=1)
    turned = value * cosine + half_turn(value) * sine
    out_ref[0] = jnp.where(which < 2, turned, value).astype(BF)


def project(numbers, rows, weight, first, second, bias, side, cosine, sine):
    tokens, width = rows.shape
    columns = weight.shape[3]
    step = 256
    steps = columns // step
    return stage(
        project_kernel,
        "project",
        [shape_of((3, tokens, columns), BF), shape_of((3, tokens, PAIR), BF)],
        [
            whole(rows),
            pl.BlockSpec((weight.shape[0], 1, weight.shape[2], step), lambda j, n, a: (0, j, 0, n)),
            pl.BlockSpec((1, 1, RANK, width), lambda j, n, a: (j, a[0], 0, 0)),
            pl.BlockSpec((1, 1, RANK, width), lambda j, n, a: (j, a[1], 0, 0)),
            pl.BlockSpec((1, 1, RANK, step), lambda j, n, a: (j, a[0], 0, a[2] * steps + n)),
            pl.BlockSpec((1, 1, RANK, step), lambda j, n, a: (j, a[1], 0, a[2] * steps + n)),
            pl.BlockSpec((3, step), lambda j, n, a: (0, a[2] * steps + n)),
            whole(side),
            whole(cosine),
            whole(sine),
        ],
        [
            pl.BlockSpec((1, tokens, step), lambda j, n, a: (j, 0, n)),
            pl.BlockSpec((1, tokens, PAIR), lambda j, n, a: (j, 0, 0)),
        ],
        grid=(3, steps),
        prefetch=1,
    )(numbers, rows, weight, first, first, second, second, bias, side, cosine, sine)


def probabilities(query, keys, query_place, query_start, key_place):
    scores = dot_nt(query, keys) * (HEAD_DIM**-0.5)
    allowed = (key_place <= query_place) & (key_place >= query_start)
    scores = jnp.where(allowed, scores, masked_score)
    top = jnp.max(scores, axis=1, keepdims=True)
    raised = jnp.exp(scores - top)
    return raised * (1.0 / jnp.sum(raised, axis=1, keepdims=True))


def attend_kernel(query_ref, key_ref, value_ref, place_ref, start_ref, key_place_ref, out_ref):
    keys = key_ref[...].reshape(-1, HEAD_DIM)
    values = value_ref[...].reshape(-1, HEAD_DIM)
    probs = probabilities(query_ref[0], keys, place_ref[...], start_ref[...], key_place_ref[...])
    out_ref[...] = dot(probs.astype(BF), values).astype(BF)


def attend(projected, pairs, place, start, key_place):
    tokens, columns = projected.shape[1:]
    step = 256
    keys = pairs.shape[0] * pairs.shape[2]
    half = pairs.shape[2]
    return pl.pallas_call(
        attend_kernel,
        grid=(columns // HEAD_DIM, tokens // step),
        out_shape=jax.ShapeDtypeStruct((tokens, columns), BF),
        in_specs=[
            pl.BlockSpec((1, step, HEAD_DIM), lambda h, i: (0, i, h)),
            pl.BlockSpec((2, 1, half, HEAD_DIM), lambda h, i: (0, 0, 0, h)),
            pl.BlockSpec((2, 1, half, HEAD_DIM), lambda h, i: (0, 1, 0, h)),
            pl.BlockSpec((step, 1), lambda h, i: (i, 0)),
            pl.BlockSpec((step, 1), lambda h, i: (i, 0)),
            pl.BlockSpec((1, keys), lambda h, i: (0, 0)),
        ],
        out_specs=pl.BlockSpec((step, HEAD_DIM), lambda h, i: (i, h)),
        compiler_params=pltpu.CompilerParams(vmem_limit_bytes=VMEM_LIMIT),
        name="attend",
    )(projected, pairs, pairs, place, start, key_place)


def after_attention_kernel(
    numbers_ref,
    mixed_ref,
    weight_ref,
    rows_ref,
    first_a_ref,
    first_b_ref,
    second_a_ref,
    second_b_ref,
    gain_ref,
    ffn_a_ref,
    ffn_b_ref,
    router_ref,
    router_a_ref,
    router_b_ref,
    mix_ref,
    routes_ref,
    side_ref,
    residual_ref,
    normed_ref,
    small_ref,
    main_ref,
    rest_ref,
    main_notes_ref,
    rest_notes_ref,
    lanes_ref,
):
    step = pl.program_id(0)
    side = side_ref[...]
    pick = pair_pick(side, 1)

    @pl.when(step == 0)
    def lanes():
        first = pair_of(first_a_ref, first_b_ref, 0)
        lanes_ref[...] = (dot_nt(mixed_ref[...], first) * pick).astype(BF)

    columns = weight_ref.shape[1]
    here = pl.ds(pl.multiple_of(step * columns, columns), columns)
    second = pair_of(second_a_ref, second_b_ref, 0)
    residual_ref[:, here] = rows_ref[0].astype(F32) + (
        dot(mixed_ref[...], weight_ref[...]) + dot(lanes_ref[...], second)
    )

    @pl.when(step == pl.num_programs(0) - 1)
    def last():
        tokens = residual_ref.shape[0]
        experts = router_ref.shape[1]
        normed = rms_forward(residual_ref[...], gain_ref[...]).astype(BF)
        normed_ref[...] = normed
        router_lanes = (dot_nt(normed, pair_of(ffn_a_ref, ffn_b_ref, 0)) * pick).astype(BF)
        router_second = jnp.concatenate([router_a_ref[0], router_b_ref[0]], axis=0)
        logits = dot(normed, router_ref[...]) + dot(router_lanes, router_second)
        expert_hot, main_hot, rest_hot = routing(routes_ref[0], experts)
        chosen = [jnp.sum(hot * logits, axis=1, keepdims=True) for hot in expert_hot]
        top = jnp.maximum(jnp.maximum(chosen[0], chosen[1]), jnp.maximum(chosen[2], chosen[3]))
        raised = [jnp.exp(value - top) for value in chosen]
        total = sum(raised)
        gates = [value / total for value in raised]
        mix = logistic(
            jnp.sum(normed.astype(F32) * mix_ref[...].astype(F32), axis=1, keepdims=True)
        )
        small_ref[...] = padded(
            jnp.concatenate(
                [lanes_ref[...].astype(F32), router_lanes.astype(F32), *gates, mix], axis=1
            )
        )
        main, rest = rows_to_slots(main_hot, rest_hot, normed)
        main_ref[...] = main
        rest_ref[...] = rest
        adapter = jnp.where(side > 0.5, numbers_ref[1], numbers_ref[0])
        lane = lane_index((tokens, 128))
        adapter_hot = (lane == adapter).astype(F32)
        main_notes, rest_notes = None, None
        for k in range(TOP):
            high, low = two_parts(gates[k])
            notes = jnp.where(
                lane == ADAPTER_COUNT,
                high.astype(F32),
                jnp.where(lane == ADAPTER_COUNT + 1, low.astype(F32), adapter_hot),
            ).astype(BF)
            main_part = dot_tn(main_hot[k].astype(BF), notes)
            rest_part = dot_tn(rest_hot[k].astype(BF), notes)
            main_notes = main_part if k == 0 else main_notes + main_part
            rest_notes = rest_part if k == 0 else rest_notes + rest_part
        main_notes_ref[...] = main_notes.astype(BF)
        rest_notes_ref[...] = rest_notes.astype(BF)


def after_attention(
    numbers, mixed, weight, rows, first, second, gain, ffn_first, router, router_second, mix, routes, side
):
    tokens, width = mixed.shape
    experts = router.shape[1]
    step = 512
    kept = lambda *shape: pl.BlockSpec(shape, lambda n, a: (0,) * len(shape))
    outs = [
        ((tokens, width), F32),
        ((tokens, width), BF),
        ((tokens, 128), F32),
        ((experts * MAIN, width), BF),
        ((experts * 16, width // 4), BF),
        ((experts * MAIN, 128), BF),
        ((experts * 16, 128), BF),
    ]
    return stage(
        after_attention_kernel,
        "after_attention",
        [shape_of(*out) for out in outs],
        [
            whole(mixed),
            pl.BlockSpec((width, step), lambda n, a: (0, n)),
            pl.BlockSpec((1, tokens, step), lambda n, a: (0, 0, n)),
            pl.BlockSpec((1, 1, RANK, width), lambda n, a: (3, a[0], 0, 0)),
            pl.BlockSpec((1, 1, RANK, width), lambda n, a: (3, a[1], 0, 0)),
            pl.BlockSpec((1, 1, RANK, step), lambda n, a: (3, a[0], 0, n)),
            pl.BlockSpec((1, 1, RANK, step), lambda n, a: (3, a[1], 0, n)),
            whole(gain),
            pl.BlockSpec((1, 1, RANK, width), lambda n, a: (0, a[0], 0, 0)),
            pl.BlockSpec((1, 1, RANK, width), lambda n, a: (0, a[1], 0, 0)),
            whole(router),
            pl.BlockSpec((1, RANK, experts), lambda n, a: (a[0], 0, 0)),
            pl.BlockSpec((1, RANK, experts), lambda n, a: (a[1], 0, 0)),
            whole(mix),
            whole(routes),
            whole(side),
        ],
        [kept(*shape) for shape, kind in outs],
        grid=(width // step,),
        scratch=[pltpu.VMEM((tokens, PAIR), BF)],
        prefetch=1,
    )(
        numbers, mixed, weight, rows, first, first, second, second, gain, ffn_first, ffn_first, router,
        router_second, router_second, mix, routes, side,
    )


def in_owner_columns(total, target, columns):
    count = total.shape[0]
    for owner in range(total.shape[1] // columns):
        part = total[:, owner * columns : (owner + 1) * columns].astype(BF)
        target[:count, owner * 128 : (owner + 1) * 128] = padded(part)


def x_step(step):
    return step + step // 2 * (1 - 2 * (step % 2))


def shared_kernel(plan, *refs):
    amount = len(plan)
    inputs, refs = refs[:amount], refs[amount:]
    normed_ref, grads_hbm, weights_hbm, side_ref, picked_ref, second_ref, mix_ref = refs[:7]
    outputs, refs = refs[7 : 7 + amount], refs[7 + amount :]
    parts_refs, values_ref, adapter_ref, refs = refs[:2], refs[2], refs[3], refs[4:]
    own, move_sems, refs = refs[:amount], refs[amount : amount + 4], refs[amount + 4 :]
    rows_buf, grads_buf, gate_buf, up_buf, down_buf = refs[:5]
    parts_buf, values_buf, total, refs = refs[5:7], refs[7], refs[8], refs[9:]
    rows_send, rows_recv, parts_send, parts_recv, load_sem, parts_sem = refs

    units, width = gate_buf.shape[1:]
    along, tokens = rows_buf.shape[:2]
    me = place_in("x")
    loads = [
        pltpu.make_async_copy(normed_ref, rows_buf.at[me], load_sem.at[0]),
        pltpu.make_async_copy(grads_hbm, grads_buf, load_sem.at[1]),
    ]
    loads += [
        pltpu.make_async_copy(weights_hbm.at[:, pl.ds(i * units, units)], target, load_sem.at[2 + i])
        for i, target in enumerate((gate_buf, up_buf, down_buf))
    ]
    for load in loads:
        load.start()
    mover = Mover(plan, inputs, outputs, own, *move_sems)
    mover.take()
    greet(plan + (("gather", "x"),))

    def rows_copy(offset):
        return remote(
            normed_ref,
            rows_buf.at[me],
            rows_send.at[offset],
            rows_recv.at[offset],
            device_of("x", lax.rem(me + offset, along)),
        )

    def parts_copy(kind, offset):
        peer = lax.rem(me + along - offset, along)
        return remote(
            parts_buf[kind].at[peer],
            parts_refs[kind].at[me],
            parts_send.at[kind, offset],
            parts_recv.at[kind, offset],
            device_of("x", peer),
        )

    def own_parts(kind):
        return pltpu.make_async_copy(
            parts_buf[kind].at[me], parts_refs[kind].at[me], parts_sem.at[kind]
        )

    for offset in (1, 3, 2):
        rows_copy(offset).start()
    mover.start()
    for load in loads:
        load.wait()
    total[...] = jnp.zeros_like(total)

    def block(step, carry):
        offset = x_step(step)
        source = lax.rem(me + along - offset, along)

        @pl.when(step > 0)
        def arrived():
            rows_copy(offset).wait_recv()

        rows, grads = rows_buf[source], grads_buf[source]
        grads_f = grads.astype(F32)
        pick = pair_pick(side_ref[source], 1)
        second_gate, second_up = second_ref[:PAIR], second_ref[PAIR : 2 * PAIR]
        down_first = second_ref[2 * PAIR :]
        weight_gate = gate_buf[...].reshape(-1, width)
        weight_up = up_buf[...].reshape(-1, width)
        weight_down = down_buf[...].reshape(-1, width)
        lanes_gate = (dot_nt(rows, picked_ref[:PAIR]) * pick).astype(BF)
        lanes_up = (dot_nt(rows, picked_ref[PAIR : 2 * PAIR]) * pick).astype(BF)
        mix = logistic(jnp.sum(rows.astype(F32) * mix_ref[...].astype(F32), axis=1, keepdims=True))
        grad_shared = (mix * grads_f).astype(BF)
        grad_side = (dot_nt(grad_shared, picked_ref[2 * PAIR :]) * pick).astype(BF)
        gate = dot_nt(rows, weight_gate) + dot(lanes_gate, second_gate)
        upper = dot_nt(rows, weight_up) + dot(lanes_up, second_up)
        hidden = (gate * logistic(gate) * upper).astype(BF)
        grad_hidden = dot_nt(grad_shared, weight_down) + dot(grad_side, down_first)
        grad_gate, grad_upper = swiglu_backward(gate, upper, grad_hidden)
        grad_rows = dot(grad_gate, weight_gate) + dot(grad_upper, weight_up)
        parts_buf[0][source] = grad_rows.astype(BF)
        value = dot(hidden, weight_down)
        values_buf[source] = value.astype(BF)
        mix_sum = jnp.sum(grads_f * value, axis=1, keepdims=True)
        side = (dot_nt(hidden, down_first) * pick).astype(BF)
        grad_lanes_gate = (dot_nt(grad_gate, second_gate) * pick).astype(BF)
        grad_lanes_up = (dot_nt(grad_upper, second_up) * pick).astype(BF)
        parts_buf[1][source] = padded(
            jnp.concatenate([side, grad_lanes_gate, grad_lanes_up, *two_parts(mix_sum)], axis=1)
        )
        total[:PAIR] += dot_tn(lanes_gate, grad_gate)
        total[PAIR : 2 * PAIR] += dot_tn(lanes_up, grad_upper)
        total[2 * PAIR :] += dot_tn(grad_side, hidden)

        @pl.when(step == 0)
        def keep():
            for kind in range(2):
                own_parts(kind).start()

        @pl.when(step > 0)
        def send():
            for kind in range(2):
                parts_copy(kind, offset).start()

        return carry

    lax.fori_loop(0, along, block, 0)
    values_out = pltpu.make_async_copy(values_buf, values_ref, parts_sem.at[2])
    values_out.start()
    in_owner_columns(total, adapter_ref, units)
    mover.finish()
    for kind in range(2):
        own_parts(kind).wait()
    for offset in range(1, along):
        rows_copy(offset).wait_send()
        for kind in range(2):
            parts_copy(kind, offset).wait()
    values_out.wait()


def shared_expert(number, normed, items, grads, weights, side, picked, second, mix):
    tokens, width = normed.shape
    plan = tuple((kind, group) for kind, group, array in items)
    arrays = [array for kind, group, array in items]
    along = GROUP_SIZE["x"]
    shards_of, units = weights.shape[0], weights.shape[1] // 3
    hidden = shards_of * units
    vmem = pl.BlockSpec(memory_space=pltpu.VMEM)
    parts = [(along, tokens, width), (along, tokens, 128), (along, tokens, width)]
    return pl.pallas_call(
        functools.partial(shared_kernel, plan),
        out_shape=[shape_of(array.shape, BF) for array in arrays]
        + [shape_of(part, BF) for part in parts]
        + [shape_of((3 * PAIR, shards_of * 128), BF)],
        in_specs=[HBM] * (len(items) + 3) + [vmem] * 4,
        out_specs=[HBM] * (len(items) + 3) + [vmem],
        scratch_shapes=mover_scratch(items)
        + [pltpu.VMEM((along, tokens, width), BF)] * 2
        + [pltpu.VMEM((shards_of, units, width), BF)] * 3
        + [pltpu.VMEM(part, BF) for part in parts]
        + [pltpu.VMEM((3 * PAIR, hidden), F32)]
        + [
            pltpu.SemaphoreType.DMA((along,)),
            pltpu.SemaphoreType.DMA((along,)),
            pltpu.SemaphoreType.DMA((2, along)),
            pltpu.SemaphoreType.DMA((2, along)),
            pltpu.SemaphoreType.DMA((5,)),
            pltpu.SemaphoreType.DMA((3,)),
        ],
        compiler_params=pltpu.CompilerParams(
            collective_id=number, has_side_effects=True, vmem_limit_bytes=VMEM_LIMIT
        ),
        name="shared_expert",
    )(*arrays, normed, grads, weights, side, picked, second, mix)


BACK = 6
ROUTED_STEPS = 4


def routed_kernel(*refs):
    held_hbm, gate_up_hbm, down_hbm, values_hbm = refs[:6], refs[6], refs[7], refs[8]
    first_ref, second_ref, down_first_ref, down_second_ref = refs[9:13]
    back_refs, values_ref, refs = refs[13 : 13 + BACK], refs[13 + BACK], refs[14 + BACK :]
    adapter_ref = refs[0]
    own, move_sems, refs = refs[1:2], refs[2:6], refs[6:]
    held, back_buf, refs = refs[:6], refs[6 : 6 + BACK], refs[6 + BACK :]
    gate_up_buf, down_buf, total, total_down = refs[:4]
    send_sem, recv_sem, load_sem, own_sem = refs[4:]

    me = place_in("f")
    experts = GROUP_SIZE["f"]
    loads = [
        pltpu.make_async_copy(source, target, load_sem.at[i])
        for i, (source, target) in enumerate(zip(held_hbm, held))
    ]
    loads += [
        pltpu.make_async_copy(gate_up_hbm.at[0, 0], gate_up_buf.at[0], load_sem.at[6]),
        pltpu.make_async_copy(gate_up_hbm.at[0, 1], gate_up_buf.at[1], load_sem.at[7]),
        pltpu.make_async_copy(down_hbm.at[0], down_buf, load_sem.at[8]),
    ]
    for load in loads:
        load.start()
    mover = Mover((("swap", "x"),), (values_hbm,), (values_ref,), own, *move_sems)
    mover.take()
    greet((("rows", "f"), ("swap", "x")))
    mover.start()
    total[...] = jnp.zeros_like(total)
    total_down[...] = jnp.zeros_like(total_down)

    def back_copy(kind, peer, landing):
        return remote(
            block_of(back_buf[kind], "rows", experts, peer),
            block_of(back_refs[kind], "rows", experts, me),
            send_sem.at[kind, peer],
            recv_sem.at[kind, landing],
            device_of("f", peer),
        )

    def own_copy(kind):
        return pltpu.make_async_copy(
            block_of(back_buf[kind], "rows", experts, me),
            block_of(back_refs[kind], "rows", experts, me),
            own_sem.at[kind],
        )

    steps = ROUTED_STEPS
    selectors = rest_selectors(experts // steps)
    spread = (row_index((128, LANES)) == lane_index((128, LANES)) // RANK).astype(BF)
    fold = (row_index((LANES, 128)) % RANK == lane_index((LANES, 128))).astype(BF)
    fold_later = (row_index((LANES, 128)) % RANK == lane_index((LANES, 128)) - RANK).astype(BF)
    for load in loads:
        load.wait()
    count, rest_count = held[0].shape[0] // steps, held[1].shape[0] // steps

    def block(step, carry):
        number = lax.rem(me + 1 + step, steps)
        peers = [number + steps * turn for turn in range(experts // steps)]

        def read(ref):
            depth = ref.shape[0] // experts
            blocks = [ref[pl.ds(pl.multiple_of(peer * depth, depth), depth)] for peer in peers]
            return jnp.concatenate(blocks, axis=0)

        def write(ref, value):
            depth = ref.shape[0] // experts
            for turn, peer in enumerate(peers):
                part = value[turn * depth : (turn + 1) * depth]
                ref[pl.ds(pl.multiple_of(peer * depth, depth), depth)] = part

        rows = jnp.concatenate([read(held[0]), rest_to_rows(selectors, read(held[1]))], axis=0)
        grads = jnp.concatenate([read(held[2]), rest_to_rows(selectors, read(held[3]))], axis=0)
        notes = jnp.concatenate(
            [read(held[4]), dot(selectors[0], read(held[5])).astype(BF)], axis=0
        )
        pick = dot(notes, spread)
        gate_of = (
            notes[:, ADAPTER_COUNT : ADAPTER_COUNT + 1].astype(F32)
            + notes[:, ADAPTER_COUNT + 1 : ADAPTER_COUNT + 2].astype(F32)
        )
        grads_f = grads.astype(F32)
        lanes_gate = (dot_nt(rows, first_ref[0]) * pick).astype(BF)
        lanes_up = (dot_nt(rows, first_ref[1]) * pick).astype(BF)
        grad_routed = (gate_of * grads_f).astype(BF)
        grad_side = (dot_nt(grads, down_second_ref[1]) * gate_of * pick).astype(BF)
        gate = dot(rows, gate_up_buf[0]) + dot(lanes_gate, second_ref[0])
        upper = dot(rows, gate_up_buf[1]) + dot(lanes_up, second_ref[1])
        hidden = (gate * logistic(gate) * upper).astype(BF)
        grad_hidden = dot_nt(grad_routed, down_buf[...]) + dot(grad_side, down_first_ref[...])
        grad_gate, grad_upper = swiglu_backward(gate, upper, grad_hidden)
        side = (dot_nt(hidden, down_first_ref[...]).astype(BF).astype(F32) * pick).astype(BF)
        value = dot(hidden, down_buf[...]) + dot(side, down_second_ref[1])
        gate_grad = jnp.sum(grads_f * value, axis=1, keepdims=True)
        result = (gate_of * value).astype(BF)
        write(back_buf[4], result[:count])
        write(back_buf[5], rows_to_rest(selectors, result[count:]))
        back = (dot_nt(grad_gate, gate_up_buf[0]) + dot_nt(grad_upper, gate_up_buf[1])).astype(BF)
        back_gate = (dot_nt(grad_gate, second_ref[0]) * pick).astype(BF)
        back_up = (dot_nt(grad_upper, second_ref[1]) * pick).astype(BF)
        high, low = two_parts(gate_grad)
        lane = lane_index((count + rest_count // 4, 128))
        back_notes = jnp.where(
            lane == PAIR,
            high.astype(F32),
            jnp.where(
                lane == PAIR + 1, low.astype(F32), dot(back_gate, fold) + dot(back_up, fold_later)
            ),
        ).astype(BF)
        write(back_buf[0], back[:count])
        write(back_buf[1], rows_to_rest(selectors, back[count:]))
        write(back_buf[2], back_notes[:count])
        write(back_buf[3], dot_tn(selectors[0], back_notes[count:]).astype(BF))
        for peer in peers:

            @pl.when(peer == me)
            def keep():
                for kind in range(BACK):
                    own_copy(kind).start()

            @pl.when(peer != me)
            def send():
                for kind in range(BACK):
                    back_copy(kind, peer, me).start()

        total[:LANES] += dot_tn(lanes_gate, grad_gate)
        total[LANES : 2 * LANES] += dot_tn(lanes_up, grad_upper)
        total[2 * LANES :] += dot_tn(grad_side, hidden)
        total_down[...] += dot_tn(side, grad_routed)
        return carry

    lax.fori_loop(0, steps, block, 0)
    in_owner_columns(total, adapter_ref, total.shape[1] // experts)
    adapter_ref[3 * LANES :, :] = total_down[...].astype(BF)
    mover.finish()
    for kind in range(BACK):
        own_copy(kind).wait()

    def settle(offset, carry):
        peer = lax.rem(me + offset, experts)
        for kind in range(BACK):
            copy = back_copy(kind, peer, peer)
            copy.wait_send()
            copy.wait_recv()
        return carry

    lax.fori_loop(1, experts, settle, 0)


def routed_expert(number, held, values, first, second, down_first, down_second, gate_up, down):
    width, hidden = gate_up.shape[2:]
    experts = GROUP_SIZE["f"]
    vmem = pl.BlockSpec(memory_space=pltpu.VMEM)
    back = [held[0], held[1], held[4], held[5], held[0], held[1]]
    items = [("swap", "x", values)]
    return pl.pallas_call(
        routed_kernel,
        out_shape=[shape_of(array.shape, BF) for array in (*back, values)]
        + [shape_of((4 * LANES, experts * 128), BF)],
        in_specs=[HBM] * 9 + [vmem] * 4,
        out_specs=[HBM] * (BACK + 1) + [vmem],
        scratch_shapes=mover_scratch(items)
        + [pltpu.VMEM(array.shape, BF) for array in held]
        + [pltpu.VMEM(array.shape, BF) for array in back]
        + [
            pltpu.VMEM((2, width, hidden), BF),
            pltpu.VMEM((hidden, width), BF),
            pltpu.VMEM((3 * LANES, hidden), F32),
            pltpu.VMEM((LANES, width), F32),
            pltpu.SemaphoreType.DMA((BACK, experts)),
            pltpu.SemaphoreType.DMA((BACK, experts)),
            pltpu.SemaphoreType.DMA((9,)),
            pltpu.SemaphoreType.DMA((BACK,)),
        ],
        compiler_params=pltpu.CompilerParams(
            collective_id=number, has_side_effects=True, vmem_limit_bytes=VMEM_LIMIT
        ),
        name="routed_expert",
    )(*held, gate_up, down, values, first, second, down_first, down_second)


def after_experts_kernel(
    numbers_ref,
    parts_ref,
    part_notes_ref,
    main_ref,
    rest_ref,
    main_notes_ref,
    rest_notes_ref,
    grads_ref,
    normed_ref,
    residual_ref,
    small_ref,
    mixed_ref,
    routes_ref,
    side_ref,
    ffn_a_ref,
    ffn_b_ref,
    router_ref,
    router_a_ref,
    router_b_ref,
    mix_ref,
    gain_ref,
    down_a_ref,
    down_b_ref,
    first_a_ref,
    first_b_ref,
    second_a_ref,
    second_b_ref,
    weight_hbm,
    grad_residual_ref,
    grad_mixed_ref,
    adapter_ref,
    router_grad_ref,
    shared_side_ref,
    weight_ref,
    sem,
):
    load = pltpu.make_async_copy(weight_hbm, weight_ref, sem)
    load.start()
    experts = router_ref.shape[1]
    side = side_ref[...]
    pick = pair_pick(side, 1)
    grads = grads_ref[0]
    grads_f = grads.astype(F32)
    normed = normed_ref[...]
    out_lanes = small_ref[:, :PAIR].astype(BF)
    router_lanes = small_ref[:, PAIR : 2 * PAIR].astype(BF)
    gates = [small_ref[:, 2 * PAIR + k : 2 * PAIR + k + 1] for k in range(TOP)]
    mix = small_ref[:, 2 * PAIR + TOP : 2 * PAIR + TOP + 1]
    notes = sum(part_notes_ref[i].astype(F32) for i in range(part_notes_ref.shape[0]))
    shared_side = notes[:, :PAIR].astype(BF)
    shared_side_ref[...] = padded(shared_side)
    down_second = pair_of(down_a_ref, down_b_ref, 0)
    mix_total = (
        notes[:, 3 * PAIR : 3 * PAIR + 1]
        + notes[:, 3 * PAIR + 1 : 3 * PAIR + 2]
        + jnp.sum(shared_side.astype(F32) * dot_nt(grads, down_second), axis=1, keepdims=True)
    )
    grad_mix = mix_total * mix * (1.0 - mix)
    grad_shared = (mix * grads_f).astype(BF)
    expert_hot, main_hot, rest_hot = routing(routes_ref[0], experts)
    grad_gates = []
    mask = quarter_mask(rest_hot[0].shape, 0)
    token_notes = None
    for k in range(TOP):
        mine = dot(main_hot[k].astype(BF), main_notes_ref[...]) + dot(
            (rest_hot[k] * mask).astype(BF), rest_notes_ref[...]
        )
        grad_gates.append(mine[:, PAIR : PAIR + 1] + mine[:, PAIR + 1 : PAIR + 2])
        token_notes = mine if k == 0 else token_notes + mine
    inner = sum(gate * grad for gate, grad in zip(gates, grad_gates))
    grad_logits = sum(
        hot * (gate * (grad - inner)) for hot, gate, grad in zip(expert_hot, gates, grad_gates)
    )
    logits_high, logits_low = two_parts(grad_logits)
    router_second = jnp.concatenate([router_a_ref[0], router_b_ref[0]], axis=0)
    grad_router_lanes = dot_nt(logits_high, router_second) + dot_nt(logits_low, router_second)
    router_grad = dot_tn(router_lanes, logits_high) + dot_tn(router_lanes, logits_low)
    of_row = jnp.where(row_index((PAIR, 128)) < RANK, numbers_ref[0], numbers_ref[1]).astype(F32)
    router_grad_ref[...] = jnp.where(
        lane_index((PAIR, 128)) == experts, of_row, padded(router_grad)
    ).astype(BF)
    lane_grads = (
        jnp.concatenate(
            [
                grad_router_lanes,
                notes[:, PAIR : 3 * PAIR],
                token_notes[:, :RANK],
                token_notes[:, :RANK],
                token_notes[:, RANK:PAIR],
                token_notes[:, RANK:PAIR],
            ],
            axis=1,
        )
        * pair_pick(side, 5)
    ).astype(BF)
    factors = ffn_a_ref.shape[0]
    ffn_first = jnp.concatenate([pair_of(ffn_a_ref, ffn_b_ref, i) for i in range(factors)], axis=0)
    grad_second = (
        grad_mix * mix_ref[...].astype(F32)
        + dot_nt(logits_high, router_ref[...])
        + dot_nt(logits_low, router_ref[...])
        + sum(parts_ref[i].astype(F32) for i in range(parts_ref.shape[0]))
        + slots_to_rows(main_hot, rest_hot, main_ref[...], rest_ref[...])
        + dot(lane_grads, ffn_first)
    )
    grad_residual = grads_f + rms_backward(residual_ref[...], gain_ref[...], grad_second)
    grad_residual_ref[...] = grad_residual
    grad_attended = grad_residual.astype(BF)
    first, second = pair_of(first_a_ref, first_b_ref, 0), pair_of(second_a_ref, second_b_ref, 0)
    grad_out_lanes = (dot_nt(grad_attended, second) * pick).astype(BF)
    adapter_ref[...] = jnp.concatenate(
        [
            dot_tn(lane_grads, normed),
            dot_tn(grad_out_lanes, mixed_ref[...]),
            dot_tn(out_lanes, grad_attended),
            dot_tn(shared_side, grad_shared),
        ],
        axis=0,
    ).astype(BF)
    load.wait()
    grad_mixed_ref[...] = (
        dot_nt(grad_attended, weight_ref[...]) + dot(grad_out_lanes, first)
    ).astype(BF)


def after_experts(
    numbers, parts, part_notes, main, rest, main_notes, rest_notes, grads, normed, residual, small, mixed,
    routes, side, ffn_first, router, router_second, mix, gain, down_second, first, second, weight,
):
    tokens, width = normed.shape
    experts = router.shape[1]
    factors = ffn_first.shape[0]
    last = lambda which: pl.BlockSpec((1, 1, RANK, width), lambda n, a: (3, a[which], 0, 0))
    outs = [
        ((tokens, width), F32),
        ((tokens, width), BF),
        (((factors + 3) * PAIR, width), BF),
        ((PAIR, 128), BF),
        ((tokens, 128), BF),
    ]
    plain = (
        parts, part_notes, main, rest, main_notes, rest_notes, grads, normed, residual, small, mixed, routes,
        side,
    )
    return stage(
        after_experts_kernel,
        "after_experts",
        [shape_of(*out) for out in outs],
        [whole(array) for array in plain]
        + [
            of_sequence(0, (factors, 1, RANK, width)),
            of_sequence(1, (factors, 1, RANK, width)),
            whole(router),
            pl.BlockSpec((1, RANK, experts), lambda n, a: (a[0], 0, 0)),
            pl.BlockSpec((1, RANK, experts), lambda n, a: (a[1], 0, 0)),
            whole(mix),
            whole(gain),
            of_sequence(0, (1, 1, RANK, width)),
            of_sequence(1, (1, 1, RANK, width)),
            last(0),
            last(1),
            last(0),
            last(1),
            HBM,
        ],
        [pl.BlockSpec(shape, lambda n, a: (0, 0)) for shape, kind in outs],
        scratch=[pltpu.VMEM(weight.shape, BF), pltpu.SemaphoreType.DMA],
        prefetch=1,
    )(
        numbers, *plain, ffn_first, ffn_first, router, router_second, router_second, mix, gain, down_second,
        down_second, first, first, second, second, weight,
    )


def attention_back_kernel(plan, heads_plan, *refs):
    amount = len(plan)
    inputs, refs = refs[:amount], refs[amount:]
    mixed_hbm, query_hbm, pairs_hbm, weight_hbm = refs[:4]
    place_ref, start_ref, key_place_ref, cos_ref, sin_ref, side_ref, lanes_ref, second_ref = refs[4:12]
    results, refs = refs[12:20], refs[20:]
    outputs, refs = refs[:amount], refs[amount:]
    heads_got, parts_ref, notes_ref, out_ref, refs = refs[0], refs[1], refs[2], refs[3], refs[4:]
    own, move_sems, refs = refs[:amount], refs[amount : amount + 4], refs[amount + 4 :]
    heads_own, heads_sems, refs = refs[:1], refs[1:5], refs[5:]
    mixed_buf, query_buf, pairs_buf, weight_buf = refs[:4]
    sent_buf, got_buf, grads_buf, heads_buf, parts_buf, notes_buf = refs[4:10]
    mixed_send, mixed_recv, pair_send, pair_recv, parts_send, parts_recv, load_sem, own_sem = refs[10:]

    x, y = place_in("x"), place_in("y")
    along, tokens, columns = mixed_buf.shape
    rows_all = along * tokens
    heads = columns // HEAD_DIM
    loads = [
        pltpu.make_async_copy(block_of(mixed_hbm, "columns", along, x), mixed_buf.at[x], load_sem.at[0]),
        pltpu.make_async_copy(query_hbm.at[0], query_buf, load_sem.at[1]),
        pltpu.make_async_copy(pairs_hbm, pairs_buf, load_sem.at[2]),
    ]
    loads += [
        pltpu.make_async_copy(weight_hbm.at[:, j], weight_buf.at[j], load_sem.at[3 + j])
        for j in range(3)
    ]
    for load in loads:
        load.start()
    mover = Mover(plan, inputs, outputs, own, *move_sems)
    mover.take()
    greet((("rows", "f"), ("swap", "x"), ("swap", "y")))

    def mixed_copy(offset):
        peer = lax.rem(x + offset, along)
        return remote(
            block_of(mixed_hbm, "columns", along, peer),
            mixed_buf.at[x],
            mixed_send.at[offset],
            mixed_recv.at[offset],
            device_of("x", peer),
        )

    def pair_copy(head):
        return remote(
            sent_buf.at[1 - y, head],
            got_buf.at[head],
            pair_send.at[head],
            pair_recv.at[head],
            device_of("y", 1 - y),
        )

    def parts_copy(offset):
        peer = lax.rem(x + offset, along)
        return remote(
            parts_buf.at[peer],
            parts_ref.at[x],
            parts_send.at[0, offset],
            parts_recv.at[0, offset],
            device_of("x", peer),
        )

    def notes_copy(offset):
        peer = lax.rem(x + offset, along)
        return remote(
            notes_buf.at[peer],
            notes_ref.at[x],
            parts_send.at[1, offset],
            parts_recv.at[1, offset],
            device_of("x", peer),
        )

    for offset in (2, 1, 3):
        mixed_copy(offset).start()
    for load in loads[:3]:
        load.wait()
    for offset in (1, 3, 2):
        mixed_copy(offset).wait_recv()

    step = rows_all // 2

    def head_block(head, carry):
        here = pl.ds(pl.multiple_of(head * HEAD_DIM, HEAD_DIM), HEAD_DIM)
        keys = pairs_buf[:, 0, :, here].reshape(-1, HEAD_DIM)
        values = pairs_buf[:, 1, :, here].reshape(-1, HEAD_DIM)
        key_total, value_total = None, None
        for i in range(2):
            at = slice(i * step, (i + 1) * step)
            query = query_buf[at, here]
            blocks = along // 2
            grad = mixed_buf[i * blocks : (i + 1) * blocks, :, here].reshape(step, HEAD_DIM)
            probs = probabilities(query, keys, place_ref[at], start_ref[at], key_place_ref[...])
            grad_probs = dot_nt(grad, values)
            mean = jnp.sum(probs * grad_probs, axis=1, keepdims=True)
            grad_scores = (probs * (grad_probs - mean)).astype(BF)
            grad_query = dot(grad_scores, keys) * (HEAD_DIM**-0.5)
            grads_buf[0, at, here] = (
                grad_query * cos_ref[at] - half_turn(grad_query) * sin_ref[at]
            ).astype(BF)
            grad_keys = dot_tn(grad_scores, query) * (HEAD_DIM**-0.5)
            grad_values = dot_tn(probs.astype(BF), grad)
            key_total = grad_keys if i == 0 else key_total + grad_keys
            value_total = grad_values if i == 0 else value_total + grad_values
        for half in range(2):
            at = slice(half * rows_all, (half + 1) * rows_all)
            sent_buf[half, head, 0] = key_total[at].astype(BF)
            sent_buf[half, head, 1] = value_total[at].astype(BF)
        pair_copy(head).start()
        return carry

    lax.fori_loop(0, heads, head_block, 0)
    combine_kernel(*results, out_ref)

    def head_sum(head, carry):
        here = pl.ds(pl.multiple_of(head * HEAD_DIM, HEAD_DIM), HEAD_DIM)
        pair_copy(head).wait_recv()
        key = sent_buf[y, head, 0].astype(F32) + got_buf[head, 0].astype(F32)
        grads_buf[1, :, here] = (key * cos_ref[...] - half_turn(key) * sin_ref[...]).astype(BF)
        value = sent_buf[y, head, 1].astype(F32) + got_buf[head, 1].astype(F32)
        grads_buf[2, :, here] = value.astype(BF)
        return carry

    lax.fori_loop(0, heads, head_sum, 0)
    pick = pair_pick(side_ref[...], 1)
    notes = []
    heads_buf[...] = jnp.zeros_like(heads_buf)
    own_columns = pl.ds(pl.multiple_of(x * columns, columns), columns)
    for j in range(3):
        at = slice(j * PAIR, (j + 1) * PAIR)
        notes.append((dot_nt(grads_buf[j], second_ref[at]) * pick).astype(BF))
        heads_buf[at, own_columns] = dot_tn(lanes_ref[j], grads_buf[j]).astype(BF)
    notes_buf[...] = padded(jnp.concatenate(notes, axis=1)).reshape(notes_buf.shape)
    heads_mover = Mover(heads_plan, (heads_buf,), (heads_got,), heads_own, *heads_sems)
    heads_mover.take()
    heads_mover.start()
    for offset in (1, 3, 2):
        notes_copy(offset).start()
    mover.start()
    own_notes = pltpu.make_async_copy(notes_buf.at[x], notes_ref.at[x], own_sem.at[0])
    own_notes.start()
    for load in loads[3:]:
        load.wait()

    def own_parts():
        return pltpu.make_async_copy(parts_buf.at[x], parts_ref.at[x], own_sem.at[1])

    def row_block(number, carry):
        offset = x_step(lax.rem(number + 1, along))
        peer = lax.rem(x + offset, along)
        at = pl.ds(pl.multiple_of(peer * tokens, tokens), tokens)
        total = None
        for j in range(3):
            part = dot_nt(grads_buf[j, at], weight_buf[j].reshape(-1, columns))
            total = part if total is None else total + part
        parts_buf[peer] = total.astype(BF)

        @pl.when(number < along - 1)
        def send():
            parts_copy(offset).start()

        @pl.when(number == along - 1)
        def keep():
            own_parts().start()

        return carry

    lax.fori_loop(0, along, row_block, 0)
    mover.finish()
    heads_mover.finish()
    own_notes.wait()
    own_parts().wait()

    def pairs_sent(head, carry):
        pair_copy(head).wait_send()
        return carry

    lax.fori_loop(0, heads, pairs_sent, 0)
    for offset in range(1, along):
        mixed_copy(offset).wait_send()
        parts_copy(offset).wait()
        notes_copy(offset).wait()


def attention_back(number, items, mixed, query, pairs, weight, small, results):
    plan = tuple((kind, group) for kind, group, array in items)
    arrays = [array for kind, group, array in items]
    along = GROUP_SIZE["x"]
    tokens, width = mixed.shape
    columns = width // along
    heads = columns // HEAD_DIM
    rows_all = along * tokens
    heads_items = [("from_columns", "f", shape_of((3 * PAIR, width), BF))]
    vmem = pl.BlockSpec(memory_space=pltpu.VMEM)
    outs = [shape_of(exchanged_shape(kind, group, array.shape), BF) for kind, group, array in items]
    outs += [
        shape_of(exchanged_shape("from_columns", "f", (3 * PAIR, width)), BF),
        shape_of((along, tokens, width), BF),
        shape_of((along, tokens, 128), BF),
        shape_of((1, tokens, width), BF),
    ]
    dma = pltpu.SemaphoreType.DMA
    return pl.pallas_call(
        functools.partial(attention_back_kernel, plan, (("from_columns", "f"),)),
        out_shape=outs,
        in_specs=[HBM] * (len(items) + 4) + [vmem] * (len(small) + len(results)),
        out_specs=[HBM] * (len(items) + 3) + [vmem],
        scratch_shapes=mover_scratch(items)
        + mover_scratch(heads_items)
        + [
            pltpu.VMEM((along, tokens, columns), BF),
            pltpu.VMEM((rows_all, columns), BF),
            pltpu.VMEM(pairs.shape, BF),
            pltpu.VMEM((3, *weight.shape[:1], *weight.shape[2:]), BF),
            pltpu.VMEM((2, heads, 2, rows_all, HEAD_DIM), BF),
            pltpu.VMEM((heads, 2, rows_all, HEAD_DIM), BF),
            pltpu.VMEM((3, rows_all, columns), BF),
            pltpu.VMEM((3 * PAIR, width), BF),
            pltpu.VMEM((along, tokens, width), BF),
            pltpu.VMEM((along, tokens, 128), BF),
            dma((along,)),
            dma((along,)),
            dma((heads,)),
            dma((heads,)),
            dma((2, along)),
            dma((2, along)),
            dma((6,)),
            dma((2,)),
        ],
        compiler_params=pltpu.CompilerParams(
            collective_id=number, has_side_effects=True, vmem_limit_bytes=VMEM_LIMIT
        ),
        name="attention_back",
    )(*arrays, mixed, query, pairs, weight, *small, *results)


def lane_expansion(ids_ref, group):
    ids = ids_ref[group][:, GROUP_SIZE["f"] : GROUP_SIZE["f"] + 1].astype(F32)
    lane = lane_index((PAIR, LANES))
    same = (lane // RANK).astype(F32) == ids
    return (same & (lane % RANK == row_index((PAIR, LANES)) % RANK)).astype(BF)


def expanded(expansions, got_ref, factor):
    total = None
    for group, expansion in enumerate(expansions):
        part = dot_tn(expansion, got_ref[group, factor * PAIR : (factor + 1) * PAIR, :])
        total = part if total is None else total + part
    return total.astype(BF)


FINISH = (
    (("from_columns", "f"),),
    (("from_columns", "f"),),
    (("rows", "c"), ("rows", "y")),
    (("gather", "c"), ("gather", "c"), ("gather", "c")),
    (("gather", "c"),),
)


def finish_kernel(*refs):
    parts_ref, notes_ref, rows_ref, normed_ref, residual_ref, gain_ref, first_ref = refs[:7]
    ids_ref, early_ref, shared_ref, heads_ref, column_ref, expert_hbm = refs[7:13]
    grad_out, attn_in, attn_out, ffn_out, router_out, shared_out = refs[13:19]
    expert_out, expert_in_out, down_out, refs = refs[19], refs[20], refs[21], refs[22:]
    late_buf, late_got, early_buf, early_parts, shared_buf, shared_parts = refs[:6]
    expert_got, late_sum, early_row, shared_row, expert_sum = refs[6:11]
    late_all, early_all, shared_all, expert_all, refs = *refs[11:15], refs[15:]
    ends = (
        ((expert_hbm,), (expert_got,)),
        ((late_buf,), (late_got,)),
        ((early_buf, shared_buf), (early_parts, shared_parts)),
        ((early_row, shared_row, expert_sum), (early_all, shared_all, expert_all)),
        ((late_sum,), (late_all,)),
    )
    movers = []
    for plan, (inputs, outputs) in zip(FINISH, ends):
        own, sems, refs = refs[: len(plan)], refs[len(plan) : len(plan) + 4], refs[len(plan) + 4 :]
        movers.append(Mover(plan, inputs, outputs, own, *sems))

    def begin(mover):
        mover.take()
        mover.start()

    movers[0].take()
    greet((("rows", "f"), ("rows", "c"), ("rows", "y")))
    movers[0].start()

    lanes = sum(notes_ref[i].astype(F32) for i in range(notes_ref.shape[0]))[:, : 3 * PAIR]
    lanes = lanes.astype(BF)
    late_buf[...] = dot_tn(lanes, normed_ref[...]).astype(BF)
    begin(movers[1])

    groups = ids_ref.shape[0]
    expansions = [lane_expansion(ids_ref, group) for group in range(groups)]
    row = 0
    for got in (early_ref, heads_ref):
        for factor in range(got.shape[1] // PAIR):
            early_buf[row : row + LANES, :] = expanded(expansions, got, factor)
            row += LANES
    router = None
    for group in range(groups):
        part = dot_tn(expansions[group], ids_ref[group])
        router = part if router is None else router + part
    router = jnp.sum(router * column_ref[...].astype(F32), axis=1, keepdims=True)
    early_buf[row : row + LANES, :] = jnp.broadcast_to(router, (LANES, 128)).astype(BF)
    for factor in range(shared_ref.shape[1] // PAIR):
        shared_buf[factor * LANES : (factor + 1) * LANES, :] = expanded(
            expansions, shared_ref, factor
        )
    begin(movers[2])

    grad = sum(parts_ref[i].astype(F32) for i in range(parts_ref.shape[0]))
    grad = grad + dot(lanes, first_ref[...])
    total = residual_ref[...] + rms_backward(rows_ref[0].astype(F32), gain_ref[...], grad)
    grad_out[0] = total.astype(BF)

    movers[0].finish()
    expert_sum[...] = sum(expert_got[i].astype(F32) for i in range(groups)).astype(BF)
    movers[2].finish()
    count = early_row.shape[0]
    early_row[...] = sum(
        early_parts[i * count : (i + 1) * count].astype(F32) for i in range(GROUP_SIZE["c"])
    ).astype(BF)
    count = shared_row.shape[0]
    shared_row[...] = (
        shared_parts[:count].astype(F32) + shared_parts[count:].astype(F32)
    ).astype(BF)
    begin(movers[3])
    movers[1].finish()
    for factor in range(late_got.shape[1] // PAIR):
        late_sum[factor * LANES : (factor + 1) * LANES, :] = expanded(expansions, late_got, factor)
    begin(movers[4])

    movers[3].finish()
    early = early_all[...].reshape(-1, 128).astype(F32)
    expert = expert_all[...].reshape(-1, 128).astype(F32)
    factor = [early[i * LANES : (i + 1) * LANES] for i in range(early.shape[0] // LANES)]
    attn_in[3 * LANES :, :] = factor[5]
    attn_out[: 3 * LANES, :] = jnp.concatenate(factor[8:11], axis=0)
    attn_out[3 * LANES :, :] = factor[6]
    ffn_out[...] = jnp.concatenate(factor[:5], axis=0)
    router_out[...] = factor[11][:, : router_out.shape[1]]
    down_out[:LANES, :] = factor[7]
    down_out[LANES:, :] = expert[3 * LANES :]
    expert_out[...] = expert[: 2 * LANES, : expert_out.shape[1]]
    expert_in_out[...] = expert[2 * LANES : 3 * LANES, : expert_in_out.shape[1]]
    along = GROUP_SIZE["x"]
    columns = shared_out.shape[1] // along
    quarters = [
        shared_all[2 * i : 2 * i + 2].reshape(-1, 128)[:, :columns].astype(F32) for i in range(along)
    ]
    shared_out[...] = jnp.concatenate(quarters, axis=1)
    movers[4].finish()
    attn_in[: 3 * LANES, :] = sum(late_all[i].astype(F32) for i in range(GROUP_SIZE["c"]))


def finish(
    number, parts, notes, rows, normed, residual, gain, first, ids, early, shared, heads, column, expert,
    shared_columns, expert_columns,
):
    tokens, width = normed.shape
    groups, ctx = GROUP_SIZE["f"], GROUP_SIZE["c"]
    early_rows = ((early.shape[1] + heads.shape[1]) // PAIR + 1) * LANES
    late_rows = first.shape[0] // PAIR * LANES
    shared_rows = shared.shape[1] // PAIR * LANES
    expert_rows = expert.shape[0]
    vmem = pl.BlockSpec(memory_space=pltpu.VMEM)
    bufs = [
        first.shape,
        (groups, first.shape[0], 128),
        (early_rows, 128),
        (early_rows, 128),
        (shared_rows, 128),
        (shared_rows, 128),
        (groups, expert_rows, 128),
        (late_rows, 128),
        (early_rows // ctx, 128),
        (shared_rows // 2, 128),
        (expert_rows, 128),
        (ctx, late_rows, 128),
        (ctx, early_rows // ctx, 128),
        (ctx, shared_rows // 2, 128),
        (ctx, expert_rows, 128),
    ]
    sent = ((expert.shape,), (bufs[0],), (bufs[2], bufs[4]), (bufs[8], bufs[9], bufs[10]), (bufs[7],))
    scratch = [pltpu.VMEM(buf, BF) for buf in bufs]
    for plan, shapes in zip(FINISH, sent):
        scratch += mover_scratch(
            [(kind, group, shape_of(shape, BF)) for (kind, group), shape in zip(plan, shapes)]
        )
    outs = [
        shape_of(rows.shape, BF),
        shape_of((4 * LANES, 128), F32),
        shape_of((4 * LANES, 128), F32),
        shape_of((5 * LANES, 128), F32),
        shape_of((LANES, 1), F32),
        shape_of((3 * LANES, shared_columns), F32),
        shape_of((2 * LANES, expert_columns), F32),
        shape_of((LANES, expert_columns), F32),
        shape_of((2 * LANES, 128), F32),
    ]
    return pl.pallas_call(
        finish_kernel,
        out_shape=outs,
        in_specs=[vmem] * 12 + [HBM],
        out_specs=[vmem] * len(outs),
        scratch_shapes=scratch,
        compiler_params=pltpu.CompilerParams(
            collective_id=number, has_side_effects=True, vmem_limit_bytes=VMEM_LIMIT
        ),
        name="finish",
    )(parts, notes, rows, normed, residual, gain, first, ids, early, shared, heads, column, expert)


def combine_kernel(
    main_ref, rest_ref, routes_ref, residual_ref, parts_ref, side_ref, small_ref, picked_ref, out_ref
):
    experts = main_ref.shape[0] // MAIN
    unused, main_hot, rest_hot = routing(routes_ref[0], experts)
    mixture = slots_to_rows(main_hot, rest_hot, main_ref[...], rest_ref[...])
    shared = sum(parts_ref[i].astype(F32) for i in range(parts_ref.shape[0]))
    shared = shared + dot(side_ref[:, :PAIR], picked_ref[2 * PAIR :])
    mix = small_ref[:, 2 * PAIR + TOP : 2 * PAIR + TOP + 1]
    out_ref[0] = (residual_ref[...] + mixture + mix * shared).astype(BF)


def shards(
    layer_hidden_input,
    output_cotangent,
    sequence_pair_lengths,
    block_placement_order,
    sequence_adapter_index,
    token_expert_choices,
    attention_norm_gain,
    feedforward_norm_gain,
    query_key_value_weight,
    output_projection_weight,
    query_key_value_bias,
    router_weight_matrix,
    shared_gate_up_weight,
    shared_down_weight,
    shared_sigmoid_gate,
    routed_gate_up_weight,
    routed_down_weight,
    attention_adapter_first,
    attention_adapter_second,
    feedforward_adapter_first,
    router_adapter_second,
    shared_gate_adapter_second,
    shared_down_adapter_first,
    routed_gate_adapter_second,
    routed_down_adapter_first,
    down_adapter_second,
):
    tokens, width = layer_hidden_input.shape[1:]
    experts = router_weight_matrix.shape[1]
    capacity = tokens * TOP // experts * 9 // 8
    tail = capacity - MAIN
    ctx_count = lax.axis_size("ctx")
    group_rows = tokens * ctx_count
    along = ctx_count // 2
    rows_shared = tokens * along
    x_index = lax.axis_index("ctx") // 2
    y_index = lax.axis_index("ctx") % 2
    head_columns = width // along
    hidden = shared_down_weight.shape[0]
    quarter = hidden // along
    shards_of = lax.axis_size("fsdp")
    lengths = sequence_pair_lengths[0]
    order = block_placement_order[0]
    adapters = sequence_adapter_index[0]
    block_size = group_rows // order.shape[0]

    qkv_own = lax.dynamic_slice_in_dim(
        query_key_value_weight, x_index * head_columns, head_columns, 2
    ).reshape(-1, head_columns)
    out_weight = lax.all_gather(output_projection_weight, "fsdp", tiled=True)
    units = -(-quarter // 32) * 32
    own_up = jnp.swapaxes(
        lax.dynamic_slice_in_dim(shared_gate_up_weight, x_index * quarter, quarter, 2), 1, 2
    )
    own_down = lax.dynamic_slice_in_dim(shared_down_weight, x_index * quarter, quarter, 0)
    own_shared = jnp.pad(
        jnp.concatenate([own_up, own_down[None]]), ((0, 0), (0, units - quarter), (0, 0))
    ).reshape(3 * units, width)

    def of_group(factor):
        parts = [lax.dynamic_index_in_dim(factor, adapters[s], -3, keepdims=True) for s in range(2)]
        both = jnp.concatenate(parts, axis=-3)
        return both.reshape(both.shape[:-3] + (PAIR, both.shape[-1]))

    shared_second = jnp.concatenate(
        [
            of_group(shared_gate_adapter_second).reshape(2 * PAIR, hidden * shards_of),
            of_group(shared_down_adapter_first),
        ],
        axis=0,
    )
    shared_second = lax.dynamic_index_in_dim(
        shared_second.reshape(3 * PAIR, shards_of, along, quarter), x_index, 2, keepdims=False
    )
    shared_second = jnp.pad(shared_second, ((0, 0), (0, 0), (0, units - quarter)))
    shared_second = shared_second.reshape(3 * PAIR, shards_of * units)
    numbers = jnp.concatenate([adapters, x_index[None].astype(jnp.int32)])

    start = lengths[0]
    block_rows = jnp.arange(block_size, dtype=jnp.int32)
    blocks = order.reshape(along, 2, -1)
    key_places = (jnp.swapaxes(blocks, 0, 1).reshape(-1)[:, None] * block_size + block_rows).reshape(
        1, group_rows
    )
    own_blocks = lax.dynamic_index_in_dim(blocks, y_index, 1, keepdims=False).reshape(-1)
    places = own_blocks[:, None] * block_size + block_rows
    second = places >= start
    fractions = jnp.arange(0, HEAD_DIM, 2).astype(F32) / HEAD_DIM
    speeds = rope_theta ** (-fractions)
    bases = jnp.stack([own_blocks * block_size, own_blocks * block_size - start])
    base_angles = bases.astype(F32)[:, :, None, None] * speeds
    base_angles = jnp.concatenate([base_angles, base_angles], axis=3)
    base_cos, base_sin = jnp.cos(base_angles), jnp.sin(base_angles)
    base_cos = jnp.where(second[:, :, None], base_cos[1], base_cos[0])
    base_sin = jnp.where(second[:, :, None], base_sin[1], base_sin[0])
    row_angles = block_rows.astype(F32)[:, None] * speeds[None, :]
    row_angles = jnp.concatenate([row_angles, row_angles], axis=1)
    row_cos, row_sin = jnp.cos(row_angles), jnp.sin(row_angles)
    cosine = base_cos * row_cos - base_sin * row_sin
    sine = base_sin * row_cos + base_cos * row_sin
    sine = jnp.where(jnp.arange(HEAD_DIM) < HEAD_DIM // 2, -sine, sine)
    cosine, sine = cosine.reshape(rows_shared, HEAD_DIM), sine.reshape(rows_shared, HEAD_DIM)
    place_column = places.reshape(rows_shared, 1)
    start_column = jnp.where(second, start, 0).reshape(rows_shared, 1)
    side_shared = second.astype(F32).reshape(rows_shared, 1)
    side = lax.dynamic_slice_in_dim(side_shared, x_index * tokens, tokens)

    attention_gain = attention_norm_gain[None, :]
    feedforward_gain = feedforward_norm_gain[None, :]
    mix_weight = shared_sigmoid_gate[None, :]
    routed_second = routed_gate_adapter_second.reshape(2, LANES, -1)
    routed_first = routed_down_adapter_first.reshape(LANES, -1)
    ffn_flat = feedforward_adapter_first.reshape(-1, LANES, width)[3:]
    down_flat = down_adapter_second.reshape(2, LANES, width)

    normed_one, sent_grads_main, sent_grads_rest, picked, picked_first, picked_second = prologue(
        numbers,
        layer_hidden_input,
        output_cotangent,
        attention_gain,
        token_expert_choices,
        feedforward_adapter_first,
        down_adapter_second,
        attention_adapter_first,
        attention_adapter_second,
        experts,
        head_columns,
    )
    own_shared, normed_one = lax.optimization_barrier((own_shared, normed_one))
    shared_weight = lax.all_gather(own_shared, "fsdp")
    qkv, normed_shared = exchange(
        "gather_first", 0, ("share", "s", qkv_own), ("gather", "x", normed_one)
    )
    qkv = qkv.reshape(shards_of, 3, tokens, head_columns)
    projected, qkv_lanes = project(
        numbers,
        normed_shared.reshape(rows_shared, width),
        qkv,
        attention_adapter_first,
        attention_adapter_second,
        query_key_value_bias,
        side_shared,
        cosine,
        sine,
    )
    pairs, grads_shared = exchange(
        "keys", 1, ("gather", "y", projected[1:]), ("gather", "x", output_cotangent[0])
    )
    mixed_heads = attend(projected, pairs, place_column, start_column, key_places)
    (mixed,) = exchange(
        "mixed", 2, ("to_columns", "x", mixed_heads.reshape(along, tokens, head_columns))
    )
    residual, normed_two, small, sent_main, sent_rest, notes_main, notes_rest = after_attention(
        numbers,
        mixed,
        out_weight,
        layer_hidden_input,
        attention_adapter_first,
        attention_adapter_second,
        feedforward_gain,
        feedforward_adapter_first,
        router_weight_matrix,
        router_adapter_second,
        mix_weight,
        token_expert_choices,
        side,
    )
    *held, parts_rows, parts_lanes, value_part, shared_columns = shared_expert(
        3,
        normed_two,
        [
            ("rows", "f", array)
            for array in (
                sent_main,
                sent_rest,
                sent_grads_main,
                sent_grads_rest,
                notes_main,
                notes_rest,
            )
        ],
        grads_shared,
        shared_weight,
        side_shared.reshape(along, tokens, 1),
        picked,
        shared_second,
        mix_weight,
    )
    (
        got_main,
        got_rest,
        got_notes_main,
        got_notes_rest,
        result_main,
        result_rest,
        value_parts,
        expert_columns,
    ) = routed_expert(
        4,
        held,
        value_part,
        ffn_flat,
        routed_second,
        routed_first,
        down_flat,
        routed_gate_up_weight,
        routed_down_weight,
    )
    expert_rows = lax.psum_scatter(expert_columns, "ctx", tiled=True)
    grad_residual, grad_mixed, early_columns, router_rows, shared_side = after_experts(
        numbers,
        parts_rows,
        parts_lanes,
        got_main,
        got_rest,
        got_notes_main,
        got_notes_rest,
        output_cotangent,
        normed_two,
        residual,
        small,
        mixed,
        token_expert_choices,
        side,
        feedforward_adapter_first,
        router_weight_matrix,
        router_adapter_second,
        mix_weight,
        feedforward_gain,
        down_adapter_second,
        attention_adapter_first,
        attention_adapter_second,
        out_weight,
    )

    early_got, shared_got, router_got, heads_got, first_parts, first_lanes, output_value = (
        attention_back(
            5,
            [
                ("from_columns", "f", early_columns),
                ("from_columns", "f", shared_columns),
                ("gather", "f", router_rows),
            ],
            grad_mixed,
            projected,
            pairs,
            qkv,
            (
                place_column,
                start_column,
                key_places,
                cosine,
                sine,
                side_shared,
                qkv_lanes,
                picked_second,
            ),
            (
                result_main,
                result_rest,
                token_expert_choices,
                residual,
                value_parts,
                shared_side,
                small,
                picked,
            ),
        )
    )
    own_column = (jnp.arange(128) == lax.axis_index("fsdp")).astype(BF)[None, :]
    grads = finish(
        6,
        first_parts,
        first_lanes,
        layer_hidden_input,
        normed_one,
        grad_residual,
        attention_gain,
        picked_first,
        router_got,
        early_got,
        shared_got,
        heads_got,
        own_column,
        expert_rows,
        along * quarter,
        routed_down_weight.shape[1] // shards_of,
    )

    def by_adapter(rows):
        parts = rows.reshape(-1, ADAPTER_COUNT, RANK, rows.shape[1])
        return parts[0] if parts.shape[0] == 1 else parts

    shared_total = grads[5]
    return (
        output_value,
        grads[0],
        by_adapter(grads[1]),
        by_adapter(grads[2]),
        by_adapter(grads[3]),
        by_adapter(grads[4]),
        by_adapter(shared_total[: 2 * LANES]),
        by_adapter(shared_total[2 * LANES :]),
        by_adapter(grads[6]),
        by_adapter(grads[7]),
        by_adapter(grads[8]),
    )


def solution(mesh):
    return jax.shard_map(
        shards,
        mesh=mesh,
        in_specs=(
            P("fsdp", "ctx", None),
            P("fsdp", "ctx", None),
            P("fsdp", None),
            P("fsdp", None),
            P("fsdp", None),
            P("fsdp", "ctx", None),
            P(),
            P(),
            P(None, "fsdp", None),
            P("fsdp", None),
            P(),
            P(),
            P(None, None, "fsdp"),
            P("fsdp", None),
            P(),
            P("fsdp", None, None, None),
            P("fsdp", None, None),
            P(),
            P(),
            P(),
            P(),
            P(),
            P(),
            P(),
            P(),
            P(),
        ),
        out_specs=(
            P("fsdp", "ctx", None),
            P("fsdp", "ctx", None),
            P(None, None, None, "fsdp"),
            P(None, None, None, "fsdp"),
            P(None, None, None, "fsdp"),
            P(None, None, "fsdp"),
            P(None, None, None, "fsdp"),
            P(None, None, "fsdp"),
            P(None, None, None, "fsdp"),
            P(None, None, "fsdp"),
            P(None, None, None, "fsdp"),
        ),
        check_vma=False,
    )
```

```python
import functools

import jax
import jax.numpy as jnp
from jax import lax
from jax.experimental import pallas as pl
from jax.experimental.pallas import tpu as pltpu
from jax.sharding import PartitionSpec as P

HEADS = 16
HEAD_DIM = 128
TOP = 4
ADAPTER_COUNT = 8
RANK = 16
LANES = ADAPTER_COUNT * RANK
PAIR = 2 * RANK
MAIN = 32

norm_eps = 1e-06
rope_theta = 1000000.0
masked_score = -1e30
highest = lax.Precision.HIGHEST
MESH = pl.DeviceIdType.MESH
BF = jnp.bfloat16
F32 = jnp.float32
VMEM_LIMIT = 56 * 2**20


def dot(left, right):
    return jnp.dot(left, right, preferred_element_type=F32)


def dot_nt(left, right):
    return lax.dot_general(left, right, (((1,), (1,)), ((), ())), preferred_element_type=F32)


def dot_tn(left, right):
    return lax.dot_general(left, right, (((0,), (0,)), ((), ())), preferred_element_type=F32)


GROUP_SIZE = {"x": 4, "y": 2, "c": 8, "f": 16}


def place_in(group):
    ctx, fsdp = lax.axis_index("ctx"), lax.axis_index("fsdp")
    return {"x": ctx // 2, "y": ctx % 2, "c": ctx, "f": fsdp}[group]


def device_of(group, index):
    ctx, fsdp = lax.axis_index("ctx"), lax.axis_index("fsdp")
    if group == "x":
        return (index * 2 + ctx % 2, fsdp)
    if group == "y":
        return ((ctx // 2) * 2 + index, fsdp)
    if group == "c":
        return (index, fsdp)
    return (ctx, index)


def chip():
    ctx, fsdp = lax.axis_index("ctx"), lax.axis_index("fsdp")
    return ctx % 2 * 2 + fsdp // 8, fsdp // 2 % 4, fsdp % 2


def device_at(y, z, core):
    return (lax.axis_index("ctx") // 2 * 2 + y // 2, y % 2 * 8 + z * 2 + core)


def shard_at(y, z, core):
    return y % 2 * 8 + z * 2 + core


def exchanged_shape(kind, group, shape):
    if kind == "share":
        return (GROUP_SIZE["f"],) + shape
    count = GROUP_SIZE[group]
    if kind == "gather":
        return (count,) + shape
    if kind in ("swap", "rows", "half"):
        return shape
    if kind == "from_columns":
        return (count, shape[0], shape[1] // count)
    return (shape[1], count * shape[2])


def own_shape(kind, group, shape):
    if kind in ("gather", "share"):
        return shape
    count = GROUP_SIZE[group]
    if kind in ("rows", "half"):
        return (shape[0] // count,) + shape[1:]
    if kind == "from_columns":
        return (shape[0], shape[1] // count)
    return shape[1:]


def copies_of(kind, group):
    return 23 if kind == "share" else GROUP_SIZE[group] - 1


def soon(offset):
    return offset % 4 >= 2


def block_of(ref, kind, count, index):
    if kind == "rows":
        depth = ref.shape[0] // count
        return ref.at[pl.ds(pl.multiple_of(index * depth, depth), depth)]
    if kind == "columns":
        width = ref.shape[1] // count
        return ref.at[:, pl.ds(pl.multiple_of(index * width, width), width)]
    return ref.at[index]


def source_of(kind, group, ref, index):
    if kind in ("gather", "share"):
        return ref
    cut = {"rows": "rows", "half": "rows", "from_columns": "columns"}.get(kind, "first")
    return block_of(ref, cut, GROUP_SIZE[group], index)


def target_of(kind, group, ref, index):
    cut = {"rows": "rows", "half": "rows", "to_columns": "columns"}.get(kind, "first")
    return block_of(ref, cut, GROUP_SIZE["f" if kind == "share" else group], index)


def remote(source, target, send, recv, device):
    return pltpu.make_async_remote_copy(
        src_ref=source,
        dst_ref=target,
        send_sem=send,
        recv_sem=recv,
        device_id=device,
        device_id_type=MESH,
    )


def greet(plan):
    barrier = pltpu.get_barrier_semaphore()
    count = 0
    for group in sorted({group for kind, group in plan}):
        if group == "s":
            y, z, core = chip()
            peers = [device_at(y, lax.rem(z + d, 4), core) for d in (1, 2, 3)]
            peers += [device_at(lax.rem(y + d, 4), z, core) for d in (1, 3)]
            peers += [device_at(y, z, 1 - core)]
        else:
            size = GROUP_SIZE[group]
            mine = place_in(group)
            peers = [device_of(group, lax.rem(mine + d, size)) for d in range(1, size)]
        for peer in peers:
            pl.semaphore_signal(barrier, inc=1, device_id=peer, device_id_type=MESH)
        count += len(peers)
    pl.semaphore_wait(barrier, count)


class Share:
    def __init__(self, source, target, send, recv, first):
        self.target = target
        self.sems = (send, recv, first)
        y, z, core = self.place = chip()
        self.order = (1, 3, 2)
        self.source = source
        self.along_z = [
            self.copy(source, shard_at(y, z, core), None, i, device_at(y, lax.rem(z + d, 4), core))
            for i, d in enumerate(self.order)
        ]
        self.along_y, self.across = [], []

    def copy(self, source, shard, half, number, device):
        send, recv, first = self.sems
        target = self.target.at[shard]
        if half is not None:
            target = target.at[half]
        return remote(source, target, send.at[first + number], recv.at[first + number], device)

    def halves(self):
        half = self.target.shape[1] // 2
        return pl.ds(0, half), pl.ds(half, half)

    def forward(self, number, source, z):
        y, unused, core = self.place
        unused, my_z, unused = self.place
        shard = shard_at(y, z, core)
        for i, (half, d) in enumerate(zip(self.halves(), (3, 1))):
            copy = self.copy(
                source.at[half], shard, half, 3 + 2 * number + i, device_at(lax.rem(y + d, 4), my_z, core)
            )
            copy.start()
            self.along_y.append(copy)
        copy = self.copy(source, shard, None, 11 + number, device_at(y, my_z, 1 - core))
        copy.start()
        self.across.append(copy)

    def start(self):
        for copy in self.along_z:
            copy.start()
        self.forward(0, self.source, self.place[1])

    def finish(self):
        y, z, core = self.place
        for i, d in enumerate(self.order):
            self.along_z[i].wait_recv()
            from_z = lax.rem(z + 4 - d, 4)
            self.forward(i + 1, self.target.at[shard_at(y, from_z, core)], from_z)
        for number in range(4):
            from_z = z if number == 0 else lax.rem(z + 4 - self.order[number - 1], 4)
            shard = shard_at(y + 1, from_z, core)
            for i, half in enumerate(self.halves()):
                self.along_y[2 * number + i].wait_recv()
                block = self.target.at[shard].at[half]
                copy = self.copy(block, shard, half, 15 + 2 * number + i, device_at(y, z, 1 - core))
                copy.start()
                self.across.append(copy)
        for copy in self.along_z + self.along_y:
            copy.wait_send()
        for copy in self.across:
            copy.wait()


class Mover:
    def __init__(self, plan, inputs, outputs, own, send, recv, in_sem, out_sem):
        self.plan, self.inputs, self.outputs, self.own = plan, inputs, outputs, own
        self.send, self.recv, self.in_sem, self.out_sem = send, recv, in_sem, out_sem
        self.taken, self.copies, self.shares = [], [], []

    def own_place(self, item):
        kind, group = self.plan[item]
        return shard_at(*chip()) if kind == "share" else place_in(group)

    def take(self):
        for item, (kind, group) in enumerate(self.plan):
            block = source_of(kind, group, self.inputs[item], self.own_place(item))
            copy = pltpu.make_async_copy(block, self.own[item], self.in_sem.at[item])
            copy.start()
            self.taken.append(copy)

    def start(self):
        slot = 0
        for item, (kind, group) in enumerate(self.plan):
            source, target = self.inputs[item], self.outputs[item]
            if kind == "share":
                share = Share(source, target, self.send, self.recv, slot)
                share.start()
                self.shares.append(share)
            else:
                count = GROUP_SIZE[group]
                mine = place_in(group)
                for offset in range(1, count):
                    if kind == "half" and not soon(offset):
                        continue
                    peer = lax.rem(mine + offset, count)
                    copy = remote(
                        source_of(kind, group, source, peer),
                        target_of(kind, group, target, mine),
                        self.send.at[slot + offset - 1],
                        self.recv.at[slot + offset - 1],
                        device_of(group, peer),
                    )
                    copy.start()
                    self.copies.append(copy)
            slot += copies_of(kind, group)
        for item, (kind, group) in enumerate(self.plan):
            self.taken[item].wait()
            block = target_of(kind, group, self.outputs[item], self.own_place(item))
            copy = pltpu.make_async_copy(self.own[item], block, self.out_sem.at[item])
            copy.start()
            self.copies.append(copy)

    def finish(self):
        for share in self.shares:
            share.finish()
        for copy in self.copies:
            copy.wait()


def exchange_kernel(plan, *refs):
    amount = len(plan)
    mover = Mover(
        plan, refs[:amount], refs[amount : 2 * amount], refs[2 * amount : 3 * amount], *refs[3 * amount :]
    )
    mover.take()
    greet(plan)
    mover.start()
    mover.finish()


def mover_scratch(items):
    plan = tuple((kind, group) for kind, group, array in items)
    slots = sum(copies_of(kind, group) for kind, group in plan)
    return [
        pltpu.VMEM(own_shape(kind, group, array.shape), array.dtype) for kind, group, array in items
    ] + [
        pltpu.SemaphoreType.DMA((slots,)),
        pltpu.SemaphoreType.DMA((slots,)),
        pltpu.SemaphoreType.DMA((len(items),)),
        pltpu.SemaphoreType.DMA((len(items),)),
    ]


def exchange(name, number, *items):
    plan = tuple((kind, group) for kind, group, array in items)
    arrays = [array for kind, group, array in items]
    return pl.pallas_call(
        functools.partial(exchange_kernel, plan),
        out_shape=[
            jax.ShapeDtypeStruct(exchanged_shape(kind, group, array.shape), array.dtype)
            for kind, group, array in items
        ],
        in_specs=[pl.BlockSpec(memory_space=pltpu.HBM)] * len(items),
        out_specs=[pl.BlockSpec(memory_space=pltpu.HBM)] * len(items),
        scratch_shapes=mover_scratch(items),
        compiler_params=pltpu.CompilerParams(
            collective_id=number, has_side_effects=True, vmem_limit_bytes=16 * 2**20
        ),
        name=name,
    )(*arrays)


def rms_forward(values, gain):
    mean_square = jnp.mean(values * values, axis=-1, keepdims=True)
    return values * lax.rsqrt(mean_square + norm_eps) * gain.astype(F32)


def rms_backward(values, gain, grad_result):
    scale = lax.rsqrt(jnp.mean(values * values, axis=-1, keepdims=True) + norm_eps)
    scaled = gain.astype(F32) * grad_result
    inner = jnp.mean(values * scaled, axis=-1, keepdims=True)
    return scale * scaled - values * (scale * scale * scale) * inner


def logistic(values):
    return 1.0 / (1.0 + jnp.exp(-values))


def swiglu_backward(gate, upper, grad_hidden):
    sigma = logistic(gate)
    grad_gate = grad_hidden * upper * sigma * (1.0 + gate * (1.0 - sigma))
    grad_upper = grad_hidden * gate * sigma
    return (grad_gate.astype(BF), grad_upper.astype(BF))


def two_parts(values):
    high = values.astype(BF)
    return high, (values - high.astype(F32)).astype(BF)


def lane_index(shape):
    return lax.broadcasted_iota(jnp.int32, shape, 1)


def row_index(shape):
    return lax.broadcasted_iota(jnp.int32, shape, 0)


def pair_pick(second, copies):
    shape = (second.shape[0], PAIR * copies)
    of_lane = (lane_index(shape) % PAIR >= RANK).astype(F32)
    return (of_lane == second).astype(F32)


def pair_of(first_ref, last_ref, index):
    return jnp.concatenate([first_ref[index, 0], last_ref[index, 0]], axis=0)


def padded(values):
    rest = 128 - values.shape[1]
    return jnp.concatenate([values, jnp.zeros((values.shape[0], rest), values.dtype)], axis=1)


def routing(routes, experts):
    tokens = routes.shape[0]
    expert_lane = lane_index((tokens, experts))
    expert_hot = [(routes[:, k : k + 1] == expert_lane).astype(F32) for k in range(TOP)]
    count = sum(expert_hot)
    below = (row_index((tokens, tokens)) > lane_index((tokens, tokens))).astype(BF)
    earlier = dot(below, count.astype(BF))
    rank = [jnp.sum(hot * earlier, axis=1, keepdims=True).astype(jnp.int32) for hot in expert_hot]
    main_lane = lane_index((tokens, experts * MAIN))
    rest_lane = lane_index((tokens, experts * 16))
    rest_code = (rest_lane // 16) * 4 + rest_lane % 4
    main_hot, rest_hot = [], []
    for k in range(TOP):
        expert = routes[:, k : k + 1]
        main_slot = jnp.where(rank[k] < MAIN, expert * MAIN + rank[k], -1)
        rest_slot = jnp.where(rank[k] < MAIN, -1, expert * 4 + rank[k] - MAIN)
        main_hot.append((main_lane == main_slot).astype(F32))
        rest_hot.append((rest_code == rest_slot).astype(F32))
    return expert_hot, main_hot, rest_hot


def quarter_mask(shape, quarter):
    return (lane_index(shape) % 16 // 4 == quarter).astype(F32)


def rows_to_slots(main_hot, rest_hot, rows):
    main = dot_tn(sum(main_hot).astype(BF), rows).astype(BF)
    rest_sum = sum(rest_hot)
    width = rows.shape[1] // 4
    rest = None
    for quarter in range(4):
        hot = (rest_sum * quarter_mask(rest_sum.shape, quarter)).astype(BF)
        part = dot_tn(hot, rows[:, quarter * width : (quarter + 1) * width])
        rest = part if rest is None else rest + part
    return main, rest.astype(BF)


def slots_to_rows(main_hot, rest_hot, main, rest):
    rest_sum = sum(rest_hot)
    parts = [
        dot((rest_sum * quarter_mask(rest_sum.shape, quarter)).astype(BF), rest)
        for quarter in range(4)
    ]
    return dot(sum(main_hot).astype(BF), main) + jnp.concatenate(parts, axis=1)


def rest_selectors(sources):
    shape = (4 * sources, 16 * sources)
    row, lane = row_index(shape), lane_index(shape)
    same = (lane // 16 == row // 4) & (lane % 4 == row % 4)
    return [(same & (lane % 16 // 4 == quarter)).astype(BF) for quarter in range(4)]


def rest_to_rows(selectors, rest):
    return jnp.concatenate([dot(selector, rest) for selector in selectors], axis=1).astype(BF)


def rows_to_rest(selectors, rows):
    width = rows.shape[1] // 4
    total = None
    for quarter in range(4):
        part = dot_tn(selectors[quarter], rows[:, quarter * width : (quarter + 1) * width])
        total = part if total is None else total + part
    return total.astype(BF)


def stage(kernel, name, out_shape, in_specs, out_specs, grid=(1,), scratch=(), prefetch=0):
    return pl.pallas_call(
        kernel,
        out_shape=out_shape,
        grid_spec=pltpu.PrefetchScalarGridSpec(
            num_scalar_prefetch=prefetch,
            grid=grid,
            in_specs=in_specs,
            out_specs=out_specs,
            scratch_shapes=list(scratch),
        ),
        compiler_params=pltpu.CompilerParams(vmem_limit_bytes=VMEM_LIMIT),
        name=name,
    )


def whole(array):
    zeros = (0,) * len(array.shape)
    return pl.BlockSpec(array.shape, lambda *unused: zeros)


def of_sequence(which, block):
    return pl.BlockSpec(block, lambda *at: (0, at[-1][which], 0, 0))


def shape_of(shape, kind):
    return jax.ShapeDtypeStruct(shape, kind)


HBM = pl.BlockSpec(memory_space=pltpu.HBM)


def prologue_kernel(
    numbers_ref,
    rows_ref,
    grads_ref,
    gain_ref,
    routes_ref,
    ffn_a_ref,
    ffn_b_ref,
    down_a_ref,
    down_b_ref,
    first_a_ref,
    first_b_ref,
    second_a_ref,
    second_b_ref,
    normed_ref,
    main_ref,
    rest_ref,
    picked_ref,
    first_ref,
    second_ref,
):
    normed_ref[...] = rms_forward(rows_ref[0].astype(F32), gain_ref[...]).astype(BF)
    experts = main_ref.shape[0] // MAIN
    unused, main_hot, rest_hot = routing(routes_ref[0], experts)
    main, rest = rows_to_slots(main_hot, rest_hot, grads_ref[0])
    main_ref[...] = main
    rest_ref[...] = rest
    picked_ref[...] = jnp.concatenate(
        [
            pair_of(ffn_a_ref, ffn_b_ref, 1),
            pair_of(ffn_a_ref, ffn_b_ref, 2),
            pair_of(down_a_ref, down_b_ref, 0),
        ],
        axis=0,
    )
    for j in range(3):
        first_ref[j * PAIR : (j + 1) * PAIR, :] = pair_of(first_a_ref, first_b_ref, j)
        second_ref[j * PAIR : (j + 1) * PAIR, :] = pair_of(second_a_ref, second_b_ref, j)


def prologue(
    numbers, rows, grads, gain, routes, ffn_first, down_second, first, second, experts, columns
):
    tokens, width = rows.shape[1:]
    heads = lambda which: pl.BlockSpec(
        (3, 1, RANK, columns), lambda n, a: (0, a[which], 0, a[2])
    )
    outs = [
        (tokens, width),
        (experts * MAIN, width),
        (experts * 16, width // 4),
        (3 * PAIR, width),
        (3 * PAIR, width),
        (3 * PAIR, columns),
    ]
    return stage(
        prologue_kernel,
        "prologue",
        [shape_of(shape, BF) for shape in outs],
        [
            whole(rows),
            whole(grads),
            whole(gain),
            whole(routes),
            of_sequence(0, (3, 1, RANK, width)),
            of_sequence(1, (3, 1, RANK, width)),
            of_sequence(0, (1, 1, RANK, width)),
            of_sequence(1, (1, 1, RANK, width)),
            of_sequence(0, (3, 1, RANK, width)),
            of_sequence(1, (3, 1, RANK, width)),
            heads(0),
            heads(1),
        ],
        [pl.BlockSpec(shape, lambda n, a: (0, 0)) for shape in outs],
        prefetch=1,
    )(
        numbers, rows, grads, gain, routes, ffn_first, ffn_first, down_second, down_second, first, first,
        second, second,
    )


def half_turn(values):
    parts = []
    for head in range(values.shape[1] // HEAD_DIM):
        part = values[:, head * HEAD_DIM : (head + 1) * HEAD_DIM]
        parts.append(jnp.concatenate([part[:, 64:], part[:, :64]], axis=1))
    return jnp.concatenate(parts, axis=1) if len(parts) > 1 else parts[0]


def project_kernel(
    numbers_ref,
    rows_ref,
    weight_ref,
    first_a_ref,
    first_b_ref,
    second_a_ref,
    second_b_ref,
    bias_ref,
    side_ref,
    cos_ref,
    sin_ref,
    out_ref,
    lanes_ref,
):
    which = pl.program_id(0)

    @pl.when(pl.program_id(1) == 0)
    def lanes():
        first = pair_of(first_a_ref, first_b_ref, 0)
        picked = dot_nt(rows_ref[...], first) * pair_pick(side_ref[...], 1)
        lanes_ref[0] = picked.astype(BF)

    weight = weight_ref[...].reshape(rows_ref.shape[1], weight_ref.shape[3])
    bias = bias_ref[...].astype(F32)
    bias = jnp.sum(jnp.where(row_index(bias.shape) == which, bias, 0.0), axis=0, keepdims=True)
    second = pair_of(second_a_ref, second_b_ref, 0)
    value = dot(rows_ref[...], weight) + bias + dot(lanes_ref[0], second)
    copies = value.shape[1] // HEAD_DIM
    cosine = jnp.concatenate([cos_ref[...]] * copies, axis=1)
    sine = jnp.concatenate([sin_ref[...]] * copies, axis=1)
    turned = value * cosine + half_turn(value) * sine
    out_ref[0] = jnp.where(which < 2, turned, value).astype(BF)


def project(numbers, rows, weight, first, second, bias, side, cosine, sine):
    tokens, width = rows.shape
    columns = weight.shape[3]
    step = 256
    steps = columns // step
    return stage(
        project_kernel,
        "project",
        [shape_of((3, tokens, columns), BF), shape_of((3, tokens, PAIR), BF)],
        [
            whole(rows),
            pl.BlockSpec((weight.shape[0], 1, weight.shape[2], step), lambda j, n, a: (0, j, 0, n)),
            pl.BlockSpec((1, 1, RANK, width), lambda j, n, a: (j, a[0], 0, 0)),
            pl.BlockSpec((1, 1, RANK, width), lambda j, n, a: (j, a[1], 0, 0)),
            pl.BlockSpec((1, 1, RANK, step), lambda j, n, a: (j, a[0], 0, a[2] * steps + n)),
            pl.BlockSpec((1, 1, RANK, step), lambda j, n, a: (j, a[1], 0, a[2] * steps + n)),
            pl.BlockSpec((3, step), lambda j, n, a: (0, a[2] * steps + n)),
            whole(side),
            whole(cosine),
            whole(sine),
        ],
        [
            pl.BlockSpec((1, tokens, step), lambda j, n, a: (j, 0, n)),
            pl.BlockSpec((1, tokens, PAIR), lambda j, n, a: (j, 0, 0)),
        ],
        grid=(3, steps),
        prefetch=1,
    )(numbers, rows, weight, first, first, second, second, bias, side, cosine, sine)


def probabilities(query, keys, query_place, query_start, key_place):
    scores = dot_nt(query, keys) * (HEAD_DIM**-0.5)
    allowed = (key_place <= query_place) & (key_place >= query_start)
    scores = jnp.where(allowed, scores, masked_score)
    top = jnp.max(scores, axis=1, keepdims=True)
    raised = jnp.exp(scores - top)
    return raised * (1.0 / jnp.sum(raised, axis=1, keepdims=True))


def attend_kernel(query_ref, key_ref, value_ref, place_ref, start_ref, key_place_ref, out_ref):
    keys = key_ref[...].reshape(-1, HEAD_DIM)
    values = value_ref[...].reshape(-1, HEAD_DIM)
    probs = probabilities(query_ref[0], keys, place_ref[...], start_ref[...], key_place_ref[...])
    out_ref[...] = dot(probs.astype(BF), values).astype(BF)


def attend(projected, pairs, place, start, key_place):
    tokens, columns = projected.shape[1:]
    step = 256
    keys = pairs.shape[0] * pairs.shape[2]
    half = pairs.shape[2]
    return pl.pallas_call(
        attend_kernel,
        grid=(columns // HEAD_DIM, tokens // step),
        out_shape=jax.ShapeDtypeStruct((tokens, columns), BF),
        in_specs=[
            pl.BlockSpec((1, step, HEAD_DIM), lambda h, i: (0, i, h)),
            pl.BlockSpec((2, 1, half, HEAD_DIM), lambda h, i: (0, 0, 0, h)),
            pl.BlockSpec((2, 1, half, HEAD_DIM), lambda h, i: (0, 1, 0, h)),
            pl.BlockSpec((step, 1), lambda h, i: (i, 0)),
            pl.BlockSpec((step, 1), lambda h, i: (i, 0)),
            pl.BlockSpec((1, keys), lambda h, i: (0, 0)),
        ],
        out_specs=pl.BlockSpec((step, HEAD_DIM), lambda h, i: (i, h)),
        compiler_params=pltpu.CompilerParams(vmem_limit_bytes=VMEM_LIMIT),
        name="attend",
    )(projected, pairs, pairs, place, start, key_place)


def after_attention_kernel(
    numbers_ref,
    mixed_ref,
    weight_ref,
    rows_ref,
    first_a_ref,
    first_b_ref,
    second_a_ref,
    second_b_ref,
    gain_ref,
    ffn_a_ref,
    ffn_b_ref,
    router_ref,
    router_a_ref,
    router_b_ref,
    mix_ref,
    routes_ref,
    side_ref,
    residual_ref,
    normed_ref,
    small_ref,
    main_ref,
    rest_ref,
    main_notes_ref,
    rest_notes_ref,
    lanes_ref,
):
    step = pl.program_id(0)
    side = side_ref[...]
    pick = pair_pick(side, 1)

    @pl.when(step == 0)
    def lanes():
        first = pair_of(first_a_ref, first_b_ref, 0)
        lanes_ref[...] = (dot_nt(mixed_ref[...], first) * pick).astype(BF)

    columns = weight_ref.shape[1]
    here = pl.ds(pl.multiple_of(step * columns, columns), columns)
    second = pair_of(second_a_ref, second_b_ref, 0)
    residual_ref[:, here] = rows_ref[0].astype(F32) + (
        dot(mixed_ref[...], weight_ref[...]) + dot(lanes_ref[...], second)
    )

    @pl.when(step == pl.num_programs(0) - 1)
    def last():
        tokens = residual_ref.shape[0]
        experts = router_ref.shape[1]
        normed = rms_forward(residual_ref[...], gain_ref[...]).astype(BF)
        normed_ref[...] = normed
        router_lanes = (dot_nt(normed, pair_of(ffn_a_ref, ffn_b_ref, 0)) * pick).astype(BF)
        router_second = jnp.concatenate([router_a_ref[0], router_b_ref[0]], axis=0)
        logits = dot(normed, router_ref[...]) + dot(router_lanes, router_second)
        expert_hot, main_hot, rest_hot = routing(routes_ref[0], experts)
        chosen = [jnp.sum(hot * logits, axis=1, keepdims=True) for hot in expert_hot]
        top = jnp.maximum(jnp.maximum(chosen[0], chosen[1]), jnp.maximum(chosen[2], chosen[3]))
        raised = [jnp.exp(value - top) for value in chosen]
        total = sum(raised)
        gates = [value / total for value in raised]
        mix = logistic(
            jnp.sum(normed.astype(F32) * mix_ref[...].astype(F32), axis=1, keepdims=True)
        )
        small_ref[...] = padded(
            jnp.concatenate(
                [lanes_ref[...].astype(F32), router_lanes.astype(F32), *gates, mix], axis=1
            )
        )
        main, rest = rows_to_slots(main_hot, rest_hot, normed)
        main_ref[...] = main
        rest_ref[...] = rest
        adapter = jnp.where(side > 0.5, numbers_ref[1], numbers_ref[0])
        lane = lane_index((tokens, 128))
        adapter_hot = (lane == adapter).astype(F32)
        main_notes, rest_notes = None, None
        for k in range(TOP):
            high, low = two_parts(gates[k])
            notes = jnp.where(
                lane == ADAPTER_COUNT,
                high.astype(F32),
                jnp.where(lane == ADAPTER_COUNT + 1, low.astype(F32), adapter_hot),
            ).astype(BF)
            main_part = dot_tn(main_hot[k].astype(BF), notes)
            rest_part = dot_tn(rest_hot[k].astype(BF), notes)
            main_notes = main_part if k == 0 else main_notes + main_part
            rest_notes = rest_part if k == 0 else rest_notes + rest_part
        main_notes_ref[...] = main_notes.astype(BF)
        rest_notes_ref[...] = rest_notes.astype(BF)


def after_attention(
    numbers, mixed, weight, rows, first, second, gain, ffn_first, router, router_second, mix, routes, side
):
    tokens, width = mixed.shape
    experts = router.shape[1]
    step = 512
    kept = lambda *shape: pl.BlockSpec(shape, lambda n, a: (0,) * len(shape))
    outs = [
        ((tokens, width), F32),
        ((tokens, width), BF),
        ((tokens, 128), F32),
        ((experts * MAIN, width), BF),
        ((experts * 16, width // 4), BF),
        ((experts * MAIN, 128), BF),
        ((experts * 16, 128), BF),
    ]
    return stage(
        after_attention_kernel,
        "after_attention",
        [shape_of(*out) for out in outs],
        [
            whole(mixed),
            pl.BlockSpec((width, step), lambda n, a: (0, n)),
            pl.BlockSpec((1, tokens, step), lambda n, a: (0, 0, n)),
            pl.BlockSpec((1, 1, RANK, width), lambda n, a: (3, a[0], 0, 0)),
            pl.BlockSpec((1, 1, RANK, width), lambda n, a: (3, a[1], 0, 0)),
            pl.BlockSpec((1, 1, RANK, step), lambda n, a: (3, a[0], 0, n)),
            pl.BlockSpec((1, 1, RANK, step), lambda n, a: (3, a[1], 0, n)),
            whole(gain),
            pl.BlockSpec((1, 1, RANK, width), lambda n, a: (0, a[0], 0, 0)),
            pl.BlockSpec((1, 1, RANK, width), lambda n, a: (0, a[1], 0, 0)),
            whole(router),
            pl.BlockSpec((1, RANK, experts), lambda n, a: (a[0], 0, 0)),
            pl.BlockSpec((1, RANK, experts), lambda n, a: (a[1], 0, 0)),
            whole(mix),
            whole(routes),
            whole(side),
        ],
        [kept(*shape) for shape, kind in outs],
        grid=(width // step,),
        scratch=[pltpu.VMEM((tokens, PAIR), BF)],
        prefetch=1,
    )(
        numbers, mixed, weight, rows, first, first, second, second, gain, ffn_first, ffn_first, router,
        router_second, router_second, mix, routes, side,
    )


def in_owner_columns(total, target, columns):
    count = total.shape[0]
    for owner in range(total.shape[1] // columns):
        part = total[:, owner * columns : (owner + 1) * columns].astype(BF)
        target[:count, owner * 128 : (owner + 1) * 128] = padded(part)


def x_step(step):
    return step + step // 2 * (1 - 2 * (step % 2))


def shared_kernel(plan, *refs):
    amount = len(plan)
    inputs, refs = refs[:amount], refs[amount:]
    normed_ref, grads_hbm, weights_hbm, side_ref, picked_ref, second_ref, mix_ref = refs[:7]
    outputs, refs = refs[7 : 7 + amount], refs[7 + amount :]
    parts_refs, values_ref, adapter_ref, refs = refs[:2], refs[2], refs[3], refs[4:]
    own, move_sems, refs = refs[:amount], refs[amount : amount + 4], refs[amount + 4 :]
    rows_buf, grads_buf, gate_buf, up_buf, down_buf = refs[:5]
    parts_buf, values_buf, total, refs = refs[5:7], refs[7], refs[8], refs[9:]
    rows_send, rows_recv, parts_send, parts_recv, load_sem, parts_sem = refs

    units, width = gate_buf.shape[1:]
    along, tokens = rows_buf.shape[:2]
    me = place_in("x")
    loads = [
        pltpu.make_async_copy(normed_ref, rows_buf.at[me], load_sem.at[0]),
        pltpu.make_async_copy(grads_hbm, grads_buf, load_sem.at[1]),
    ]
    loads += [
        pltpu.make_async_copy(weights_hbm.at[:, pl.ds(i * units, units)], target, load_sem.at[2 + i])
        for i, target in enumerate((gate_buf, up_buf, down_buf))
    ]
    for load in loads:
        load.start()
    mover = Mover(plan, inputs, outputs, own, *move_sems)
    mover.take()
    greet(plan + (("gather", "x"),))

    def rows_copy(offset):
        return remote(
            normed_ref,
            rows_buf.at[me],
            rows_send.at[offset],
            rows_recv.at[offset],
            device_of("x", lax.rem(me + offset, along)),
        )

    def parts_copy(kind, offset):
        peer = lax.rem(me + along - offset, along)
        return remote(
            parts_buf[kind].at[peer],
            parts_refs[kind].at[me],
            parts_send.at[kind, offset],
            parts_recv.at[kind, offset],
            device_of("x", peer),
        )

    def own_parts(kind):
        return pltpu.make_async_copy(
            parts_buf[kind].at[me], parts_refs[kind].at[me], parts_sem.at[kind]
        )

    for offset in (1, 3, 2):
        rows_copy(offset).start()
    mover.start()
    for load in loads:
        load.wait()
    total[...] = jnp.zeros_like(total)

    def block(step, carry):
        offset = x_step(step)
        source = lax.rem(me + along - offset, along)

        @pl.when(step > 0)
        def arrived():
            rows_copy(offset).wait_recv()

        rows, grads = rows_buf[source], grads_buf[source]
        grads_f = grads.astype(F32)
        pick = pair_pick(side_ref[source], 1)
        second_gate, second_up = second_ref[:PAIR], second_ref[PAIR : 2 * PAIR]
        down_first = second_ref[2 * PAIR :]
        weight_gate = gate_buf[...].reshape(-1, width)
        weight_up = up_buf[...].reshape(-1, width)
        weight_down = down_buf[...].reshape(-1, width)
        lanes_gate = (dot_nt(rows, picked_ref[:PAIR]) * pick).astype(BF)
        lanes_up = (dot_nt(rows, picked_ref[PAIR : 2 * PAIR]) * pick).astype(BF)
        mix = logistic(jnp.sum(rows.astype(F32) * mix_ref[...].astype(F32), axis=1, keepdims=True))
        grad_shared = (mix * grads_f).astype(BF)
        grad_side = (dot_nt(grad_shared, picked_ref[2 * PAIR :]) * pick).astype(BF)
        gate = dot_nt(rows, weight_gate) + dot(lanes_gate, second_gate)
        upper = dot_nt(rows, weight_up) + dot(lanes_up, second_up)
        hidden = (gate * logistic(gate) * upper).astype(BF)
        grad_hidden = dot_nt(grad_shared, weight_down) + dot(grad_side, down_first)
        grad_gate, grad_upper = swiglu_backward(gate, upper, grad_hidden)
        grad_rows = dot(grad_gate, weight_gate) + dot(grad_upper, weight_up)
        parts_buf[0][source] = grad_rows.astype(BF)
        value = dot(hidden, weight_down)
        values_buf[source] = value.astype(BF)
        mix_sum = jnp.sum(grads_f * value, axis=1, keepdims=True)
        side = (dot_nt(hidden, down_first) * pick).astype(BF)
        grad_lanes_gate = (dot_nt(grad_gate, second_gate) * pick).astype(BF)
        grad_lanes_up = (dot_nt(grad_upper, second_up) * pick).astype(BF)
        parts_buf[1][source] = padded(
            jnp.concatenate([side, grad_lanes_gate, grad_lanes_up, *two_parts(mix_sum)], axis=1)
        )
        total[:PAIR] += dot_tn(lanes_gate, grad_gate)
        total[PAIR : 2 * PAIR] += dot_tn(lanes_up, grad_upper)
        total[2 * PAIR :] += dot_tn(grad_side, hidden)

        @pl.when(step == 0)
        def keep():
            for kind in range(2):
                own_parts(kind).start()

        @pl.when(step > 0)
        def send():
            for kind in range(2):
                parts_copy(kind, offset).start()

        return carry

    lax.fori_loop(0, along, block, 0)
    values_out = pltpu.make_async_copy(values_buf, values_ref, parts_sem.at[2])
    values_out.start()
    in_owner_columns(total, adapter_ref, units)
    mover.finish()
    for kind in range(2):
        own_parts(kind).wait()
    for offset in range(1, along):
        rows_copy(offset).wait_send()
        for kind in range(2):
            parts_copy(kind, offset).wait()
    values_out.wait()


def shared_expert(number, normed, items, grads, weights, side, picked, second, mix):
    tokens, width = normed.shape
    plan = tuple((kind, group) for kind, group, array in items)
    arrays = [array for kind, group, array in items]
    along = GROUP_SIZE["x"]
    shards_of, units = weights.shape[0], weights.shape[1] // 3
    hidden = shards_of * units
    vmem = pl.BlockSpec(memory_space=pltpu.VMEM)
    parts = [(along, tokens, width), (along, tokens, 128), (along, tokens, width)]
    return pl.pallas_call(
        functools.partial(shared_kernel, plan),
        out_shape=[shape_of(array.shape, BF) for array in arrays]
        + [shape_of(part, BF) for part in parts]
        + [shape_of((3 * PAIR, shards_of * 128), BF)],
        in_specs=[HBM] * (len(items) + 3) + [vmem] * 4,
        out_specs=[HBM] * (len(items) + 3) + [vmem],
        scratch_shapes=mover_scratch(items)
        + [pltpu.VMEM((along, tokens, width), BF)] * 2
        + [pltpu.VMEM((shards_of, units, width), BF)] * 3
        + [pltpu.VMEM(part, BF) for part in parts]
        + [pltpu.VMEM((3 * PAIR, hidden), F32)]
        + [
            pltpu.SemaphoreType.DMA((along,)),
            pltpu.SemaphoreType.DMA((along,)),
            pltpu.SemaphoreType.DMA((2, along)),
            pltpu.SemaphoreType.DMA((2, along)),
            pltpu.SemaphoreType.DMA((5,)),
            pltpu.SemaphoreType.DMA((3,)),
        ],
        compiler_params=pltpu.CompilerParams(
            collective_id=number, has_side_effects=True, vmem_limit_bytes=VMEM_LIMIT
        ),
        name="shared_expert",
    )(*arrays, normed, grads, weights, side, picked, second, mix)


BACK = 6
ROUTED_STEPS = 4


def routed_kernel(*refs):
    held_hbm, gate_up_hbm, down_hbm, values_hbm = refs[:6], refs[6], refs[7], refs[8]
    later_hbm, refs = refs[9:11], refs[2:]
    first_ref, second_ref, down_first_ref, down_second_ref = refs[9:13]
    back_refs, values_ref, refs = refs[13 : 13 + BACK], refs[13 + BACK], refs[14 + BACK :]
    adapter_ref = refs[0]
    own, move_sems, refs = refs[1:2], refs[2:6], refs[6:]
    held, back_buf, refs = refs[:6], refs[6 : 6 + BACK], refs[6 + BACK :]
    gate_up_buf, down_buf, total, total_down = refs[:4]
    send_sem, recv_sem, load_sem, own_sem, half_sem, later_send, later_recv = refs[4:]

    me = place_in("f")
    experts = GROUP_SIZE["f"]
    loads = [
        pltpu.make_async_copy(held_hbm[i], held[i], load_sem.at[i]) for i in (0, 1, 4, 5)
    ]
    for offset in range(experts):
        if offset == 0 or soon(offset):
            source = lax.rem(me + experts - offset, experts)
            loads += [
                pltpu.make_async_copy(
                    block_of(held_hbm[2 + i], "rows", experts, source),
                    block_of(held[2 + i], "rows", experts, source),
                    half_sem.at[i, offset],
                )
                for i in range(2)
            ]
    loads += [
        pltpu.make_async_copy(gate_up_hbm.at[0, 0], gate_up_buf.at[0], load_sem.at[6]),
        pltpu.make_async_copy(gate_up_hbm.at[0, 1], gate_up_buf.at[1], load_sem.at[7]),
        pltpu.make_async_copy(down_hbm.at[0], down_buf, load_sem.at[8]),
    ]
    for load in loads:
        load.start()
    mover = Mover((("swap", "x"),), (values_hbm,), (values_ref,), own, *move_sems)
    mover.take()
    greet((("rows", "f"), ("swap", "x")))

    def later_copy(kind, offset):
        peer = lax.rem(me + offset, experts)
        return remote(
            block_of(later_hbm[kind], "rows", experts, peer),
            block_of(held[2 + kind], "rows", experts, me),
            later_send.at[kind, offset],
            later_recv.at[kind, offset],
            device_of("f", peer),
        )

    later = [offset for offset in range(1, experts) if not soon(offset)]
    for offset in sorted(later, key=lambda offset: -(offset % 4)):
        for kind in range(2):
            later_copy(kind, offset).start()
    mover.start()
    total[...] = jnp.zeros_like(total)
    total_down[...] = jnp.zeros_like(total_down)

    def back_copy(kind, peer, landing):
        return remote(
            block_of(back_buf[kind], "rows", experts, peer),
            block_of(back_refs[kind], "rows", experts, me),
            send_sem.at[kind, peer],
            recv_sem.at[kind, landing],
            device_of("f", peer),
        )

    def own_copy(kind):
        return pltpu.make_async_copy(
            block_of(back_buf[kind], "rows", experts, me),
            block_of(back_refs[kind], "rows", experts, me),
            own_sem.at[kind],
        )

    steps = ROUTED_STEPS
    selectors = rest_selectors(experts // steps)
    spread = (row_index((128, LANES)) == lane_index((128, LANES)) // RANK).astype(BF)
    fold = (row_index((LANES, 128)) % RANK == lane_index((LANES, 128))).astype(BF)
    fold_later = (row_index((LANES, 128)) % RANK == lane_index((LANES, 128)) - RANK).astype(BF)
    for load in loads:
        load.wait()
    count, rest_count = held[0].shape[0] // steps, held[1].shape[0] // steps

    def block(step, carry):
        number = lax.rem(me + 1 + step, steps)

        for turn in (1, 0):

            @pl.when(step == 3 - turn)
            def arrived():
                for offset in later:
                    if offset % 4 == turn:
                        for kind in range(2):
                            later_copy(kind, offset).wait_recv()

        peers = [number + steps * turn for turn in range(experts // steps)]

        def read(ref):
            depth = ref.shape[0] // experts
            blocks = [ref[pl.ds(pl.multiple_of(peer * depth, depth), depth)] for peer in peers]
            return jnp.concatenate(blocks, axis=0)

        def write(ref, value):
            depth = ref.shape[0] // experts
            for turn, peer in enumerate(peers):
                part = value[turn * depth : (turn + 1) * depth]
                ref[pl.ds(pl.multiple_of(peer * depth, depth), depth)] = part

        rows = jnp.concatenate([read(held[0]), rest_to_rows(selectors, read(held[1]))], axis=0)
        grads = jnp.concatenate([read(held[2]), rest_to_rows(selectors, read(held[3]))], axis=0)
        notes = jnp.concatenate(
            [read(held[4]), dot(selectors[0], read(held[5])).astype(BF)], axis=0
        )
        pick = dot(notes, spread)
        gate_of = (
            notes[:, ADAPTER_COUNT : ADAPTER_COUNT + 1].astype(F32)
            + notes[:, ADAPTER_COUNT + 1 : ADAPTER_COUNT + 2].astype(F32)
        )
        grads_f = grads.astype(F32)
        lanes_gate = (dot_nt(rows, first_ref[0]) * pick).astype(BF)
        lanes_up = (dot_nt(rows, first_ref[1]) * pick).astype(BF)
        grad_routed = (gate_of * grads_f).astype(BF)
        grad_side = (dot_nt(grads, down_second_ref[1]) * gate_of * pick).astype(BF)
        gate = dot(rows, gate_up_buf[0]) + dot(lanes_gate, second_ref[0])
        upper = dot(rows, gate_up_buf[1]) + dot(lanes_up, second_ref[1])
        hidden = (gate * logistic(gate) * upper).astype(BF)
        grad_hidden = dot_nt(grad_routed, down_buf[...]) + dot(grad_side, down_first_ref[...])
        grad_gate, grad_upper = swiglu_backward(gate, upper, grad_hidden)
        side = (dot_nt(hidden, down_first_ref[...]).astype(BF).astype(F32) * pick).astype(BF)
        value = dot(hidden, down_buf[...]) + dot(side, down_second_ref[1])
        gate_grad = jnp.sum(grads_f * value, axis=1, keepdims=True)
        result = (gate_of * value).astype(BF)
        write(back_buf[4], result[:count])
        write(back_buf[5], rows_to_rest(selectors, result[count:]))
        back = (dot_nt(grad_gate, gate_up_buf[0]) + dot_nt(grad_upper, gate_up_buf[1])).astype(BF)
        back_gate = (dot_nt(grad_gate, second_ref[0]) * pick).astype(BF)
        back_up = (dot_nt(grad_upper, second_ref[1]) * pick).astype(BF)
        high, low = two_parts(gate_grad)
        lane = lane_index((count + rest_count // 4, 128))
        back_notes = jnp.where(
            lane == PAIR,
            high.astype(F32),
            jnp.where(
                lane == PAIR + 1, low.astype(F32), dot(back_gate, fold) + dot(back_up, fold_later)
            ),
        ).astype(BF)
        write(back_buf[0], back[:count])
        write(back_buf[1], rows_to_rest(selectors, back[count:]))
        write(back_buf[2], back_notes[:count])
        write(back_buf[3], dot_tn(selectors[0], back_notes[count:]).astype(BF))
        for peer in peers:

            @pl.when(peer == me)
            def keep():
                for kind in range(BACK):
                    own_copy(kind).start()

            @pl.when(peer != me)
            def send():
                for kind in range(BACK):
                    back_copy(kind, peer, me).start()

        total[:LANES] += dot_tn(lanes_gate, grad_gate)
        total[LANES : 2 * LANES] += dot_tn(lanes_up, grad_upper)
        total[2 * LANES :] += dot_tn(grad_side, hidden)
        total_down[...] += dot_tn(side, grad_routed)
        return carry

    lax.fori_loop(0, steps, block, 0)
    in_owner_columns(total, adapter_ref, total.shape[1] // experts)
    adapter_ref[3 * LANES :, :] = total_down[...].astype(BF)
    mover.finish()
    for offset in later:
        for kind in range(2):
            later_copy(kind, offset).wait_send()
    for kind in range(BACK):
        own_copy(kind).wait()

    def settle(offset, carry):
        peer = lax.rem(me + offset, experts)
        for kind in range(BACK):
            copy = back_copy(kind, peer, peer)
            copy.wait_send()
            copy.wait_recv()
        return carry

    lax.fori_loop(1, experts, settle, 0)


def routed_expert(number, held, later, values, first, second, down_first, down_second, gate_up, down):
    width, hidden = gate_up.shape[2:]
    experts = GROUP_SIZE["f"]
    vmem = pl.BlockSpec(memory_space=pltpu.VMEM)
    back = [held[0], held[1], held[4], held[5], held[0], held[1]]
    items = [("swap", "x", values)]
    return pl.pallas_call(
        routed_kernel,
        out_shape=[shape_of(array.shape, BF) for array in (*back, values)]
        + [shape_of((4 * LANES, experts * 128), BF)],
        in_specs=[HBM] * 11 + [vmem] * 4,
        out_specs=[HBM] * (BACK + 1) + [vmem],
        scratch_shapes=mover_scratch(items)
        + [pltpu.VMEM(array.shape, BF) for array in held]
        + [pltpu.VMEM(array.shape, BF) for array in back]
        + [
            pltpu.VMEM((2, width, hidden), BF),
            pltpu.VMEM((hidden, width), BF),
            pltpu.VMEM((3 * LANES, hidden), F32),
            pltpu.VMEM((LANES, width), F32),
            pltpu.SemaphoreType.DMA((BACK, experts)),
            pltpu.SemaphoreType.DMA((BACK, experts)),
            pltpu.SemaphoreType.DMA((9,)),
            pltpu.SemaphoreType.DMA((BACK,)),
            pltpu.SemaphoreType.DMA((2, experts)),
            pltpu.SemaphoreType.DMA((2, experts)),
            pltpu.SemaphoreType.DMA((2, experts)),
        ],
        compiler_params=pltpu.CompilerParams(
            collective_id=number, has_side_effects=True, vmem_limit_bytes=VMEM_LIMIT
        ),
        name="routed_expert",
    )(*held, gate_up, down, values, *later, first, second, down_first, down_second)


def after_experts_kernel(
    numbers_ref,
    parts_ref,
    part_notes_ref,
    main_ref,
    rest_ref,
    main_notes_ref,
    rest_notes_ref,
    grads_ref,
    normed_ref,
    residual_ref,
    small_ref,
    mixed_ref,
    routes_ref,
    side_ref,
    ffn_a_ref,
    ffn_b_ref,
    router_ref,
    router_a_ref,
    router_b_ref,
    mix_ref,
    gain_ref,
    down_a_ref,
    down_b_ref,
    first_a_ref,
    first_b_ref,
    second_a_ref,
    second_b_ref,
    weight_hbm,
    grad_residual_ref,
    grad_mixed_ref,
    adapter_ref,
    router_grad_ref,
    shared_side_ref,
    weight_ref,
    sem,
):
    load = pltpu.make_async_copy(weight_hbm, weight_ref, sem)
    load.start()
    experts = router_ref.shape[1]
    side = side_ref[...]
    pick = pair_pick(side, 1)
    grads = grads_ref[0]
    grads_f = grads.astype(F32)
    normed = normed_ref[...]
    out_lanes = small_ref[:, :PAIR].astype(BF)
    router_lanes = small_ref[:, PAIR : 2 * PAIR].astype(BF)
    gates = [small_ref[:, 2 * PAIR + k : 2 * PAIR + k + 1] for k in range(TOP)]
    mix = small_ref[:, 2 * PAIR + TOP : 2 * PAIR + TOP + 1]
    notes = sum(part_notes_ref[i].astype(F32) for i in range(part_notes_ref.shape[0]))
    shared_side = notes[:, :PAIR].astype(BF)
    shared_side_ref[...] = padded(shared_side)
    down_second = pair_of(down_a_ref, down_b_ref, 0)
    mix_total = (
        notes[:, 3 * PAIR : 3 * PAIR + 1]
        + notes[:, 3 * PAIR + 1 : 3 * PAIR + 2]
        + jnp.sum(shared_side.astype(F32) * dot_nt(grads, down_second), axis=1, keepdims=True)
    )
    grad_mix = mix_total * mix * (1.0 - mix)
    grad_shared = (mix * grads_f).astype(BF)
    expert_hot, main_hot, rest_hot = routing(routes_ref[0], experts)
    grad_gates = []
    mask = quarter_mask(rest_hot[0].shape, 0)
    token_notes = None
    for k in range(TOP):
        mine = dot(main_hot[k].astype(BF), main_notes_ref[...]) + dot(
            (rest_hot[k] * mask).astype(BF), rest_notes_ref[...]
        )
        grad_gates.append(mine[:, PAIR : PAIR + 1] + mine[:, PAIR + 1 : PAIR + 2])
        token_notes = mine if k == 0 else token_notes + mine
    inner = sum(gate * grad for gate, grad in zip(gates, grad_gates))
    grad_logits = sum(
        hot * (gate * (grad - inner)) for hot, gate, grad in zip(expert_hot, gates, grad_gates)
    )
    logits_high, logits_low = two_parts(grad_logits)
    router_second = jnp.concatenate([router_a_ref[0], router_b_ref[0]], axis=0)
    grad_router_lanes = dot_nt(logits_high, router_second) + dot_nt(logits_low, router_second)
    router_grad = dot_tn(router_lanes, logits_high) + dot_tn(router_lanes, logits_low)
    of_row = jnp.where(row_index((PAIR, 128)) < RANK, numbers_ref[0], numbers_ref[1]).astype(F32)
    router_grad_ref[...] = jnp.where(
        lane_index((PAIR, 128)) == experts, of_row, padded(router_grad)
    ).astype(BF)
    lane_grads = (
        jnp.concatenate(
            [
                grad_router_lanes,
                notes[:, PAIR : 3 * PAIR],
                token_notes[:, :RANK],
                token_notes[:, :RANK],
                token_notes[:, RANK:PAIR],
                token_notes[:, RANK:PAIR],
            ],
            axis=1,
        )
        * pair_pick(side, 5)
    ).astype(BF)
    factors = ffn_a_ref.shape[0]
    ffn_first = jnp.concatenate([pair_of(ffn_a_ref, ffn_b_ref, i) for i in range(factors)], axis=0)
    grad_second = (
        grad_mix * mix_ref[...].astype(F32)
        + dot_nt(logits_high, router_ref[...])
        + dot_nt(logits_low, router_ref[...])
        + sum(parts_ref[i].astype(F32) for i in range(parts_ref.shape[0]))
        + slots_to_rows(main_hot, rest_hot, main_ref[...], rest_ref[...])
        + dot(lane_grads, ffn_first)
    )
    grad_residual = grads_f + rms_backward(residual_ref[...], gain_ref[...], grad_second)
    grad_residual_ref[...] = grad_residual
    grad_attended = grad_residual.astype(BF)
    first, second = pair_of(first_a_ref, first_b_ref, 0), pair_of(second_a_ref, second_b_ref, 0)
    grad_out_lanes = (dot_nt(grad_attended, second) * pick).astype(BF)
    adapter_ref[...] = jnp.concatenate(
        [
            dot_tn(lane_grads, normed),
            dot_tn(grad_out_lanes, mixed_ref[...]),
            dot_tn(out_lanes, grad_attended),
            dot_tn(shared_side, grad_shared),
        ],
        axis=0,
    ).astype(BF)
    load.wait()
    grad_mixed_ref[...] = (
        dot_nt(grad_attended, weight_ref[...]) + dot(grad_out_lanes, first)
    ).astype(BF)


def after_experts(
    numbers, parts, part_notes, main, rest, main_notes, rest_notes, grads, normed, residual, small, mixed,
    routes, side, ffn_first, router, router_second, mix, gain, down_second, first, second, weight,
):
    tokens, width = normed.shape
    experts = router.shape[1]
    factors = ffn_first.shape[0]
    last = lambda which: pl.BlockSpec((1, 1, RANK, width), lambda n, a: (3, a[which], 0, 0))
    outs = [
        ((tokens, width), F32),
        ((tokens, width), BF),
        (((factors + 3) * PAIR, width), BF),
        ((PAIR, 128), BF),
        ((tokens, 128), BF),
    ]
    plain = (
        parts, part_notes, main, rest, main_notes, rest_notes, grads, normed, residual, small, mixed, routes,
        side,
    )
    return stage(
        after_experts_kernel,
        "after_experts",
        [shape_of(*out) for out in outs],
        [whole(array) for array in plain]
        + [
            of_sequence(0, (factors, 1, RANK, width)),
            of_sequence(1, (factors, 1, RANK, width)),
            whole(router),
            pl.BlockSpec((1, RANK, experts), lambda n, a: (a[0], 0, 0)),
            pl.BlockSpec((1, RANK, experts), lambda n, a: (a[1], 0, 0)),
            whole(mix),
            whole(gain),
            of_sequence(0, (1, 1, RANK, width)),
            of_sequence(1, (1, 1, RANK, width)),
            last(0),
            last(1),
            last(0),
            last(1),
            HBM,
        ],
        [pl.BlockSpec(shape, lambda n, a: (0, 0)) for shape, kind in outs],
        scratch=[pltpu.VMEM(weight.shape, BF), pltpu.SemaphoreType.DMA],
        prefetch=1,
    )(
        numbers, *plain, ffn_first, ffn_first, router, router_second, router_second, mix, gain, down_second,
        down_second, first, first, second, second, weight,
    )


def attention_back_kernel(plan, heads_plan, *refs):
    amount = len(plan)
    inputs, expert_hbm, refs = refs[:amount], refs[amount], refs[amount + 1 :]
    mixed_hbm, query_hbm, pairs_hbm, weight_hbm = refs[:4]
    place_ref, start_ref, key_place_ref, cos_ref, sin_ref, side_ref, lanes_ref, second_ref = refs[4:12]
    results, refs = refs[12:20], refs[20:]
    outputs, refs = refs[:amount], refs[amount:]
    heads_got, parts_ref, notes_ref, expert_ref, out_ref, refs = *refs[:5], refs[5:]
    own, move_sems, refs = refs[:amount], refs[amount : amount + 4], refs[amount + 4 :]
    heads_own, heads_sems, refs = refs[:1], refs[1:5], refs[5:]
    expert_own, expert_sems, refs = refs[:1], refs[1:5], refs[5:]
    mixed_buf, query_buf, pairs_buf, weight_buf = refs[:4]
    sent_buf, got_buf, grads_buf, heads_buf, parts_buf, notes_buf = refs[4:10]
    mixed_send, mixed_recv, pair_send, pair_recv, parts_send, parts_recv, load_sem, own_sem = refs[10:]

    x, y = place_in("x"), place_in("y")
    along, tokens, columns = mixed_buf.shape
    rows_all = along * tokens
    heads = columns // HEAD_DIM
    loads = [
        pltpu.make_async_copy(block_of(mixed_hbm, "columns", along, x), mixed_buf.at[x], load_sem.at[0]),
        pltpu.make_async_copy(query_hbm.at[0], query_buf, load_sem.at[1]),
        pltpu.make_async_copy(pairs_hbm, pairs_buf, load_sem.at[2]),
    ]
    loads += [
        pltpu.make_async_copy(weight_hbm.at[:, j], weight_buf.at[j], load_sem.at[3 + j])
        for j in range(3)
    ]
    for load in loads:
        load.start()
    mover = Mover(plan, inputs, outputs, own, *move_sems)
    mover.take()
    expert_mover = Mover((("rows", "x"),), (expert_hbm,), (expert_ref,), expert_own, *expert_sems)
    expert_mover.take()
    greet((("rows", "f"), ("swap", "x"), ("swap", "y")))

    def mixed_copy(offset):
        peer = lax.rem(x + offset, along)
        return remote(
            block_of(mixed_hbm, "columns", along, peer),
            mixed_buf.at[x],
            mixed_send.at[offset],
            mixed_recv.at[offset],
            device_of("x", peer),
        )

    def pair_copy(head):
        return remote(
            sent_buf.at[1 - y, head],
            got_buf.at[head],
            pair_send.at[head],
            pair_recv.at[head],
            device_of("y", 1 - y),
        )

    def parts_copy(offset):
        peer = lax.rem(x + offset, along)
        return remote(
            parts_buf.at[peer],
            parts_ref.at[x],
            parts_send.at[0, offset],
            parts_recv.at[0, offset],
            device_of("x", peer),
        )

    def notes_copy(offset):
        peer = lax.rem(x + offset, along)
        return remote(
            notes_buf.at[peer],
            notes_ref.at[x],
            parts_send.at[1, offset],
            parts_recv.at[1, offset],
            device_of("x", peer),
        )

    for offset in (2, 1, 3):
        mixed_copy(offset).start()
    expert_mover.start()
    for load in loads[:3]:
        load.wait()
    for offset in (1, 3, 2):
        mixed_copy(offset).wait_recv()

    step = rows_all // 2

    def head_block(head, carry):
        here = pl.ds(pl.multiple_of(head * HEAD_DIM, HEAD_DIM), HEAD_DIM)
        keys = pairs_buf[:, 0, :, here].reshape(-1, HEAD_DIM)
        values = pairs_buf[:, 1, :, here].reshape(-1, HEAD_DIM)
        key_total, value_total = None, None
        for i in range(2):
            at = slice(i * step, (i + 1) * step)
            query = query_buf[at, here]
            blocks = along // 2
            grad = mixed_buf[i * blocks : (i + 1) * blocks, :, here].reshape(step, HEAD_DIM)
            probs = probabilities(query, keys, place_ref[at], start_ref[at], key_place_ref[...])
            grad_probs = dot_nt(grad, values)
            mean = jnp.sum(probs * grad_probs, axis=1, keepdims=True)
            grad_scores = (probs * (grad_probs - mean)).astype(BF)
            grad_query = dot(grad_scores, keys) * (HEAD_DIM**-0.5)
            grads_buf[0, at, here] = (
                grad_query * cos_ref[at] - half_turn(grad_query) * sin_ref[at]
            ).astype(BF)
            grad_keys = dot_tn(grad_scores, query) * (HEAD_DIM**-0.5)
            grad_values = dot_tn(probs.astype(BF), grad)
            key_total = grad_keys if i == 0 else key_total + grad_keys
            value_total = grad_values if i == 0 else value_total + grad_values
        for half in range(2):
            at = slice(half * rows_all, (half + 1) * rows_all)
            sent_buf[half, head, 0] = key_total[at].astype(BF)
            sent_buf[half, head, 1] = value_total[at].astype(BF)
        pair_copy(head).start()
        return carry

    lax.fori_loop(0, heads, head_block, 0)
    combine_kernel(*results, out_ref)

    def head_sum(head, carry):
        here = pl.ds(pl.multiple_of(head * HEAD_DIM, HEAD_DIM), HEAD_DIM)
        pair_copy(head).wait_recv()
        key = sent_buf[y, head, 0].astype(F32) + got_buf[head, 0].astype(F32)
        grads_buf[1, :, here] = (key * cos_ref[...] - half_turn(key) * sin_ref[...]).astype(BF)
        value = sent_buf[y, head, 1].astype(F32) + got_buf[head, 1].astype(F32)
        grads_buf[2, :, here] = value.astype(BF)
        return carry

    lax.fori_loop(0, heads, head_sum, 0)
    pick = pair_pick(side_ref[...], 1)
    notes = []
    heads_buf[...] = jnp.zeros_like(heads_buf)
    own_columns = pl.ds(pl.multiple_of(x * columns, columns), columns)
    for j in range(3):
        at = slice(j * PAIR, (j + 1) * PAIR)
        notes.append((dot_nt(grads_buf[j], second_ref[at]) * pick).astype(BF))
        heads_buf[at, own_columns] = dot_tn(lanes_ref[j], grads_buf[j]).astype(BF)
    notes_buf[...] = padded(jnp.concatenate(notes, axis=1)).reshape(notes_buf.shape)
    heads_mover = Mover(heads_plan, (heads_buf,), (heads_got,), heads_own, *heads_sems)
    heads_mover.take()
    heads_mover.start()
    for offset in (1, 3, 2):
        notes_copy(offset).start()
    mover.start()
    own_notes = pltpu.make_async_copy(notes_buf.at[x], notes_ref.at[x], own_sem.at[0])
    own_notes.start()
    for load in loads[3:]:
        load.wait()

    def own_parts():
        return pltpu.make_async_copy(parts_buf.at[x], parts_ref.at[x], own_sem.at[1])

    def row_block(number, carry):
        offset = x_step(lax.rem(number + 1, along))
        peer = lax.rem(x + offset, along)
        at = pl.ds(pl.multiple_of(peer * tokens, tokens), tokens)
        total = None
        for j in range(3):
            part = dot_nt(grads_buf[j, at], weight_buf[j].reshape(-1, columns))
            total = part if total is None else total + part
        parts_buf[peer] = total.astype(BF)

        @pl.when(number < along - 1)
        def send():
            parts_copy(offset).start()

        @pl.when(number == along - 1)
        def keep():
            own_parts().start()

        return carry

    lax.fori_loop(0, along, row_block, 0)
    mover.finish()
    heads_mover.finish()
    expert_mover.finish()
    own_notes.wait()
    own_parts().wait()

    def pairs_sent(head, carry):
        pair_copy(head).wait_send()
        return carry

    lax.fori_loop(0, heads, pairs_sent, 0)
    for offset in range(1, along):
        mixed_copy(offset).wait_send()
        parts_copy(offset).wait()
        notes_copy(offset).wait()


def attention_back(number, items, expert, mixed, query, pairs, weight, small, results):
    plan = tuple((kind, group) for kind, group, array in items)
    arrays = [array for kind, group, array in items]
    along = GROUP_SIZE["x"]
    tokens, width = mixed.shape
    columns = width // along
    heads = columns // HEAD_DIM
    rows_all = along * tokens
    heads_items = [("from_columns", "f", shape_of((3 * PAIR, width), BF))]
    vmem = pl.BlockSpec(memory_space=pltpu.VMEM)
    outs = [shape_of(exchanged_shape(kind, group, array.shape), BF) for kind, group, array in items]
    outs += [
        shape_of(exchanged_shape("from_columns", "f", (3 * PAIR, width)), BF),
        shape_of((along, tokens, width), BF),
        shape_of((along, tokens, 128), BF),
        shape_of(expert.shape, BF),
        shape_of((1, tokens, width), BF),
    ]
    dma = pltpu.SemaphoreType.DMA
    return pl.pallas_call(
        functools.partial(attention_back_kernel, plan, (("from_columns", "f"),)),
        out_shape=outs,
        in_specs=[HBM] * (len(items) + 5) + [vmem] * (len(small) + len(results)),
        out_specs=[HBM] * (len(items) + 4) + [vmem],
        scratch_shapes=mover_scratch(items)
        + mover_scratch(heads_items)
        + mover_scratch([("rows", "x", expert)])
        + [
            pltpu.VMEM((along, tokens, columns), BF),
            pltpu.VMEM((rows_all, columns), BF),
            pltpu.VMEM(pairs.shape, BF),
            pltpu.VMEM((3, *weight.shape[:1], *weight.shape[2:]), BF),
            pltpu.VMEM((2, heads, 2, rows_all, HEAD_DIM), BF),
            pltpu.VMEM((heads, 2, rows_all, HEAD_DIM), BF),
            pltpu.VMEM((3, rows_all, columns), BF),
            pltpu.VMEM((3 * PAIR, width), BF),
            pltpu.VMEM((along, tokens, width), BF),
            pltpu.VMEM((along, tokens, 128), BF),
            dma((along,)),
            dma((along,)),
            dma((heads,)),
            dma((heads,)),
            dma((2, along)),
            dma((2, along)),
            dma((6,)),
            dma((2,)),
        ],
        compiler_params=pltpu.CompilerParams(
            collective_id=number, has_side_effects=True, vmem_limit_bytes=VMEM_LIMIT
        ),
        name="attention_back",
    )(*arrays, expert, mixed, query, pairs, weight, *small, *results)


def lane_expansion(ids_ref, group):
    ids = ids_ref[group][:, GROUP_SIZE["f"] : GROUP_SIZE["f"] + 1].astype(F32)
    lane = lane_index((PAIR, LANES))
    same = (lane // RANK).astype(F32) == ids
    return (same & (lane % RANK == row_index((PAIR, LANES)) % RANK)).astype(BF)


def expanded(expansions, got_ref, factor):
    total = None
    for group, expansion in enumerate(expansions):
        part = dot_tn(expansion, got_ref[group, factor * PAIR : (factor + 1) * PAIR, :])
        total = part if total is None else total + part
    return total.astype(BF)


FINISH = (
    (("from_columns", "f"),),
    (("from_columns", "f"),),
    (("rows", "c"), ("rows", "y")),
    (("gather", "c"), ("gather", "c"), ("gather", "c")),
    (("gather", "c"),),
)


def finish_kernel(*refs):
    parts_ref, notes_ref, rows_ref, normed_ref, residual_ref, gain_ref, first_ref = refs[:7]
    ids_ref, early_ref, shared_ref, heads_ref, column_ref, expert_ref = refs[7:13]
    grad_out, attn_in, attn_out, ffn_out, router_out, shared_out, shared_in_out = refs[13:20]
    expert_out, expert_in_out, down_out, expert_buf, refs = *refs[20:24], refs[24:]
    late_buf, late_got, early_buf, early_parts, shared_buf, shared_parts = refs[:6]
    expert_got, late_sum, early_row, shared_row, expert_sum = refs[6:11]
    late_all, early_all, shared_all, expert_all, refs = *refs[11:15], refs[15:]
    ends = (
        ((expert_buf,), (expert_got,)),
        ((late_buf,), (late_got,)),
        ((early_buf, shared_buf), (early_parts, shared_parts)),
        ((early_row, shared_row, expert_sum), (early_all, shared_all, expert_all)),
        ((late_sum,), (late_all,)),
    )
    movers = []
    for plan, (inputs, outputs) in zip(FINISH, ends):
        own, sems, refs = refs[: len(plan)], refs[len(plan) : len(plan) + 4], refs[len(plan) + 4 :]
        movers.append(Mover(plan, inputs, outputs, own, *sems))

    def begin(mover):
        mover.take()
        mover.start()

    greet((("rows", "f"), ("rows", "c"), ("rows", "y")))
    lanes = sum(notes_ref[i].astype(F32) for i in range(notes_ref.shape[0]))[:, : 3 * PAIR]
    lanes = lanes.astype(BF)
    late_buf[...] = dot_tn(lanes, normed_ref[...]).astype(BF)
    begin(movers[1])
    count = expert_buf.shape[0]
    expert_buf[...] = sum(
        expert_ref[i * count : (i + 1) * count].astype(F32) for i in range(GROUP_SIZE["x"])
    ).astype(BF)
    begin(movers[0])

    groups = ids_ref.shape[0]
    expansions = [lane_expansion(ids_ref, group) for group in range(groups)]
    row = 0
    for got in (early_ref, heads_ref):
        for factor in range(got.shape[1] // PAIR):
            early_buf[row : row + LANES, :] = expanded(expansions, got, factor)
            row += LANES
    router = None
    for group in range(groups):
        part = dot_tn(expansions[group], ids_ref[group])
        router = part if router is None else router + part
    router = jnp.sum(router * column_ref[...].astype(F32), axis=1, keepdims=True)
    early_buf[row : row + LANES, :] = jnp.broadcast_to(router, (LANES, 128)).astype(BF)
    for factor in range(shared_ref.shape[1] // PAIR):
        shared_buf[factor * LANES : (factor + 1) * LANES, :] = expanded(
            expansions, shared_ref, factor
        )
    begin(movers[2])

    grad = sum(parts_ref[i].astype(F32) for i in range(parts_ref.shape[0]))
    grad = grad + dot(lanes, first_ref[...])
    total = residual_ref[...] + rms_backward(rows_ref[0].astype(F32), gain_ref[...], grad)
    grad_out[0] = total.astype(BF)

    movers[0].finish()
    expert_sum[...] = sum(expert_got[i].astype(F32) for i in range(groups)).astype(BF)
    movers[2].finish()
    count = early_row.shape[0]
    early_row[...] = sum(
        early_parts[i * count : (i + 1) * count].astype(F32) for i in range(GROUP_SIZE["c"])
    ).astype(BF)
    count = shared_row.shape[0]
    shared_row[...] = (
        shared_parts[:count].astype(F32) + shared_parts[count:].astype(F32)
    ).astype(BF)
    begin(movers[3])
    movers[1].finish()
    for factor in range(late_got.shape[1] // PAIR):
        late_sum[factor * LANES : (factor + 1) * LANES, :] = expanded(expansions, late_got, factor)
    begin(movers[4])

    movers[3].finish()
    early = early_all[...].reshape(-1, 128).astype(F32)
    expert = jnp.concatenate(
        [
            expert_all[2 * i].astype(F32) + expert_all[2 * i + 1].astype(F32)
            for i in range(GROUP_SIZE["x"])
        ],
        axis=0,
    )
    factor = [early[i * LANES : (i + 1) * LANES] for i in range(early.shape[0] // LANES)]
    attn_in[3 * LANES :, :] = factor[5]
    attn_out[: 3 * LANES, :] = jnp.concatenate(factor[8:11], axis=0)
    attn_out[3 * LANES :, :] = factor[6]
    ffn_out[...] = jnp.concatenate(factor[:5], axis=0)
    router_out[...] = factor[11][:, : router_out.shape[1]]
    down_out[:LANES, :] = factor[7]
    down_out[LANES:, :] = expert[3 * LANES :]
    expert_out[...] = expert[: 2 * LANES, : expert_out.shape[1]]
    expert_in_out[...] = expert[2 * LANES : 3 * LANES, : expert_in_out.shape[1]]
    along = GROUP_SIZE["x"]
    columns = shared_out.shape[1] // along
    quarters = [
        shared_all[2 * i : 2 * i + 2].reshape(-1, 128)[:, :columns].astype(F32) for i in range(along)
    ]
    shared_rows = jnp.concatenate(quarters, axis=1)
    shared_out[...] = shared_rows[: 2 * LANES]
    shared_in_out[...] = shared_rows[2 * LANES :]
    movers[4].finish()
    attn_in[: 3 * LANES, :] = sum(late_all[i].astype(F32) for i in range(GROUP_SIZE["c"]))


def finish(
    number, parts, notes, rows, normed, residual, gain, first, ids, early, shared, heads, column, expert,
    shared_columns, expert_columns,
):
    tokens, width = normed.shape
    groups, ctx = GROUP_SIZE["f"], GROUP_SIZE["c"]
    early_rows = ((early.shape[1] + heads.shape[1]) // PAIR + 1) * LANES
    late_rows = first.shape[0] // PAIR * LANES
    shared_rows = shared.shape[1] // PAIR * LANES
    expert_rows = expert.shape[0] // GROUP_SIZE["x"]
    vmem = pl.BlockSpec(memory_space=pltpu.VMEM)
    bufs = [
        first.shape,
        (groups, first.shape[0], 128),
        (early_rows, 128),
        (early_rows, 128),
        (shared_rows, 128),
        (shared_rows, 128),
        (groups, expert_rows, 128),
        (late_rows, 128),
        (early_rows // ctx, 128),
        (shared_rows // 2, 128),
        (expert_rows, 128),
        (ctx, late_rows, 128),
        (ctx, early_rows // ctx, 128),
        (ctx, shared_rows // 2, 128),
        (ctx, expert_rows, 128),
    ]
    sent = (((expert_rows, width),), (bufs[0],), (bufs[2], bufs[4]), (bufs[8], bufs[9], bufs[10]), (bufs[7],))
    scratch = [pltpu.VMEM(buf, BF) for buf in ((expert_rows, width), *bufs)]
    for plan, shapes in zip(FINISH, sent):
        scratch += mover_scratch(
            [(kind, group, shape_of(shape, BF)) for (kind, group), shape in zip(plan, shapes)]
        )
    outs = [
        shape_of(rows.shape, BF),
        shape_of((4 * LANES, 128), F32),
        shape_of((4 * LANES, 128), F32),
        shape_of((5 * LANES, 128), F32),
        shape_of((LANES, 1), F32),
        shape_of((2 * LANES, shared_columns), F32),
        shape_of((LANES, shared_columns), F32),
        shape_of((2 * LANES, expert_columns), F32),
        shape_of((LANES, expert_columns), F32),
        shape_of((2 * LANES, 128), F32),
    ]
    return pl.pallas_call(
        finish_kernel,
        out_shape=outs,
        in_specs=[vmem] * 13,
        out_specs=[vmem] * len(outs),
        scratch_shapes=scratch,
        compiler_params=pltpu.CompilerParams(
            collective_id=number, has_side_effects=True, vmem_limit_bytes=VMEM_LIMIT
        ),
        name="finish",
    )(parts, notes, rows, normed, residual, gain, first, ids, early, shared, heads, column, expert)


def combine_kernel(
    main_ref, rest_ref, routes_ref, residual_ref, parts_ref, side_ref, small_ref, picked_ref, out_ref
):
    experts = main_ref.shape[0] // MAIN
    unused, main_hot, rest_hot = routing(routes_ref[0], experts)
    mixture = slots_to_rows(main_hot, rest_hot, main_ref[...], rest_ref[...])
    shared = sum(parts_ref[i].astype(F32) for i in range(parts_ref.shape[0]))
    shared = shared + dot(side_ref[:, :PAIR], picked_ref[2 * PAIR :])
    mix = small_ref[:, 2 * PAIR + TOP : 2 * PAIR + TOP + 1]
    out_ref[0] = (residual_ref[...] + mixture + mix * shared).astype(BF)


def shards(
    layer_hidden_input,
    output_cotangent,
    sequence_pair_lengths,
    block_placement_order,
    sequence_adapter_index,
    token_expert_choices,
    attention_norm_gain,
    feedforward_norm_gain,
    query_key_value_weight,
    output_projection_weight,
    query_key_value_bias,
    router_weight_matrix,
    shared_gate_up_weight,
    shared_down_weight,
    shared_sigmoid_gate,
    routed_gate_up_weight,
    routed_down_weight,
    attention_adapter_first,
    attention_adapter_second,
    feedforward_adapter_first,
    router_adapter_second,
    shared_gate_adapter_second,
    shared_down_adapter_first,
    routed_gate_adapter_second,
    routed_down_adapter_first,
    down_adapter_second,
):
    tokens, width = layer_hidden_input.shape[1:]
    experts = router_weight_matrix.shape[1]
    capacity = tokens * TOP // experts * 9 // 8
    tail = capacity - MAIN
    ctx_count = lax.axis_size("ctx")
    group_rows = tokens * ctx_count
    along = ctx_count // 2
    rows_shared = tokens * along
    x_index = lax.axis_index("ctx") // 2
    y_index = lax.axis_index("ctx") % 2
    head_columns = width // along
    hidden = shared_down_weight.shape[0]
    quarter = hidden // along
    shards_of = lax.axis_size("fsdp")
    lengths = sequence_pair_lengths[0]
    order = block_placement_order[0]
    adapters = sequence_adapter_index[0]
    block_size = group_rows // order.shape[0]

    qkv_own = lax.dynamic_slice_in_dim(
        query_key_value_weight, x_index * head_columns, head_columns, 2
    ).reshape(-1, head_columns)
    out_weight = lax.all_gather(output_projection_weight, "fsdp", tiled=True)
    units = -(-quarter // 32) * 32
    own_up = jnp.swapaxes(
        lax.dynamic_slice_in_dim(shared_gate_up_weight, x_index * quarter, quarter, 2), 1, 2
    )
    own_down = lax.dynamic_slice_in_dim(shared_down_weight, x_index * quarter, quarter, 0)
    own_shared = jnp.pad(
        jnp.concatenate([own_up, own_down[None]]), ((0, 0), (0, units - quarter), (0, 0))
    ).reshape(3 * units, width)

    def of_group(factor):
        parts = [lax.dynamic_index_in_dim(factor, adapters[s], -3, keepdims=True) for s in range(2)]
        both = jnp.concatenate(parts, axis=-3)
        return both.reshape(both.shape[:-3] + (PAIR, both.shape[-1]))

    shared_second = jnp.concatenate(
        [
            of_group(shared_gate_adapter_second).reshape(2 * PAIR, hidden * shards_of),
            of_group(shared_down_adapter_first),
        ],
        axis=0,
    )
    shared_second = lax.dynamic_index_in_dim(
        shared_second.reshape(3 * PAIR, shards_of, along, quarter), x_index, 2, keepdims=False
    )
    shared_second = jnp.pad(shared_second, ((0, 0), (0, 0), (0, units - quarter)))
    shared_second = shared_second.reshape(3 * PAIR, shards_of * units)
    numbers = jnp.concatenate([adapters, x_index[None].astype(jnp.int32)])

    start = lengths[0]
    block_rows = jnp.arange(block_size, dtype=jnp.int32)
    blocks = order.reshape(along, 2, -1)
    key_places = (jnp.swapaxes(blocks, 0, 1).reshape(-1)[:, None] * block_size + block_rows).reshape(
        1, group_rows
    )
    own_blocks = lax.dynamic_index_in_dim(blocks, y_index, 1, keepdims=False).reshape(-1)
    places = own_blocks[:, None] * block_size + block_rows
    second = places >= start
    fractions = jnp.arange(0, HEAD_DIM, 2).astype(F32) / HEAD_DIM
    speeds = rope_theta ** (-fractions)
    bases = jnp.stack([own_blocks * block_size, own_blocks * block_size - start])
    base_angles = bases.astype(F32)[:, :, None, None] * speeds
    base_angles = jnp.concatenate([base_angles, base_angles], axis=3)
    base_cos, base_sin = jnp.cos(base_angles), jnp.sin(base_angles)
    base_cos = jnp.where(second[:, :, None], base_cos[1], base_cos[0])
    base_sin = jnp.where(second[:, :, None], base_sin[1], base_sin[0])
    row_angles = block_rows.astype(F32)[:, None] * speeds[None, :]
    row_angles = jnp.concatenate([row_angles, row_angles], axis=1)
    row_cos, row_sin = jnp.cos(row_angles), jnp.sin(row_angles)
    cosine = base_cos * row_cos - base_sin * row_sin
    sine = base_sin * row_cos + base_cos * row_sin
    sine = jnp.where(jnp.arange(HEAD_DIM) < HEAD_DIM // 2, -sine, sine)
    cosine, sine = cosine.reshape(rows_shared, HEAD_DIM), sine.reshape(rows_shared, HEAD_DIM)
    place_column = places.reshape(rows_shared, 1)
    start_column = jnp.where(second, start, 0).reshape(rows_shared, 1)
    side_shared = second.astype(F32).reshape(rows_shared, 1)
    side = lax.dynamic_slice_in_dim(side_shared, x_index * tokens, tokens)

    attention_gain = attention_norm_gain[None, :]
    feedforward_gain = feedforward_norm_gain[None, :]
    mix_weight = shared_sigmoid_gate[None, :]
    routed_second = routed_gate_adapter_second.reshape(2, LANES, -1)
    routed_first = routed_down_adapter_first.reshape(LANES, -1)
    ffn_flat = feedforward_adapter_first.reshape(-1, LANES, width)[3:]
    down_flat = down_adapter_second.reshape(2, LANES, width)

    normed_one, sent_grads_main, sent_grads_rest, picked, picked_first, picked_second = prologue(
        numbers,
        layer_hidden_input,
        output_cotangent,
        attention_gain,
        token_expert_choices,
        feedforward_adapter_first,
        down_adapter_second,
        attention_adapter_first,
        attention_adapter_second,
        experts,
        head_columns,
    )
    own_shared, normed_one = lax.optimization_barrier((own_shared, normed_one))
    shared_weight = lax.all_gather(own_shared, "fsdp")
    qkv, normed_shared = exchange(
        "gather_first", 0, ("share", "s", qkv_own), ("gather", "x", normed_one)
    )
    qkv = qkv.reshape(shards_of, 3, tokens, head_columns)
    projected, qkv_lanes = project(
        numbers,
        normed_shared.reshape(rows_shared, width),
        qkv,
        attention_adapter_first,
        attention_adapter_second,
        query_key_value_bias,
        side_shared,
        cosine,
        sine,
    )
    pairs, grads_shared = exchange(
        "keys", 1, ("gather", "y", projected[1:]), ("gather", "x", output_cotangent[0])
    )
    mixed_heads = attend(projected, pairs, place_column, start_column, key_places)
    (mixed,) = exchange(
        "mixed", 2, ("to_columns", "x", mixed_heads.reshape(along, tokens, head_columns))
    )
    residual, normed_two, small, sent_main, sent_rest, notes_main, notes_rest = after_attention(
        numbers,
        mixed,
        out_weight,
        layer_hidden_input,
        attention_adapter_first,
        attention_adapter_second,
        feedforward_gain,
        feedforward_adapter_first,
        router_weight_matrix,
        router_adapter_second,
        mix_weight,
        token_expert_choices,
        side,
    )
    *held, parts_rows, parts_lanes, value_part, shared_columns = shared_expert(
        3,
        normed_two,
        [
            ("rows", "f", sent_main),
            ("rows", "f", sent_rest),
            ("half", "f", sent_grads_main),
            ("half", "f", sent_grads_rest),
            ("rows", "f", notes_main),
            ("rows", "f", notes_rest),
        ],
        grads_shared,
        shared_weight,
        side_shared.reshape(along, tokens, 1),
        picked,
        shared_second,
        mix_weight,
    )
    (
        got_main,
        got_rest,
        got_notes_main,
        got_notes_rest,
        result_main,
        result_rest,
        value_parts,
        expert_columns,
    ) = routed_expert(
        4,
        held,
        (sent_grads_main, sent_grads_rest),
        value_part,
        ffn_flat,
        routed_second,
        routed_first,
        down_flat,
        routed_gate_up_weight,
        routed_down_weight,
    )
    grad_residual, grad_mixed, early_columns, router_rows, shared_side = after_experts(
        numbers,
        parts_rows,
        parts_lanes,
        got_main,
        got_rest,
        got_notes_main,
        got_notes_rest,
        output_cotangent,
        normed_two,
        residual,
        small,
        mixed,
        token_expert_choices,
        side,
        feedforward_adapter_first,
        router_weight_matrix,
        router_adapter_second,
        mix_weight,
        feedforward_gain,
        down_adapter_second,
        attention_adapter_first,
        attention_adapter_second,
        out_weight,
    )

    early_got, shared_got, router_got, heads_got, first_parts, first_lanes, expert_parts, output_value = (
        attention_back(
            5,
            [
                ("from_columns", "f", early_columns),
                ("from_columns", "f", shared_columns),
                ("gather", "f", router_rows),
            ],
            expert_columns,
            grad_mixed,
            projected,
            pairs,
            qkv,
            (
                place_column,
                start_column,
                key_places,
                cosine,
                sine,
                side_shared,
                qkv_lanes,
                picked_second,
            ),
            (
                result_main,
                result_rest,
                token_expert_choices,
                residual,
                value_parts,
                shared_side,
                small,
                picked,
            ),
        )
    )
    own_column = (jnp.arange(128) == lax.axis_index("fsdp")).astype(BF)[None, :]
    grads = finish(
        6,
        first_parts,
        first_lanes,
        layer_hidden_input,
        normed_one,
        grad_residual,
        attention_gain,
        picked_first,
        router_got,
        early_got,
        shared_got,
        heads_got,
        own_column,
        expert_parts,
        along * quarter,
        routed_down_weight.shape[1] // shards_of,
    )

    def by_adapter(rows):
        parts = rows.reshape(-1, ADAPTER_COUNT, RANK, rows.shape[1])
        return parts[0] if parts.shape[0] == 1 else parts

    return (output_value, grads[0], *(by_adapter(rows) for rows in grads[1:]))


def solution(mesh):
    return jax.shard_map(
        shards,
        mesh=mesh,
        in_specs=(
            P("fsdp", "ctx", None),
            P("fsdp", "ctx", None),
            P("fsdp", None),
            P("fsdp", None),
            P("fsdp", None),
            P("fsdp", "ctx", None),
            P(),
            P(),
            P(None, "fsdp", None),
            P("fsdp", None),
            P(),
            P(),
            P(None, None, "fsdp"),
            P("fsdp", None),
            P(),
            P("fsdp", None, None, None),
            P("fsdp", None, None),
            P(),
            P(),
            P(),
            P(),
            P(),
            P(),
            P(),
            P(),
            P(),
        ),
        out_specs=(
            P("fsdp", "ctx", None),
            P("fsdp", "ctx", None),
            P(None, None, None, "fsdp"),
            P(None, None, None, "fsdp"),
            P(None, None, None, "fsdp"),
            P(None, None, "fsdp"),
            P(None, None, None, "fsdp"),
            P(None, None, "fsdp"),
            P(None, None, None, "fsdp"),
            P(None, None, "fsdp"),
            P(None, None, None, "fsdp"),
        ),
        check_vma=False,
    )
```

```python
import functools

import jax
import jax.numpy as jnp
from jax import lax
from jax.experimental import pallas as pl
from jax.experimental.pallas import tpu as pltpu
from jax.sharding import PartitionSpec as P

HEADS = 16
HEAD_DIM = 128
TOP = 4
ADAPTER_COUNT = 8
RANK = 16
LANES = ADAPTER_COUNT * RANK
PAIR = 2 * RANK
MAIN = 32

norm_eps = 1e-06
rope_theta = 1000000.0
masked_score = -1e30
highest = lax.Precision.HIGHEST
MESH = pl.DeviceIdType.MESH
BF = jnp.bfloat16
F32 = jnp.float32
VMEM_LIMIT = 56 * 2**20


def dot(left, right):
    return jnp.dot(left, right, preferred_element_type=F32)


def dot_nt(left, right):
    return lax.dot_general(left, right, (((1,), (1,)), ((), ())), preferred_element_type=F32)


def dot_tn(left, right):
    return lax.dot_general(left, right, (((0,), (0,)), ((), ())), preferred_element_type=F32)


GROUP_SIZE = {"x": 4, "y": 2, "c": 8, "f": 16}


def place_in(group):
    ctx, fsdp = lax.axis_index("ctx"), lax.axis_index("fsdp")
    return {"x": ctx // 2, "y": ctx % 2, "c": ctx, "f": fsdp}[group]


def device_of(group, index):
    ctx, fsdp = lax.axis_index("ctx"), lax.axis_index("fsdp")
    if group == "x":
        return (index * 2 + ctx % 2, fsdp)
    if group == "y":
        return ((ctx // 2) * 2 + index, fsdp)
    if group == "c":
        return (index, fsdp)
    return (ctx, index)


def chip():
    ctx, fsdp = lax.axis_index("ctx"), lax.axis_index("fsdp")
    return ctx % 2 * 2 + fsdp // 8, fsdp // 2 % 4, fsdp % 2


def device_at(y, z, core):
    return (lax.axis_index("ctx") // 2 * 2 + y // 2, y % 2 * 8 + z * 2 + core)


def shard_at(y, z, core):
    return y % 2 * 8 + z * 2 + core


def exchanged_shape(kind, group, shape):
    if kind == "share":
        return (GROUP_SIZE["f"],) + shape
    count = GROUP_SIZE[group]
    if kind == "gather":
        return (count,) + shape
    if kind in ("swap", "rows", "half"):
        return shape
    if kind == "from_columns":
        return (count, shape[0], shape[1] // count)
    return (shape[1], count * shape[2])


def own_shape(kind, group, shape):
    if kind in ("gather", "share"):
        return shape
    count = GROUP_SIZE[group]
    if kind in ("rows", "half"):
        return (shape[0] // count,) + shape[1:]
    if kind == "from_columns":
        return (shape[0], shape[1] // count)
    return shape[1:]


def copies_of(kind, group):
    return 23 if kind == "share" else GROUP_SIZE[group] - 1


def soon(offset):
    return offset % ROUTED_STEPS >= ROUTED_STEPS // 2


def block_of(ref, kind, count, index):
    if kind == "rows":
        depth = ref.shape[0] // count
        return ref.at[pl.ds(pl.multiple_of(index * depth, depth), depth)]
    if kind == "columns":
        width = ref.shape[1] // count
        return ref.at[:, pl.ds(pl.multiple_of(index * width, width), width)]
    return ref.at[index]


def source_of(kind, group, ref, index):
    if kind in ("gather", "share"):
        return ref
    cut = {"rows": "rows", "half": "rows", "from_columns": "columns"}.get(kind, "first")
    return block_of(ref, cut, GROUP_SIZE[group], index)


def target_of(kind, group, ref, index):
    cut = {"rows": "rows", "half": "rows", "to_columns": "columns"}.get(kind, "first")
    return block_of(ref, cut, GROUP_SIZE["f" if kind == "share" else group], index)


def remote(source, target, send, recv, device):
    return pltpu.make_async_remote_copy(
        src_ref=source,
        dst_ref=target,
        send_sem=send,
        recv_sem=recv,
        device_id=device,
        device_id_type=MESH,
    )


def greet(plan):
    barrier = pltpu.get_barrier_semaphore()
    count = 0
    for group in sorted({group for kind, group in plan}):
        if group == "s":
            y, z, core = chip()
            peers = [device_at(y, lax.rem(z + d, 4), core) for d in (1, 2, 3)]
            peers += [device_at(lax.rem(y + d, 4), z, core) for d in (1, 3)]
            peers += [device_at(y, z, 1 - core)]
        else:
            size = GROUP_SIZE[group]
            mine = place_in(group)
            peers = [device_of(group, lax.rem(mine + d, size)) for d in range(1, size)]
        for peer in peers:
            pl.semaphore_signal(barrier, inc=1, device_id=peer, device_id_type=MESH)
        count += len(peers)
    pl.semaphore_wait(barrier, count)


class Share:
    def __init__(self, source, target, send, recv, first):
        self.target = target
        self.sems = (send, recv, first)
        y, z, core = self.place = chip()
        self.order = (1, 3, 2)
        self.source = source
        self.along_z = [
            self.copy(source, shard_at(y, z, core), None, i, device_at(y, lax.rem(z + d, 4), core))
            for i, d in enumerate(self.order)
        ]
        self.along_y, self.across = [], []

    def copy(self, source, shard, half, number, device):
        send, recv, first = self.sems
        target = self.target.at[shard]
        if half is not None:
            target = target.at[half]
        return remote(source, target, send.at[first + number], recv.at[first + number], device)

    def halves(self):
        half = self.target.shape[1] // 2
        return pl.ds(0, half), pl.ds(half, half)

    def forward(self, number, source, z):
        y, unused, core = self.place
        unused, my_z, unused = self.place
        shard = shard_at(y, z, core)
        for i, (half, d) in enumerate(zip(self.halves(), (3, 1))):
            copy = self.copy(
                source.at[half], shard, half, 3 + 2 * number + i, device_at(lax.rem(y + d, 4), my_z, core)
            )
            copy.start()
            self.along_y.append(copy)
        copy = self.copy(source, shard, None, 11 + number, device_at(y, my_z, 1 - core))
        copy.start()
        self.across.append(copy)

    def start(self):
        for copy in self.along_z:
            copy.start()
        self.forward(0, self.source, self.place[1])

    def finish(self):
        y, z, core = self.place
        for i, d in enumerate(self.order):
            self.along_z[i].wait_recv()
            from_z = lax.rem(z + 4 - d, 4)
            self.forward(i + 1, self.target.at[shard_at(y, from_z, core)], from_z)
        for number in range(4):
            from_z = z if number == 0 else lax.rem(z + 4 - self.order[number - 1], 4)
            shard = shard_at(y + 1, from_z, core)
            for i, half in enumerate(self.halves()):
                self.along_y[2 * number + i].wait_recv()
                block = self.target.at[shard].at[half]
                copy = self.copy(block, shard, half, 15 + 2 * number + i, device_at(y, z, 1 - core))
                copy.start()
                self.across.append(copy)
        for copy in self.along_z + self.along_y:
            copy.wait_send()
        for copy in self.across:
            copy.wait()


class Mover:
    def __init__(self, plan, inputs, outputs, own, send, recv, in_sem, out_sem):
        self.plan, self.inputs, self.outputs, self.own = plan, inputs, outputs, own
        self.send, self.recv, self.in_sem, self.out_sem = send, recv, in_sem, out_sem
        self.taken, self.copies, self.shares = [], [], []

    def own_place(self, item):
        kind, group = self.plan[item]
        return shard_at(*chip()) if kind == "share" else place_in(group)

    def take(self):
        for item, (kind, group) in enumerate(self.plan):
            block = source_of(kind, group, self.inputs[item], self.own_place(item))
            copy = pltpu.make_async_copy(block, self.own[item], self.in_sem.at[item])
            copy.start()
            self.taken.append(copy)

    def start(self):
        slot = 0
        for item, (kind, group) in enumerate(self.plan):
            source, target = self.inputs[item], self.outputs[item]
            if kind == "share":
                share = Share(source, target, self.send, self.recv, slot)
                share.start()
                self.shares.append(share)
            else:
                count = GROUP_SIZE[group]
                mine = place_in(group)
                for offset in range(1, count):
                    if kind == "half" and not soon(offset):
                        continue
                    peer = lax.rem(mine + offset, count)
                    copy = remote(
                        source_of(kind, group, source, peer),
                        target_of(kind, group, target, mine),
                        self.send.at[slot + offset - 1],
                        self.recv.at[slot + offset - 1],
                        device_of(group, peer),
                    )
                    copy.start()
                    self.copies.append(copy)
            slot += copies_of(kind, group)
        for item, (kind, group) in enumerate(self.plan):
            self.taken[item].wait()
            block = target_of(kind, group, self.outputs[item], self.own_place(item))
            copy = pltpu.make_async_copy(self.own[item], block, self.out_sem.at[item])
            copy.start()
            self.copies.append(copy)

    def finish(self):
        for share in self.shares:
            share.finish()
        for copy in self.copies:
            copy.wait()


def exchange_kernel(plan, *refs):
    amount = len(plan)
    mover = Mover(
        plan, refs[:amount], refs[amount : 2 * amount], refs[2 * amount : 3 * amount], *refs[3 * amount :]
    )
    mover.take()
    greet(plan)
    mover.start()
    mover.finish()


def mover_scratch(items):
    plan = tuple((kind, group) for kind, group, array in items)
    slots = sum(copies_of(kind, group) for kind, group in plan)
    return [
        pltpu.VMEM(own_shape(kind, group, array.shape), array.dtype) for kind, group, array in items
    ] + [
        pltpu.SemaphoreType.DMA((slots,)),
        pltpu.SemaphoreType.DMA((slots,)),
        pltpu.SemaphoreType.DMA((len(items),)),
        pltpu.SemaphoreType.DMA((len(items),)),
    ]


def exchange(name, number, *items):
    plan = tuple((kind, group) for kind, group, array in items)
    arrays = [array for kind, group, array in items]
    return pl.pallas_call(
        functools.partial(exchange_kernel, plan),
        out_shape=[
            jax.ShapeDtypeStruct(exchanged_shape(kind, group, array.shape), array.dtype)
            for kind, group, array in items
        ],
        in_specs=[pl.BlockSpec(memory_space=pltpu.HBM)] * len(items),
        out_specs=[pl.BlockSpec(memory_space=pltpu.HBM)] * len(items),
        scratch_shapes=mover_scratch(items),
        compiler_params=pltpu.CompilerParams(
            collective_id=number, has_side_effects=True, vmem_limit_bytes=16 * 2**20
        ),
        name=name,
    )(*arrays)


def rms_forward(values, gain):
    mean_square = jnp.mean(values * values, axis=-1, keepdims=True)
    return values * lax.rsqrt(mean_square + norm_eps) * gain.astype(F32)


def rms_backward(values, gain, grad_result):
    scale = lax.rsqrt(jnp.mean(values * values, axis=-1, keepdims=True) + norm_eps)
    scaled = gain.astype(F32) * grad_result
    inner = jnp.mean(values * scaled, axis=-1, keepdims=True)
    return scale * scaled - values * (scale * scale * scale) * inner


def logistic(values):
    return 0.5 * jnp.tanh(0.5 * values) + 0.5


def swiglu(gate, upper):
    sigma = logistic(gate)
    silu = gate * sigma
    return (silu * upper).astype(BF), sigma, silu


def swiglu_backward(gate, upper, sigma, silu, grad_hidden):
    grad_gate = grad_hidden * upper * (sigma + silu * (1.0 - sigma))
    return (grad_gate.astype(BF), (grad_hidden * silu).astype(BF))


def two_parts(values):
    high = values.astype(BF)
    return high, (values - high.astype(F32)).astype(BF)


def lane_index(shape):
    return lax.broadcasted_iota(jnp.int32, shape, 1)


def row_index(shape):
    return lax.broadcasted_iota(jnp.int32, shape, 0)


def pair_pick(second, copies):
    shape = (second.shape[0], PAIR * copies)
    of_lane = (lane_index(shape) % PAIR >= RANK).astype(F32)
    return (of_lane == second).astype(F32)


def pair_of(first_ref, last_ref, index):
    return jnp.concatenate([first_ref[index, 0], last_ref[index, 0]], axis=0)


def padded(values):
    rest = 128 - values.shape[1]
    return jnp.concatenate([values, jnp.zeros((values.shape[0], rest), values.dtype)], axis=1)


def routing(routes, experts):
    tokens = routes.shape[0]
    expert_lane = lane_index((tokens, experts))
    expert_hot = [(routes[:, k : k + 1] == expert_lane).astype(F32) for k in range(TOP)]
    count = sum(expert_hot)
    below = (row_index((tokens, tokens)) > lane_index((tokens, tokens))).astype(BF)
    earlier = dot(below, count.astype(BF))
    rank = [jnp.sum(hot * earlier, axis=1, keepdims=True).astype(jnp.int32) for hot in expert_hot]
    main_lane = lane_index((tokens, experts * MAIN))
    rest_lane = lane_index((tokens, experts * 16))
    rest_code = (rest_lane // 16) * 4 + rest_lane % 4
    main_hot, rest_hot = [], []
    for k in range(TOP):
        expert = routes[:, k : k + 1]
        main_slot = jnp.where(rank[k] < MAIN, expert * MAIN + rank[k], -1)
        rest_slot = jnp.where(rank[k] < MAIN, -1, expert * 4 + rank[k] - MAIN)
        main_hot.append((main_lane == main_slot).astype(F32))
        rest_hot.append((rest_code == rest_slot).astype(F32))
    return expert_hot, main_hot, rest_hot


def quarter_mask(shape, quarter):
    return (lane_index(shape) % 16 // 4 == quarter).astype(F32)


def rows_to_slots(main_hot, rest_hot, rows):
    main = dot_tn(sum(main_hot).astype(BF), rows).astype(BF)
    rest_sum = sum(rest_hot)
    width = rows.shape[1] // 4
    rest = None
    for quarter in range(4):
        hot = (rest_sum * quarter_mask(rest_sum.shape, quarter)).astype(BF)
        part = dot_tn(hot, rows[:, quarter * width : (quarter + 1) * width])
        rest = part if rest is None else rest + part
    return main, rest.astype(BF)


def slots_to_rows(main_hot, rest_hot, main, rest):
    rest_sum = sum(rest_hot)
    parts = [
        dot((rest_sum * quarter_mask(rest_sum.shape, quarter)).astype(BF), rest)
        for quarter in range(4)
    ]
    return dot(sum(main_hot).astype(BF), main) + jnp.concatenate(parts, axis=1)


def rest_selectors(sources):
    shape = (4 * sources, 16 * sources)
    row, lane = row_index(shape), lane_index(shape)
    same = (lane // 16 == row // 4) & (lane % 4 == row % 4)
    return [(same & (lane % 16 // 4 == quarter)).astype(BF) for quarter in range(4)]


def rest_to_rows(selectors, rest):
    return jnp.concatenate([dot(selector, rest) for selector in selectors], axis=1).astype(BF)


def rows_to_rest(selectors, rows):
    width = rows.shape[1] // 4
    total = None
    for quarter in range(4):
        part = dot_tn(selectors[quarter], rows[:, quarter * width : (quarter + 1) * width])
        total = part if total is None else total + part
    return total.astype(BF)


def stage(kernel, name, out_shape, in_specs, out_specs, grid=(1,), scratch=(), prefetch=0):
    return pl.pallas_call(
        kernel,
        out_shape=out_shape,
        grid_spec=pltpu.PrefetchScalarGridSpec(
            num_scalar_prefetch=prefetch,
            grid=grid,
            in_specs=in_specs,
            out_specs=out_specs,
            scratch_shapes=list(scratch),
        ),
        compiler_params=pltpu.CompilerParams(vmem_limit_bytes=VMEM_LIMIT),
        name=name,
    )


def whole(array):
    zeros = (0,) * len(array.shape)
    return pl.BlockSpec(array.shape, lambda *unused: zeros)


def of_sequence(which, block):
    return pl.BlockSpec(block, lambda *at: (0, at[-1][which], 0, 0))


def shape_of(shape, kind):
    return jax.ShapeDtypeStruct(shape, kind)


HBM = pl.BlockSpec(memory_space=pltpu.HBM)


def prologue_kernel(
    numbers_ref,
    rows_ref,
    grads_ref,
    gain_ref,
    routes_ref,
    ffn_a_ref,
    ffn_b_ref,
    down_a_ref,
    down_b_ref,
    first_a_ref,
    first_b_ref,
    second_a_ref,
    second_b_ref,
    normed_ref,
    main_ref,
    rest_ref,
    picked_ref,
    first_ref,
    second_ref,
):
    normed_ref[...] = rms_forward(rows_ref[0].astype(F32), gain_ref[...]).astype(BF)
    experts = main_ref.shape[0] // MAIN
    unused, main_hot, rest_hot = routing(routes_ref[0], experts)
    main, rest = rows_to_slots(main_hot, rest_hot, grads_ref[0])
    main_ref[...] = main
    rest_ref[...] = rest
    picked_ref[...] = jnp.concatenate(
        [
            pair_of(ffn_a_ref, ffn_b_ref, 1),
            pair_of(ffn_a_ref, ffn_b_ref, 2),
            pair_of(down_a_ref, down_b_ref, 0),
        ],
        axis=0,
    )
    for j in range(3):
        first_ref[j * PAIR : (j + 1) * PAIR, :] = pair_of(first_a_ref, first_b_ref, j)
        second_ref[j * PAIR : (j + 1) * PAIR, :] = pair_of(second_a_ref, second_b_ref, j)


def prologue(
    numbers, rows, grads, gain, routes, ffn_first, down_second, first, second, experts, columns
):
    tokens, width = rows.shape[1:]
    heads = lambda which: pl.BlockSpec(
        (3, 1, RANK, columns), lambda n, a: (0, a[which], 0, a[2])
    )
    outs = [
        (tokens, width),
        (experts * MAIN, width),
        (experts * 16, width // 4),
        (3 * PAIR, width),
        (3 * PAIR, width),
        (3 * PAIR, columns),
    ]
    return stage(
        prologue_kernel,
        "prologue",
        [shape_of(shape, BF) for shape in outs],
        [
            whole(rows),
            whole(grads),
            whole(gain),
            whole(routes),
            of_sequence(0, (3, 1, RANK, width)),
            of_sequence(1, (3, 1, RANK, width)),
            of_sequence(0, (1, 1, RANK, width)),
            of_sequence(1, (1, 1, RANK, width)),
            of_sequence(0, (3, 1, RANK, width)),
            of_sequence(1, (3, 1, RANK, width)),
            heads(0),
            heads(1),
        ],
        [pl.BlockSpec(shape, lambda n, a: (0, 0)) for shape in outs],
        prefetch=1,
    )(
        numbers, rows, grads, gain, routes, ffn_first, ffn_first, down_second, down_second, first, first,
        second, second,
    )


def half_turn(values):
    parts = []
    for head in range(values.shape[1] // HEAD_DIM):
        part = values[:, head * HEAD_DIM : (head + 1) * HEAD_DIM]
        parts.append(jnp.concatenate([part[:, 64:], part[:, :64]], axis=1))
    return jnp.concatenate(parts, axis=1) if len(parts) > 1 else parts[0]


def project_kernel(
    numbers_ref,
    rows_ref,
    weight_ref,
    first_a_ref,
    first_b_ref,
    second_a_ref,
    second_b_ref,
    bias_ref,
    side_ref,
    cos_ref,
    sin_ref,
    out_ref,
    lanes_ref,
):
    which = pl.program_id(0)

    @pl.when(pl.program_id(1) == 0)
    def lanes():
        first = pair_of(first_a_ref, first_b_ref, 0)
        picked = dot_nt(rows_ref[...], first) * pair_pick(side_ref[...], 1)
        lanes_ref[0] = picked.astype(BF)

    weight = weight_ref[...].reshape(rows_ref.shape[1], weight_ref.shape[3])
    bias = bias_ref[...].astype(F32)
    bias = jnp.sum(jnp.where(row_index(bias.shape) == which, bias, 0.0), axis=0, keepdims=True)
    second = pair_of(second_a_ref, second_b_ref, 0)
    value = dot(rows_ref[...], weight) + bias + dot(lanes_ref[0], second)
    copies = value.shape[1] // HEAD_DIM
    cosine = jnp.concatenate([cos_ref[...]] * copies, axis=1)
    sine = jnp.concatenate([sin_ref[...]] * copies, axis=1)
    turned = value * cosine + half_turn(value) * sine
    out_ref[0] = jnp.where(which < 2, turned, value).astype(BF)


def project(numbers, rows, weight, first, second, bias, side, cosine, sine):
    tokens, width = rows.shape
    columns = weight.shape[3]
    step = 256
    steps = columns // step
    return stage(
        project_kernel,
        "project",
        [shape_of((3, tokens, columns), BF), shape_of((3, tokens, PAIR), BF)],
        [
            whole(rows),
            pl.BlockSpec((weight.shape[0], 1, weight.shape[2], step), lambda j, n, a: (0, j, 0, n)),
            pl.BlockSpec((1, 1, RANK, width), lambda j, n, a: (j, a[0], 0, 0)),
            pl.BlockSpec((1, 1, RANK, width), lambda j, n, a: (j, a[1], 0, 0)),
            pl.BlockSpec((1, 1, RANK, step), lambda j, n, a: (j, a[0], 0, a[2] * steps + n)),
            pl.BlockSpec((1, 1, RANK, step), lambda j, n, a: (j, a[1], 0, a[2] * steps + n)),
            pl.BlockSpec((3, step), lambda j, n, a: (0, a[2] * steps + n)),
            whole(side),
            whole(cosine),
            whole(sine),
        ],
        [
            pl.BlockSpec((1, tokens, step), lambda j, n, a: (j, 0, n)),
            pl.BlockSpec((1, tokens, PAIR), lambda j, n, a: (j, 0, 0)),
        ],
        grid=(3, steps),
        prefetch=1,
    )(numbers, rows, weight, first, first, second, second, bias, side, cosine, sine)


def probabilities(query, keys, query_place, query_start, key_place):
    scores = dot_nt(query, keys) * (HEAD_DIM**-0.5)
    allowed = (key_place <= query_place) & (key_place >= query_start)
    scores = jnp.where(allowed, scores, masked_score)
    top = jnp.max(scores, axis=1, keepdims=True)
    raised = jnp.exp(scores - top)
    return raised * (1.0 / jnp.sum(raised, axis=1, keepdims=True))


def attend_kernel(query_ref, key_ref, value_ref, place_ref, start_ref, key_place_ref, out_ref):
    keys = key_ref[...].reshape(-1, HEAD_DIM)
    values = value_ref[...].reshape(-1, HEAD_DIM)
    probs = probabilities(query_ref[0], keys, place_ref[...], start_ref[...], key_place_ref[...])
    out_ref[...] = dot(probs.astype(BF), values).astype(BF)


def attend(projected, pairs, place, start, key_place):
    tokens, columns = projected.shape[1:]
    step = 256
    keys = pairs.shape[0] * pairs.shape[2]
    half = pairs.shape[2]
    return pl.pallas_call(
        attend_kernel,
        grid=(columns // HEAD_DIM, tokens // step),
        out_shape=jax.ShapeDtypeStruct((tokens, columns), BF),
        in_specs=[
            pl.BlockSpec((1, step, HEAD_DIM), lambda h, i: (0, i, h)),
            pl.BlockSpec((2, 1, half, HEAD_DIM), lambda h, i: (0, 0, 0, h)),
            pl.BlockSpec((2, 1, half, HEAD_DIM), lambda h, i: (0, 1, 0, h)),
            pl.BlockSpec((step, 1), lambda h, i: (i, 0)),
            pl.BlockSpec((step, 1), lambda h, i: (i, 0)),
            pl.BlockSpec((1, keys), lambda h, i: (0, 0)),
        ],
        out_specs=pl.BlockSpec((step, HEAD_DIM), lambda h, i: (i, h)),
        compiler_params=pltpu.CompilerParams(vmem_limit_bytes=VMEM_LIMIT),
        name="attend",
    )(projected, pairs, pairs, place, start, key_place)


def after_attention_kernel(
    numbers_ref,
    mixed_ref,
    weight_ref,
    rows_ref,
    first_a_ref,
    first_b_ref,
    second_a_ref,
    second_b_ref,
    gain_ref,
    ffn_a_ref,
    ffn_b_ref,
    router_ref,
    router_a_ref,
    router_b_ref,
    mix_ref,
    routes_ref,
    side_ref,
    residual_ref,
    normed_ref,
    small_ref,
    main_ref,
    rest_ref,
    main_notes_ref,
    rest_notes_ref,
    lanes_ref,
):
    step = pl.program_id(0)
    side = side_ref[...]
    pick = pair_pick(side, 1)

    @pl.when(step == 0)
    def lanes():
        first = pair_of(first_a_ref, first_b_ref, 0)
        lanes_ref[...] = (dot_nt(mixed_ref[...], first) * pick).astype(BF)

    columns = weight_ref.shape[1]
    here = pl.ds(pl.multiple_of(step * columns, columns), columns)
    second = pair_of(second_a_ref, second_b_ref, 0)
    residual_ref[:, here] = rows_ref[0].astype(F32) + (
        dot(mixed_ref[...], weight_ref[...]) + dot(lanes_ref[...], second)
    )

    @pl.when(step == pl.num_programs(0) - 1)
    def last():
        tokens = residual_ref.shape[0]
        experts = router_ref.shape[1]
        normed = rms_forward(residual_ref[...], gain_ref[...]).astype(BF)
        normed_ref[...] = normed
        router_lanes = (dot_nt(normed, pair_of(ffn_a_ref, ffn_b_ref, 0)) * pick).astype(BF)
        router_second = jnp.concatenate([router_a_ref[0], router_b_ref[0]], axis=0)
        logits = dot(normed, router_ref[...]) + dot(router_lanes, router_second)
        expert_hot, main_hot, rest_hot = routing(routes_ref[0], experts)
        chosen = [jnp.sum(hot * logits, axis=1, keepdims=True) for hot in expert_hot]
        top = jnp.maximum(jnp.maximum(chosen[0], chosen[1]), jnp.maximum(chosen[2], chosen[3]))
        raised = [jnp.exp(value - top) for value in chosen]
        total = sum(raised)
        gates = [value / total for value in raised]
        mix = logistic(
            jnp.sum(normed.astype(F32) * mix_ref[...].astype(F32), axis=1, keepdims=True)
        )
        small_ref[...] = padded(
            jnp.concatenate(
                [lanes_ref[...].astype(F32), router_lanes.astype(F32), *gates, mix], axis=1
            )
        )
        main, rest = rows_to_slots(main_hot, rest_hot, normed)
        main_ref[...] = main
        rest_ref[...] = rest
        adapter = jnp.where(side > 0.5, numbers_ref[1], numbers_ref[0])
        lane = lane_index((tokens, 128))
        adapter_hot = (lane == adapter).astype(F32)
        main_notes, rest_notes = None, None
        for k in range(TOP):
            high, low = two_parts(gates[k])
            notes = jnp.where(
                lane == ADAPTER_COUNT,
                high.astype(F32),
                jnp.where(lane == ADAPTER_COUNT + 1, low.astype(F32), adapter_hot),
            ).astype(BF)
            main_part = dot_tn(main_hot[k].astype(BF), notes)
            rest_part = dot_tn(rest_hot[k].astype(BF), notes)
            main_notes = main_part if k == 0 else main_notes + main_part
            rest_notes = rest_part if k == 0 else rest_notes + rest_part
        main_notes_ref[...] = main_notes.astype(BF)
        rest_notes_ref[...] = rest_notes.astype(BF)


def after_attention(
    numbers, mixed, weight, rows, first, second, gain, ffn_first, router, router_second, mix, routes, side
):
    tokens, width = mixed.shape
    experts = router.shape[1]
    step = 512
    kept = lambda *shape: pl.BlockSpec(shape, lambda n, a: (0,) * len(shape))
    outs = [
        ((tokens, width), F32),
        ((tokens, width), BF),
        ((tokens, 128), F32),
        ((experts * MAIN, width), BF),
        ((experts * 16, width // 4), BF),
        ((experts * MAIN, 128), BF),
        ((experts * 16, 128), BF),
    ]
    return stage(
        after_attention_kernel,
        "after_attention",
        [shape_of(*out) for out in outs],
        [
            whole(mixed),
            pl.BlockSpec((width, step), lambda n, a: (0, n)),
            pl.BlockSpec((1, tokens, step), lambda n, a: (0, 0, n)),
            pl.BlockSpec((1, 1, RANK, width), lambda n, a: (3, a[0], 0, 0)),
            pl.BlockSpec((1, 1, RANK, width), lambda n, a: (3, a[1], 0, 0)),
            pl.BlockSpec((1, 1, RANK, step), lambda n, a: (3, a[0], 0, n)),
            pl.BlockSpec((1, 1, RANK, step), lambda n, a: (3, a[1], 0, n)),
            whole(gain),
            pl.BlockSpec((1, 1, RANK, width), lambda n, a: (0, a[0], 0, 0)),
            pl.BlockSpec((1, 1, RANK, width), lambda n, a: (0, a[1], 0, 0)),
            whole(router),
            pl.BlockSpec((1, RANK, experts), lambda n, a: (a[0], 0, 0)),
            pl.BlockSpec((1, RANK, experts), lambda n, a: (a[1], 0, 0)),
            whole(mix),
            whole(routes),
            whole(side),
        ],
        [kept(*shape) for shape, kind in outs],
        grid=(width // step,),
        scratch=[pltpu.VMEM((tokens, PAIR), BF)],
        prefetch=1,
    )(
        numbers, mixed, weight, rows, first, first, second, second, gain, ffn_first, ffn_first, router,
        router_second, router_second, mix, routes, side,
    )


def in_owner_columns(total, target, columns):
    count = total.shape[0]
    for owner in range(total.shape[1] // columns):
        part = total[:, owner * columns : (owner + 1) * columns].astype(BF)
        target[:count, owner * 128 : (owner + 1) * 128] = padded(part)


def x_step(step):
    return step + step // 2 * (1 - 2 * (step % 2))


SHARED_STEPS = 2


def shared_kernel(plan, *refs):
    amount = len(plan)
    inputs, refs = refs[:amount], refs[amount:]
    normed_ref, grads_hbm, weights_hbm, side_ref, picked_ref, first_ref, mix_ref = refs[:7]
    outputs, refs = refs[7 : 7 + amount], refs[7 + amount :]
    parts_refs, values_ref, adapter_ref, refs = refs[:2], refs[2], refs[3], refs[4:]
    own, move_sems, refs = refs[:amount], refs[amount : amount + 4], refs[amount + 4 :]
    rows_buf, grads_buf, gate_up_buf, down_buf = refs[:4]
    parts_buf, values_buf, total, refs = refs[4:6], refs[6], refs[7], refs[8:]
    rows_send, rows_recv, parts_send, parts_recv, load_sem, parts_sem = refs

    shards_of, units, wide = down_buf.shape
    along, tokens, width = rows_buf.shape
    hidden_units = shards_of * units
    me = place_in("x")
    loads = [
        pltpu.make_async_copy(normed_ref, rows_buf.at[me], load_sem.at[0]),
        pltpu.make_async_copy(grads_hbm, grads_buf, load_sem.at[1]),
    ]
    loads += [
        pltpu.make_async_copy(
            weights_hbm.at[:, pl.ds(i * units, units)],
            target.at[:, :, pl.ds(0, width)],
            load_sem.at[2 + i],
        )
        for i, target in enumerate((gate_up_buf.at[0], gate_up_buf.at[1], down_buf))
    ]
    for load in loads:
        load.start()
    mover = Mover(plan, inputs, outputs, own, *move_sems)
    mover.take()
    greet(plan + (("gather", "x"),))

    def rows_copy(offset):
        return remote(
            normed_ref,
            rows_buf.at[me],
            rows_send.at[offset],
            rows_recv.at[offset],
            device_of("x", lax.rem(me + offset, along)),
        )

    def parts_copy(kind, offset):
        peer = lax.rem(me + along - offset, along)
        return remote(
            parts_buf[kind].at[peer],
            parts_refs[kind].at[me],
            parts_send.at[kind, offset],
            parts_recv.at[kind, offset],
            device_of("x", peer),
        )

    def own_parts(kind):
        return pltpu.make_async_copy(
            parts_buf[kind].at[me], parts_refs[kind].at[me], parts_sem.at[kind]
        )

    for offset in (1, 3, 2):
        rows_copy(offset).start()
    mover.start()
    for i in range(2):
        gate_up_buf[i, :, :, width:] = first_ref[i]
    down_buf[:, :, width:] = first_ref[2]
    total[...] = jnp.zeros_like(total)
    for load in loads:
        load.wait()
    per_step = along // SHARED_STEPS

    def block(step, carry):
        offsets = [x_step(step * per_step + i) for i in range(per_step)]
        sources = [lax.rem(me + along - offset, along) for offset in offsets]
        for i, offset in enumerate(offsets):
            if i > 0:
                rows_copy(offset).wait_recv()
            else:

                @pl.when(step > 0)
                def arrived():
                    rows_copy(offset).wait_recv()

        rows = jnp.concatenate([rows_buf[source] for source in sources], axis=0)
        grads = jnp.concatenate([grads_buf[source] for source in sources], axis=0)
        side = jnp.concatenate([side_ref[source] for source in sources], axis=0)
        grads_f = grads.astype(F32)
        pick = pair_pick(side, 1)
        pick_both = pair_pick(side, 2)
        gate_up = gate_up_buf[...].reshape(2 * hidden_units, wide)
        down = down_buf[...].reshape(hidden_units, wide)
        lanes = (dot_nt(rows, picked_ref[: 2 * PAIR]) * pick_both).astype(BF)
        mix = logistic(jnp.sum(rows.astype(F32) * mix_ref[...].astype(F32), axis=1, keepdims=True))
        grad_shared = (mix * grads_f).astype(BF)
        grad_side = (dot_nt(grad_shared, picked_ref[2 * PAIR :]) * pick).astype(BF)
        both = dot_nt(jnp.concatenate([rows, padded(lanes)], axis=1), gate_up)
        gate, upper = both[:, :hidden_units], both[:, hidden_units:]
        hidden, sigma, silu = swiglu(gate, upper)
        grad_hidden = dot_nt(jnp.concatenate([grad_shared, padded(grad_side)], axis=1), down)
        grad_gate, grad_upper = swiglu_backward(gate, upper, sigma, silu, grad_hidden)
        back = dot(jnp.concatenate([grad_gate, grad_upper], axis=1), gate_up)
        grad_lanes = (back[:, width : width + 2 * PAIR] * pick_both).astype(BF)
        value = dot(hidden, down)
        side_lanes = (value[:, width : width + PAIR] * pick).astype(BF)
        value = value[:, :width]
        mix_sum = jnp.sum(grads_f * value, axis=1, keepdims=True)
        notes = padded(jnp.concatenate([side_lanes, grad_lanes, *two_parts(mix_sum)], axis=1))
        for i, source in enumerate(sources):
            at = slice(i * tokens, (i + 1) * tokens)
            parts_buf[0][source] = back[at, :width].astype(BF)
            parts_buf[1][source] = notes[at]
            values_buf[source] = value[at].astype(BF)

        for i, offset in enumerate(offsets):
            if i > 0:
                for kind in range(2):
                    parts_copy(kind, offset).start()
            else:

                @pl.when(step == 0)
                def keep():
                    for kind in range(2):
                        own_parts(kind).start()

                @pl.when(step > 0)
                def send():
                    for kind in range(2):
                        parts_copy(kind, offset).start()

        total[:PAIR] += dot_tn(lanes[:, :PAIR], grad_gate)
        total[PAIR : 2 * PAIR] += dot_tn(lanes[:, PAIR:], grad_upper)
        total[2 * PAIR :] += dot_tn(grad_side, hidden)
        return carry

    lax.fori_loop(0, SHARED_STEPS, block, 0)
    values_out = pltpu.make_async_copy(values_buf, values_ref, parts_sem.at[2])
    values_out.start()
    in_owner_columns(total, adapter_ref, units)
    mover.finish()
    for kind in range(2):
        own_parts(kind).wait()
    for offset in range(1, along):
        rows_copy(offset).wait_send()
        for kind in range(2):
            parts_copy(kind, offset).wait()
    values_out.wait()


def shared_expert(number, normed, items, grads, weights, side, picked, first, mix):
    tokens, width = normed.shape
    plan = tuple((kind, group) for kind, group, array in items)
    arrays = [array for kind, group, array in items]
    along = GROUP_SIZE["x"]
    shards_of, units = weights.shape[0], weights.shape[1] // 3
    hidden = shards_of * units
    vmem = pl.BlockSpec(memory_space=pltpu.VMEM)
    parts = [(along, tokens, width), (along, tokens, 128), (along, tokens, width)]
    return pl.pallas_call(
        functools.partial(shared_kernel, plan),
        out_shape=[shape_of(array.shape, BF) for array in arrays]
        + [shape_of(part, BF) for part in parts]
        + [shape_of((3 * PAIR, shards_of * 128), BF)],
        in_specs=[HBM] * (len(items) + 3) + [vmem] * 4,
        out_specs=[HBM] * (len(items) + 3) + [vmem],
        scratch_shapes=mover_scratch(items)
        + [pltpu.VMEM((along, tokens, width), BF)] * 2
        + [
            pltpu.VMEM((2, shards_of, units, width + 128), BF),
            pltpu.VMEM((shards_of, units, width + 128), BF),
        ]
        + [pltpu.VMEM(part, BF) for part in parts]
        + [pltpu.VMEM((3 * PAIR, hidden), F32)]
        + [
            pltpu.SemaphoreType.DMA((along,)),
            pltpu.SemaphoreType.DMA((along,)),
            pltpu.SemaphoreType.DMA((2, along)),
            pltpu.SemaphoreType.DMA((2, along)),
            pltpu.SemaphoreType.DMA((5,)),
            pltpu.SemaphoreType.DMA((3,)),
        ],
        compiler_params=pltpu.CompilerParams(
            collective_id=number, has_side_effects=True, vmem_limit_bytes=VMEM_LIMIT
        ),
        name="shared_expert",
    )(*arrays, normed, grads, weights, side, picked, first, mix)


BACK = 6
ROUTED_STEPS = 4


def routed_kernel(*refs):
    held_hbm, gate_up_hbm, down_hbm, values_hbm = refs[:6], refs[6], refs[7], refs[8]
    later_hbm, refs = refs[9:11], refs[2:]
    first_ref, second_ref, down_first_ref, down_second_ref = refs[9:13]
    back_refs, values_ref, refs = refs[13 : 13 + BACK], refs[13 + BACK], refs[14 + BACK :]
    adapter_ref = refs[0]
    own, move_sems, refs = refs[1:2], refs[2:6], refs[6:]
    held, back_buf, refs = refs[:6], refs[6 : 6 + BACK], refs[6 + BACK :]
    gate_up_buf, down_buf, total, total_down = refs[:4]
    send_sem, recv_sem, load_sem, own_sem, half_sem, later_send, later_recv = refs[4:]

    me = place_in("f")
    experts = GROUP_SIZE["f"]
    steps = ROUTED_STEPS
    loads = [
        pltpu.make_async_copy(held_hbm[i], held[i], load_sem.at[i]) for i in (0, 1, 4, 5)
    ]
    for offset in range(experts):
        if offset == 0 or soon(offset):
            source = lax.rem(me + experts - offset, experts)
            loads += [
                pltpu.make_async_copy(
                    block_of(held_hbm[2 + i], "rows", experts, source),
                    block_of(held[2 + i], "rows", experts, source),
                    half_sem.at[i, offset],
                )
                for i in range(2)
            ]
    loads += [
        pltpu.make_async_copy(gate_up_hbm.at[0, 0], gate_up_buf.at[0], load_sem.at[6]),
        pltpu.make_async_copy(gate_up_hbm.at[0, 1], gate_up_buf.at[1], load_sem.at[7]),
        pltpu.make_async_copy(down_hbm.at[0], down_buf, load_sem.at[8]),
    ]
    for load in loads:
        load.start()
    mover = Mover((("swap", "x"),), (values_hbm,), (values_ref,), own, *move_sems)
    mover.take()
    greet((("rows", "f"), ("swap", "x")))

    def later_copy(kind, offset):
        peer = lax.rem(me + offset, experts)
        return remote(
            block_of(later_hbm[kind], "rows", experts, peer),
            block_of(held[2 + kind], "rows", experts, me),
            later_send.at[kind, offset],
            later_recv.at[kind, offset],
            device_of("f", peer),
        )

    later = [offset for offset in range(1, experts) if not soon(offset)]
    for offset in sorted(later, key=lambda offset: -(offset % steps)):
        for kind in range(2):
            later_copy(kind, offset).start()
    mover.start()
    total[...] = jnp.zeros_like(total)
    total_down[...] = jnp.zeros_like(total_down)

    def back_copy(kind, peer, landing):
        return remote(
            block_of(back_buf[kind], "rows", experts, peer),
            block_of(back_refs[kind], "rows", experts, me),
            send_sem.at[kind, peer],
            recv_sem.at[kind, landing],
            device_of("f", peer),
        )

    def own_copy(kind):
        return pltpu.make_async_copy(
            block_of(back_buf[kind], "rows", experts, me),
            block_of(back_refs[kind], "rows", experts, me),
            own_sem.at[kind],
        )

    selectors = rest_selectors(experts // steps)
    spread = (row_index((128, LANES)) == lane_index((128, LANES)) // RANK).astype(BF)
    fold = (row_index((LANES, 128)) % RANK == lane_index((LANES, 128))).astype(BF)
    fold_later = (row_index((LANES, 128)) % RANK == lane_index((LANES, 128)) - RANK).astype(BF)
    for load in loads:
        load.wait()
    count, rest_count = held[0].shape[0] // steps, held[1].shape[0] // steps

    def block(step, carry):
        number = lax.rem(me + 1 + step, steps)

        for turn in range(steps // 2):

            @pl.when(step == steps - 1 - turn)
            def arrived():
                for offset in later:
                    if offset % steps == turn:
                        for kind in range(2):
                            later_copy(kind, offset).wait_recv()

        peers = [number + steps * turn for turn in range(experts // steps)]

        def read(ref):
            depth = ref.shape[0] // experts
            blocks = [ref[pl.ds(pl.multiple_of(peer * depth, depth), depth)] for peer in peers]
            return jnp.concatenate(blocks, axis=0)

        def write(ref, value):
            depth = ref.shape[0] // experts
            for turn, peer in enumerate(peers):
                part = value[turn * depth : (turn + 1) * depth]
                ref[pl.ds(pl.multiple_of(peer * depth, depth), depth)] = part

        rows = jnp.concatenate([read(held[0]), rest_to_rows(selectors, read(held[1]))], axis=0)
        grads = jnp.concatenate([read(held[2]), rest_to_rows(selectors, read(held[3]))], axis=0)
        notes = jnp.concatenate(
            [read(held[4]), dot(selectors[0], read(held[5])).astype(BF)], axis=0
        )
        pick = dot(notes, spread)
        gate_of = (
            notes[:, ADAPTER_COUNT : ADAPTER_COUNT + 1].astype(F32)
            + notes[:, ADAPTER_COUNT + 1 : ADAPTER_COUNT + 2].astype(F32)
        )
        grads_f = grads.astype(F32)
        lanes_gate = (dot_nt(rows, first_ref[0]) * pick).astype(BF)
        lanes_up = (dot_nt(rows, first_ref[1]) * pick).astype(BF)
        grad_routed = (gate_of * grads_f).astype(BF)
        grad_side = (dot_nt(grads, down_second_ref[1]) * gate_of * pick).astype(BF)
        gate = dot(rows, gate_up_buf[0]) + dot(lanes_gate, second_ref[0])
        upper = dot(rows, gate_up_buf[1]) + dot(lanes_up, second_ref[1])
        hidden, sigma, silu = swiglu(gate, upper)
        grad_hidden = dot_nt(grad_routed, down_buf[...]) + dot(grad_side, down_first_ref[...])
        grad_gate, grad_upper = swiglu_backward(gate, upper, sigma, silu, grad_hidden)
        side = (dot_nt(hidden, down_first_ref[...]).astype(BF).astype(F32) * pick).astype(BF)
        value = dot(hidden, down_buf[...]) + dot(side, down_second_ref[1])
        gate_grad = jnp.sum(grads_f * value, axis=1, keepdims=True)
        result = (gate_of * value).astype(BF)
        write(back_buf[4], result[:count])
        write(back_buf[5], rows_to_rest(selectors, result[count:]))
        back = (dot_nt(grad_gate, gate_up_buf[0]) + dot_nt(grad_upper, gate_up_buf[1])).astype(BF)
        back_gate = (dot_nt(grad_gate, second_ref[0]) * pick).astype(BF)
        back_up = (dot_nt(grad_upper, second_ref[1]) * pick).astype(BF)
        high, low = two_parts(gate_grad)
        lane = lane_index((count + rest_count // 4, 128))
        back_notes = jnp.where(
            lane == PAIR,
            high.astype(F32),
            jnp.where(
                lane == PAIR + 1, low.astype(F32), dot(back_gate, fold) + dot(back_up, fold_later)
            ),
        ).astype(BF)
        write(back_buf[0], back[:count])
        write(back_buf[1], rows_to_rest(selectors, back[count:]))
        write(back_buf[2], back_notes[:count])
        write(back_buf[3], dot_tn(selectors[0], back_notes[count:]).astype(BF))
        for peer in peers:

            @pl.when(peer == me)
            def keep():
                for kind in range(BACK):
                    own_copy(kind).start()

            @pl.when(peer != me)
            def send():
                for kind in range(BACK):
                    back_copy(kind, peer, me).start()

        total[:LANES] += dot_tn(lanes_gate, grad_gate)
        total[LANES : 2 * LANES] += dot_tn(lanes_up, grad_upper)
        total[2 * LANES :] += dot_tn(grad_side, hidden)
        total_down[...] += dot_tn(side, grad_routed)
        return carry

    lax.fori_loop(0, steps, block, 0)
    in_owner_columns(total, adapter_ref, total.shape[1] // experts)
    adapter_ref[3 * LANES :, :] = total_down[...].astype(BF)
    mover.finish()
    for offset in later:
        for kind in range(2):
            later_copy(kind, offset).wait_send()
    for kind in range(BACK):
        own_copy(kind).wait()

    def settle(offset, carry):
        peer = lax.rem(me + offset, experts)
        for kind in range(BACK):
            copy = back_copy(kind, peer, peer)
            copy.wait_send()
            copy.wait_recv()
        return carry

    lax.fori_loop(1, experts, settle, 0)


def routed_expert(number, held, later, values, first, second, down_first, down_second, gate_up, down):
    width, hidden = gate_up.shape[2:]
    experts = GROUP_SIZE["f"]
    vmem = pl.BlockSpec(memory_space=pltpu.VMEM)
    back = [held[0], held[1], held[4], held[5], held[0], held[1]]
    items = [("swap", "x", values)]
    return pl.pallas_call(
        routed_kernel,
        out_shape=[shape_of(array.shape, BF) for array in (*back, values)]
        + [shape_of((4 * LANES, experts * 128), BF)],
        in_specs=[HBM] * 11 + [vmem] * 4,
        out_specs=[HBM] * (BACK + 1) + [vmem],
        scratch_shapes=mover_scratch(items)
        + [pltpu.VMEM(array.shape, BF) for array in held]
        + [pltpu.VMEM(array.shape, BF) for array in back]
        + [
            pltpu.VMEM((2, width, hidden), BF),
            pltpu.VMEM((hidden, width), BF),
            pltpu.VMEM((3 * LANES, hidden), F32),
            pltpu.VMEM((LANES, width), F32),
            pltpu.SemaphoreType.DMA((BACK, experts)),
            pltpu.SemaphoreType.DMA((BACK, experts)),
            pltpu.SemaphoreType.DMA((9,)),
            pltpu.SemaphoreType.DMA((BACK,)),
            pltpu.SemaphoreType.DMA((2, experts)),
            pltpu.SemaphoreType.DMA((2, experts)),
            pltpu.SemaphoreType.DMA((2, experts)),
        ],
        compiler_params=pltpu.CompilerParams(
            collective_id=number, has_side_effects=True, vmem_limit_bytes=VMEM_LIMIT
        ),
        name="routed_expert",
    )(*held, gate_up, down, values, *later, first, second, down_first, down_second)


def after_experts_kernel(
    numbers_ref,
    parts_ref,
    part_notes_ref,
    main_ref,
    rest_ref,
    main_notes_ref,
    rest_notes_ref,
    grads_ref,
    normed_ref,
    residual_ref,
    small_ref,
    mixed_ref,
    routes_ref,
    side_ref,
    ffn_a_ref,
    ffn_b_ref,
    router_ref,
    router_a_ref,
    router_b_ref,
    mix_ref,
    gain_ref,
    down_a_ref,
    down_b_ref,
    first_a_ref,
    first_b_ref,
    second_a_ref,
    second_b_ref,
    weight_hbm,
    grad_residual_ref,
    grad_mixed_ref,
    adapter_ref,
    router_grad_ref,
    shared_side_ref,
    weight_ref,
    sem,
):
    load = pltpu.make_async_copy(weight_hbm, weight_ref, sem)
    load.start()
    experts = router_ref.shape[1]
    side = side_ref[...]
    pick = pair_pick(side, 1)
    grads = grads_ref[0]
    grads_f = grads.astype(F32)
    normed = normed_ref[...]
    out_lanes = small_ref[:, :PAIR].astype(BF)
    router_lanes = small_ref[:, PAIR : 2 * PAIR].astype(BF)
    gates = [small_ref[:, 2 * PAIR + k : 2 * PAIR + k + 1] for k in range(TOP)]
    mix = small_ref[:, 2 * PAIR + TOP : 2 * PAIR + TOP + 1]
    notes = sum(part_notes_ref[i].astype(F32) for i in range(part_notes_ref.shape[0]))
    shared_side = notes[:, :PAIR].astype(BF)
    shared_side_ref[...] = padded(shared_side)
    down_second = pair_of(down_a_ref, down_b_ref, 0)
    mix_total = (
        notes[:, 3 * PAIR : 3 * PAIR + 1]
        + notes[:, 3 * PAIR + 1 : 3 * PAIR + 2]
        + jnp.sum(shared_side.astype(F32) * dot_nt(grads, down_second), axis=1, keepdims=True)
    )
    grad_mix = mix_total * mix * (1.0 - mix)
    grad_shared = (mix * grads_f).astype(BF)
    expert_hot, main_hot, rest_hot = routing(routes_ref[0], experts)
    grad_gates = []
    mask = quarter_mask(rest_hot[0].shape, 0)
    token_notes = None
    for k in range(TOP):
        mine = dot(main_hot[k].astype(BF), main_notes_ref[...]) + dot(
            (rest_hot[k] * mask).astype(BF), rest_notes_ref[...]
        )
        grad_gates.append(mine[:, PAIR : PAIR + 1] + mine[:, PAIR + 1 : PAIR + 2])
        token_notes = mine if k == 0 else token_notes + mine
    inner = sum(gate * grad for gate, grad in zip(gates, grad_gates))
    grad_logits = sum(
        hot * (gate * (grad - inner)) for hot, gate, grad in zip(expert_hot, gates, grad_gates)
    )
    logits_high, logits_low = two_parts(grad_logits)
    router_second = jnp.concatenate([router_a_ref[0], router_b_ref[0]], axis=0)
    grad_router_lanes = dot_nt(logits_high, router_second) + dot_nt(logits_low, router_second)
    router_grad = dot_tn(router_lanes, logits_high) + dot_tn(router_lanes, logits_low)
    of_row = jnp.where(row_index((PAIR, 128)) < RANK, numbers_ref[0], numbers_ref[1]).astype(F32)
    router_grad_ref[...] = jnp.where(
        lane_index((PAIR, 128)) == experts, of_row, padded(router_grad)
    ).astype(BF)
    lane_grads = (
        jnp.concatenate(
            [
                grad_router_lanes,
                notes[:, PAIR : 3 * PAIR],
                token_notes[:, :RANK],
                token_notes[:, :RANK],
                token_notes[:, RANK:PAIR],
                token_notes[:, RANK:PAIR],
            ],
            axis=1,
        )
        * pair_pick(side, 5)
    ).astype(BF)
    factors = ffn_a_ref.shape[0]
    ffn_first = jnp.concatenate([pair_of(ffn_a_ref, ffn_b_ref, i) for i in range(factors)], axis=0)
    grad_second = (
        grad_mix * mix_ref[...].astype(F32)
        + dot_nt(logits_high, router_ref[...])
        + dot_nt(logits_low, router_ref[...])
        + sum(parts_ref[i].astype(F32) for i in range(parts_ref.shape[0]))
        + slots_to_rows(main_hot, rest_hot, main_ref[...], rest_ref[...])
        + dot(lane_grads, ffn_first)
    )
    grad_residual = grads_f + rms_backward(residual_ref[...], gain_ref[...], grad_second)
    grad_residual_ref[...] = grad_residual
    grad_attended = grad_residual.astype(BF)
    first, second = pair_of(first_a_ref, first_b_ref, 0), pair_of(second_a_ref, second_b_ref, 0)
    grad_out_lanes = (dot_nt(grad_attended, second) * pick).astype(BF)
    adapter_ref[...] = jnp.concatenate(
        [
            dot_tn(lane_grads, normed),
            dot_tn(grad_out_lanes, mixed_ref[...]),
            dot_tn(out_lanes, grad_attended),
            dot_tn(shared_side, grad_shared),
        ],
        axis=0,
    ).astype(BF)
    load.wait()
    grad_mixed_ref[...] = (
        dot_nt(grad_attended, weight_ref[...]) + dot(grad_out_lanes, first)
    ).astype(BF)


def after_experts(
    numbers, parts, part_notes, main, rest, main_notes, rest_notes, grads, normed, residual, small, mixed,
    routes, side, ffn_first, router, router_second, mix, gain, down_second, first, second, weight,
):
    tokens, width = normed.shape
    experts = router.shape[1]
    factors = ffn_first.shape[0]
    last = lambda which: pl.BlockSpec((1, 1, RANK, width), lambda n, a: (3, a[which], 0, 0))
    outs = [
        ((tokens, width), F32),
        ((tokens, width), BF),
        (((factors + 3) * PAIR, width), BF),
        ((PAIR, 128), BF),
        ((tokens, 128), BF),
    ]
    plain = (
        parts, part_notes, main, rest, main_notes, rest_notes, grads, normed, residual, small, mixed, routes,
        side,
    )
    return stage(
        after_experts_kernel,
        "after_experts",
        [shape_of(*out) for out in outs],
        [whole(array) for array in plain]
        + [
            of_sequence(0, (factors, 1, RANK, width)),
            of_sequence(1, (factors, 1, RANK, width)),
            whole(router),
            pl.BlockSpec((1, RANK, experts), lambda n, a: (a[0], 0, 0)),
            pl.BlockSpec((1, RANK, experts), lambda n, a: (a[1], 0, 0)),
            whole(mix),
            whole(gain),
            of_sequence(0, (1, 1, RANK, width)),
            of_sequence(1, (1, 1, RANK, width)),
            last(0),
            last(1),
            last(0),
            last(1),
            HBM,
        ],
        [pl.BlockSpec(shape, lambda n, a: (0, 0)) for shape, kind in outs],
        scratch=[pltpu.VMEM(weight.shape, BF), pltpu.SemaphoreType.DMA],
        prefetch=1,
    )(
        numbers, *plain, ffn_first, ffn_first, router, router_second, router_second, mix, gain, down_second,
        down_second, first, first, second, second, weight,
    )


def attention_back_kernel(plan, heads_plan, *refs):
    amount = len(plan)
    inputs, expert_hbm, refs = refs[:amount], refs[amount], refs[amount + 1 :]
    mixed_hbm, query_hbm, pairs_hbm, weight_hbm = refs[:4]
    place_ref, start_ref, key_place_ref, cos_ref, sin_ref, side_ref, lanes_ref, second_ref = refs[4:12]
    results, refs = refs[12:20], refs[20:]
    outputs, refs = refs[:amount], refs[amount:]
    heads_got, parts_ref, notes_ref, expert_ref, out_ref, refs = *refs[:5], refs[5:]
    own, move_sems, refs = refs[:amount], refs[amount : amount + 4], refs[amount + 4 :]
    heads_own, heads_sems, refs = refs[:1], refs[1:5], refs[5:]
    expert_own, expert_sems, refs = refs[:1], refs[1:5], refs[5:]
    mixed_buf, query_buf, pairs_buf, weight_buf = refs[:4]
    sent_buf, got_buf, grads_buf, heads_buf, parts_buf, notes_buf = refs[4:10]
    mixed_send, mixed_recv, pair_send, pair_recv, parts_send, parts_recv, load_sem, own_sem = refs[10:]

    x, y = place_in("x"), place_in("y")
    along, tokens, columns = mixed_buf.shape
    rows_all = along * tokens
    heads = columns // HEAD_DIM
    loads = [
        pltpu.make_async_copy(block_of(mixed_hbm, "columns", along, x), mixed_buf.at[x], load_sem.at[0]),
        pltpu.make_async_copy(query_hbm.at[0], query_buf, load_sem.at[1]),
        pltpu.make_async_copy(pairs_hbm, pairs_buf, load_sem.at[2]),
    ]
    loads += [
        pltpu.make_async_copy(weight_hbm.at[:, j], weight_buf.at[j], load_sem.at[3 + j])
        for j in range(3)
    ]
    for load in loads:
        load.start()
    mover = Mover(plan, inputs, outputs, own, *move_sems)
    mover.take()
    expert_mover = Mover((("rows", "x"),), (expert_hbm,), (expert_ref,), expert_own, *expert_sems)
    expert_mover.take()
    greet((("rows", "f"), ("swap", "x"), ("swap", "y")))

    def mixed_copy(offset):
        peer = lax.rem(x + offset, along)
        return remote(
            block_of(mixed_hbm, "columns", along, peer),
            mixed_buf.at[x],
            mixed_send.at[offset],
            mixed_recv.at[offset],
            device_of("x", peer),
        )

    def pair_copy(head):
        return remote(
            sent_buf.at[1 - y, head],
            got_buf.at[head],
            pair_send.at[head],
            pair_recv.at[head],
            device_of("y", 1 - y),
        )

    def parts_copy(offset):
        peer = lax.rem(x + offset, along)
        return remote(
            parts_buf.at[peer],
            parts_ref.at[x],
            parts_send.at[0, offset],
            parts_recv.at[0, offset],
            device_of("x", peer),
        )

    def notes_copy(offset):
        peer = lax.rem(x + offset, along)
        return remote(
            notes_buf.at[peer],
            notes_ref.at[x],
            parts_send.at[1, offset],
            parts_recv.at[1, offset],
            device_of("x", peer),
        )

    for offset in (2, 1, 3):
        mixed_copy(offset).start()
    for load in loads[:3]:
        load.wait()
    for offset in (1, 3, 2):
        mixed_copy(offset).wait_recv()
    expert_mover.start()

    step = rows_all // 2

    def head_block(head, carry):
        here = pl.ds(pl.multiple_of(head * HEAD_DIM, HEAD_DIM), HEAD_DIM)
        keys = pairs_buf[:, 0, :, here].reshape(-1, HEAD_DIM)
        values = pairs_buf[:, 1, :, here].reshape(-1, HEAD_DIM)
        key_total, value_total = None, None
        for i in range(2):
            at = slice(i * step, (i + 1) * step)
            query = query_buf[at, here]
            blocks = along // 2
            grad = mixed_buf[i * blocks : (i + 1) * blocks, :, here].reshape(step, HEAD_DIM)
            probs = probabilities(query, keys, place_ref[at], start_ref[at], key_place_ref[...])
            grad_probs = dot_nt(grad, values)
            mean = jnp.sum(probs * grad_probs, axis=1, keepdims=True)
            grad_scores = (probs * (grad_probs - mean)).astype(BF)
            grad_query = dot(grad_scores, keys) * (HEAD_DIM**-0.5)
            grads_buf[0, at, here] = (
                grad_query * cos_ref[at] - half_turn(grad_query) * sin_ref[at]
            ).astype(BF)
            grad_keys = dot_tn(grad_scores, query) * (HEAD_DIM**-0.5)
            grad_values = dot_tn(probs.astype(BF), grad)
            key_total = grad_keys if i == 0 else key_total + grad_keys
            value_total = grad_values if i == 0 else value_total + grad_values
        for half in range(2):
            at = slice(half * rows_all, (half + 1) * rows_all)
            sent_buf[half, head, 0] = key_total[at].astype(BF)
            sent_buf[half, head, 1] = value_total[at].astype(BF)
        pair_copy(head).start()
        return carry

    lax.fori_loop(0, heads, head_block, 0)
    combine_kernel(*results, out_ref)

    def head_sum(head, carry):
        here = pl.ds(pl.multiple_of(head * HEAD_DIM, HEAD_DIM), HEAD_DIM)
        pair_copy(head).wait_recv()
        key = sent_buf[y, head, 0].astype(F32) + got_buf[head, 0].astype(F32)
        grads_buf[1, :, here] = (key * cos_ref[...] - half_turn(key) * sin_ref[...]).astype(BF)
        value = sent_buf[y, head, 1].astype(F32) + got_buf[head, 1].astype(F32)
        grads_buf[2, :, here] = value.astype(BF)
        return carry

    lax.fori_loop(0, heads, head_sum, 0)
    pick = pair_pick(side_ref[...], 1)
    notes = []
    heads_buf[...] = jnp.zeros_like(heads_buf)
    own_columns = pl.ds(pl.multiple_of(x * columns, columns), columns)
    for j in range(3):
        at = slice(j * PAIR, (j + 1) * PAIR)
        notes.append((dot_nt(grads_buf[j], second_ref[at]) * pick).astype(BF))
        heads_buf[at, own_columns] = dot_tn(lanes_ref[j], grads_buf[j]).astype(BF)
    notes_buf[...] = padded(jnp.concatenate(notes, axis=1)).reshape(notes_buf.shape)
    heads_mover = Mover(heads_plan, (heads_buf,), (heads_got,), heads_own, *heads_sems)
    heads_mover.take()
    heads_mover.start()
    for offset in (1, 3, 2):
        notes_copy(offset).start()
    mover.start()
    own_notes = pltpu.make_async_copy(notes_buf.at[x], notes_ref.at[x], own_sem.at[0])
    own_notes.start()
    for load in loads[3:]:
        load.wait()

    def own_parts():
        return pltpu.make_async_copy(parts_buf.at[x], parts_ref.at[x], own_sem.at[1])

    def row_block(number, carry):
        offset = x_step(lax.rem(number + 1, along))
        peer = lax.rem(x + offset, along)
        at = pl.ds(pl.multiple_of(peer * tokens, tokens), tokens)
        total = None
        for j in range(3):
            part = dot_nt(grads_buf[j, at], weight_buf[j].reshape(-1, columns))
            total = part if total is None else total + part
        parts_buf[peer] = total.astype(BF)

        @pl.when(number < along - 1)
        def send():
            parts_copy(offset).start()

        @pl.when(number == along - 1)
        def keep():
            own_parts().start()

        return carry

    lax.fori_loop(0, along, row_block, 0)
    mover.finish()
    heads_mover.finish()
    expert_mover.finish()
    own_notes.wait()
    own_parts().wait()

    def pairs_sent(head, carry):
        pair_copy(head).wait_send()
        return carry

    lax.fori_loop(0, heads, pairs_sent, 0)
    for offset in range(1, along):
        mixed_copy(offset).wait_send()
        parts_copy(offset).wait()
        notes_copy(offset).wait()


def attention_back(number, items, expert, mixed, query, pairs, weight, small, results):
    plan = tuple((kind, group) for kind, group, array in items)
    arrays = [array for kind, group, array in items]
    along = GROUP_SIZE["x"]
    tokens, width = mixed.shape
    columns = width // along
    heads = columns // HEAD_DIM
    rows_all = along * tokens
    heads_items = [("from_columns", "f", shape_of((3 * PAIR, width), BF))]
    vmem = pl.BlockSpec(memory_space=pltpu.VMEM)
    outs = [shape_of(exchanged_shape(kind, group, array.shape), BF) for kind, group, array in items]
    outs += [
        shape_of(exchanged_shape("from_columns", "f", (3 * PAIR, width)), BF),
        shape_of((along, tokens, width), BF),
        shape_of((along, tokens, 128), BF),
        shape_of(expert.shape, BF),
        shape_of((1, tokens, width), BF),
    ]
    dma = pltpu.SemaphoreType.DMA
    return pl.pallas_call(
        functools.partial(attention_back_kernel, plan, (("from_columns", "f"),)),
        out_shape=outs,
        in_specs=[HBM] * (len(items) + 5) + [vmem] * (len(small) + len(results)),
        out_specs=[HBM] * (len(items) + 4) + [vmem],
        scratch_shapes=mover_scratch(items)
        + mover_scratch(heads_items)
        + mover_scratch([("rows", "x", expert)])
        + [
            pltpu.VMEM((along, tokens, columns), BF),
            pltpu.VMEM((rows_all, columns), BF),
            pltpu.VMEM(pairs.shape, BF),
            pltpu.VMEM((3, *weight.shape[:1], *weight.shape[2:]), BF),
            pltpu.VMEM((2, heads, 2, rows_all, HEAD_DIM), BF),
            pltpu.VMEM((heads, 2, rows_all, HEAD_DIM), BF),
            pltpu.VMEM((3, rows_all, columns), BF),
            pltpu.VMEM((3 * PAIR, width), BF),
            pltpu.VMEM((along, tokens, width), BF),
            pltpu.VMEM((along, tokens, 128), BF),
            dma((along,)),
            dma((along,)),
            dma((heads,)),
            dma((heads,)),
            dma((2, along)),
            dma((2, along)),
            dma((6,)),
            dma((2,)),
        ],
        compiler_params=pltpu.CompilerParams(
            collective_id=number, has_side_effects=True, vmem_limit_bytes=VMEM_LIMIT
        ),
        name="attention_back",
    )(*arrays, expert, mixed, query, pairs, weight, *small, *results)


def lane_expansion(ids_ref, group):
    ids = ids_ref[group][:, GROUP_SIZE["f"] : GROUP_SIZE["f"] + 1].astype(F32)
    lane = lane_index((PAIR, LANES))
    same = (lane // RANK).astype(F32) == ids
    return (same & (lane % RANK == row_index((PAIR, LANES)) % RANK)).astype(BF)


def expanded(expansions, got_ref, factor):
    total = None
    for group, expansion in enumerate(expansions):
        part = dot_tn(expansion, got_ref[group, factor * PAIR : (factor + 1) * PAIR, :])
        total = part if total is None else total + part
    return total.astype(BF)


FINISH = (
    (("from_columns", "f"),),
    (("from_columns", "f"),),
    (("rows", "c"), ("rows", "y")),
    (("gather", "c"), ("gather", "c"), ("gather", "c")),
    (("rows", "c"),),
    (("gather", "c"),),
)


def finish_kernel(*refs):
    parts_ref, notes_ref, rows_ref, normed_ref, residual_ref, gain_ref, first_ref = refs[:7]
    ids_ref, early_ref, shared_ref, heads_ref, column_ref, expert_ref = refs[7:13]
    grad_out, attn_in, attn_out, ffn_out, router_out, shared_out, shared_in_out = refs[13:20]
    expert_out, expert_in_out, down_out, expert_buf, refs = *refs[20:24], refs[24:]
    late_buf, late_got, early_buf, early_parts, shared_buf, shared_parts = refs[:6]
    expert_got, late_sum, early_row, shared_row, expert_sum = refs[6:11]
    late_all, early_all, shared_all, expert_all, late_parts, late_row, refs = *refs[11:17], refs[17:]
    ends = (
        ((expert_buf,), (expert_got,)),
        ((late_buf,), (late_got,)),
        ((early_buf, shared_buf), (early_parts, shared_parts)),
        ((early_row, shared_row, expert_sum), (early_all, shared_all, expert_all)),
        ((late_sum,), (late_parts,)),
        ((late_row,), (late_all,)),
    )
    movers = []
    for plan, (inputs, outputs) in zip(FINISH, ends):
        own, sems, refs = refs[: len(plan)], refs[len(plan) : len(plan) + 4], refs[len(plan) + 4 :]
        movers.append(Mover(plan, inputs, outputs, own, *sems))

    def begin(mover):
        mover.take()
        mover.start()

    greet((("rows", "f"), ("rows", "c"), ("rows", "y")))
    lanes = sum(notes_ref[i].astype(F32) for i in range(notes_ref.shape[0]))[:, : 3 * PAIR]
    lanes = lanes.astype(BF)
    late_buf[...] = dot_tn(lanes, normed_ref[...]).astype(BF)
    begin(movers[1])
    count = expert_buf.shape[0]
    expert_buf[...] = sum(
        expert_ref[i * count : (i + 1) * count].astype(F32) for i in range(GROUP_SIZE["x"])
    ).astype(BF)
    begin(movers[0])

    groups = ids_ref.shape[0]
    expansions = [lane_expansion(ids_ref, group) for group in range(groups)]
    row = 0
    for got in (early_ref, heads_ref):
        for factor in range(got.shape[1] // PAIR):
            early_buf[row : row + LANES, :] = expanded(expansions, got, factor)
            row += LANES
    router = None
    for group in range(groups):
        part = dot_tn(expansions[group], ids_ref[group])
        router = part if router is None else router + part
    router = jnp.sum(router * column_ref[...].astype(F32), axis=1, keepdims=True)
    early_buf[row : row + LANES, :] = jnp.broadcast_to(router, (LANES, 128)).astype(BF)
    for factor in range(shared_ref.shape[1] // PAIR):
        shared_buf[factor * LANES : (factor + 1) * LANES, :] = expanded(
            expansions, shared_ref, factor
        )
    begin(movers[2])

    grad = sum(parts_ref[i].astype(F32) for i in range(parts_ref.shape[0]))
    grad = grad + dot(lanes, first_ref[...])
    total = residual_ref[...] + rms_backward(rows_ref[0].astype(F32), gain_ref[...], grad)
    grad_out[0] = total.astype(BF)

    movers[1].finish()
    for factor in range(late_got.shape[1] // PAIR):
        late_sum[factor * LANES : (factor + 1) * LANES, :] = expanded(expansions, late_got, factor)
    begin(movers[4])
    movers[0].finish()
    expert_sum[...] = sum(expert_got[i].astype(F32) for i in range(groups)).astype(BF)
    movers[2].finish()
    count = early_row.shape[0]
    early_row[...] = sum(
        early_parts[i * count : (i + 1) * count].astype(F32) for i in range(GROUP_SIZE["c"])
    ).astype(BF)
    count = shared_row.shape[0]
    shared_row[...] = (
        shared_parts[:count].astype(F32) + shared_parts[count:].astype(F32)
    ).astype(BF)
    begin(movers[3])
    movers[4].finish()
    count = late_row.shape[0]
    late_row[...] = sum(
        late_parts[i * count : (i + 1) * count].astype(F32) for i in range(GROUP_SIZE["c"])
    ).astype(BF)
    begin(movers[5])

    movers[3].finish()
    early = early_all[...].reshape(-1, 128).astype(F32)
    expert = jnp.concatenate(
        [
            expert_all[2 * i].astype(F32) + expert_all[2 * i + 1].astype(F32)
            for i in range(GROUP_SIZE["x"])
        ],
        axis=0,
    )
    factor = [early[i * LANES : (i + 1) * LANES] for i in range(early.shape[0] // LANES)]
    attn_in[3 * LANES :, :] = factor[5]
    attn_out[: 3 * LANES, :] = jnp.concatenate(factor[8:11], axis=0)
    attn_out[3 * LANES :, :] = factor[6]
    ffn_out[...] = jnp.concatenate(factor[:5], axis=0)
    router_out[...] = factor[11][:, : router_out.shape[1]]
    down_out[:LANES, :] = factor[7]
    down_out[LANES:, :] = expert[3 * LANES :]
    expert_out[...] = expert[: 2 * LANES, : expert_out.shape[1]]
    expert_in_out[...] = expert[2 * LANES : 3 * LANES, : expert_in_out.shape[1]]
    along = GROUP_SIZE["x"]
    columns = shared_out.shape[1] // along
    quarters = [
        shared_all[2 * i : 2 * i + 2].reshape(-1, 128)[:, :columns].astype(F32) for i in range(along)
    ]
    shared_rows = jnp.concatenate(quarters, axis=1)
    shared_out[...] = shared_rows[: 2 * LANES]
    shared_in_out[...] = shared_rows[2 * LANES :]
    movers[5].finish()
    attn_in[: 3 * LANES, :] = late_all[...].reshape(-1, 128).astype(F32)


def finish(
    number, parts, notes, rows, normed, residual, gain, first, ids, early, shared, heads, column, expert,
    shared_columns, expert_columns,
):
    tokens, width = normed.shape
    groups, ctx = GROUP_SIZE["f"], GROUP_SIZE["c"]
    early_rows = ((early.shape[1] + heads.shape[1]) // PAIR + 1) * LANES
    late_rows = first.shape[0] // PAIR * LANES
    shared_rows = shared.shape[1] // PAIR * LANES
    expert_rows = expert.shape[0] // GROUP_SIZE["x"]
    vmem = pl.BlockSpec(memory_space=pltpu.VMEM)
    bufs = [
        first.shape,
        (groups, first.shape[0], 128),
        (early_rows, 128),
        (early_rows, 128),
        (shared_rows, 128),
        (shared_rows, 128),
        (groups, expert_rows, 128),
        (late_rows, 128),
        (early_rows // ctx, 128),
        (shared_rows // 2, 128),
        (expert_rows, 128),
        (ctx, late_rows // ctx, 128),
        (ctx, early_rows // ctx, 128),
        (ctx, shared_rows // 2, 128),
        (ctx, expert_rows, 128),
        (late_rows, 128),
        (late_rows // ctx, 128),
    ]
    sent = (((expert_rows, width),), (bufs[0],), (bufs[2], bufs[4]), (bufs[8], bufs[9], bufs[10]), (bufs[7],), (bufs[16],))
    scratch = [pltpu.VMEM(buf, BF) for buf in ((expert_rows, width), *bufs)]
    for plan, shapes in zip(FINISH, sent):
        scratch += mover_scratch(
            [(kind, group, shape_of(shape, BF)) for (kind, group), shape in zip(plan, shapes)]
        )
    outs = [
        shape_of(rows.shape, BF),
        shape_of((4 * LANES, 128), F32),
        shape_of((4 * LANES, 128), F32),
        shape_of((5 * LANES, 128), F32),
        shape_of((LANES, 1), F32),
        shape_of((2 * LANES, shared_columns), F32),
        shape_of((LANES, shared_columns), F32),
        shape_of((2 * LANES, expert_columns), F32),
        shape_of((LANES, expert_columns), F32),
        shape_of((2 * LANES, 128), F32),
    ]
    return pl.pallas_call(
        finish_kernel,
        out_shape=outs,
        in_specs=[vmem] * 13,
        out_specs=[vmem] * len(outs),
        scratch_shapes=scratch,
        compiler_params=pltpu.CompilerParams(
            collective_id=number, has_side_effects=True, vmem_limit_bytes=VMEM_LIMIT
        ),
        name="finish",
    )(parts, notes, rows, normed, residual, gain, first, ids, early, shared, heads, column, expert)


def combine_kernel(
    main_ref, rest_ref, routes_ref, residual_ref, parts_ref, side_ref, small_ref, picked_ref, out_ref
):
    experts = main_ref.shape[0] // MAIN
    unused, main_hot, rest_hot = routing(routes_ref[0], experts)
    mixture = slots_to_rows(main_hot, rest_hot, main_ref[...], rest_ref[...])
    shared = sum(parts_ref[i].astype(F32) for i in range(parts_ref.shape[0]))
    shared = shared + dot(side_ref[:, :PAIR], picked_ref[2 * PAIR :])
    mix = small_ref[:, 2 * PAIR + TOP : 2 * PAIR + TOP + 1]
    out_ref[0] = (residual_ref[...] + mixture + mix * shared).astype(BF)


def shards(
    layer_hidden_input,
    output_cotangent,
    sequence_pair_lengths,
    block_placement_order,
    sequence_adapter_index,
    token_expert_choices,
    attention_norm_gain,
    feedforward_norm_gain,
    query_key_value_weight,
    output_projection_weight,
    query_key_value_bias,
    router_weight_matrix,
    shared_gate_up_weight,
    shared_down_weight,
    shared_sigmoid_gate,
    routed_gate_up_weight,
    routed_down_weight,
    attention_adapter_first,
    attention_adapter_second,
    feedforward_adapter_first,
    router_adapter_second,
    shared_gate_adapter_second,
    shared_down_adapter_first,
    routed_gate_adapter_second,
    routed_down_adapter_first,
    down_adapter_second,
):
    tokens, width = layer_hidden_input.shape[1:]
    experts = router_weight_matrix.shape[1]
    capacity = tokens * TOP // experts * 9 // 8
    tail = capacity - MAIN
    ctx_count = lax.axis_size("ctx")
    group_rows = tokens * ctx_count
    along = ctx_count // 2
    rows_shared = tokens * along
    x_index = lax.axis_index("ctx") // 2
    y_index = lax.axis_index("ctx") % 2
    head_columns = width // along
    hidden = shared_down_weight.shape[0]
    quarter = hidden // along
    shards_of = lax.axis_size("fsdp")
    lengths = sequence_pair_lengths[0]
    order = block_placement_order[0]
    adapters = sequence_adapter_index[0]
    block_size = group_rows // order.shape[0]

    qkv_own = lax.dynamic_slice_in_dim(
        query_key_value_weight, x_index * head_columns, head_columns, 2
    ).reshape(-1, head_columns)
    out_weight = lax.all_gather(output_projection_weight, "fsdp", tiled=True)
    units = -(-quarter // 32) * 32
    own_up = jnp.swapaxes(
        lax.dynamic_slice_in_dim(shared_gate_up_weight, x_index * quarter, quarter, 2), 1, 2
    )
    own_down = lax.dynamic_slice_in_dim(shared_down_weight, x_index * quarter, quarter, 0)
    own_shared = jnp.pad(
        jnp.concatenate([own_up, own_down[None]]), ((0, 0), (0, units - quarter), (0, 0))
    ).reshape(3 * units, width)

    def of_group(factor):
        parts = [lax.dynamic_index_in_dim(factor, adapters[s], -3, keepdims=True) for s in range(2)]
        both = jnp.concatenate(parts, axis=-3)
        return both.reshape(both.shape[:-3] + (PAIR, both.shape[-1]))

    shared_second = jnp.concatenate(
        [
            of_group(shared_gate_adapter_second).reshape(2 * PAIR, hidden * shards_of),
            of_group(shared_down_adapter_first),
        ],
        axis=0,
    )
    shared_second = lax.dynamic_index_in_dim(
        shared_second.reshape(3 * PAIR, shards_of, along, quarter), x_index, 2, keepdims=False
    )
    shared_second = jnp.pad(shared_second, ((0, 0), (0, 0), (0, units - quarter)))
    shared_second = shared_second.reshape(3, PAIR, shards_of, units).transpose(0, 2, 3, 1)
    shared_second = jnp.stack(
        [
            jnp.pad(shared_second[i], ((0, 0), (0, 0), (before, 128 - PAIR - before)))
            for i, before in enumerate((0, PAIR, 0))
        ]
    )
    numbers = jnp.concatenate([adapters, x_index[None].astype(jnp.int32)])

    start = lengths[0]
    block_rows = jnp.arange(block_size, dtype=jnp.int32)
    blocks = order.reshape(along, 2, -1)
    key_places = (jnp.swapaxes(blocks, 0, 1).reshape(-1)[:, None] * block_size + block_rows).reshape(
        1, group_rows
    )
    own_blocks = lax.dynamic_index_in_dim(blocks, y_index, 1, keepdims=False).reshape(-1)
    places = own_blocks[:, None] * block_size + block_rows
    second = places >= start
    fractions = jnp.arange(0, HEAD_DIM, 2).astype(F32) / HEAD_DIM
    speeds = rope_theta ** (-fractions)
    bases = jnp.stack([own_blocks * block_size, own_blocks * block_size - start])
    base_angles = bases.astype(F32)[:, :, None, None] * speeds
    base_angles = jnp.concatenate([base_angles, base_angles], axis=3)
    base_cos, base_sin = jnp.cos(base_angles), jnp.sin(base_angles)
    base_cos = jnp.where(second[:, :, None], base_cos[1], base_cos[0])
    base_sin = jnp.where(second[:, :, None], base_sin[1], base_sin[0])
    row_angles = block_rows.astype(F32)[:, None] * speeds[None, :]
    row_angles = jnp.concatenate([row_angles, row_angles], axis=1)
    row_cos, row_sin = jnp.cos(row_angles), jnp.sin(row_angles)
    cosine = base_cos * row_cos - base_sin * row_sin
    sine = base_sin * row_cos + base_cos * row_sin
    sine = jnp.where(jnp.arange(HEAD_DIM) < HEAD_DIM // 2, -sine, sine)
    cosine, sine = cosine.reshape(rows_shared, HEAD_DIM), sine.reshape(rows_shared, HEAD_DIM)
    place_column = places.reshape(rows_shared, 1)
    start_column = jnp.where(second, start, 0).reshape(rows_shared, 1)
    side_shared = second.astype(F32).reshape(rows_shared, 1)
    side = lax.dynamic_slice_in_dim(side_shared, x_index * tokens, tokens)

    attention_gain = attention_norm_gain[None, :]
    feedforward_gain = feedforward_norm_gain[None, :]
    mix_weight = shared_sigmoid_gate[None, :]
    routed_second = routed_gate_adapter_second.reshape(2, LANES, -1)
    routed_first = routed_down_adapter_first.reshape(LANES, -1)
    ffn_flat = feedforward_adapter_first.reshape(-1, LANES, width)[3:]
    down_flat = down_adapter_second.reshape(2, LANES, width)

    normed_one, sent_grads_main, sent_grads_rest, picked, picked_first, picked_second = prologue(
        numbers,
        layer_hidden_input,
        output_cotangent,
        attention_gain,
        token_expert_choices,
        feedforward_adapter_first,
        down_adapter_second,
        attention_adapter_first,
        attention_adapter_second,
        experts,
        head_columns,
    )
    own_shared, normed_one = lax.optimization_barrier((own_shared, normed_one))
    shared_weight = lax.all_gather(own_shared, "fsdp")
    qkv, normed_shared = exchange(
        "gather_first", 0, ("share", "s", qkv_own), ("gather", "x", normed_one)
    )
    qkv = qkv.reshape(shards_of, 3, tokens, head_columns)
    projected, qkv_lanes = project(
        numbers,
        normed_shared.reshape(rows_shared, width),
        qkv,
        attention_adapter_first,
        attention_adapter_second,
        query_key_value_bias,
        side_shared,
        cosine,
        sine,
    )
    pairs, grads_shared = exchange(
        "keys", 1, ("gather", "y", projected[1:]), ("gather", "x", output_cotangent[0])
    )
    mixed_heads = attend(projected, pairs, place_column, start_column, key_places)
    (mixed,) = exchange(
        "mixed", 2, ("to_columns", "x", mixed_heads.reshape(along, tokens, head_columns))
    )
    residual, normed_two, small, sent_main, sent_rest, notes_main, notes_rest = after_attention(
        numbers,
        mixed,
        out_weight,
        layer_hidden_input,
        attention_adapter_first,
        attention_adapter_second,
        feedforward_gain,
        feedforward_adapter_first,
        router_weight_matrix,
        router_adapter_second,
        mix_weight,
        token_expert_choices,
        side,
    )
    *held, parts_rows, parts_lanes, value_part, shared_columns = shared_expert(
        3,
        normed_two,
        [
            ("rows", "f", sent_main),
            ("rows", "f", sent_rest),
            ("half", "f", sent_grads_main),
            ("half", "f", sent_grads_rest),
            ("rows", "f", notes_main),
            ("rows", "f", notes_rest),
        ],
        grads_shared,
        shared_weight,
        side_shared.reshape(along, tokens, 1),
        picked,
        shared_second,
        mix_weight,
    )
    (
        got_main,
        got_rest,
        got_notes_main,
        got_notes_rest,
        result_main,
        result_rest,
        value_parts,
        expert_columns,
    ) = routed_expert(
        4,
        held,
        (sent_grads_main, sent_grads_rest),
        value_part,
        ffn_flat,
        routed_second,
        routed_first,
        down_flat,
        routed_gate_up_weight,
        routed_down_weight,
    )
    grad_residual, grad_mixed, early_columns, router_rows, shared_side = after_experts(
        numbers,
        parts_rows,
        parts_lanes,
        got_main,
        got_rest,
        got_notes_main,
        got_notes_rest,
        output_cotangent,
        normed_two,
        residual,
        small,
        mixed,
        token_expert_choices,
        side,
        feedforward_adapter_first,
        router_weight_matrix,
        router_adapter_second,
        mix_weight,
        feedforward_gain,
        down_adapter_second,
        attention_adapter_first,
        attention_adapter_second,
        out_weight,
    )

    early_got, shared_got, router_got, heads_got, first_parts, first_lanes, expert_parts, output_value = (
        attention_back(
            5,
            [
                ("from_columns", "f", early_columns),
                ("from_columns", "f", shared_columns),
                ("gather", "f", router_rows),
            ],
            expert_columns,
            grad_mixed,
            projected,
            pairs,
            qkv,
            (
                place_column,
                start_column,
                key_places,
                cosine,
                sine,
                side_shared,
                qkv_lanes,
                picked_second,
            ),
            (
                result_main,
                result_rest,
                token_expert_choices,
                residual,
                value_parts,
                shared_side,
                small,
                picked,
            ),
        )
    )
    own_column = (jnp.arange(128) == lax.axis_index("fsdp")).astype(BF)[None, :]
    grads = finish(
        6,
        first_parts,
        first_lanes,
        layer_hidden_input,
        normed_one,
        grad_residual,
        attention_gain,
        picked_first,
        router_got,
        early_got,
        shared_got,
        heads_got,
        own_column,
        expert_parts,
        along * quarter,
        routed_down_weight.shape[1] // shards_of,
    )

    def by_adapter(rows):
        parts = rows.reshape(-1, ADAPTER_COUNT, RANK, rows.shape[1])
        return parts[0] if parts.shape[0] == 1 else parts

    return (output_value, grads[0], *(by_adapter(rows) for rows in grads[1:]))


def solution(mesh):
    return jax.shard_map(
        shards,
        mesh=mesh,
        in_specs=(
            P("fsdp", "ctx", None),
            P("fsdp", "ctx", None),
            P("fsdp", None),
            P("fsdp", None),
            P("fsdp", None),
            P("fsdp", "ctx", None),
            P(),
            P(),
            P(None, "fsdp", None),
            P("fsdp", None),
            P(),
            P(),
            P(None, None, "fsdp"),
            P("fsdp", None),
            P(),
            P("fsdp", None, None, None),
            P("fsdp", None, None),
            P(),
            P(),
            P(),
            P(),
            P(),
            P(),
            P(),
            P(),
            P(),
        ),
        out_specs=(
            P("fsdp", "ctx", None),
            P("fsdp", "ctx", None),
            P(None, None, None, "fsdp"),
            P(None, None, None, "fsdp"),
            P(None, None, None, "fsdp"),
            P(None, None, "fsdp"),
            P(None, None, None, "fsdp"),
            P(None, None, "fsdp"),
            P(None, None, None, "fsdp"),
            P(None, None, "fsdp"),
            P(None, None, None, "fsdp"),
        ),
        check_vma=False,
    )
```

```python
import functools

import jax
import jax.numpy as jnp
from jax import lax
from jax.experimental import pallas as pl
from jax.experimental.pallas import tpu as pltpu
from jax.sharding import PartitionSpec as P

HEADS = 16
HEAD_DIM = 128
TOP = 4
ADAPTER_COUNT = 8
RANK = 16
LANES = ADAPTER_COUNT * RANK
PAIR = 2 * RANK
MAIN = 32

norm_eps = 1e-06
rope_theta = 1000000.0
masked_score = -1e30
highest = lax.Precision.HIGHEST
MESH = pl.DeviceIdType.MESH
BF = jnp.bfloat16
F32 = jnp.float32
VMEM_LIMIT = 56 * 2**20


def dot(left, right):
    return jnp.dot(left, right, preferred_element_type=F32)


def dot_nt(left, right):
    return lax.dot_general(left, right, (((1,), (1,)), ((), ())), preferred_element_type=F32)


def dot_tn(left, right):
    return lax.dot_general(left, right, (((0,), (0,)), ((), ())), preferred_element_type=F32)


GROUP_SIZE = {"x": 4, "y": 2, "c": 8, "f": 16}


def place_in(group):
    ctx, fsdp = lax.axis_index("ctx"), lax.axis_index("fsdp")
    return {"x": ctx // 2, "y": ctx % 2, "c": ctx, "f": fsdp}[group]


def device_of(group, index):
    ctx, fsdp = lax.axis_index("ctx"), lax.axis_index("fsdp")
    if group == "x":
        return (index * 2 + ctx % 2, fsdp)
    if group == "y":
        return ((ctx // 2) * 2 + index, fsdp)
    if group == "c":
        return (index, fsdp)
    return (ctx, index)


def chip():
    ctx, fsdp = lax.axis_index("ctx"), lax.axis_index("fsdp")
    return ctx % 2 * 2 + fsdp // 8, fsdp // 2 % 4, fsdp % 2


def device_at(y, z, core):
    return (lax.axis_index("ctx") // 2 * 2 + y // 2, y % 2 * 8 + z * 2 + core)


def shard_at(y, z, core):
    return y % 2 * 8 + z * 2 + core


def exchanged_shape(kind, group, shape):
    if kind == "share":
        return (GROUP_SIZE["f"],) + shape
    count = GROUP_SIZE[group]
    if kind == "gather":
        return (count,) + shape
    if kind in ("swap", "rows", "half"):
        return shape
    if kind == "from_columns":
        return (count, shape[0], shape[1] // count)
    return (shape[1], count * shape[2])


def own_shape(kind, group, shape):
    if kind in ("gather", "share"):
        return shape
    count = GROUP_SIZE[group]
    if kind in ("rows", "half"):
        return (shape[0] // count,) + shape[1:]
    if kind == "from_columns":
        return (shape[0], shape[1] // count)
    return shape[1:]


def copies_of(kind, group):
    return 23 if kind == "share" else GROUP_SIZE[group] - 1


def soon(offset):
    return offset % ROUTED_STEPS >= ROUTED_STEPS // 2


def block_of(ref, kind, count, index):
    if kind == "rows":
        depth = ref.shape[0] // count
        return ref.at[pl.ds(pl.multiple_of(index * depth, depth), depth)]
    if kind == "columns":
        width = ref.shape[1] // count
        return ref.at[:, pl.ds(pl.multiple_of(index * width, width), width)]
    return ref.at[index]


def source_of(kind, group, ref, index):
    if kind in ("gather", "share"):
        return ref
    cut = {"rows": "rows", "half": "rows", "from_columns": "columns"}.get(kind, "first")
    return block_of(ref, cut, GROUP_SIZE[group], index)


def target_of(kind, group, ref, index):
    cut = {"rows": "rows", "half": "rows", "to_columns": "columns"}.get(kind, "first")
    return block_of(ref, cut, GROUP_SIZE["f" if kind == "share" else group], index)


def remote(source, target, send, recv, device):
    return pltpu.make_async_remote_copy(
        src_ref=source,
        dst_ref=target,
        send_sem=send,
        recv_sem=recv,
        device_id=device,
        device_id_type=MESH,
    )


def greet(plan):
    barrier = pltpu.get_barrier_semaphore()
    count = 0
    for group in sorted({group for kind, group in plan}):
        if group == "s":
            y, z, core = chip()
            peers = [device_at(y, lax.rem(z + d, 4), core) for d in (1, 2, 3)]
            peers += [device_at(lax.rem(y + d, 4), z, core) for d in (1, 3)]
            peers += [device_at(y, z, 1 - core)]
        else:
            size = GROUP_SIZE[group]
            mine = place_in(group)
            peers = [device_of(group, lax.rem(mine + d, size)) for d in range(1, size)]
        for peer in peers:
            pl.semaphore_signal(barrier, inc=1, device_id=peer, device_id_type=MESH)
        count += len(peers)
    pl.semaphore_wait(barrier, count)


class Share:
    def __init__(self, source, target, send, recv, first):
        self.target = target
        self.sems = (send, recv, first)
        y, z, core = self.place = chip()
        self.order = (1, 3, 2)
        self.source = source
        self.along_z = [
            self.copy(source, shard_at(y, z, core), None, i, device_at(y, lax.rem(z + d, 4), core))
            for i, d in enumerate(self.order)
        ]
        self.along_y, self.across = [], []

    def copy(self, source, shard, half, number, device):
        send, recv, first = self.sems
        target = self.target.at[shard]
        if half is not None:
            target = target.at[half]
        return remote(source, target, send.at[first + number], recv.at[first + number], device)

    def halves(self):
        half = self.target.shape[1] // 2
        return pl.ds(0, half), pl.ds(half, half)

    def forward(self, number, source, z):
        y, unused, core = self.place
        unused, my_z, unused = self.place
        shard = shard_at(y, z, core)
        for i, (half, d) in enumerate(zip(self.halves(), (3, 1))):
            copy = self.copy(
                source.at[half], shard, half, 3 + 2 * number + i, device_at(lax.rem(y + d, 4), my_z, core)
            )
            copy.start()
            self.along_y.append(copy)
        copy = self.copy(source, shard, None, 11 + number, device_at(y, my_z, 1 - core))
        copy.start()
        self.across.append(copy)

    def start(self):
        for copy in self.along_z:
            copy.start()
        self.forward(0, self.source, self.place[1])

    def finish(self):
        y, z, core = self.place
        for i, d in enumerate(self.order):
            self.along_z[i].wait_recv()
            from_z = lax.rem(z + 4 - d, 4)
            self.forward(i + 1, self.target.at[shard_at(y, from_z, core)], from_z)
        for number in range(4):
            from_z = z if number == 0 else lax.rem(z + 4 - self.order[number - 1], 4)
            shard = shard_at(y + 1, from_z, core)
            for i, half in enumerate(self.halves()):
                self.along_y[2 * number + i].wait_recv()
                block = self.target.at[shard].at[half]
                copy = self.copy(block, shard, half, 15 + 2 * number + i, device_at(y, z, 1 - core))
                copy.start()
                self.across.append(copy)
        for copy in self.along_z + self.along_y:
            copy.wait_send()
        for copy in self.across:
            copy.wait()


class Mover:
    def __init__(self, plan, inputs, outputs, own, send, recv, in_sem, out_sem):
        self.plan, self.inputs, self.outputs, self.own = plan, inputs, outputs, own
        self.send, self.recv, self.in_sem, self.out_sem = send, recv, in_sem, out_sem
        self.taken, self.copies, self.shares = [], [], []

    def own_place(self, item):
        kind, group = self.plan[item]
        return shard_at(*chip()) if kind == "share" else place_in(group)

    def take(self):
        for item, (kind, group) in enumerate(self.plan):
            block = source_of(kind, group, self.inputs[item], self.own_place(item))
            copy = pltpu.make_async_copy(block, self.own[item], self.in_sem.at[item])
            copy.start()
            self.taken.append(copy)

    def start(self):
        slot = 0
        for item, (kind, group) in enumerate(self.plan):
            source, target = self.inputs[item], self.outputs[item]
            if kind == "share":
                share = Share(source, target, self.send, self.recv, slot)
                share.start()
                self.shares.append(share)
            else:
                count = GROUP_SIZE[group]
                mine = place_in(group)
                for offset in range(1, count):
                    if kind == "half" and not soon(offset):
                        continue
                    peer = lax.rem(mine + offset, count)
                    copy = remote(
                        source_of(kind, group, source, peer),
                        target_of(kind, group, target, mine),
                        self.send.at[slot + offset - 1],
                        self.recv.at[slot + offset - 1],
                        device_of(group, peer),
                    )
                    copy.start()
                    self.copies.append(copy)
            slot += copies_of(kind, group)
        for item, (kind, group) in enumerate(self.plan):
            self.taken[item].wait()
            block = target_of(kind, group, self.outputs[item], self.own_place(item))
            copy = pltpu.make_async_copy(self.own[item], block, self.out_sem.at[item])
            copy.start()
            self.copies.append(copy)

    def finish(self):
        for share in self.shares:
            share.finish()
        for copy in self.copies:
            copy.wait()


def exchange_kernel(plan, *refs):
    amount = len(plan)
    mover = Mover(
        plan, refs[:amount], refs[amount : 2 * amount], refs[2 * amount : 3 * amount], *refs[3 * amount :]
    )
    mover.take()
    greet(plan)
    mover.start()
    mover.finish()


def mover_scratch(items):
    plan = tuple((kind, group) for kind, group, array in items)
    slots = sum(copies_of(kind, group) for kind, group in plan)
    return [
        pltpu.VMEM(own_shape(kind, group, array.shape), array.dtype) for kind, group, array in items
    ] + [
        pltpu.SemaphoreType.DMA((slots,)),
        pltpu.SemaphoreType.DMA((slots,)),
        pltpu.SemaphoreType.DMA((len(items),)),
        pltpu.SemaphoreType.DMA((len(items),)),
    ]


def exchange(name, number, *items):
    plan = tuple((kind, group) for kind, group, array in items)
    arrays = [array for kind, group, array in items]
    return pl.pallas_call(
        functools.partial(exchange_kernel, plan),
        out_shape=[
            jax.ShapeDtypeStruct(exchanged_shape(kind, group, array.shape), array.dtype)
            for kind, group, array in items
        ],
        in_specs=[pl.BlockSpec(memory_space=pltpu.HBM)] * len(items),
        out_specs=[pl.BlockSpec(memory_space=pltpu.HBM)] * len(items),
        scratch_shapes=mover_scratch(items),
        compiler_params=pltpu.CompilerParams(
            collective_id=number, has_side_effects=True, vmem_limit_bytes=16 * 2**20
        ),
        name=name,
    )(*arrays)


def rms_forward(values, gain):
    mean_square = jnp.mean(values * values, axis=-1, keepdims=True)
    return values * lax.rsqrt(mean_square + norm_eps) * gain.astype(F32)


def rms_backward(values, gain, grad_result):
    scale = lax.rsqrt(jnp.mean(values * values, axis=-1, keepdims=True) + norm_eps)
    scaled = gain.astype(F32) * grad_result
    inner = jnp.mean(values * scaled, axis=-1, keepdims=True)
    return scale * scaled - values * (scale * scale * scale) * inner


def logistic(values):
    return 0.5 * jnp.tanh(0.5 * values) + 0.5


def swiglu(gate, upper):
    sigma = logistic(gate)
    silu = gate * sigma
    return (silu * upper).astype(BF), sigma, silu


def swiglu_backward(gate, upper, sigma, silu, grad_hidden):
    grad_gate = grad_hidden * upper * (sigma + silu * (1.0 - sigma))
    return (grad_gate.astype(BF), (grad_hidden * silu).astype(BF))


def two_parts(values):
    high = values.astype(BF)
    return high, (values - high.astype(F32)).astype(BF)


def lane_index(shape):
    return lax.broadcasted_iota(jnp.int32, shape, 1)


def row_index(shape):
    return lax.broadcasted_iota(jnp.int32, shape, 0)


def pair_pick(second, copies):
    shape = (second.shape[0], PAIR * copies)
    of_lane = (lane_index(shape) % PAIR >= RANK).astype(F32)
    return (of_lane == second).astype(F32)


def pair_of(first_ref, last_ref, index):
    return jnp.concatenate([first_ref[index, 0], last_ref[index, 0]], axis=0)


def padded(values):
    rest = 128 - values.shape[1]
    return jnp.concatenate([values, jnp.zeros((values.shape[0], rest), values.dtype)], axis=1)


def routing(routes, experts):
    tokens = routes.shape[0]
    expert_lane = lane_index((tokens, experts))
    expert_hot = [(routes[:, k : k + 1] == expert_lane).astype(F32) for k in range(TOP)]
    count = sum(expert_hot)
    below = (row_index((tokens, tokens)) > lane_index((tokens, tokens))).astype(BF)
    earlier = dot(below, count.astype(BF))
    rank = [jnp.sum(hot * earlier, axis=1, keepdims=True).astype(jnp.int32) for hot in expert_hot]
    main_lane = lane_index((tokens, experts * MAIN))
    rest_lane = lane_index((tokens, experts * 16))
    rest_code = (rest_lane // 16) * 4 + rest_lane % 4
    main_hot, rest_hot = [], []
    for k in range(TOP):
        expert = routes[:, k : k + 1]
        main_slot = jnp.where(rank[k] < MAIN, expert * MAIN + rank[k], -1)
        rest_slot = jnp.where(rank[k] < MAIN, -1, expert * 4 + rank[k] - MAIN)
        main_hot.append((main_lane == main_slot).astype(F32))
        rest_hot.append((rest_code == rest_slot).astype(F32))
    return expert_hot, main_hot, rest_hot


def quarter_mask(shape, quarter):
    return (lane_index(shape) % 16 // 4 == quarter).astype(F32)


def rows_to_slots(main_hot, rest_hot, rows):
    main = dot_tn(sum(main_hot).astype(BF), rows).astype(BF)
    rest_sum = sum(rest_hot)
    width = rows.shape[1] // 4
    rest = None
    for quarter in range(4):
        hot = (rest_sum * quarter_mask(rest_sum.shape, quarter)).astype(BF)
        part = dot_tn(hot, rows[:, quarter * width : (quarter + 1) * width])
        rest = part if rest is None else rest + part
    return main, rest.astype(BF)


def slots_to_rows(main_hot, rest_hot, main, rest):
    rest_sum = sum(rest_hot)
    parts = [
        dot((rest_sum * quarter_mask(rest_sum.shape, quarter)).astype(BF), rest)
        for quarter in range(4)
    ]
    return dot(sum(main_hot).astype(BF), main) + jnp.concatenate(parts, axis=1)


def rest_selectors(sources):
    shape = (4 * sources, 16 * sources)
    row, lane = row_index(shape), lane_index(shape)
    same = (lane // 16 == row // 4) & (lane % 4 == row % 4)
    return [(same & (lane % 16 // 4 == quarter)).astype(BF) for quarter in range(4)]


def rest_to_rows(selectors, rest):
    return jnp.concatenate([dot(selector, rest) for selector in selectors], axis=1).astype(BF)


def rows_to_rest(selectors, rows):
    width = rows.shape[1] // 4
    total = None
    for quarter in range(4):
        part = dot_tn(selectors[quarter], rows[:, quarter * width : (quarter + 1) * width])
        total = part if total is None else total + part
    return total.astype(BF)


def stage(kernel, name, out_shape, in_specs, out_specs, grid=(1,), scratch=(), prefetch=0):
    return pl.pallas_call(
        kernel,
        out_shape=out_shape,
        grid_spec=pltpu.PrefetchScalarGridSpec(
            num_scalar_prefetch=prefetch,
            grid=grid,
            in_specs=in_specs,
            out_specs=out_specs,
            scratch_shapes=list(scratch),
        ),
        compiler_params=pltpu.CompilerParams(vmem_limit_bytes=VMEM_LIMIT),
        name=name,
    )


def whole(array):
    zeros = (0,) * len(array.shape)
    return pl.BlockSpec(array.shape, lambda *unused: zeros)


def of_sequence(which, block):
    return pl.BlockSpec(block, lambda *at: (0, at[-1][which], 0, 0))


def shape_of(shape, kind):
    return jax.ShapeDtypeStruct(shape, kind)


HBM = pl.BlockSpec(memory_space=pltpu.HBM)


def prologue_kernel(
    numbers_ref,
    rows_ref,
    grads_ref,
    gain_ref,
    routes_ref,
    ffn_a_ref,
    ffn_b_ref,
    down_a_ref,
    down_b_ref,
    first_a_ref,
    first_b_ref,
    second_a_ref,
    second_b_ref,
    normed_ref,
    main_ref,
    rest_ref,
    picked_ref,
    first_ref,
    second_ref,
):
    normed_ref[...] = rms_forward(rows_ref[0].astype(F32), gain_ref[...]).astype(BF)
    experts = main_ref.shape[0] // MAIN
    unused, main_hot, rest_hot = routing(routes_ref[0], experts)
    main, rest = rows_to_slots(main_hot, rest_hot, grads_ref[0])
    main_ref[...] = main
    rest_ref[...] = rest
    picked_ref[...] = jnp.concatenate(
        [
            pair_of(ffn_a_ref, ffn_b_ref, 1),
            pair_of(ffn_a_ref, ffn_b_ref, 2),
            pair_of(down_a_ref, down_b_ref, 0),
        ],
        axis=0,
    )
    for j in range(3):
        first_ref[j * PAIR : (j + 1) * PAIR, :] = pair_of(first_a_ref, first_b_ref, j)
        second_ref[j * PAIR : (j + 1) * PAIR, :] = pair_of(second_a_ref, second_b_ref, j)


def prologue(
    numbers, rows, grads, gain, routes, ffn_first, down_second, first, second, experts, columns
):
    tokens, width = rows.shape[1:]
    heads = lambda which: pl.BlockSpec(
        (3, 1, RANK, columns), lambda n, a: (0, a[which], 0, a[2])
    )
    outs = [
        (tokens, width),
        (experts * MAIN, width),
        (experts * 16, width // 4),
        (3 * PAIR, width),
        (3 * PAIR, width),
        (3 * PAIR, columns),
    ]
    return stage(
        prologue_kernel,
        "prologue",
        [shape_of(shape, BF) for shape in outs],
        [
            whole(rows),
            whole(grads),
            whole(gain),
            whole(routes),
            of_sequence(0, (3, 1, RANK, width)),
            of_sequence(1, (3, 1, RANK, width)),
            of_sequence(0, (1, 1, RANK, width)),
            of_sequence(1, (1, 1, RANK, width)),
            of_sequence(0, (3, 1, RANK, width)),
            of_sequence(1, (3, 1, RANK, width)),
            heads(0),
            heads(1),
        ],
        [pl.BlockSpec(shape, lambda n, a: (0, 0)) for shape in outs],
        prefetch=1,
    )(
        numbers, rows, grads, gain, routes, ffn_first, ffn_first, down_second, down_second, first, first,
        second, second,
    )


def half_turn(values):
    parts = []
    for head in range(values.shape[1] // HEAD_DIM):
        part = values[:, head * HEAD_DIM : (head + 1) * HEAD_DIM]
        parts.append(jnp.concatenate([part[:, 64:], part[:, :64]], axis=1))
    return jnp.concatenate(parts, axis=1) if len(parts) > 1 else parts[0]


def project_kernel(
    numbers_ref,
    rows_ref,
    weight_ref,
    first_a_ref,
    first_b_ref,
    second_a_ref,
    second_b_ref,
    bias_ref,
    side_ref,
    cos_ref,
    sin_ref,
    out_ref,
    lanes_ref,
):
    which = pl.program_id(0)

    @pl.when(pl.program_id(1) == 0)
    def lanes():
        first = pair_of(first_a_ref, first_b_ref, 0)
        picked = dot_nt(rows_ref[...], first) * pair_pick(side_ref[...], 1)
        lanes_ref[0] = picked.astype(BF)

    weight = weight_ref[...].reshape(rows_ref.shape[1], weight_ref.shape[3])
    bias = bias_ref[...].astype(F32)
    bias = jnp.sum(jnp.where(row_index(bias.shape) == which, bias, 0.0), axis=0, keepdims=True)
    second = pair_of(second_a_ref, second_b_ref, 0)
    value = dot(rows_ref[...], weight) + bias + dot(lanes_ref[0], second)
    copies = value.shape[1] // HEAD_DIM
    cosine = jnp.concatenate([cos_ref[...]] * copies, axis=1)
    sine = jnp.concatenate([sin_ref[...]] * copies, axis=1)
    turned = value * cosine + half_turn(value) * sine
    out_ref[0] = jnp.where(which < 2, turned, value).astype(BF)


def project(numbers, rows, weight, first, second, bias, side, cosine, sine):
    tokens, width = rows.shape
    columns = weight.shape[3]
    step = 256
    steps = columns // step
    return stage(
        project_kernel,
        "project",
        [shape_of((3, tokens, columns), BF), shape_of((3, tokens, PAIR), BF)],
        [
            whole(rows),
            pl.BlockSpec((weight.shape[0], 1, weight.shape[2], step), lambda j, n, a: (0, j, 0, n)),
            pl.BlockSpec((1, 1, RANK, width), lambda j, n, a: (j, a[0], 0, 0)),
            pl.BlockSpec((1, 1, RANK, width), lambda j, n, a: (j, a[1], 0, 0)),
            pl.BlockSpec((1, 1, RANK, step), lambda j, n, a: (j, a[0], 0, a[2] * steps + n)),
            pl.BlockSpec((1, 1, RANK, step), lambda j, n, a: (j, a[1], 0, a[2] * steps + n)),
            pl.BlockSpec((3, step), lambda j, n, a: (0, a[2] * steps + n)),
            whole(side),
            whole(cosine),
            whole(sine),
        ],
        [
            pl.BlockSpec((1, tokens, step), lambda j, n, a: (j, 0, n)),
            pl.BlockSpec((1, tokens, PAIR), lambda j, n, a: (j, 0, 0)),
        ],
        grid=(3, steps),
        prefetch=1,
    )(numbers, rows, weight, first, first, second, second, bias, side, cosine, sine)


def probabilities(query, keys, query_place, query_start, key_place):
    scores = dot_nt(query, keys) * (HEAD_DIM**-0.5)
    allowed = (key_place <= query_place) & (key_place >= query_start)
    scores = jnp.where(allowed, scores, masked_score)
    top = jnp.max(scores, axis=1, keepdims=True)
    raised = jnp.exp(scores - top)
    return raised * (1.0 / jnp.sum(raised, axis=1, keepdims=True))


def attend_kernel(query_ref, key_ref, value_ref, place_ref, start_ref, key_place_ref, out_ref):
    keys = key_ref[...].reshape(-1, HEAD_DIM)
    values = value_ref[...].reshape(-1, HEAD_DIM)
    probs = probabilities(query_ref[0], keys, place_ref[...], start_ref[...], key_place_ref[...])
    out_ref[...] = dot(probs.astype(BF), values).astype(BF)


def attend(projected, pairs, place, start, key_place):
    tokens, columns = projected.shape[1:]
    step = 256
    keys = pairs.shape[0] * pairs.shape[2]
    half = pairs.shape[2]
    return pl.pallas_call(
        attend_kernel,
        grid=(columns // HEAD_DIM, tokens // step),
        out_shape=jax.ShapeDtypeStruct((tokens, columns), BF),
        in_specs=[
            pl.BlockSpec((1, step, HEAD_DIM), lambda h, i: (0, i, h)),
            pl.BlockSpec((2, 1, half, HEAD_DIM), lambda h, i: (0, 0, 0, h)),
            pl.BlockSpec((2, 1, half, HEAD_DIM), lambda h, i: (0, 1, 0, h)),
            pl.BlockSpec((step, 1), lambda h, i: (i, 0)),
            pl.BlockSpec((step, 1), lambda h, i: (i, 0)),
            pl.BlockSpec((1, keys), lambda h, i: (0, 0)),
        ],
        out_specs=pl.BlockSpec((step, HEAD_DIM), lambda h, i: (i, h)),
        compiler_params=pltpu.CompilerParams(vmem_limit_bytes=VMEM_LIMIT),
        name="attend",
    )(projected, pairs, pairs, place, start, key_place)


def after_attention_kernel(
    numbers_ref,
    mixed_ref,
    weight_ref,
    rows_ref,
    first_a_ref,
    first_b_ref,
    second_a_ref,
    second_b_ref,
    gain_ref,
    ffn_a_ref,
    ffn_b_ref,
    router_ref,
    router_a_ref,
    router_b_ref,
    mix_ref,
    routes_ref,
    side_ref,
    residual_ref,
    normed_ref,
    small_ref,
    main_ref,
    rest_ref,
    main_notes_ref,
    rest_notes_ref,
    lanes_ref,
):
    step = pl.program_id(0)
    side = side_ref[...]
    pick = pair_pick(side, 1)

    @pl.when(step == 0)
    def lanes():
        first = pair_of(first_a_ref, first_b_ref, 0)
        lanes_ref[...] = (dot_nt(mixed_ref[...], first) * pick).astype(BF)

    columns = weight_ref.shape[1]
    here = pl.ds(pl.multiple_of(step * columns, columns), columns)
    second = pair_of(second_a_ref, second_b_ref, 0)
    residual_ref[:, here] = rows_ref[0].astype(F32) + (
        dot(mixed_ref[...], weight_ref[...]) + dot(lanes_ref[...], second)
    )

    @pl.when(step == pl.num_programs(0) - 1)
    def last():
        tokens = residual_ref.shape[0]
        experts = router_ref.shape[1]
        normed = rms_forward(residual_ref[...], gain_ref[...]).astype(BF)
        normed_ref[...] = normed
        router_lanes = (dot_nt(normed, pair_of(ffn_a_ref, ffn_b_ref, 0)) * pick).astype(BF)
        router_second = jnp.concatenate([router_a_ref[0], router_b_ref[0]], axis=0)
        logits = dot(normed, router_ref[...]) + dot(router_lanes, router_second)
        expert_hot, main_hot, rest_hot = routing(routes_ref[0], experts)
        chosen = [jnp.sum(hot * logits, axis=1, keepdims=True) for hot in expert_hot]
        top = jnp.maximum(jnp.maximum(chosen[0], chosen[1]), jnp.maximum(chosen[2], chosen[3]))
        raised = [jnp.exp(value - top) for value in chosen]
        total = sum(raised)
        gates = [value / total for value in raised]
        mix = logistic(
            jnp.sum(normed.astype(F32) * mix_ref[...].astype(F32), axis=1, keepdims=True)
        )
        small_ref[...] = padded(
            jnp.concatenate(
                [lanes_ref[...].astype(F32), router_lanes.astype(F32), *gates, mix], axis=1
            )
        )
        main, rest = rows_to_slots(main_hot, rest_hot, normed)
        main_ref[...] = main
        rest_ref[...] = rest
        adapter = jnp.where(side > 0.5, numbers_ref[1], numbers_ref[0])
        lane = lane_index((tokens, 128))
        adapter_hot = (lane == adapter).astype(F32)
        main_notes, rest_notes = None, None
        for k in range(TOP):
            high, low = two_parts(gates[k])
            notes = jnp.where(
                lane == ADAPTER_COUNT,
                high.astype(F32),
                jnp.where(lane == ADAPTER_COUNT + 1, low.astype(F32), adapter_hot),
            ).astype(BF)
            main_part = dot_tn(main_hot[k].astype(BF), notes)
            rest_part = dot_tn(rest_hot[k].astype(BF), notes)
            main_notes = main_part if k == 0 else main_notes + main_part
            rest_notes = rest_part if k == 0 else rest_notes + rest_part
        main_notes_ref[...] = main_notes.astype(BF)
        rest_notes_ref[...] = rest_notes.astype(BF)


def after_attention(
    numbers, mixed, weight, rows, first, second, gain, ffn_first, router, router_second, mix, routes, side
):
    tokens, width = mixed.shape
    experts = router.shape[1]
    step = 512
    kept = lambda *shape: pl.BlockSpec(shape, lambda n, a: (0,) * len(shape))
    outs = [
        ((tokens, width), F32),
        ((tokens, width), BF),
        ((tokens, 128), F32),
        ((experts * MAIN, width), BF),
        ((experts * 16, width // 4), BF),
        ((experts * MAIN, 128), BF),
        ((experts * 16, 128), BF),
    ]
    return stage(
        after_attention_kernel,
        "after_attention",
        [shape_of(*out) for out in outs],
        [
            whole(mixed),
            pl.BlockSpec((width, step), lambda n, a: (0, n)),
            pl.BlockSpec((1, tokens, step), lambda n, a: (0, 0, n)),
            pl.BlockSpec((1, 1, RANK, width), lambda n, a: (3, a[0], 0, 0)),
            pl.BlockSpec((1, 1, RANK, width), lambda n, a: (3, a[1], 0, 0)),
            pl.BlockSpec((1, 1, RANK, step), lambda n, a: (3, a[0], 0, n)),
            pl.BlockSpec((1, 1, RANK, step), lambda n, a: (3, a[1], 0, n)),
            whole(gain),
            pl.BlockSpec((1, 1, RANK, width), lambda n, a: (0, a[0], 0, 0)),
            pl.BlockSpec((1, 1, RANK, width), lambda n, a: (0, a[1], 0, 0)),
            whole(router),
            pl.BlockSpec((1, RANK, experts), lambda n, a: (a[0], 0, 0)),
            pl.BlockSpec((1, RANK, experts), lambda n, a: (a[1], 0, 0)),
            whole(mix),
            whole(routes),
            whole(side),
        ],
        [kept(*shape) for shape, kind in outs],
        grid=(width // step,),
        scratch=[pltpu.VMEM((tokens, PAIR), BF)],
        prefetch=1,
    )(
        numbers, mixed, weight, rows, first, first, second, second, gain, ffn_first, ffn_first, router,
        router_second, router_second, mix, routes, side,
    )


def in_owner_columns(total, target, columns):
    count = total.shape[0]
    for owner in range(total.shape[1] // columns):
        part = total[:, owner * columns : (owner + 1) * columns].astype(BF)
        target[:count, owner * 128 : (owner + 1) * 128] = padded(part)


def x_step(step):
    return step + step // 2 * (1 - 2 * (step % 2))


SHARED_STEPS = 4


def shared_kernel(plan, *refs):
    amount = len(plan)
    inputs, refs = refs[:amount], refs[amount:]
    normed_ref, grads_hbm, weights_hbm, side_ref, picked_ref, first_ref, mix_ref = refs[:7]
    outputs, refs = refs[7 : 7 + amount], refs[7 + amount :]
    parts_refs, values_ref, adapter_ref, refs = refs[:2], refs[2], refs[3], refs[4:]
    own, move_sems, refs = refs[:amount], refs[amount : amount + 4], refs[amount + 4 :]
    rows_buf, grads_buf, gate_up_buf, down_buf = refs[:4]
    parts_buf, values_buf, total, refs = refs[4:6], refs[6], refs[7], refs[8:]
    rows_send, rows_recv, parts_send, parts_recv, load_sem, parts_sem = refs

    shards_of, units, wide = down_buf.shape
    along, tokens, width = rows_buf.shape
    hidden_units = shards_of * units
    me = place_in("x")
    loads = [
        pltpu.make_async_copy(normed_ref, rows_buf.at[me], load_sem.at[0]),
        pltpu.make_async_copy(grads_hbm, grads_buf, load_sem.at[1]),
    ]
    loads += [
        pltpu.make_async_copy(
            weights_hbm.at[:, pl.ds(i * units, units)],
            target.at[:, :, pl.ds(0, width)],
            load_sem.at[2 + i],
        )
        for i, target in enumerate((gate_up_buf.at[0], gate_up_buf.at[1], down_buf))
    ]
    for load in loads:
        load.start()
    mover = Mover(plan, inputs, outputs, own, *move_sems)
    mover.take()
    greet(plan + (("gather", "x"),))

    def rows_copy(offset):
        return remote(
            normed_ref,
            rows_buf.at[me],
            rows_send.at[offset],
            rows_recv.at[offset],
            device_of("x", lax.rem(me + offset, along)),
        )

    def parts_copy(kind, offset):
        peer = lax.rem(me + along - offset, along)
        return remote(
            parts_buf[kind].at[peer],
            parts_refs[kind].at[me],
            parts_send.at[kind, offset],
            parts_recv.at[kind, offset],
            device_of("x", peer),
        )

    def own_parts(kind):
        return pltpu.make_async_copy(
            parts_buf[kind].at[me], parts_refs[kind].at[me], parts_sem.at[kind]
        )

    for offset in (1, 3, 2):
        rows_copy(offset).start()
    mover.start()
    for i in range(2):
        gate_up_buf[i, :, :, width:] = first_ref[i]
    down_buf[:, :, width:] = first_ref[2]
    total[...] = jnp.zeros_like(total)
    for load in loads[:2]:
        load.wait()
    per_step = along // SHARED_STEPS

    def block(step, carry):
        offsets = [x_step(step * per_step + i) for i in range(per_step)]
        sources = [lax.rem(me + along - offset, along) for offset in offsets]
        for i, offset in enumerate(offsets):
            if i > 0:
                rows_copy(offset).wait_recv()
            else:

                @pl.when(step > 0)
                def arrived():
                    rows_copy(offset).wait_recv()

        rows = jnp.concatenate([rows_buf[source] for source in sources], axis=0)
        grads = jnp.concatenate([grads_buf[source] for source in sources], axis=0)
        side = jnp.concatenate([side_ref[source] for source in sources], axis=0)
        grads_f = grads.astype(F32)
        pick = pair_pick(side, 1)
        pick_both = pair_pick(side, 2)
        lanes = (dot_nt(rows, picked_ref[: 2 * PAIR]) * pick_both).astype(BF)
        mix = logistic(jnp.sum(rows.astype(F32) * mix_ref[...].astype(F32), axis=1, keepdims=True))
        grad_shared = (mix * grads_f).astype(BF)
        grad_side = (dot_nt(grad_shared, picked_ref[2 * PAIR :]) * pick).astype(BF)

        @pl.when(step == 0)
        def gate_up_loaded():
            for load in loads[2:4]:
                load.wait()

        both = dot_nt(jnp.concatenate([rows, padded(lanes)], axis=1), gate_up_buf[...].reshape(-1, wide))
        gate, upper = both[:, :hidden_units], both[:, hidden_units:]
        hidden, sigma, silu = swiglu(gate, upper)

        @pl.when(step == 0)
        def down_loaded():
            loads[4].wait()

        down = down_buf[...].reshape(hidden_units, wide)
        grad_hidden = dot_nt(jnp.concatenate([grad_shared, padded(grad_side)], axis=1), down)
        grad_gate, grad_upper = swiglu_backward(gate, upper, sigma, silu, grad_hidden)
        gate_up = gate_up_buf[...].reshape(2 * hidden_units, wide)
        back = dot(jnp.concatenate([grad_gate, grad_upper], axis=1), gate_up)
        grad_lanes = (back[:, width : width + 2 * PAIR] * pick_both).astype(BF)
        value = dot(hidden, down)
        side_lanes = (value[:, width : width + PAIR] * pick).astype(BF)
        value = value[:, :width]
        mix_sum = jnp.sum(grads_f * value, axis=1, keepdims=True)
        notes = padded(jnp.concatenate([side_lanes, grad_lanes, *two_parts(mix_sum)], axis=1))
        for i, source in enumerate(sources):
            at = slice(i * tokens, (i + 1) * tokens)
            parts_buf[0][source] = back[at, :width].astype(BF)
            parts_buf[1][source] = notes[at]
            values_buf[source] = value[at].astype(BF)

        for i, offset in enumerate(offsets):
            if i > 0:
                for kind in range(2):
                    parts_copy(kind, offset).start()
            else:

                @pl.when(step == 0)
                def keep():
                    for kind in range(2):
                        own_parts(kind).start()

                @pl.when(step > 0)
                def send():
                    for kind in range(2):
                        parts_copy(kind, offset).start()

        total[:PAIR] += dot_tn(lanes[:, :PAIR], grad_gate)
        total[PAIR : 2 * PAIR] += dot_tn(lanes[:, PAIR:], grad_upper)
        total[2 * PAIR :] += dot_tn(grad_side, hidden)
        return carry

    lax.fori_loop(0, SHARED_STEPS, block, 0)
    values_out = pltpu.make_async_copy(values_buf, values_ref, parts_sem.at[2])
    values_out.start()
    in_owner_columns(total, adapter_ref, units)
    mover.finish()
    for kind in range(2):
        own_parts(kind).wait()
    for offset in range(1, along):
        rows_copy(offset).wait_send()
        for kind in range(2):
            parts_copy(kind, offset).wait()
    values_out.wait()


def shared_expert(number, normed, items, grads, weights, side, picked, first, mix):
    tokens, width = normed.shape
    plan = tuple((kind, group) for kind, group, array in items)
    arrays = [array for kind, group, array in items]
    along = GROUP_SIZE["x"]
    shards_of, units = weights.shape[0], weights.shape[1] // 3
    hidden = shards_of * units
    vmem = pl.BlockSpec(memory_space=pltpu.VMEM)
    parts = [(along, tokens, width), (along, tokens, 128), (along, tokens, width)]
    return pl.pallas_call(
        functools.partial(shared_kernel, plan),
        out_shape=[shape_of(array.shape, BF) for array in arrays]
        + [shape_of(part, BF) for part in parts]
        + [shape_of((3 * PAIR, shards_of * 128), BF)],
        in_specs=[HBM] * (len(items) + 3) + [vmem] * 4,
        out_specs=[HBM] * (len(items) + 3) + [vmem],
        scratch_shapes=mover_scratch(items)
        + [pltpu.VMEM((along, tokens, width), BF)] * 2
        + [
            pltpu.VMEM((2, shards_of, units, width + 128), BF),
            pltpu.VMEM((shards_of, units, width + 128), BF),
        ]
        + [pltpu.VMEM(part, BF) for part in parts]
        + [pltpu.VMEM((3 * PAIR, hidden), F32)]
        + [
            pltpu.SemaphoreType.DMA((along,)),
            pltpu.SemaphoreType.DMA((along,)),
            pltpu.SemaphoreType.DMA((2, along)),
            pltpu.SemaphoreType.DMA((2, along)),
            pltpu.SemaphoreType.DMA((5,)),
            pltpu.SemaphoreType.DMA((3,)),
        ],
        compiler_params=pltpu.CompilerParams(
            collective_id=number, has_side_effects=True, vmem_limit_bytes=VMEM_LIMIT
        ),
        name="shared_expert",
    )(*arrays, normed, grads, weights, side, picked, first, mix)


BACK = 6
ROUTED_STEPS = 4


def routed_kernel(*refs):
    held_hbm, gate_up_hbm, down_hbm, values_hbm = refs[:6], refs[6], refs[7], refs[8]
    later_hbm, refs = refs[9:11], refs[2:]
    first_ref, second_ref, down_first_ref, down_second_ref = refs[9:13]
    back_refs, values_ref, refs = refs[13 : 13 + BACK], refs[13 + BACK], refs[14 + BACK :]
    adapter_ref = refs[0]
    own, move_sems, refs = refs[1:2], refs[2:6], refs[6:]
    held, back_buf, refs = refs[:6], refs[6 : 6 + BACK], refs[6 + BACK :]
    gate_up_buf, down_buf, total, total_down = refs[:4]
    send_sem, recv_sem, load_sem, own_sem, half_sem, later_send, later_recv = refs[4:]

    me = place_in("f")
    experts = GROUP_SIZE["f"]
    steps = ROUTED_STEPS
    loads = [
        pltpu.make_async_copy(held_hbm[i], held[i], load_sem.at[i]) for i in (0, 1, 4, 5)
    ]
    for offset in range(experts):
        if offset == 0 or soon(offset):
            source = lax.rem(me + experts - offset, experts)
            loads += [
                pltpu.make_async_copy(
                    block_of(held_hbm[2 + i], "rows", experts, source),
                    block_of(held[2 + i], "rows", experts, source),
                    half_sem.at[i, offset],
                )
                for i in range(2)
            ]
    loads += [
        pltpu.make_async_copy(gate_up_hbm.at[0, 0], gate_up_buf.at[0], load_sem.at[6]),
        pltpu.make_async_copy(gate_up_hbm.at[0, 1], gate_up_buf.at[1], load_sem.at[7]),
        pltpu.make_async_copy(down_hbm.at[0], down_buf, load_sem.at[8]),
    ]
    for load in loads:
        load.start()
    mover = Mover((("swap", "x"),), (values_hbm,), (values_ref,), own, *move_sems)
    mover.take()
    greet((("rows", "f"), ("swap", "x")))

    def later_copy(kind, offset):
        peer = lax.rem(me + offset, experts)
        return remote(
            block_of(later_hbm[kind], "rows", experts, peer),
            block_of(held[2 + kind], "rows", experts, me),
            later_send.at[kind, offset],
            later_recv.at[kind, offset],
            device_of("f", peer),
        )

    later = [offset for offset in range(1, experts) if not soon(offset)]
    for offset in sorted(later, key=lambda offset: -(offset % steps)):
        for kind in range(2):
            later_copy(kind, offset).start()
    mover.start()
    total[...] = jnp.zeros_like(total)
    total_down[...] = jnp.zeros_like(total_down)

    def back_copy(kind, peer, landing):
        return remote(
            block_of(back_buf[kind], "rows", experts, peer),
            block_of(back_refs[kind], "rows", experts, me),
            send_sem.at[kind, peer],
            recv_sem.at[kind, landing],
            device_of("f", peer),
        )

    def own_copy(kind):
        return pltpu.make_async_copy(
            block_of(back_buf[kind], "rows", experts, me),
            block_of(back_refs[kind], "rows", experts, me),
            own_sem.at[kind],
        )

    selectors = rest_selectors(experts // steps)
    spread = (row_index((128, LANES)) == lane_index((128, LANES)) // RANK).astype(BF)
    fold = (row_index((LANES, 128)) % RANK == lane_index((LANES, 128))).astype(BF)
    fold_later = (row_index((LANES, 128)) % RANK == lane_index((LANES, 128)) - RANK).astype(BF)
    for load in loads[:-3]:
        load.wait()
    count, rest_count = held[0].shape[0] // steps, held[1].shape[0] // steps

    def block(step, carry):
        number = lax.rem(me + 1 + step, steps)

        for turn in range(steps // 2):

            @pl.when(step == steps - 1 - turn)
            def arrived():
                for offset in later:
                    if offset % steps == turn:
                        for kind in range(2):
                            later_copy(kind, offset).wait_recv()

        peers = [number + steps * turn for turn in range(experts // steps)]

        def read(ref):
            depth = ref.shape[0] // experts
            blocks = [ref[pl.ds(pl.multiple_of(peer * depth, depth), depth)] for peer in peers]
            return jnp.concatenate(blocks, axis=0)

        def write(ref, value):
            depth = ref.shape[0] // experts
            for turn, peer in enumerate(peers):
                part = value[turn * depth : (turn + 1) * depth]
                ref[pl.ds(pl.multiple_of(peer * depth, depth), depth)] = part

        rows = jnp.concatenate([read(held[0]), rest_to_rows(selectors, read(held[1]))], axis=0)
        grads = jnp.concatenate([read(held[2]), rest_to_rows(selectors, read(held[3]))], axis=0)
        notes = jnp.concatenate(
            [read(held[4]), dot(selectors[0], read(held[5])).astype(BF)], axis=0
        )
        pick = dot(notes, spread)
        gate_of = (
            notes[:, ADAPTER_COUNT : ADAPTER_COUNT + 1].astype(F32)
            + notes[:, ADAPTER_COUNT + 1 : ADAPTER_COUNT + 2].astype(F32)
        )
        grads_f = grads.astype(F32)
        lanes_gate = (dot_nt(rows, first_ref[0]) * pick).astype(BF)
        lanes_up = (dot_nt(rows, first_ref[1]) * pick).astype(BF)
        grad_routed = (gate_of * grads_f).astype(BF)
        grad_side = (dot_nt(grads, down_second_ref[1]) * gate_of * pick).astype(BF)

        @pl.when(step == 0)
        def gate_up_loaded():
            for load in loads[-3:-1]:
                load.wait()

        gate = dot(rows, gate_up_buf[0]) + dot(lanes_gate, second_ref[0])
        upper = dot(rows, gate_up_buf[1]) + dot(lanes_up, second_ref[1])
        hidden, sigma, silu = swiglu(gate, upper)

        @pl.when(step == 0)
        def down_loaded():
            loads[-1].wait()

        grad_hidden = dot_nt(grad_routed, down_buf[...]) + dot(grad_side, down_first_ref[...])
        grad_gate, grad_upper = swiglu_backward(gate, upper, sigma, silu, grad_hidden)
        side = (dot_nt(hidden, down_first_ref[...]).astype(BF).astype(F32) * pick).astype(BF)
        value = dot(hidden, down_buf[...]) + dot(side, down_second_ref[1])
        gate_grad = jnp.sum(grads_f * value, axis=1, keepdims=True)
        result = (gate_of * value).astype(BF)
        write(back_buf[4], result[:count])
        write(back_buf[5], rows_to_rest(selectors, result[count:]))
        back = (dot_nt(grad_gate, gate_up_buf[0]) + dot_nt(grad_upper, gate_up_buf[1])).astype(BF)
        back_gate = (dot_nt(grad_gate, second_ref[0]) * pick).astype(BF)
        back_up = (dot_nt(grad_upper, second_ref[1]) * pick).astype(BF)
        high, low = two_parts(gate_grad)
        lane = lane_index((count + rest_count // 4, 128))
        back_notes = jnp.where(
            lane == PAIR,
            high.astype(F32),
            jnp.where(
                lane == PAIR + 1, low.astype(F32), dot(back_gate, fold) + dot(back_up, fold_later)
            ),
        ).astype(BF)
        write(back_buf[0], back[:count])
        write(back_buf[1], rows_to_rest(selectors, back[count:]))
        write(back_buf[2], back_notes[:count])
        write(back_buf[3], dot_tn(selectors[0], back_notes[count:]).astype(BF))
        for peer in peers:

            @pl.when(peer == me)
            def keep():
                for kind in range(BACK):
                    own_copy(kind).start()

            @pl.when(peer != me)
            def send():
                for kind in range(BACK):
                    back_copy(kind, peer, me).start()

        total[:LANES] += dot_tn(lanes_gate, grad_gate)
        total[LANES : 2 * LANES] += dot_tn(lanes_up, grad_upper)
        total[2 * LANES :] += dot_tn(grad_side, hidden)
        total_down[...] += dot_tn(side, grad_routed)
        return carry

    lax.fori_loop(0, steps, block, 0)
    in_owner_columns(total, adapter_ref, total.shape[1] // experts)
    adapter_ref[3 * LANES :, :] = total_down[...].astype(BF)
    mover.finish()
    for offset in later:
        for kind in range(2):
            later_copy(kind, offset).wait_send()
    for kind in range(BACK):
        own_copy(kind).wait()

    def settle(offset, carry):
        peer = lax.rem(me + offset, experts)
        for kind in range(BACK):
            copy = back_copy(kind, peer, peer)
            copy.wait_send()
            copy.wait_recv()
        return carry

    lax.fori_loop(1, experts, settle, 0)


def routed_expert(number, held, later, values, first, second, down_first, down_second, gate_up, down):
    width, hidden = gate_up.shape[2:]
    experts = GROUP_SIZE["f"]
    vmem = pl.BlockSpec(memory_space=pltpu.VMEM)
    back = [held[0], held[1], held[4], held[5], held[0], held[1]]
    items = [("swap", "x", values)]
    return pl.pallas_call(
        routed_kernel,
        out_shape=[shape_of(array.shape, BF) for array in (*back, values)]
        + [shape_of((4 * LANES, experts * 128), BF)],
        in_specs=[HBM] * 11 + [vmem] * 4,
        out_specs=[HBM] * (BACK + 1) + [vmem],
        scratch_shapes=mover_scratch(items)
        + [pltpu.VMEM(array.shape, BF) for array in held]
        + [pltpu.VMEM(array.shape, BF) for array in back]
        + [
            pltpu.VMEM((2, width, hidden), BF),
            pltpu.VMEM((hidden, width), BF),
            pltpu.VMEM((3 * LANES, hidden), F32),
            pltpu.VMEM((LANES, width), F32),
            pltpu.SemaphoreType.DMA((BACK, experts)),
            pltpu.SemaphoreType.DMA((BACK, experts)),
            pltpu.SemaphoreType.DMA((9,)),
            pltpu.SemaphoreType.DMA((BACK,)),
            pltpu.SemaphoreType.DMA((2, experts)),
            pltpu.SemaphoreType.DMA((2, experts)),
            pltpu.SemaphoreType.DMA((2, experts)),
        ],
        compiler_params=pltpu.CompilerParams(
            collective_id=number, has_side_effects=True, vmem_limit_bytes=VMEM_LIMIT
        ),
        name="routed_expert",
    )(*held, gate_up, down, values, *later, first, second, down_first, down_second)


def after_experts_kernel(
    numbers_ref,
    parts_ref,
    part_notes_ref,
    main_ref,
    rest_ref,
    main_notes_ref,
    rest_notes_ref,
    grads_ref,
    normed_ref,
    residual_ref,
    small_ref,
    mixed_ref,
    routes_ref,
    side_ref,
    ffn_a_ref,
    ffn_b_ref,
    router_ref,
    router_a_ref,
    router_b_ref,
    mix_ref,
    gain_ref,
    down_a_ref,
    down_b_ref,
    first_a_ref,
    first_b_ref,
    second_a_ref,
    second_b_ref,
    weight_hbm,
    grad_residual_ref,
    grad_mixed_ref,
    adapter_ref,
    router_grad_ref,
    shared_side_ref,
    weight_ref,
    sem,
):
    load = pltpu.make_async_copy(weight_hbm, weight_ref, sem)
    load.start()
    experts = router_ref.shape[1]
    side = side_ref[...]
    pick = pair_pick(side, 1)
    grads = grads_ref[0]
    grads_f = grads.astype(F32)
    normed = normed_ref[...]
    out_lanes = small_ref[:, :PAIR].astype(BF)
    router_lanes = small_ref[:, PAIR : 2 * PAIR].astype(BF)
    gates = [small_ref[:, 2 * PAIR + k : 2 * PAIR + k + 1] for k in range(TOP)]
    mix = small_ref[:, 2 * PAIR + TOP : 2 * PAIR + TOP + 1]
    notes = sum(part_notes_ref[i].astype(F32) for i in range(part_notes_ref.shape[0]))
    shared_side = notes[:, :PAIR].astype(BF)
    shared_side_ref[...] = padded(shared_side)
    down_second = pair_of(down_a_ref, down_b_ref, 0)
    mix_total = (
        notes[:, 3 * PAIR : 3 * PAIR + 1]
        + notes[:, 3 * PAIR + 1 : 3 * PAIR + 2]
        + jnp.sum(shared_side.astype(F32) * dot_nt(grads, down_second), axis=1, keepdims=True)
    )
    grad_mix = mix_total * mix * (1.0 - mix)
    grad_shared = (mix * grads_f).astype(BF)
    expert_hot, main_hot, rest_hot = routing(routes_ref[0], experts)
    grad_gates = []
    mask = quarter_mask(rest_hot[0].shape, 0)
    token_notes = None
    for k in range(TOP):
        mine = dot(main_hot[k].astype(BF), main_notes_ref[...]) + dot(
            (rest_hot[k] * mask).astype(BF), rest_notes_ref[...]
        )
        grad_gates.append(mine[:, PAIR : PAIR + 1] + mine[:, PAIR + 1 : PAIR + 2])
        token_notes = mine if k == 0 else token_notes + mine
    inner = sum(gate * grad for gate, grad in zip(gates, grad_gates))
    grad_logits = sum(
        hot * (gate * (grad - inner)) for hot, gate, grad in zip(expert_hot, gates, grad_gates)
    )
    logits_high, logits_low = two_parts(grad_logits)
    router_second = jnp.concatenate([router_a_ref[0], router_b_ref[0]], axis=0)
    grad_router_lanes = dot_nt(logits_high, router_second) + dot_nt(logits_low, router_second)
    router_grad = dot_tn(router_lanes, logits_high) + dot_tn(router_lanes, logits_low)
    of_row = jnp.where(row_index((PAIR, 128)) < RANK, numbers_ref[0], numbers_ref[1]).astype(F32)
    router_grad_ref[...] = jnp.where(
        lane_index((PAIR, 128)) == experts, of_row, padded(router_grad)
    ).astype(BF)
    lane_grads = (
        jnp.concatenate(
            [
                grad_router_lanes,
                notes[:, PAIR : 3 * PAIR],
                token_notes[:, :RANK],
                token_notes[:, :RANK],
                token_notes[:, RANK:PAIR],
                token_notes[:, RANK:PAIR],
            ],
            axis=1,
        )
        * pair_pick(side, 5)
    ).astype(BF)
    factors = ffn_a_ref.shape[0]
    ffn_first = jnp.concatenate([pair_of(ffn_a_ref, ffn_b_ref, i) for i in range(factors)], axis=0)
    grad_second = (
        grad_mix * mix_ref[...].astype(F32)
        + dot_nt(logits_high, router_ref[...])
        + dot_nt(logits_low, router_ref[...])
        + sum(parts_ref[i].astype(F32) for i in range(parts_ref.shape[0]))
        + slots_to_rows(main_hot, rest_hot, main_ref[...], rest_ref[...])
        + dot(lane_grads, ffn_first)
    )
    grad_residual = grads_f + rms_backward(residual_ref[...], gain_ref[...], grad_second)
    grad_residual_ref[...] = grad_residual
    grad_attended = grad_residual.astype(BF)
    first, second = pair_of(first_a_ref, first_b_ref, 0), pair_of(second_a_ref, second_b_ref, 0)
    grad_out_lanes = (dot_nt(grad_attended, second) * pick).astype(BF)
    adapter_ref[...] = jnp.concatenate(
        [
            dot_tn(lane_grads, normed),
            dot_tn(grad_out_lanes, mixed_ref[...]),
            dot_tn(out_lanes, grad_attended),
            dot_tn(shared_side, grad_shared),
        ],
        axis=0,
    ).astype(BF)
    load.wait()
    grad_mixed_ref[...] = (
        dot_nt(grad_attended, weight_ref[...]) + dot(grad_out_lanes, first)
    ).astype(BF)


def after_experts(
    numbers, parts, part_notes, main, rest, main_notes, rest_notes, grads, normed, residual, small, mixed,
    routes, side, ffn_first, router, router_second, mix, gain, down_second, first, second, weight,
):
    tokens, width = normed.shape
    experts = router.shape[1]
    factors = ffn_first.shape[0]
    last = lambda which: pl.BlockSpec((1, 1, RANK, width), lambda n, a: (3, a[which], 0, 0))
    outs = [
        ((tokens, width), F32),
        ((tokens, width), BF),
        (((factors + 3) * PAIR, width), BF),
        ((PAIR, 128), BF),
        ((tokens, 128), BF),
    ]
    plain = (
        parts, part_notes, main, rest, main_notes, rest_notes, grads, normed, residual, small, mixed, routes,
        side,
    )
    return stage(
        after_experts_kernel,
        "after_experts",
        [shape_of(*out) for out in outs],
        [whole(array) for array in plain]
        + [
            of_sequence(0, (factors, 1, RANK, width)),
            of_sequence(1, (factors, 1, RANK, width)),
            whole(router),
            pl.BlockSpec((1, RANK, experts), lambda n, a: (a[0], 0, 0)),
            pl.BlockSpec((1, RANK, experts), lambda n, a: (a[1], 0, 0)),
            whole(mix),
            whole(gain),
            of_sequence(0, (1, 1, RANK, width)),
            of_sequence(1, (1, 1, RANK, width)),
            last(0),
            last(1),
            last(0),
            last(1),
            HBM,
        ],
        [pl.BlockSpec(shape, lambda n, a: (0, 0)) for shape, kind in outs],
        scratch=[pltpu.VMEM(weight.shape, BF), pltpu.SemaphoreType.DMA],
        prefetch=1,
    )(
        numbers, *plain, ffn_first, ffn_first, router, router_second, router_second, mix, gain, down_second,
        down_second, first, first, second, second, weight,
    )


def attention_back_kernel(plan, heads_plan, *refs):
    amount = len(plan)
    inputs, expert_hbm, refs = refs[:amount], refs[amount], refs[amount + 1 :]
    mixed_hbm, query_hbm, pairs_hbm, weight_hbm = refs[:4]
    place_ref, start_ref, key_place_ref, cos_ref, sin_ref, side_ref, lanes_ref, second_ref = refs[4:12]
    results, ends, refs = list(refs[12:20]), list(refs[20:26]), refs[26:]
    out_ref, end_outs, refs = refs[0], refs[1:11], refs[11:]
    outputs, refs = refs[:amount], refs[amount:]
    heads_got, parts_ref, notes_ref, expert_ref, refs = *refs[:4], refs[4:]
    late_bufs, late_sem, refs = refs[:6], refs[6], refs[7:]
    end_scratch, refs = refs[:END_SCRATCH], refs[END_SCRATCH:]
    own, move_sems, refs = refs[:amount], refs[amount : amount + 4], refs[amount + 4 :]
    heads_own, heads_sems, refs = refs[:1], refs[1:5], refs[5:]
    expert_own, expert_sems, refs = refs[:1], refs[1:5], refs[5:]
    mixed_buf, query_buf, pairs_buf, weight_buf = refs[:4]
    sent_buf, got_buf, grads_buf, heads_buf, parts_buf, notes_buf = refs[4:10]
    mixed_send, mixed_recv, pair_send, pair_recv, parts_send, parts_recv, load_sem, own_sem = refs[10:]

    x, y = place_in("x"), place_in("y")
    along, tokens, columns = mixed_buf.shape
    rows_all = along * tokens
    heads = columns // HEAD_DIM
    loads = [
        pltpu.make_async_copy(block_of(mixed_hbm, "columns", along, x), mixed_buf.at[x], load_sem.at[0]),
        pltpu.make_async_copy(query_hbm.at[0], query_buf, load_sem.at[1]),
        pltpu.make_async_copy(pairs_hbm, pairs_buf, load_sem.at[2]),
    ]
    loads += [
        pltpu.make_async_copy(weight_hbm.at[:, j], weight_buf.at[j], load_sem.at[3 + j])
        for j in range(3)
    ]
    for load in loads:
        load.start()
    late_loads = []
    for i, (group, place) in enumerate(LATE):
        refs_of = (results, ends)[group]
        late_loads.append(pltpu.make_async_copy(refs_of[place], late_bufs[i], late_sem.at[i]))
        refs_of[place] = late_bufs[i]
    for load in late_loads:
        load.start()
    mover = Mover(plan, inputs, outputs, own, *move_sems)
    mover.take()
    expert_mover = Mover((("rows", "x"),), (expert_hbm,), (expert_ref,), expert_own, *expert_sems)
    expert_mover.take()
    greet((("rows", "f"), ("swap", "x"), ("swap", "y"), ("rows", "c")))

    def mixed_copy(offset):
        peer = lax.rem(x + offset, along)
        return remote(
            block_of(mixed_hbm, "columns", along, peer),
            mixed_buf.at[x],
            mixed_send.at[offset],
            mixed_recv.at[offset],
            device_of("x", peer),
        )

    def pair_copy(head):
        return remote(
            sent_buf.at[1 - y, head],
            got_buf.at[head],
            pair_send.at[head],
            pair_recv.at[head],
            device_of("y", 1 - y),
        )

    def parts_copy(offset):
        peer = lax.rem(x + offset, along)
        return remote(
            parts_buf.at[peer],
            parts_ref.at[x],
            parts_send.at[0, offset],
            parts_recv.at[0, offset],
            device_of("x", peer),
        )

    def notes_copy(offset):
        peer = lax.rem(x + offset, along)
        return remote(
            notes_buf.at[peer],
            notes_ref.at[x],
            parts_send.at[1, offset],
            parts_recv.at[1, offset],
            device_of("x", peer),
        )

    for offset in (2, 1, 3):
        mixed_copy(offset).start()
    for load in loads[:3]:
        load.wait()
    for offset in (1, 3, 2):
        mixed_copy(offset).wait_recv()
    expert_mover.start()

    step = rows_all // 2

    def head_block(head, carry):
        here = pl.ds(pl.multiple_of(head * HEAD_DIM, HEAD_DIM), HEAD_DIM)
        keys = pairs_buf[:, 0, :, here].reshape(-1, HEAD_DIM)
        values = pairs_buf[:, 1, :, here].reshape(-1, HEAD_DIM)
        key_total, value_total = None, None
        for i in range(2):
            at = slice(i * step, (i + 1) * step)
            query = query_buf[at, here]
            blocks = along // 2
            grad = mixed_buf[i * blocks : (i + 1) * blocks, :, here].reshape(step, HEAD_DIM)
            probs = probabilities(query, keys, place_ref[at], start_ref[at], key_place_ref[...])
            grad_probs = dot_nt(grad, values)
            mean = jnp.sum(probs * grad_probs, axis=1, keepdims=True)
            grad_scores = (probs * (grad_probs - mean)).astype(BF)
            grad_query = dot(grad_scores, keys) * (HEAD_DIM**-0.5)
            grads_buf[0, at, here] = (
                grad_query * cos_ref[at] - half_turn(grad_query) * sin_ref[at]
            ).astype(BF)
            grad_keys = dot_tn(grad_scores, query) * (HEAD_DIM**-0.5)
            grad_values = dot_tn(probs.astype(BF), grad)
            key_total = grad_keys if i == 0 else key_total + grad_keys
            value_total = grad_values if i == 0 else value_total + grad_values
        for half in range(2):
            at = slice(half * rows_all, (half + 1) * rows_all)
            sent_buf[half, head, 0] = key_total[at].astype(BF)
            sent_buf[half, head, 1] = value_total[at].astype(BF)
        pair_copy(head).start()
        return carry

    lax.fori_loop(0, heads, head_block, 0)
    for load in late_loads:
        load.wait()
    combine_kernel(*results, out_ref)

    def head_sum(head, carry):
        here = pl.ds(pl.multiple_of(head * HEAD_DIM, HEAD_DIM), HEAD_DIM)
        pair_copy(head).wait_recv()
        key = sent_buf[y, head, 0].astype(F32) + got_buf[head, 0].astype(F32)
        grads_buf[1, :, here] = (key * cos_ref[...] - half_turn(key) * sin_ref[...]).astype(BF)
        value = sent_buf[y, head, 1].astype(F32) + got_buf[head, 1].astype(F32)
        grads_buf[2, :, here] = value.astype(BF)
        return carry

    lax.fori_loop(0, heads, head_sum, 0)
    pick = pair_pick(side_ref[...], 1)
    notes = []
    heads_buf[...] = jnp.zeros_like(heads_buf)
    own_columns = pl.ds(pl.multiple_of(x * columns, columns), columns)
    for j in range(3):
        at = slice(j * PAIR, (j + 1) * PAIR)
        notes.append((dot_nt(grads_buf[j], second_ref[at]) * pick).astype(BF))
        heads_buf[at, own_columns] = dot_tn(lanes_ref[j], grads_buf[j]).astype(BF)
    notes_buf[...] = padded(jnp.concatenate(notes, axis=1)).reshape(notes_buf.shape)
    heads_mover = Mover(heads_plan, (heads_buf,), (heads_got,), heads_own, *heads_sems)
    heads_mover.take()
    heads_mover.start()
    for offset in (1, 3, 2):
        notes_copy(offset).start()
    mover.start()
    own_notes = pltpu.make_async_copy(notes_buf.at[x], notes_ref.at[x], own_sem.at[0])
    own_notes.start()
    for load in loads[3:]:
        load.wait()

    def own_parts():
        return pltpu.make_async_copy(parts_buf.at[x], parts_ref.at[x], own_sem.at[1])

    def row_block(number, carry):
        offset = x_step(lax.rem(number + 1, along))
        peer = lax.rem(x + offset, along)
        at = pl.ds(pl.multiple_of(peer * tokens, tokens), tokens)
        total = None
        for j in range(3):
            part = dot_nt(grads_buf[j, at], weight_buf[j].reshape(-1, columns))
            total = part if total is None else total + part
        parts_buf[peer] = total.astype(BF)

        @pl.when(number < along - 1)
        def send():
            parts_copy(offset).start()

        @pl.when(number == along - 1)
        def keep():
            own_parts().start()

        return carry

    lax.fori_loop(0, along, row_block, 0)
    mover.finish()
    heads_mover.finish()
    expert_mover.finish()
    own_notes.wait()
    own_parts().wait()

    def pairs_sent(head, carry):
        pair_copy(head).wait_send()
        return carry

    lax.fori_loop(0, heads, pairs_sent, 0)
    for offset in range(1, along):
        mixed_copy(offset).wait_send()
        parts_copy(offset).wait()
        notes_copy(offset).wait()
    early_got, shared_got, router_got = outputs
    got = (router_got, early_got, shared_got, heads_got, ends[5], expert_ref)
    finish_kernel(parts_ref, notes_ref, *ends[:5], *got, *end_outs, *end_scratch)


LATE = ((0, 0), (0, 3), (0, 4), (1, 0), (1, 1), (1, 2))
END_SCRATCH = 18 + 6 * 4 + 9


def attention_back(number, items, expert, mixed, query, pairs, weight, small, results, ends, columns_of):
    plan = tuple((kind, group) for kind, group, array in items)
    arrays = [array for kind, group, array in items]
    along = GROUP_SIZE["x"]
    tokens, width = mixed.shape
    columns = width // along
    heads = columns // HEAD_DIM
    rows_all = along * tokens
    heads_items = [("from_columns", "f", shape_of((3 * PAIR, width), BF))]
    vmem = pl.BlockSpec(memory_space=pltpu.VMEM)
    got = [exchanged_shape(kind, group, array.shape) for kind, group, array in items]
    got += [
        exchanged_shape("from_columns", "f", (3 * PAIR, width)),
        (along, tokens, width),
        (along, tokens, 128),
        expert.shape,
    ]
    late = [(results, ends)[group][place] for group, place in LATE]
    in_specs = [[vmem] * len(results), [vmem] * len(ends)]
    for group, place in LATE:
        in_specs[group][place] = HBM
    end_outs, end_scratch = finish_shapes(ends[0], ends[4], items, expert, columns_of)
    assert len(end_scratch) == END_SCRATCH
    dma = pltpu.SemaphoreType.DMA
    return pl.pallas_call(
        functools.partial(attention_back_kernel, plan, (("from_columns", "f"),)),
        out_shape=[shape_of((1, tokens, width), BF), *end_outs],
        in_specs=[HBM] * (len(items) + 5) + [vmem] * len(small) + in_specs[0] + in_specs[1],
        out_specs=[vmem] * (1 + len(end_outs)),
        scratch_shapes=[pltpu.VMEM(shape, BF) for shape in got]
        + [pltpu.VMEM(array.shape, array.dtype) for array in late]
        + [dma((len(LATE),))]
        + end_scratch
        + mover_scratch(items)
        + mover_scratch(heads_items)
        + mover_scratch([("rows", "x", expert)])
        + [
            pltpu.VMEM((along, tokens, columns), BF),
            pltpu.VMEM((rows_all, columns), BF),
            pltpu.VMEM(pairs.shape, BF),
            pltpu.VMEM((3, *weight.shape[:1], *weight.shape[2:]), BF),
            pltpu.VMEM((2, heads, 2, rows_all, HEAD_DIM), BF),
            pltpu.VMEM((heads, 2, rows_all, HEAD_DIM), BF),
            pltpu.VMEM((3, rows_all, columns), BF),
            pltpu.VMEM((3 * PAIR, width), BF),
            pltpu.VMEM((along, tokens, width), BF),
            pltpu.VMEM((along, tokens, 128), BF),
            dma((along,)),
            dma((along,)),
            dma((heads,)),
            dma((heads,)),
            dma((2, along)),
            dma((2, along)),
            dma((6,)),
            dma((2,)),
        ],
        compiler_params=pltpu.CompilerParams(
            collective_id=number, has_side_effects=True, vmem_limit_bytes=VMEM_LIMIT
        ),
        name="attention_back",
    )(*arrays, expert, mixed, query, pairs, weight, *small, *results, *ends)


def lane_expansion(ids_ref, group):
    ids = ids_ref[group][:, GROUP_SIZE["f"] : GROUP_SIZE["f"] + 1].astype(F32)
    lane = lane_index((PAIR, LANES))
    same = (lane // RANK).astype(F32) == ids
    return (same & (lane % RANK == row_index((PAIR, LANES)) % RANK)).astype(BF)


def expanded(expansions, got_ref, factor):
    total = None
    for group, expansion in enumerate(expansions):
        part = dot_tn(expansion, got_ref[group, factor * PAIR : (factor + 1) * PAIR, :])
        total = part if total is None else total + part
    return total.astype(BF)


FINISH = (
    (("from_columns", "f"),),
    (("from_columns", "f"),),
    (("rows", "c"), ("rows", "y")),
    (("gather", "c"), ("gather", "c"), ("gather", "c")),
    (("rows", "c"),),
    (("gather", "c"),),
)


def finish_kernel(*refs):
    parts_ref, notes_ref, rows_ref, normed_ref, residual_ref, gain_ref, first_ref = refs[:7]
    ids_ref, early_ref, shared_ref, heads_ref, column_ref, expert_ref = refs[7:13]
    grad_out, attn_in, attn_out, ffn_out, router_out, shared_out, shared_in_out = refs[13:20]
    expert_out, expert_in_out, down_out, expert_buf, refs = *refs[20:24], refs[24:]
    late_buf, late_got, early_buf, early_parts, shared_buf, shared_parts = refs[:6]
    expert_got, late_sum, early_row, shared_row, expert_sum = refs[6:11]
    late_all, early_all, shared_all, expert_all, late_parts, late_row, refs = *refs[11:17], refs[17:]
    ends = (
        ((expert_buf,), (expert_got,)),
        ((late_buf,), (late_got,)),
        ((early_buf, shared_buf), (early_parts, shared_parts)),
        ((early_row, shared_row, expert_sum), (early_all, shared_all, expert_all)),
        ((late_sum,), (late_parts,)),
        ((late_row,), (late_all,)),
    )
    movers = []
    for plan, (inputs, outputs) in zip(FINISH, ends):
        own, sems, refs = refs[: len(plan)], refs[len(plan) : len(plan) + 4], refs[len(plan) + 4 :]
        movers.append(Mover(plan, inputs, outputs, own, *sems))

    def begin(mover):
        mover.take()
        mover.start()

    lanes = sum(notes_ref[i].astype(F32) for i in range(notes_ref.shape[0]))[:, : 3 * PAIR]
    lanes = lanes.astype(BF)
    late_buf[...] = dot_tn(lanes, normed_ref[...]).astype(BF)
    begin(movers[1])
    count = expert_buf.shape[0]
    expert_buf[...] = sum(
        expert_ref[i * count : (i + 1) * count].astype(F32) for i in range(GROUP_SIZE["x"])
    ).astype(BF)
    begin(movers[0])

    groups = ids_ref.shape[0]
    expansions = [lane_expansion(ids_ref, group) for group in range(groups)]
    row = 0
    for got in (early_ref, heads_ref):
        for factor in range(got.shape[1] // PAIR):
            early_buf[row : row + LANES, :] = expanded(expansions, got, factor)
            row += LANES
    router = None
    for group in range(groups):
        part = dot_tn(expansions[group], ids_ref[group])
        router = part if router is None else router + part
    router = jnp.sum(router * column_ref[...].astype(F32), axis=1, keepdims=True)
    early_buf[row : row + LANES, :] = jnp.broadcast_to(router, (LANES, 128)).astype(BF)
    for factor in range(shared_ref.shape[1] // PAIR):
        shared_buf[factor * LANES : (factor + 1) * LANES, :] = expanded(
            expansions, shared_ref, factor
        )
    begin(movers[2])

    grad = sum(parts_ref[i].astype(F32) for i in range(parts_ref.shape[0]))
    grad = grad + dot(lanes, first_ref[...])
    total = residual_ref[...] + rms_backward(rows_ref[0].astype(F32), gain_ref[...], grad)
    grad_out[0] = total.astype(BF)

    movers[1].finish()
    for factor in range(late_got.shape[1] // PAIR):
        late_sum[factor * LANES : (factor + 1) * LANES, :] = expanded(expansions, late_got, factor)
    begin(movers[4])
    movers[0].finish()
    expert_sum[...] = sum(expert_got[i].astype(F32) for i in range(groups)).astype(BF)
    movers[2].finish()
    count = early_row.shape[0]
    early_row[...] = sum(
        early_parts[i * count : (i + 1) * count].astype(F32) for i in range(GROUP_SIZE["c"])
    ).astype(BF)
    count = shared_row.shape[0]
    shared_row[...] = (
        shared_parts[:count].astype(F32) + shared_parts[count:].astype(F32)
    ).astype(BF)
    begin(movers[3])
    movers[4].finish()
    count = late_row.shape[0]
    late_row[...] = sum(
        late_parts[i * count : (i + 1) * count].astype(F32) for i in range(GROUP_SIZE["c"])
    ).astype(BF)
    begin(movers[5])

    movers[3].finish()
    early = early_all[...].reshape(-1, 128).astype(F32)
    expert = jnp.concatenate(
        [
            expert_all[2 * i].astype(F32) + expert_all[2 * i + 1].astype(F32)
            for i in range(GROUP_SIZE["x"])
        ],
        axis=0,
    )
    factor = [early[i * LANES : (i + 1) * LANES] for i in range(early.shape[0] // LANES)]
    attn_in[3 * LANES :, :] = factor[5]
    attn_out[: 3 * LANES, :] = jnp.concatenate(factor[8:11], axis=0)
    attn_out[3 * LANES :, :] = factor[6]
    ffn_out[...] = jnp.concatenate(factor[:5], axis=0)
    router_out[...] = factor[11][:, : router_out.shape[1]]
    down_out[:LANES, :] = factor[7]
    down_out[LANES:, :] = expert[3 * LANES :]
    expert_out[...] = expert[: 2 * LANES, : expert_out.shape[1]]
    expert_in_out[...] = expert[2 * LANES : 3 * LANES, : expert_in_out.shape[1]]
    along = GROUP_SIZE["x"]
    columns = shared_out.shape[1] // along
    quarters = [
        shared_all[2 * i : 2 * i + 2].reshape(-1, 128)[:, :columns].astype(F32) for i in range(along)
    ]
    shared_rows = jnp.concatenate(quarters, axis=1)
    shared_out[...] = shared_rows[: 2 * LANES]
    shared_in_out[...] = shared_rows[2 * LANES :]
    movers[5].finish()
    attn_in[: 3 * LANES, :] = late_all[...].reshape(-1, 128).astype(F32)


def finish_shapes(rows, first, items, expert, columns_of):
    width = rows.shape[2]
    early, shared = items[0][2], items[1][2]
    shared_columns, expert_columns = columns_of
    groups, ctx = GROUP_SIZE["f"], GROUP_SIZE["c"]
    early_rows = ((early.shape[0] + first.shape[0]) // PAIR + 1) * LANES
    late_rows = first.shape[0] // PAIR * LANES
    shared_rows = shared.shape[0] // PAIR * LANES
    expert_rows = expert.shape[0] // GROUP_SIZE["x"]
    bufs = [
        first.shape,
        (groups, first.shape[0], 128),
        (early_rows, 128),
        (early_rows, 128),
        (shared_rows, 128),
        (shared_rows, 128),
        (groups, expert_rows, 128),
        (late_rows, 128),
        (early_rows // ctx, 128),
        (shared_rows // 2, 128),
        (expert_rows, 128),
        (ctx, late_rows // ctx, 128),
        (ctx, early_rows // ctx, 128),
        (ctx, shared_rows // 2, 128),
        (ctx, expert_rows, 128),
        (late_rows, 128),
        (late_rows // ctx, 128),
    ]
    sent = (((expert_rows, width),), (bufs[0],), (bufs[2], bufs[4]), (bufs[8], bufs[9], bufs[10]), (bufs[7],), (bufs[16],))
    scratch = [pltpu.VMEM(buf, BF) for buf in ((expert_rows, width), *bufs)]
    for plan, shapes in zip(FINISH, sent):
        scratch += mover_scratch(
            [(kind, group, shape_of(shape, BF)) for (kind, group), shape in zip(plan, shapes)]
        )
    outs = [
        shape_of(rows.shape, BF),
        shape_of((4 * LANES, 128), F32),
        shape_of((4 * LANES, 128), F32),
        shape_of((5 * LANES, 128), F32),
        shape_of((LANES, 1), F32),
        shape_of((2 * LANES, shared_columns), F32),
        shape_of((LANES, shared_columns), F32),
        shape_of((2 * LANES, expert_columns), F32),
        shape_of((LANES, expert_columns), F32),
        shape_of((2 * LANES, 128), F32),
    ]
    return outs, scratch


def combine_kernel(
    main_ref, rest_ref, routes_ref, residual_ref, parts_ref, side_ref, small_ref, picked_ref, out_ref
):
    experts = main_ref.shape[0] // MAIN
    unused, main_hot, rest_hot = routing(routes_ref[0], experts)
    mixture = slots_to_rows(main_hot, rest_hot, main_ref[...], rest_ref[...])
    shared = sum(parts_ref[i].astype(F32) for i in range(parts_ref.shape[0]))
    shared = shared + dot(side_ref[:, :PAIR], picked_ref[2 * PAIR :])
    mix = small_ref[:, 2 * PAIR + TOP : 2 * PAIR + TOP + 1]
    out_ref[0] = (residual_ref[...] + mixture + mix * shared).astype(BF)


def shards(
    layer_hidden_input,
    output_cotangent,
    sequence_pair_lengths,
    block_placement_order,
    sequence_adapter_index,
    token_expert_choices,
    attention_norm_gain,
    feedforward_norm_gain,
    query_key_value_weight,
    output_projection_weight,
    query_key_value_bias,
    router_weight_matrix,
    shared_gate_up_weight,
    shared_down_weight,
    shared_sigmoid_gate,
    routed_gate_up_weight,
    routed_down_weight,
    attention_adapter_first,
    attention_adapter_second,
    feedforward_adapter_first,
    router_adapter_second,
    shared_gate_adapter_second,
    shared_down_adapter_first,
    routed_gate_adapter_second,
    routed_down_adapter_first,
    down_adapter_second,
):
    tokens, width = layer_hidden_input.shape[1:]
    experts = router_weight_matrix.shape[1]
    capacity = tokens * TOP // experts * 9 // 8
    tail = capacity - MAIN
    ctx_count = lax.axis_size("ctx")
    group_rows = tokens * ctx_count
    along = ctx_count // 2
    rows_shared = tokens * along
    x_index = lax.axis_index("ctx") // 2
    y_index = lax.axis_index("ctx") % 2
    head_columns = width // along
    hidden = shared_down_weight.shape[0]
    quarter = hidden // along
    shards_of = lax.axis_size("fsdp")
    lengths = sequence_pair_lengths[0]
    order = block_placement_order[0]
    adapters = sequence_adapter_index[0]
    block_size = group_rows // order.shape[0]

    qkv_own = lax.dynamic_slice_in_dim(
        query_key_value_weight, x_index * head_columns, head_columns, 2
    ).reshape(-1, head_columns)
    out_weight = lax.all_gather(output_projection_weight, "fsdp", tiled=True)
    units = -(-quarter // 32) * 32
    own_up = jnp.swapaxes(
        lax.dynamic_slice_in_dim(shared_gate_up_weight, x_index * quarter, quarter, 2), 1, 2
    )
    own_down = lax.dynamic_slice_in_dim(shared_down_weight, x_index * quarter, quarter, 0)
    own_shared = jnp.pad(
        jnp.concatenate([own_up, own_down[None]]), ((0, 0), (0, units - quarter), (0, 0))
    ).reshape(3 * units, width)

    def of_group(factor):
        parts = [lax.dynamic_index_in_dim(factor, adapters[s], -3, keepdims=True) for s in range(2)]
        both = jnp.concatenate(parts, axis=-3)
        return both.reshape(both.shape[:-3] + (PAIR, both.shape[-1]))

    shared_second = jnp.concatenate(
        [
            of_group(shared_gate_adapter_second).reshape(2 * PAIR, hidden * shards_of),
            of_group(shared_down_adapter_first),
        ],
        axis=0,
    )
    shared_second = lax.dynamic_index_in_dim(
        shared_second.reshape(3 * PAIR, shards_of, along, quarter), x_index, 2, keepdims=False
    )
    shared_second = jnp.pad(shared_second, ((0, 0), (0, 0), (0, units - quarter)))
    shared_second = shared_second.reshape(3, PAIR, shards_of, units).transpose(0, 2, 3, 1)
    shared_second = jnp.stack(
        [
            jnp.pad(shared_second[i], ((0, 0), (0, 0), (before, 128 - PAIR - before)))
            for i, before in enumerate((0, PAIR, 0))
        ]
    )
    numbers = jnp.concatenate([adapters, x_index[None].astype(jnp.int32)])

    start = lengths[0]
    block_rows = jnp.arange(block_size, dtype=jnp.int32)
    blocks = order.reshape(along, 2, -1)
    key_places = (jnp.swapaxes(blocks, 0, 1).reshape(-1)[:, None] * block_size + block_rows).reshape(
        1, group_rows
    )
    own_blocks = lax.dynamic_index_in_dim(blocks, y_index, 1, keepdims=False).reshape(-1)
    places = own_blocks[:, None] * block_size + block_rows
    second = places >= start
    fractions = jnp.arange(0, HEAD_DIM, 2).astype(F32) / HEAD_DIM
    speeds = rope_theta ** (-fractions)
    bases = jnp.stack([own_blocks * block_size, own_blocks * block_size - start])
    base_angles = bases.astype(F32)[:, :, None, None] * speeds
    base_angles = jnp.concatenate([base_angles, base_angles], axis=3)
    base_cos, base_sin = jnp.cos(base_angles), jnp.sin(base_angles)
    base_cos = jnp.where(second[:, :, None], base_cos[1], base_cos[0])
    base_sin = jnp.where(second[:, :, None], base_sin[1], base_sin[0])
    row_angles = block_rows.astype(F32)[:, None] * speeds[None, :]
    row_angles = jnp.concatenate([row_angles, row_angles], axis=1)
    row_cos, row_sin = jnp.cos(row_angles), jnp.sin(row_angles)
    cosine = base_cos * row_cos - base_sin * row_sin
    sine = base_sin * row_cos + base_cos * row_sin
    sine = jnp.where(jnp.arange(HEAD_DIM) < HEAD_DIM // 2, -sine, sine)
    cosine, sine = cosine.reshape(rows_shared, HEAD_DIM), sine.reshape(rows_shared, HEAD_DIM)
    place_column = places.reshape(rows_shared, 1)
    start_column = jnp.where(second, start, 0).reshape(rows_shared, 1)
    side_shared = second.astype(F32).reshape(rows_shared, 1)
    side = lax.dynamic_slice_in_dim(side_shared, x_index * tokens, tokens)

    attention_gain = attention_norm_gain[None, :]
    feedforward_gain = feedforward_norm_gain[None, :]
    mix_weight = shared_sigmoid_gate[None, :]
    routed_second = routed_gate_adapter_second.reshape(2, LANES, -1)
    routed_first = routed_down_adapter_first.reshape(LANES, -1)
    ffn_flat = feedforward_adapter_first.reshape(-1, LANES, width)[3:]
    down_flat = down_adapter_second.reshape(2, LANES, width)

    normed_one, sent_grads_main, sent_grads_rest, picked, picked_first, picked_second = prologue(
        numbers,
        layer_hidden_input,
        output_cotangent,
        attention_gain,
        token_expert_choices,
        feedforward_adapter_first,
        down_adapter_second,
        attention_adapter_first,
        attention_adapter_second,
        experts,
        head_columns,
    )
    own_shared, normed_one = lax.optimization_barrier((own_shared, normed_one))
    shared_weight = lax.all_gather(own_shared, "fsdp")
    qkv, normed_shared = exchange(
        "gather_first", 0, ("share", "s", qkv_own), ("gather", "x", normed_one)
    )
    qkv = qkv.reshape(shards_of, 3, tokens, head_columns)
    projected, qkv_lanes = project(
        numbers,
        normed_shared.reshape(rows_shared, width),
        qkv,
        attention_adapter_first,
        attention_adapter_second,
        query_key_value_bias,
        side_shared,
        cosine,
        sine,
    )
    pairs, grads_shared = exchange(
        "keys", 1, ("gather", "y", projected[1:]), ("gather", "x", output_cotangent[0])
    )
    mixed_heads = attend(projected, pairs, place_column, start_column, key_places)
    (mixed,) = exchange(
        "mixed", 2, ("to_columns", "x", mixed_heads.reshape(along, tokens, head_columns))
    )
    residual, normed_two, small, sent_main, sent_rest, notes_main, notes_rest = after_attention(
        numbers,
        mixed,
        out_weight,
        layer_hidden_input,
        attention_adapter_first,
        attention_adapter_second,
        feedforward_gain,
        feedforward_adapter_first,
        router_weight_matrix,
        router_adapter_second,
        mix_weight,
        token_expert_choices,
        side,
    )
    *held, parts_rows, parts_lanes, value_part, shared_columns = shared_expert(
        3,
        normed_two,
        [
            ("rows", "f", sent_main),
            ("rows", "f", sent_rest),
            ("half", "f", sent_grads_main),
            ("half", "f", sent_grads_rest),
            ("rows", "f", notes_main),
            ("rows", "f", notes_rest),
        ],
        grads_shared,
        shared_weight,
        side_shared.reshape(along, tokens, 1),
        picked,
        shared_second,
        mix_weight,
    )
    (
        got_main,
        got_rest,
        got_notes_main,
        got_notes_rest,
        result_main,
        result_rest,
        value_parts,
        expert_columns,
    ) = routed_expert(
        4,
        held,
        (sent_grads_main, sent_grads_rest),
        value_part,
        ffn_flat,
        routed_second,
        routed_first,
        down_flat,
        routed_gate_up_weight,
        routed_down_weight,
    )
    grad_residual, grad_mixed, early_columns, router_rows, shared_side = after_experts(
        numbers,
        parts_rows,
        parts_lanes,
        got_main,
        got_rest,
        got_notes_main,
        got_notes_rest,
        output_cotangent,
        normed_two,
        residual,
        small,
        mixed,
        token_expert_choices,
        side,
        feedforward_adapter_first,
        router_weight_matrix,
        router_adapter_second,
        mix_weight,
        feedforward_gain,
        down_adapter_second,
        attention_adapter_first,
        attention_adapter_second,
        out_weight,
    )

    own_column = (jnp.arange(128) == lax.axis_index("fsdp")).astype(BF)[None, :]
    output_value, *grads = attention_back(
        5,
        [
            ("from_columns", "f", early_columns),
            ("from_columns", "f", shared_columns),
            ("gather", "f", router_rows),
        ],
        expert_columns,
        grad_mixed,
        projected,
        pairs,
        qkv,
        (
            place_column,
            start_column,
            key_places,
            cosine,
            sine,
            side_shared,
            qkv_lanes,
            picked_second,
        ),
        (
            result_main,
            result_rest,
            token_expert_choices,
            residual,
            value_parts,
            shared_side,
            small,
            picked,
        ),
        (
            layer_hidden_input,
            normed_one,
            grad_residual,
            attention_gain,
            picked_first,
            own_column,
        ),
        (along * quarter, routed_down_weight.shape[1] // shards_of),
    )

    def by_adapter(rows):
        parts = rows.reshape(-1, ADAPTER_COUNT, RANK, rows.shape[1])
        return parts[0] if parts.shape[0] == 1 else parts

    return (output_value, grads[0], *(by_adapter(rows) for rows in grads[1:]))


def solution(mesh):
    return jax.shard_map(
        shards,
        mesh=mesh,
        in_specs=(
            P("fsdp", "ctx", None),
            P("fsdp", "ctx", None),
            P("fsdp", None),
            P("fsdp", None),
            P("fsdp", None),
            P("fsdp", "ctx", None),
            P(),
            P(),
            P(None, "fsdp", None),
            P("fsdp", None),
            P(),
            P(),
            P(None, None, "fsdp"),
            P("fsdp", None),
            P(),
            P("fsdp", None, None, None),
            P("fsdp", None, None),
            P(),
            P(),
            P(),
            P(),
            P(),
            P(),
            P(),
            P(),
            P(),
        ),
        out_specs=(
            P("fsdp", "ctx", None),
            P("fsdp", "ctx", None),
            P(None, None, None, "fsdp"),
            P(None, None, None, "fsdp"),
            P(None, None, None, "fsdp"),
            P(None, None, "fsdp"),
            P(None, None, None, "fsdp"),
            P(None, None, "fsdp"),
            P(None, None, None, "fsdp"),
            P(None, None, "fsdp"),
            P(None, None, None, "fsdp"),
        ),
        check_vma=False,
    )
```

```python
import functools

import jax
import jax.numpy as jnp
from jax import lax
from jax.experimental import pallas as pl
from jax.experimental.pallas import tpu as pltpu
from jax.sharding import PartitionSpec as P

HEADS = 16
HEAD_DIM = 128
TOP = 4
ADAPTER_COUNT = 8
RANK = 16
LANES = ADAPTER_COUNT * RANK
PAIR = 2 * RANK
MAIN = 32

norm_eps = 1e-06
rope_theta = 1000000.0
masked_score = -1e30
highest = lax.Precision.HIGHEST
MESH = pl.DeviceIdType.MESH
BF = jnp.bfloat16
F32 = jnp.float32
VMEM_LIMIT = 56 * 2**20


def dot(left, right):
    return jnp.dot(left, right, preferred_element_type=F32)


def dot_nt(left, right):
    return lax.dot_general(left, right, (((1,), (1,)), ((), ())), preferred_element_type=F32)


def dot_tn(left, right):
    return lax.dot_general(left, right, (((0,), (0,)), ((), ())), preferred_element_type=F32)


GROUP_SIZE = {"x": 4, "y": 2, "c": 8, "f": 16}


def place_in(group):
    ctx, fsdp = lax.axis_index("ctx"), lax.axis_index("fsdp")
    return {"x": ctx // 2, "y": ctx % 2, "c": ctx, "f": fsdp}[group]


def device_of(group, index):
    ctx, fsdp = lax.axis_index("ctx"), lax.axis_index("fsdp")
    if group == "x":
        return (index * 2 + ctx % 2, fsdp)
    if group == "y":
        return ((ctx // 2) * 2 + index, fsdp)
    if group == "c":
        return (index, fsdp)
    return (ctx, index)


def chip():
    ctx, fsdp = lax.axis_index("ctx"), lax.axis_index("fsdp")
    return ctx % 2 * 2 + fsdp // 8, fsdp // 2 % 4, fsdp % 2


def device_at(y, z, core):
    return (lax.axis_index("ctx") // 2 * 2 + y // 2, y % 2 * 8 + z * 2 + core)


def shard_at(y, z, core):
    return y % 2 * 8 + z * 2 + core


def exchanged_shape(kind, group, shape):
    if kind == "share":
        return (GROUP_SIZE["f"],) + shape
    count = GROUP_SIZE[group]
    if kind == "gather":
        return (count,) + shape
    if kind in ("swap", "rows", "half"):
        return shape
    if kind == "from_columns":
        return (count, shape[0], shape[1] // count)
    return (shape[1], count * shape[2])


def own_shape(kind, group, shape):
    if kind in ("gather", "share"):
        return shape
    count = GROUP_SIZE[group]
    if kind in ("rows", "half"):
        return (shape[0] // count,) + shape[1:]
    if kind == "from_columns":
        return (shape[0], shape[1] // count)
    return shape[1:]


def copies_of(kind, group):
    return 23 if kind == "share" else GROUP_SIZE[group] - 1


def soon(offset):
    return offset % ROUTED_STEPS >= ROUTED_STEPS // 2


def block_of(ref, kind, count, index):
    if kind == "rows":
        depth = ref.shape[0] // count
        return ref.at[pl.ds(pl.multiple_of(index * depth, depth), depth)]
    if kind == "columns":
        width = ref.shape[1] // count
        return ref.at[:, pl.ds(pl.multiple_of(index * width, width), width)]
    return ref.at[index]


def source_of(kind, group, ref, index):
    if kind in ("gather", "share"):
        return ref
    cut = {"rows": "rows", "half": "rows", "from_columns": "columns"}.get(kind, "first")
    return block_of(ref, cut, GROUP_SIZE[group], index)


def target_of(kind, group, ref, index):
    cut = {"rows": "rows", "half": "rows", "to_columns": "columns"}.get(kind, "first")
    return block_of(ref, cut, GROUP_SIZE["f" if kind == "share" else group], index)


def remote(source, target, send, recv, device):
    return pltpu.make_async_remote_copy(
        src_ref=source,
        dst_ref=target,
        send_sem=send,
        recv_sem=recv,
        device_id=device,
        device_id_type=MESH,
    )


def greet(plan):
    barrier = pltpu.get_barrier_semaphore()
    count = 0
    for group in sorted({group for kind, group in plan}):
        if group == "s":
            y, z, core = chip()
            peers = [device_at(y, lax.rem(z + d, 4), core) for d in (1, 2, 3)]
            peers += [device_at(lax.rem(y + d, 4), z, core) for d in (1, 3)]
            peers += [device_at(y, z, 1 - core)]
        else:
            size = GROUP_SIZE[group]
            mine = place_in(group)
            peers = [device_of(group, lax.rem(mine + d, size)) for d in range(1, size)]
        for peer in peers:
            pl.semaphore_signal(barrier, inc=1, device_id=peer, device_id_type=MESH)
        count += len(peers)
    pl.semaphore_wait(barrier, count)


class Share:
    def __init__(self, source, target, send, recv, first):
        self.target = target
        self.sems = (send, recv, first)
        y, z, core = self.place = chip()
        self.order = (1, 3, 2)
        self.source = source
        self.along_z = [
            self.copy(source, shard_at(y, z, core), None, i, device_at(y, lax.rem(z + d, 4), core))
            for i, d in enumerate(self.order)
        ]
        self.along_y, self.across = [], []

    def copy(self, source, shard, half, number, device):
        send, recv, first = self.sems
        target = self.target.at[shard]
        if half is not None:
            target = target.at[half]
        return remote(source, target, send.at[first + number], recv.at[first + number], device)

    def halves(self):
        half = self.target.shape[1] // 2
        return pl.ds(0, half), pl.ds(half, half)

    def forward(self, number, source, z):
        y, unused, core = self.place
        unused, my_z, unused = self.place
        shard = shard_at(y, z, core)
        for i, (half, d) in enumerate(zip(self.halves(), (3, 1))):
            copy = self.copy(
                source.at[half], shard, half, 3 + 2 * number + i, device_at(lax.rem(y + d, 4), my_z, core)
            )
            copy.start()
            self.along_y.append(copy)
        copy = self.copy(source, shard, None, 11 + number, device_at(y, my_z, 1 - core))
        copy.start()
        self.across.append(copy)

    def start(self):
        for copy in self.along_z:
            copy.start()
        self.forward(0, self.source, self.place[1])

    def finish(self):
        y, z, core = self.place
        for i, d in enumerate(self.order):
            self.along_z[i].wait_recv()
            from_z = lax.rem(z + 4 - d, 4)
            self.forward(i + 1, self.target.at[shard_at(y, from_z, core)], from_z)
        for number in range(4):
            from_z = z if number == 0 else lax.rem(z + 4 - self.order[number - 1], 4)
            shard = shard_at(y + 1, from_z, core)
            for i, half in enumerate(self.halves()):
                self.along_y[2 * number + i].wait_recv()
                block = self.target.at[shard].at[half]
                copy = self.copy(block, shard, half, 15 + 2 * number + i, device_at(y, z, 1 - core))
                copy.start()
                self.across.append(copy)
        for copy in self.along_z + self.along_y:
            copy.wait_send()
        for copy in self.across:
            copy.wait()


class Mover:
    def __init__(self, plan, inputs, outputs, own, send, recv, in_sem, out_sem):
        self.plan, self.inputs, self.outputs, self.own = plan, inputs, outputs, own
        self.send, self.recv, self.in_sem, self.out_sem = send, recv, in_sem, out_sem
        self.taken, self.copies, self.shares = [], [], []

    def own_place(self, item):
        kind, group = self.plan[item]
        return shard_at(*chip()) if kind == "share" else place_in(group)

    def take(self):
        for item, (kind, group) in enumerate(self.plan):
            block = source_of(kind, group, self.inputs[item], self.own_place(item))
            copy = pltpu.make_async_copy(block, self.own[item], self.in_sem.at[item])
            copy.start()
            self.taken.append(copy)

    def start(self):
        slot = 0
        for item, (kind, group) in enumerate(self.plan):
            source, target = self.inputs[item], self.outputs[item]
            if kind == "share":
                share = Share(source, target, self.send, self.recv, slot)
                share.start()
                self.shares.append(share)
            else:
                count = GROUP_SIZE[group]
                mine = place_in(group)
                for offset in range(1, count):
                    if kind == "half" and not soon(offset):
                        continue
                    peer = lax.rem(mine + offset, count)
                    copy = remote(
                        source_of(kind, group, source, peer),
                        target_of(kind, group, target, mine),
                        self.send.at[slot + offset - 1],
                        self.recv.at[slot + offset - 1],
                        device_of(group, peer),
                    )
                    copy.start()
                    self.copies.append(copy)
            slot += copies_of(kind, group)
        for item, (kind, group) in enumerate(self.plan):
            self.taken[item].wait()
            block = target_of(kind, group, self.outputs[item], self.own_place(item))
            copy = pltpu.make_async_copy(self.own[item], block, self.out_sem.at[item])
            copy.start()
            self.copies.append(copy)

    def finish(self):
        for share in self.shares:
            share.finish()
        for copy in self.copies:
            copy.wait()


def exchange_kernel(plan, *refs):
    amount = len(plan)
    mover = Mover(
        plan, refs[:amount], refs[amount : 2 * amount], refs[2 * amount : 3 * amount], *refs[3 * amount :]
    )
    mover.take()
    greet(plan)
    mover.start()
    mover.finish()


def mover_scratch(items):
    plan = tuple((kind, group) for kind, group, array in items)
    slots = sum(copies_of(kind, group) for kind, group in plan)
    return [
        pltpu.VMEM(own_shape(kind, group, array.shape), array.dtype) for kind, group, array in items
    ] + [
        pltpu.SemaphoreType.DMA((slots,)),
        pltpu.SemaphoreType.DMA((slots,)),
        pltpu.SemaphoreType.DMA((len(items),)),
        pltpu.SemaphoreType.DMA((len(items),)),
    ]


def exchange(name, number, *items):
    plan = tuple((kind, group) for kind, group, array in items)
    arrays = [array for kind, group, array in items]
    return pl.pallas_call(
        functools.partial(exchange_kernel, plan),
        out_shape=[
            jax.ShapeDtypeStruct(exchanged_shape(kind, group, array.shape), array.dtype)
            for kind, group, array in items
        ],
        in_specs=[pl.BlockSpec(memory_space=pltpu.HBM)] * len(items),
        out_specs=[pl.BlockSpec(memory_space=pltpu.HBM)] * len(items),
        scratch_shapes=mover_scratch(items),
        compiler_params=pltpu.CompilerParams(
            collective_id=number, has_side_effects=True, vmem_limit_bytes=16 * 2**20
        ),
        name=name,
    )(*arrays)


def rms_forward(values, gain):
    mean_square = jnp.mean(values * values, axis=-1, keepdims=True)
    return values * lax.rsqrt(mean_square + norm_eps) * gain.astype(F32)


def rms_backward(values, gain, grad_result):
    scale = lax.rsqrt(jnp.mean(values * values, axis=-1, keepdims=True) + norm_eps)
    scaled = gain.astype(F32) * grad_result
    inner = jnp.mean(values * scaled, axis=-1, keepdims=True)
    return scale * scaled - values * (scale * scale * scale) * inner


def logistic(values):
    return 0.5 * jnp.tanh(0.5 * values) + 0.5


def swiglu(gate, upper):
    sigma = logistic(gate)
    silu = gate * sigma
    return (silu * upper).astype(BF), sigma, silu


def swiglu_backward(gate, upper, sigma, silu, grad_hidden):
    grad_gate = grad_hidden * upper * (sigma + silu * (1.0 - sigma))
    return (grad_gate.astype(BF), (grad_hidden * silu).astype(BF))


def two_parts(values):
    high = values.astype(BF)
    return high, (values - high.astype(F32)).astype(BF)


def lane_index(shape):
    return lax.broadcasted_iota(jnp.int32, shape, 1)


def row_index(shape):
    return lax.broadcasted_iota(jnp.int32, shape, 0)


def pair_pick(second, copies):
    shape = (second.shape[0], PAIR * copies)
    of_lane = (lane_index(shape) % PAIR >= RANK).astype(F32)
    return (of_lane == second).astype(F32)


def pair_of(first_ref, last_ref, index):
    return jnp.concatenate([first_ref[index, 0], last_ref[index, 0]], axis=0)


def padded(values):
    rest = 128 - values.shape[1]
    return jnp.concatenate([values, jnp.zeros((values.shape[0], rest), values.dtype)], axis=1)


def routing(routes, experts):
    tokens = routes.shape[0]
    expert_lane = lane_index((tokens, experts))
    expert_hot = [(routes[:, k : k + 1] == expert_lane).astype(F32) for k in range(TOP)]
    count = sum(expert_hot)
    below = (row_index((tokens, tokens)) > lane_index((tokens, tokens))).astype(BF)
    earlier = dot(below, count.astype(BF))
    rank = [jnp.sum(hot * earlier, axis=1, keepdims=True).astype(jnp.int32) for hot in expert_hot]
    main_lane = lane_index((tokens, experts * MAIN))
    rest_lane = lane_index((tokens, experts * 16))
    rest_code = (rest_lane // 16) * 4 + rest_lane % 4
    main_hot, rest_hot = [], []
    for k in range(TOP):
        expert = routes[:, k : k + 1]
        main_slot = jnp.where(rank[k] < MAIN, expert * MAIN + rank[k], -1)
        rest_slot = jnp.where(rank[k] < MAIN, -1, expert * 4 + rank[k] - MAIN)
        main_hot.append((main_lane == main_slot).astype(F32))
        rest_hot.append((rest_code == rest_slot).astype(F32))
    return expert_hot, main_hot, rest_hot


def quarter_mask(shape, quarter):
    return (lane_index(shape) % 16 // 4 == quarter).astype(F32)


def rows_to_slots(main_hot, rest_hot, rows):
    main = dot_tn(sum(main_hot).astype(BF), rows).astype(BF)
    rest_sum = sum(rest_hot)
    width = rows.shape[1] // 4
    rest = None
    for quarter in range(4):
        hot = (rest_sum * quarter_mask(rest_sum.shape, quarter)).astype(BF)
        part = dot_tn(hot, rows[:, quarter * width : (quarter + 1) * width])
        rest = part if rest is None else rest + part
    return main, rest.astype(BF)


def slots_to_rows(main_hot, rest_hot, main, rest):
    rest_sum = sum(rest_hot)
    parts = [
        dot((rest_sum * quarter_mask(rest_sum.shape, quarter)).astype(BF), rest)
        for quarter in range(4)
    ]
    return dot(sum(main_hot).astype(BF), main) + jnp.concatenate(parts, axis=1)


def rest_selectors(sources):
    shape = (4 * sources, 16 * sources)
    row, lane = row_index(shape), lane_index(shape)
    same = (lane // 16 == row // 4) & (lane % 4 == row % 4)
    return [(same & (lane % 16 // 4 == quarter)).astype(BF) for quarter in range(4)]


def rest_to_rows(selectors, rest):
    return jnp.concatenate([dot(selector, rest) for selector in selectors], axis=1).astype(BF)


def rows_to_rest(selectors, rows):
    width = rows.shape[1] // 4
    total = None
    for quarter in range(4):
        part = dot_tn(selectors[quarter], rows[:, quarter * width : (quarter + 1) * width])
        total = part if total is None else total + part
    return total.astype(BF)


def stage(kernel, name, out_shape, in_specs, out_specs, grid=(1,), scratch=(), prefetch=0):
    return pl.pallas_call(
        kernel,
        out_shape=out_shape,
        grid_spec=pltpu.PrefetchScalarGridSpec(
            num_scalar_prefetch=prefetch,
            grid=grid,
            in_specs=in_specs,
            out_specs=out_specs,
            scratch_shapes=list(scratch),
        ),
        compiler_params=pltpu.CompilerParams(vmem_limit_bytes=VMEM_LIMIT),
        name=name,
    )


def whole(array):
    zeros = (0,) * len(array.shape)
    return pl.BlockSpec(array.shape, lambda *unused: zeros)


def of_sequence(which, block):
    return pl.BlockSpec(block, lambda *at: (0, at[-1][which], 0, 0))


def shape_of(shape, kind):
    return jax.ShapeDtypeStruct(shape, kind)


HBM = pl.BlockSpec(memory_space=pltpu.HBM)


def prologue_kernel(
    numbers_ref,
    rows_ref,
    grads_ref,
    gain_ref,
    routes_ref,
    ffn_a_ref,
    ffn_b_ref,
    down_a_ref,
    down_b_ref,
    first_a_ref,
    first_b_ref,
    second_a_ref,
    second_b_ref,
    normed_ref,
    main_ref,
    rest_ref,
    picked_ref,
    first_ref,
    second_ref,
):
    normed_ref[...] = rms_forward(rows_ref[0].astype(F32), gain_ref[...]).astype(BF)
    experts = main_ref.shape[0] // MAIN
    unused, main_hot, rest_hot = routing(routes_ref[0], experts)
    main, rest = rows_to_slots(main_hot, rest_hot, grads_ref[0])
    main_ref[...] = main
    rest_ref[...] = rest
    picked_ref[...] = jnp.concatenate(
        [
            pair_of(ffn_a_ref, ffn_b_ref, 1),
            pair_of(ffn_a_ref, ffn_b_ref, 2),
            pair_of(down_a_ref, down_b_ref, 0),
        ],
        axis=0,
    )
    for j in range(3):
        first_ref[j * PAIR : (j + 1) * PAIR, :] = pair_of(first_a_ref, first_b_ref, j)
        second_ref[j * PAIR : (j + 1) * PAIR, :] = pair_of(second_a_ref, second_b_ref, j)


def prologue(
    numbers, rows, grads, gain, routes, ffn_first, down_second, first, second, experts, columns
):
    tokens, width = rows.shape[1:]
    heads = lambda which: pl.BlockSpec(
        (3, 1, RANK, columns), lambda n, a: (0, a[which], 0, a[2])
    )
    outs = [
        (tokens, width),
        (experts * MAIN, width),
        (experts * 16, width // 4),
        (3 * PAIR, width),
        (3 * PAIR, width),
        (3 * PAIR, columns),
    ]
    return stage(
        prologue_kernel,
        "prologue",
        [shape_of(shape, BF) for shape in outs],
        [
            whole(rows),
            whole(grads),
            whole(gain),
            whole(routes),
            of_sequence(0, (3, 1, RANK, width)),
            of_sequence(1, (3, 1, RANK, width)),
            of_sequence(0, (1, 1, RANK, width)),
            of_sequence(1, (1, 1, RANK, width)),
            of_sequence(0, (3, 1, RANK, width)),
            of_sequence(1, (3, 1, RANK, width)),
            heads(0),
            heads(1),
        ],
        [pl.BlockSpec(shape, lambda n, a: (0, 0)) for shape in outs],
        prefetch=1,
    )(
        numbers, rows, grads, gain, routes, ffn_first, ffn_first, down_second, down_second, first, first,
        second, second,
    )


def half_turn(values):
    parts = []
    for head in range(values.shape[1] // HEAD_DIM):
        part = values[:, head * HEAD_DIM : (head + 1) * HEAD_DIM]
        parts.append(jnp.concatenate([part[:, 64:], part[:, :64]], axis=1))
    return jnp.concatenate(parts, axis=1) if len(parts) > 1 else parts[0]


def project_kernel(
    numbers_ref,
    rows_ref,
    weight_ref,
    first_a_ref,
    first_b_ref,
    second_a_ref,
    second_b_ref,
    bias_ref,
    side_ref,
    cos_ref,
    sin_ref,
    out_ref,
    lanes_ref,
):
    which = pl.program_id(0)

    @pl.when(pl.program_id(1) == 0)
    def lanes():
        first = pair_of(first_a_ref, first_b_ref, 0)
        picked = dot_nt(rows_ref[...], first) * pair_pick(side_ref[...], 1)
        lanes_ref[0] = picked.astype(BF)

    weight = weight_ref[...].reshape(rows_ref.shape[1], weight_ref.shape[3])
    bias = bias_ref[...].astype(F32)
    bias = jnp.sum(jnp.where(row_index(bias.shape) == which, bias, 0.0), axis=0, keepdims=True)
    second = pair_of(second_a_ref, second_b_ref, 0)
    value = dot(rows_ref[...], weight) + bias + dot(lanes_ref[0], second)
    copies = value.shape[1] // HEAD_DIM
    cosine = jnp.concatenate([cos_ref[...]] * copies, axis=1)
    sine = jnp.concatenate([sin_ref[...]] * copies, axis=1)
    turned = value * cosine + half_turn(value) * sine
    out_ref[0] = jnp.where(which < 2, turned, value).astype(BF)


def project(numbers, rows, weight, first, second, bias, side, cosine, sine):
    tokens, width = rows.shape
    columns = weight.shape[3]
    step = 256
    steps = columns // step
    return stage(
        project_kernel,
        "project",
        [shape_of((3, tokens, columns), BF), shape_of((3, tokens, PAIR), BF)],
        [
            whole(rows),
            pl.BlockSpec((weight.shape[0], 1, weight.shape[2], step), lambda j, n, a: (0, j, 0, n)),
            pl.BlockSpec((1, 1, RANK, width), lambda j, n, a: (j, a[0], 0, 0)),
            pl.BlockSpec((1, 1, RANK, width), lambda j, n, a: (j, a[1], 0, 0)),
            pl.BlockSpec((1, 1, RANK, step), lambda j, n, a: (j, a[0], 0, a[2] * steps + n)),
            pl.BlockSpec((1, 1, RANK, step), lambda j, n, a: (j, a[1], 0, a[2] * steps + n)),
            pl.BlockSpec((3, step), lambda j, n, a: (0, a[2] * steps + n)),
            whole(side),
            whole(cosine),
            whole(sine),
        ],
        [
            pl.BlockSpec((1, tokens, step), lambda j, n, a: (j, 0, n)),
            pl.BlockSpec((1, tokens, PAIR), lambda j, n, a: (j, 0, 0)),
        ],
        grid=(3, steps),
        prefetch=1,
    )(numbers, rows, weight, first, first, second, second, bias, side, cosine, sine)


def probabilities(query, keys, query_place, query_start, key_place):
    scores = dot_nt(query, keys) * (HEAD_DIM**-0.5)
    allowed = (key_place <= query_place) & (key_place >= query_start)
    scores = jnp.where(allowed, scores, masked_score)
    top = jnp.max(scores, axis=1, keepdims=True)
    raised = jnp.exp(scores - top)
    return raised * (1.0 / jnp.sum(raised, axis=1, keepdims=True))


def attend_kernel(query_ref, key_ref, value_ref, place_ref, start_ref, key_place_ref, out_ref):
    keys = key_ref[...].reshape(-1, HEAD_DIM)
    values = value_ref[...].reshape(-1, HEAD_DIM)
    probs = probabilities(query_ref[0], keys, place_ref[...], start_ref[...], key_place_ref[...])
    out_ref[...] = dot(probs.astype(BF), values).astype(BF)


def attend(projected, pairs, place, start, key_place):
    tokens, columns = projected.shape[1:]
    step = 256
    keys = pairs.shape[0] * pairs.shape[2]
    half = pairs.shape[2]
    return pl.pallas_call(
        attend_kernel,
        grid=(columns // HEAD_DIM, tokens // step),
        out_shape=jax.ShapeDtypeStruct((tokens, columns), BF),
        in_specs=[
            pl.BlockSpec((1, step, HEAD_DIM), lambda h, i: (0, i, h)),
            pl.BlockSpec((2, 1, half, HEAD_DIM), lambda h, i: (0, 0, 0, h)),
            pl.BlockSpec((2, 1, half, HEAD_DIM), lambda h, i: (0, 1, 0, h)),
            pl.BlockSpec((step, 1), lambda h, i: (i, 0)),
            pl.BlockSpec((step, 1), lambda h, i: (i, 0)),
            pl.BlockSpec((1, keys), lambda h, i: (0, 0)),
        ],
        out_specs=pl.BlockSpec((step, HEAD_DIM), lambda h, i: (i, h)),
        compiler_params=pltpu.CompilerParams(vmem_limit_bytes=VMEM_LIMIT),
        name="attend",
    )(projected, pairs, pairs, place, start, key_place)


def after_attention_kernel(
    numbers_ref,
    mixed_ref,
    weight_ref,
    rows_ref,
    first_a_ref,
    first_b_ref,
    second_a_ref,
    second_b_ref,
    gain_ref,
    ffn_a_ref,
    ffn_b_ref,
    router_ref,
    router_a_ref,
    router_b_ref,
    mix_ref,
    routes_ref,
    side_ref,
    residual_ref,
    normed_ref,
    small_ref,
    main_ref,
    rest_ref,
    main_notes_ref,
    rest_notes_ref,
    lanes_ref,
):
    step = pl.program_id(0)
    side = side_ref[...]
    pick = pair_pick(side, 1)

    @pl.when(step == 0)
    def lanes():
        first = pair_of(first_a_ref, first_b_ref, 0)
        lanes_ref[...] = (dot_nt(mixed_ref[...], first) * pick).astype(BF)

    columns = weight_ref.shape[1]
    here = pl.ds(pl.multiple_of(step * columns, columns), columns)
    second = pair_of(second_a_ref, second_b_ref, 0)
    residual_ref[:, here] = rows_ref[0].astype(F32) + (
        dot(mixed_ref[...], weight_ref[...]) + dot(lanes_ref[...], second)
    )

    @pl.when(step == pl.num_programs(0) - 1)
    def last():
        tokens = residual_ref.shape[0]
        experts = router_ref.shape[1]
        normed = rms_forward(residual_ref[...], gain_ref[...]).astype(BF)
        normed_ref[...] = normed
        router_lanes = (dot_nt(normed, pair_of(ffn_a_ref, ffn_b_ref, 0)) * pick).astype(BF)
        router_second = jnp.concatenate([router_a_ref[0], router_b_ref[0]], axis=0)
        logits = dot(normed, router_ref[...]) + dot(router_lanes, router_second)
        expert_hot, main_hot, rest_hot = routing(routes_ref[0], experts)
        chosen = [jnp.sum(hot * logits, axis=1, keepdims=True) for hot in expert_hot]
        top = jnp.maximum(jnp.maximum(chosen[0], chosen[1]), jnp.maximum(chosen[2], chosen[3]))
        raised = [jnp.exp(value - top) for value in chosen]
        total = sum(raised)
        gates = [value / total for value in raised]
        mix = logistic(
            jnp.sum(normed.astype(F32) * mix_ref[...].astype(F32), axis=1, keepdims=True)
        )
        small_ref[...] = padded(
            jnp.concatenate(
                [lanes_ref[...].astype(F32), router_lanes.astype(F32), *gates, mix], axis=1
            )
        )
        main, rest = rows_to_slots(main_hot, rest_hot, normed)
        main_ref[...] = main
        rest_ref[...] = rest
        adapter = jnp.where(side > 0.5, numbers_ref[1], numbers_ref[0])
        lane = lane_index((tokens, 128))
        adapter_hot = (lane == adapter).astype(F32)
        main_notes, rest_notes = None, None
        for k in range(TOP):
            high, low = two_parts(gates[k])
            notes = jnp.where(
                lane == ADAPTER_COUNT,
                high.astype(F32),
                jnp.where(lane == ADAPTER_COUNT + 1, low.astype(F32), adapter_hot),
            ).astype(BF)
            main_part = dot_tn(main_hot[k].astype(BF), notes)
            rest_part = dot_tn(rest_hot[k].astype(BF), notes)
            main_notes = main_part if k == 0 else main_notes + main_part
            rest_notes = rest_part if k == 0 else rest_notes + rest_part
        main_notes_ref[...] = main_notes.astype(BF)
        rest_notes_ref[...] = rest_notes.astype(BF)


def after_attention(
    numbers, mixed, weight, rows, first, second, gain, ffn_first, router, router_second, mix, routes, side
):
    tokens, width = mixed.shape
    experts = router.shape[1]
    step = 512
    kept = lambda *shape: pl.BlockSpec(shape, lambda n, a: (0,) * len(shape))
    outs = [
        ((tokens, width), F32),
        ((tokens, width), BF),
        ((tokens, 128), F32),
        ((experts * MAIN, width), BF),
        ((experts * 16, width // 4), BF),
        ((experts * MAIN, 128), BF),
        ((experts * 16, 128), BF),
    ]
    return stage(
        after_attention_kernel,
        "after_attention",
        [shape_of(*out) for out in outs],
        [
            whole(mixed),
            pl.BlockSpec((width, step), lambda n, a: (0, n)),
            pl.BlockSpec((1, tokens, step), lambda n, a: (0, 0, n)),
            pl.BlockSpec((1, 1, RANK, width), lambda n, a: (3, a[0], 0, 0)),
            pl.BlockSpec((1, 1, RANK, width), lambda n, a: (3, a[1], 0, 0)),
            pl.BlockSpec((1, 1, RANK, step), lambda n, a: (3, a[0], 0, n)),
            pl.BlockSpec((1, 1, RANK, step), lambda n, a: (3, a[1], 0, n)),
            whole(gain),
            pl.BlockSpec((1, 1, RANK, width), lambda n, a: (0, a[0], 0, 0)),
            pl.BlockSpec((1, 1, RANK, width), lambda n, a: (0, a[1], 0, 0)),
            whole(router),
            pl.BlockSpec((1, RANK, experts), lambda n, a: (a[0], 0, 0)),
            pl.BlockSpec((1, RANK, experts), lambda n, a: (a[1], 0, 0)),
            whole(mix),
            whole(routes),
            whole(side),
        ],
        [kept(*shape) for shape, kind in outs],
        grid=(width // step,),
        scratch=[pltpu.VMEM((tokens, PAIR), BF)],
        prefetch=1,
    )(
        numbers, mixed, weight, rows, first, first, second, second, gain, ffn_first, ffn_first, router,
        router_second, router_second, mix, routes, side,
    )


def in_owner_columns(total, target, columns):
    count = total.shape[0]
    for owner in range(total.shape[1] // columns):
        part = total[:, owner * columns : (owner + 1) * columns].astype(BF)
        target[:count, owner * 128 : (owner + 1) * 128] = padded(part)


def x_step(step):
    return step + step // 2 * (1 - 2 * (step % 2))


SHARED_STEPS = 4


def shared_kernel(plan, *refs):
    amount = len(plan)
    inputs, refs = refs[:amount], refs[amount:]
    normed_ref, grads_hbm, weights_hbm, side_ref, picked_ref, first_ref, mix_ref = refs[:7]
    outputs, refs = refs[7 : 7 + amount], refs[7 + amount :]
    parts_refs, values_ref, adapter_ref, refs = refs[:2], refs[2], refs[3], refs[4:]
    own, move_sems, refs = refs[:amount], refs[amount : amount + 4], refs[amount + 4 :]
    rows_buf, grads_buf, gate_up_buf, down_buf = refs[:4]
    parts_buf, values_buf, total, refs = refs[4:6], refs[6], refs[7], refs[8:]
    rows_send, rows_recv, parts_send, parts_recv, load_sem, parts_sem = refs

    shards_of, units, wide = down_buf.shape
    along, tokens, width = rows_buf.shape
    hidden_units = shards_of * units
    me = place_in("x")
    loads = [
        pltpu.make_async_copy(normed_ref, rows_buf.at[me], load_sem.at[0]),
        pltpu.make_async_copy(grads_hbm, grads_buf, load_sem.at[1]),
    ]
    loads += [
        pltpu.make_async_copy(
            weights_hbm.at[:, pl.ds(i * units, units)],
            target.at[:, :, pl.ds(0, width)],
            load_sem.at[2 + i],
        )
        for i, target in enumerate((gate_up_buf.at[0], gate_up_buf.at[1], down_buf))
    ]
    for load in loads:
        load.start()
    mover = Mover(plan, inputs, outputs, own, *move_sems)
    mover.take()
    greet(plan + (("gather", "x"),))

    def rows_copy(offset):
        return remote(
            normed_ref,
            rows_buf.at[me],
            rows_send.at[offset],
            rows_recv.at[offset],
            device_of("x", lax.rem(me + offset, along)),
        )

    def parts_copy(kind, offset):
        peer = lax.rem(me + along - offset, along)
        return remote(
            parts_buf[kind].at[peer],
            parts_refs[kind].at[me],
            parts_send.at[kind, offset],
            parts_recv.at[kind, offset],
            device_of("x", peer),
        )

    def own_parts(kind):
        return pltpu.make_async_copy(
            parts_buf[kind].at[me], parts_refs[kind].at[me], parts_sem.at[kind]
        )

    for offset in (1, 3, 2):
        rows_copy(offset).start()
    mover.start()
    for i in range(2):
        gate_up_buf[i, :, :, width:] = first_ref[i]
    down_buf[:, :, width:] = first_ref[2]
    total[...] = jnp.zeros_like(total)
    for load in loads[:2]:
        load.wait()
    per_step = along // SHARED_STEPS

    def block(step, carry):
        offsets = [x_step(step * per_step + i) for i in range(per_step)]
        sources = [lax.rem(me + along - offset, along) for offset in offsets]
        for i, offset in enumerate(offsets):
            if i > 0:
                rows_copy(offset).wait_recv()
            else:

                @pl.when(step > 0)
                def arrived():
                    rows_copy(offset).wait_recv()

        rows = jnp.concatenate([rows_buf[source] for source in sources], axis=0)
        grads = jnp.concatenate([grads_buf[source] for source in sources], axis=0)
        side = jnp.concatenate([side_ref[source] for source in sources], axis=0)
        grads_f = grads.astype(F32)
        pick = pair_pick(side, 1)
        pick_both = pair_pick(side, 2)
        lanes = (dot_nt(rows, picked_ref[: 2 * PAIR]) * pick_both).astype(BF)
        mix = logistic(jnp.sum(rows.astype(F32) * mix_ref[...].astype(F32), axis=1, keepdims=True))
        grad_shared = (mix * grads_f).astype(BF)
        grad_side = (dot_nt(grad_shared, picked_ref[2 * PAIR :]) * pick).astype(BF)

        @pl.when(step == 0)
        def gate_up_loaded():
            for load in loads[2:4]:
                load.wait()

        both = dot_nt(jnp.concatenate([rows, padded(lanes)], axis=1), gate_up_buf[...].reshape(-1, wide))
        gate, upper = both[:, :hidden_units], both[:, hidden_units:]
        hidden, sigma, silu = swiglu(gate, upper)

        @pl.when(step == 0)
        def down_loaded():
            loads[4].wait()

        down = down_buf[...].reshape(hidden_units, wide)
        grad_hidden = dot_nt(jnp.concatenate([grad_shared, padded(grad_side)], axis=1), down)
        grad_gate, grad_upper = swiglu_backward(gate, upper, sigma, silu, grad_hidden)
        gate_up = gate_up_buf[...].reshape(2 * hidden_units, wide)
        back = dot(jnp.concatenate([grad_gate, grad_upper], axis=1), gate_up)
        grad_lanes = (back[:, width : width + 2 * PAIR] * pick_both).astype(BF)
        value = dot(hidden, down)
        side_lanes = (value[:, width : width + PAIR] * pick).astype(BF)
        value = value[:, :width]
        mix_sum = jnp.sum(grads_f * value, axis=1, keepdims=True)
        notes = padded(jnp.concatenate([side_lanes, grad_lanes, *two_parts(mix_sum)], axis=1))
        for i, source in enumerate(sources):
            at = slice(i * tokens, (i + 1) * tokens)
            parts_buf[0][source] = back[at, :width].astype(BF)
            parts_buf[1][source] = notes[at]
            values_buf[source] = value[at].astype(BF)

        for i, offset in enumerate(offsets):
            if i > 0:
                for kind in range(2):
                    parts_copy(kind, offset).start()
            else:

                @pl.when(step == 0)
                def keep():
                    for kind in range(2):
                        own_parts(kind).start()

                @pl.when(step > 0)
                def send():
                    for kind in range(2):
                        parts_copy(kind, offset).start()

        total[:PAIR] += dot_tn(lanes[:, :PAIR], grad_gate)
        total[PAIR : 2 * PAIR] += dot_tn(lanes[:, PAIR:], grad_upper)
        total[2 * PAIR :] += dot_tn(grad_side, hidden)
        return carry

    lax.fori_loop(0, SHARED_STEPS, block, 0)
    values_out = pltpu.make_async_copy(values_buf, values_ref, parts_sem.at[2])
    values_out.start()
    in_owner_columns(total, adapter_ref, units)
    mover.finish()
    for kind in range(2):
        own_parts(kind).wait()
    for offset in range(1, along):
        rows_copy(offset).wait_send()
        for kind in range(2):
            parts_copy(kind, offset).wait()
    values_out.wait()


def shared_expert(number, normed, items, grads, weights, side, picked, first, mix):
    tokens, width = normed.shape
    plan = tuple((kind, group) for kind, group, array in items)
    arrays = [array for kind, group, array in items]
    along = GROUP_SIZE["x"]
    shards_of, units = weights.shape[0], weights.shape[1] // 3
    hidden = shards_of * units
    vmem = pl.BlockSpec(memory_space=pltpu.VMEM)
    parts = [(along, tokens, width), (along, tokens, 128), (along, tokens, width)]
    return pl.pallas_call(
        functools.partial(shared_kernel, plan),
        out_shape=[shape_of(array.shape, BF) for array in arrays]
        + [shape_of(part, BF) for part in parts]
        + [shape_of((3 * PAIR, shards_of * 128), BF)],
        in_specs=[HBM] * (len(items) + 3) + [vmem] * 4,
        out_specs=[HBM] * (len(items) + 3) + [vmem],
        scratch_shapes=mover_scratch(items)
        + [pltpu.VMEM((along, tokens, width), BF)] * 2
        + [
            pltpu.VMEM((2, shards_of, units, width + 128), BF),
            pltpu.VMEM((shards_of, units, width + 128), BF),
        ]
        + [pltpu.VMEM(part, BF) for part in parts]
        + [pltpu.VMEM((3 * PAIR, hidden), F32)]
        + [
            pltpu.SemaphoreType.DMA((along,)),
            pltpu.SemaphoreType.DMA((along,)),
            pltpu.SemaphoreType.DMA((2, along)),
            pltpu.SemaphoreType.DMA((2, along)),
            pltpu.SemaphoreType.DMA((5,)),
            pltpu.SemaphoreType.DMA((3,)),
        ],
        compiler_params=pltpu.CompilerParams(
            collective_id=number, has_side_effects=True, vmem_limit_bytes=VMEM_LIMIT
        ),
        name="shared_expert",
    )(*arrays, normed, grads, weights, side, picked, first, mix)


BACK = 6
ROUTED_STEPS = 4


def routed_kernel(*refs):
    held_hbm, gate_up_hbm, down_hbm, values_hbm = refs[:6], refs[6], refs[7], refs[8]
    later_hbm, refs = refs[9:11], refs[2:]
    first_ref, second_ref, down_first_ref, down_second_ref = refs[9:13]
    back_refs, values_ref, refs = refs[13 : 13 + BACK], refs[13 + BACK], refs[14 + BACK :]
    adapter_ref = refs[0]
    own, move_sems, refs = refs[1:2], refs[2:6], refs[6:]
    held, back_buf, refs = refs[:6], refs[6 : 6 + BACK], refs[6 + BACK :]
    gate_up_buf, down_buf, total, total_down = refs[:4]
    send_sem, recv_sem, load_sem, own_sem, half_sem, later_send, later_recv = refs[4:]

    me = place_in("f")
    experts = GROUP_SIZE["f"]
    steps = ROUTED_STEPS
    loads = [
        pltpu.make_async_copy(held_hbm[i], held[i], load_sem.at[i]) for i in (0, 1, 4, 5)
    ]
    for offset in range(experts):
        if offset == 0 or soon(offset):
            source = lax.rem(me + experts - offset, experts)
            loads += [
                pltpu.make_async_copy(
                    block_of(held_hbm[2 + i], "rows", experts, source),
                    block_of(held[2 + i], "rows", experts, source),
                    half_sem.at[i, offset],
                )
                for i in range(2)
            ]
    loads += [
        pltpu.make_async_copy(gate_up_hbm.at[0, 0], gate_up_buf.at[0], load_sem.at[6]),
        pltpu.make_async_copy(gate_up_hbm.at[0, 1], gate_up_buf.at[1], load_sem.at[7]),
        pltpu.make_async_copy(down_hbm.at[0], down_buf, load_sem.at[8]),
    ]
    for load in loads:
        load.start()
    mover = Mover((("swap", "x"),), (values_hbm,), (values_ref,), own, *move_sems)
    mover.take()
    greet((("rows", "f"), ("swap", "x")))

    def later_copy(kind, offset):
        peer = lax.rem(me + offset, experts)
        return remote(
            block_of(later_hbm[kind], "rows", experts, peer),
            block_of(held[2 + kind], "rows", experts, me),
            later_send.at[kind, offset],
            later_recv.at[kind, offset],
            device_of("f", peer),
        )

    later = [offset for offset in range(1, experts) if not soon(offset)]
    for offset in sorted(later, key=lambda offset: -(offset % steps)):
        for kind in range(2):
            later_copy(kind, offset).start()
    mover.start()
    total[...] = jnp.zeros_like(total)
    total_down[...] = jnp.zeros_like(total_down)

    def back_copy(kind, peer, landing):
        return remote(
            block_of(back_buf[kind], "rows", experts, peer),
            block_of(back_refs[kind], "rows", experts, me),
            send_sem.at[kind, peer],
            recv_sem.at[kind, landing],
            device_of("f", peer),
        )

    def own_copy(kind):
        return pltpu.make_async_copy(
            block_of(back_buf[kind], "rows", experts, me),
            block_of(back_refs[kind], "rows", experts, me),
            own_sem.at[kind],
        )

    selectors = rest_selectors(experts // steps)
    spread = (row_index((128, LANES)) == lane_index((128, LANES)) // RANK).astype(BF)
    fold = (row_index((LANES, 128)) % RANK == lane_index((LANES, 128))).astype(BF)
    fold_later = (row_index((LANES, 128)) % RANK == lane_index((LANES, 128)) - RANK).astype(BF)
    for load in loads[:-3]:
        load.wait()
    count, rest_count = held[0].shape[0] // steps, held[1].shape[0] // steps

    def block(step, carry):
        number = lax.rem(me + 1 + step, steps)

        for turn in range(steps // 2):

            @pl.when(step == steps - 1 - turn)
            def arrived():
                for offset in later:
                    if offset % steps == turn:
                        for kind in range(2):
                            later_copy(kind, offset).wait_recv()

        peers = [number + steps * turn for turn in range(experts // steps)]

        def read(ref):
            depth = ref.shape[0] // experts
            blocks = [ref[pl.ds(pl.multiple_of(peer * depth, depth), depth)] for peer in peers]
            return jnp.concatenate(blocks, axis=0)

        def write(ref, value):
            depth = ref.shape[0] // experts
            for turn, peer in enumerate(peers):
                part = value[turn * depth : (turn + 1) * depth]
                ref[pl.ds(pl.multiple_of(peer * depth, depth), depth)] = part

        rows = jnp.concatenate([read(held[0]), rest_to_rows(selectors, read(held[1]))], axis=0)
        grads = jnp.concatenate([read(held[2]), rest_to_rows(selectors, read(held[3]))], axis=0)
        notes = jnp.concatenate(
            [read(held[4]), dot(selectors[0], read(held[5])).astype(BF)], axis=0
        )
        pick = dot(notes, spread)
        gate_of = (
            notes[:, ADAPTER_COUNT : ADAPTER_COUNT + 1].astype(F32)
            + notes[:, ADAPTER_COUNT + 1 : ADAPTER_COUNT + 2].astype(F32)
        )
        grads_f = grads.astype(F32)
        lanes_gate = (dot_nt(rows, first_ref[0]) * pick).astype(BF)
        lanes_up = (dot_nt(rows, first_ref[1]) * pick).astype(BF)
        grad_routed = (gate_of * grads_f).astype(BF)
        grad_side = (dot_nt(grads, down_second_ref[1]) * gate_of * pick).astype(BF)

        @pl.when(step == 0)
        def gate_up_loaded():
            for load in loads[-3:-1]:
                load.wait()

        gate = dot(rows, gate_up_buf[0]) + dot(lanes_gate, second_ref[0])
        upper = dot(rows, gate_up_buf[1]) + dot(lanes_up, second_ref[1])
        hidden, sigma, silu = swiglu(gate, upper)

        @pl.when(step == 0)
        def down_loaded():
            loads[-1].wait()

        grad_hidden = dot_nt(grad_routed, down_buf[...]) + dot(grad_side, down_first_ref[...])
        grad_gate, grad_upper = swiglu_backward(gate, upper, sigma, silu, grad_hidden)
        side = (dot_nt(hidden, down_first_ref[...]).astype(BF).astype(F32) * pick).astype(BF)
        value = dot(hidden, down_buf[...]) + dot(side, down_second_ref[1])
        gate_grad = jnp.sum(grads_f * value, axis=1, keepdims=True)
        result = (gate_of * value).astype(BF)
        write(back_buf[4], result[:count])
        write(back_buf[5], rows_to_rest(selectors, result[count:]))
        back = (dot_nt(grad_gate, gate_up_buf[0]) + dot_nt(grad_upper, gate_up_buf[1])).astype(BF)
        back_gate = (dot_nt(grad_gate, second_ref[0]) * pick).astype(BF)
        back_up = (dot_nt(grad_upper, second_ref[1]) * pick).astype(BF)
        high, low = two_parts(gate_grad)
        lane = lane_index((count + rest_count // 4, 128))
        back_notes = jnp.where(
            lane == PAIR,
            high.astype(F32),
            jnp.where(
                lane == PAIR + 1, low.astype(F32), dot(back_gate, fold) + dot(back_up, fold_later)
            ),
        ).astype(BF)
        write(back_buf[0], back[:count])
        write(back_buf[1], rows_to_rest(selectors, back[count:]))
        write(back_buf[2], back_notes[:count])
        write(back_buf[3], dot_tn(selectors[0], back_notes[count:]).astype(BF))
        for peer in peers:

            @pl.when(peer == me)
            def keep():
                for kind in range(BACK):
                    own_copy(kind).start()

            @pl.when(peer != me)
            def send():
                for kind in range(BACK):
                    back_copy(kind, peer, me).start()

        total[:LANES] += dot_tn(lanes_gate, grad_gate)
        total[LANES : 2 * LANES] += dot_tn(lanes_up, grad_upper)
        total[2 * LANES :] += dot_tn(grad_side, hidden)
        total_down[...] += dot_tn(side, grad_routed)
        return carry

    lax.fori_loop(0, steps, block, 0)
    in_owner_columns(total, adapter_ref, total.shape[1] // experts)
    adapter_ref[3 * LANES :, :] = total_down[...].astype(BF)
    mover.finish()
    for offset in later:
        for kind in range(2):
            later_copy(kind, offset).wait_send()
    for kind in range(BACK):
        own_copy(kind).wait()

    def settle(offset, carry):
        peer = lax.rem(me + offset, experts)
        for kind in range(BACK):
            copy = back_copy(kind, peer, peer)
            copy.wait_send()
            copy.wait_recv()
        return carry

    lax.fori_loop(1, experts, settle, 0)


def routed_expert(number, held, later, values, first, second, down_first, down_second, gate_up, down):
    width, hidden = gate_up.shape[2:]
    experts = GROUP_SIZE["f"]
    vmem = pl.BlockSpec(memory_space=pltpu.VMEM)
    back = [held[0], held[1], held[4], held[5], held[0], held[1]]
    items = [("swap", "x", values)]
    return pl.pallas_call(
        routed_kernel,
        out_shape=[shape_of(array.shape, BF) for array in (*back, values)]
        + [shape_of((4 * LANES, experts * 128), BF)],
        in_specs=[HBM] * 11 + [vmem] * 4,
        out_specs=[HBM] * (BACK + 1) + [vmem],
        scratch_shapes=mover_scratch(items)
        + [pltpu.VMEM(array.shape, BF) for array in held]
        + [pltpu.VMEM(array.shape, BF) for array in back]
        + [
            pltpu.VMEM((2, width, hidden), BF),
            pltpu.VMEM((hidden, width), BF),
            pltpu.VMEM((3 * LANES, hidden), F32),
            pltpu.VMEM((LANES, width), F32),
            pltpu.SemaphoreType.DMA((BACK, experts)),
            pltpu.SemaphoreType.DMA((BACK, experts)),
            pltpu.SemaphoreType.DMA((9,)),
            pltpu.SemaphoreType.DMA((BACK,)),
            pltpu.SemaphoreType.DMA((2, experts)),
            pltpu.SemaphoreType.DMA((2, experts)),
            pltpu.SemaphoreType.DMA((2, experts)),
        ],
        compiler_params=pltpu.CompilerParams(
            collective_id=number, has_side_effects=True, vmem_limit_bytes=VMEM_LIMIT
        ),
        name="routed_expert",
    )(*held, gate_up, down, values, *later, first, second, down_first, down_second)


def after_experts_kernel(
    numbers_ref,
    parts_ref,
    part_notes_ref,
    main_ref,
    rest_ref,
    main_notes_ref,
    rest_notes_ref,
    grads_ref,
    normed_ref,
    residual_ref,
    small_ref,
    mixed_ref,
    routes_ref,
    side_ref,
    ffn_a_ref,
    ffn_b_ref,
    router_ref,
    router_a_ref,
    router_b_ref,
    mix_ref,
    gain_ref,
    down_a_ref,
    down_b_ref,
    first_a_ref,
    first_b_ref,
    second_a_ref,
    second_b_ref,
    weight_hbm,
    grad_residual_ref,
    grad_mixed_ref,
    adapter_ref,
    router_grad_ref,
    shared_side_ref,
    weight_ref,
    sem,
):
    load = pltpu.make_async_copy(weight_hbm, weight_ref, sem)
    load.start()
    experts = router_ref.shape[1]
    side = side_ref[...]
    pick = pair_pick(side, 1)
    grads = grads_ref[0]
    grads_f = grads.astype(F32)
    normed = normed_ref[...]
    out_lanes = small_ref[:, :PAIR].astype(BF)
    router_lanes = small_ref[:, PAIR : 2 * PAIR].astype(BF)
    gates = [small_ref[:, 2 * PAIR + k : 2 * PAIR + k + 1] for k in range(TOP)]
    mix = small_ref[:, 2 * PAIR + TOP : 2 * PAIR + TOP + 1]
    notes = sum(part_notes_ref[i].astype(F32) for i in range(part_notes_ref.shape[0]))
    shared_side = notes[:, :PAIR].astype(BF)
    shared_side_ref[...] = padded(shared_side)
    down_second = pair_of(down_a_ref, down_b_ref, 0)
    mix_total = (
        notes[:, 3 * PAIR : 3 * PAIR + 1]
        + notes[:, 3 * PAIR + 1 : 3 * PAIR + 2]
        + jnp.sum(shared_side.astype(F32) * dot_nt(grads, down_second), axis=1, keepdims=True)
    )
    grad_mix = mix_total * mix * (1.0 - mix)
    grad_shared = (mix * grads_f).astype(BF)
    expert_hot, main_hot, rest_hot = routing(routes_ref[0], experts)
    grad_gates = []
    mask = quarter_mask(rest_hot[0].shape, 0)
    token_notes = None
    for k in range(TOP):
        mine = dot(main_hot[k].astype(BF), main_notes_ref[...]) + dot(
            (rest_hot[k] * mask).astype(BF), rest_notes_ref[...]
        )
        grad_gates.append(mine[:, PAIR : PAIR + 1] + mine[:, PAIR + 1 : PAIR + 2])
        token_notes = mine if k == 0 else token_notes + mine
    inner = sum(gate * grad for gate, grad in zip(gates, grad_gates))
    grad_logits = sum(
        hot * (gate * (grad - inner)) for hot, gate, grad in zip(expert_hot, gates, grad_gates)
    )
    logits_high, logits_low = two_parts(grad_logits)
    router_second = jnp.concatenate([router_a_ref[0], router_b_ref[0]], axis=0)
    grad_router_lanes = dot_nt(logits_high, router_second) + dot_nt(logits_low, router_second)
    router_grad = dot_tn(router_lanes, logits_high) + dot_tn(router_lanes, logits_low)
    of_row = jnp.where(row_index((PAIR, 128)) < RANK, numbers_ref[0], numbers_ref[1]).astype(F32)
    router_grad_ref[...] = jnp.where(
        lane_index((PAIR, 128)) == experts, of_row, padded(router_grad)
    ).astype(BF)
    lane_grads = (
        jnp.concatenate(
            [
                grad_router_lanes,
                notes[:, PAIR : 3 * PAIR],
                token_notes[:, :RANK],
                token_notes[:, :RANK],
                token_notes[:, RANK:PAIR],
                token_notes[:, RANK:PAIR],
            ],
            axis=1,
        )
        * pair_pick(side, 5)
    ).astype(BF)
    factors = ffn_a_ref.shape[0]
    ffn_first = jnp.concatenate([pair_of(ffn_a_ref, ffn_b_ref, i) for i in range(factors)], axis=0)
    grad_second = (
        grad_mix * mix_ref[...].astype(F32)
        + dot_nt(logits_high, router_ref[...])
        + dot_nt(logits_low, router_ref[...])
        + sum(parts_ref[i].astype(F32) for i in range(parts_ref.shape[0]))
        + slots_to_rows(main_hot, rest_hot, main_ref[...], rest_ref[...])
        + dot(lane_grads, ffn_first)
    )
    grad_residual = grads_f + rms_backward(residual_ref[...], gain_ref[...], grad_second)
    grad_residual_ref[...] = grad_residual
    grad_attended = grad_residual.astype(BF)
    first, second = pair_of(first_a_ref, first_b_ref, 0), pair_of(second_a_ref, second_b_ref, 0)
    grad_out_lanes = (dot_nt(grad_attended, second) * pick).astype(BF)
    adapter_ref[...] = jnp.concatenate(
        [
            dot_tn(lane_grads, normed),
            dot_tn(grad_out_lanes, mixed_ref[...]),
            dot_tn(out_lanes, grad_attended),
            dot_tn(shared_side, grad_shared),
        ],
        axis=0,
    ).astype(BF)
    load.wait()
    grad_mixed_ref[...] = (
        dot_nt(grad_attended, weight_ref[...]) + dot(grad_out_lanes, first)
    ).astype(BF)


def after_experts(
    numbers, parts, part_notes, main, rest, main_notes, rest_notes, grads, normed, residual, small, mixed,
    routes, side, ffn_first, router, router_second, mix, gain, down_second, first, second, weight,
):
    tokens, width = normed.shape
    experts = router.shape[1]
    factors = ffn_first.shape[0]
    last = lambda which: pl.BlockSpec((1, 1, RANK, width), lambda n, a: (3, a[which], 0, 0))
    outs = [
        ((tokens, width), F32),
        ((tokens, width), BF),
        (((factors + 3) * PAIR, width), BF),
        ((PAIR, 128), BF),
        ((tokens, 128), BF),
    ]
    plain = (
        parts, part_notes, main, rest, main_notes, rest_notes, grads, normed, residual, small, mixed, routes,
        side,
    )
    return stage(
        after_experts_kernel,
        "after_experts",
        [shape_of(*out) for out in outs],
        [whole(array) for array in plain]
        + [
            of_sequence(0, (factors, 1, RANK, width)),
            of_sequence(1, (factors, 1, RANK, width)),
            whole(router),
            pl.BlockSpec((1, RANK, experts), lambda n, a: (a[0], 0, 0)),
            pl.BlockSpec((1, RANK, experts), lambda n, a: (a[1], 0, 0)),
            whole(mix),
            whole(gain),
            of_sequence(0, (1, 1, RANK, width)),
            of_sequence(1, (1, 1, RANK, width)),
            last(0),
            last(1),
            last(0),
            last(1),
            HBM,
        ],
        [pl.BlockSpec(shape, lambda n, a: (0, 0)) for shape, kind in outs],
        scratch=[pltpu.VMEM(weight.shape, BF), pltpu.SemaphoreType.DMA],
        prefetch=1,
    )(
        numbers, *plain, ffn_first, ffn_first, router, router_second, router_second, mix, gain, down_second,
        down_second, first, first, second, second, weight,
    )


def attention_back_kernel(plan, heads_plan, *refs):
    amount = len(plan)
    inputs, expert_hbm, refs = refs[:amount], refs[amount], refs[amount + 1 :]
    mixed_hbm, query_hbm, pairs_hbm, weight_hbm = refs[:4]
    place_ref, start_ref, key_place_ref, cos_ref, sin_ref, side_ref, lanes_ref, second_ref = refs[4:12]
    results, ends, refs = list(refs[12:20]), list(refs[20:26]), refs[26:]
    out_ref, end_outs, refs = refs[0], refs[1:11], refs[11:]
    outputs, refs = refs[:amount], refs[amount:]
    heads_got, parts_ref, notes_ref, expert_ref, refs = *refs[:4], refs[4:]
    late_bufs, late_sem, refs = refs[:6], refs[6], refs[7:]
    end_scratch, refs = refs[:END_SCRATCH], refs[END_SCRATCH:]
    own, move_sems, refs = refs[:amount], refs[amount : amount + 4], refs[amount + 4 :]
    heads_own, heads_sems, refs = refs[:1], refs[1:5], refs[5:]
    expert_own, expert_sems, refs = refs[:1], refs[1:5], refs[5:]
    mixed_buf, query_buf, pairs_buf, weight_buf = refs[:4]
    sent_buf, got_buf, grads_buf, heads_buf, parts_buf, notes_buf = refs[4:10]
    mixed_send, mixed_recv, pair_send, pair_recv, parts_send, parts_recv, load_sem, own_sem = refs[10:]

    x, y = place_in("x"), place_in("y")
    along, tokens, columns = mixed_buf.shape
    rows_all = along * tokens
    heads = columns // HEAD_DIM
    loads = [
        pltpu.make_async_copy(block_of(mixed_hbm, "columns", along, x), mixed_buf.at[x], load_sem.at[0]),
        pltpu.make_async_copy(query_hbm.at[0], query_buf, load_sem.at[1]),
        pltpu.make_async_copy(pairs_hbm, pairs_buf, load_sem.at[2]),
    ]
    loads += [
        pltpu.make_async_copy(weight_hbm.at[:, j], weight_buf.at[j], load_sem.at[3 + j])
        for j in range(3)
    ]
    for load in loads:
        load.start()
    late_loads = []
    for i, (group, place) in enumerate(LATE):
        refs_of = (results, ends)[group]
        late_loads.append(pltpu.make_async_copy(refs_of[place], late_bufs[i], late_sem.at[i]))
        refs_of[place] = late_bufs[i]
    for load in late_loads:
        load.start()
    mover = Mover(plan, inputs, outputs, own, *move_sems)
    mover.take()
    expert_mover = Mover((("rows", "x"),), (expert_hbm,), (expert_ref,), expert_own, *expert_sems)
    expert_mover.take()
    greet((("rows", "f"), ("swap", "x"), ("swap", "y"), ("rows", "c")))

    def mixed_copy(offset):
        peer = lax.rem(x + offset, along)
        return remote(
            block_of(mixed_hbm, "columns", along, peer),
            mixed_buf.at[x],
            mixed_send.at[offset],
            mixed_recv.at[offset],
            device_of("x", peer),
        )

    def pair_copy(head):
        return remote(
            sent_buf.at[1 - y, head],
            got_buf.at[head],
            pair_send.at[head],
            pair_recv.at[head],
            device_of("y", 1 - y),
        )

    def parts_copy(offset):
        peer = lax.rem(x + offset, along)
        return remote(
            parts_buf.at[peer],
            parts_ref.at[x],
            parts_send.at[0, offset],
            parts_recv.at[0, offset],
            device_of("x", peer),
        )

    def notes_copy(offset):
        peer = lax.rem(x + offset, along)
        return remote(
            notes_buf.at[peer],
            notes_ref.at[x],
            parts_send.at[1, offset],
            parts_recv.at[1, offset],
            device_of("x", peer),
        )

    for offset in (2, 1, 3):
        mixed_copy(offset).start()
    for load in loads[:3]:
        load.wait()
    for offset in (1, 3, 2):
        mixed_copy(offset).wait_recv()
    expert_mover.start()

    step = rows_all // 2

    def head_block(head, carry):
        here = pl.ds(pl.multiple_of(head * HEAD_DIM, HEAD_DIM), HEAD_DIM)
        keys = pairs_buf[:, 0, :, here].reshape(-1, HEAD_DIM)
        values = pairs_buf[:, 1, :, here].reshape(-1, HEAD_DIM)
        key_total, value_total = None, None
        for i in range(2):
            at = slice(i * step, (i + 1) * step)
            query = query_buf[at, here]
            blocks = along // 2
            grad = mixed_buf[i * blocks : (i + 1) * blocks, :, here].reshape(step, HEAD_DIM)
            probs = probabilities(query, keys, place_ref[at], start_ref[at], key_place_ref[...])
            grad_probs = dot_nt(grad, values)
            mean = jnp.sum(probs * grad_probs, axis=1, keepdims=True)
            grad_scores = (probs * (grad_probs - mean)).astype(BF)
            grad_query = dot(grad_scores, keys) * (HEAD_DIM**-0.5)
            grads_buf[0, at, here] = (
                grad_query * cos_ref[at] - half_turn(grad_query) * sin_ref[at]
            ).astype(BF)
            grad_keys = dot_tn(grad_scores, query) * (HEAD_DIM**-0.5)
            grad_values = dot_tn(probs.astype(BF), grad)
            key_total = grad_keys if i == 0 else key_total + grad_keys
            value_total = grad_values if i == 0 else value_total + grad_values
        for half in range(2):
            at = slice(half * rows_all, (half + 1) * rows_all)
            sent_buf[half, head, 0] = key_total[at].astype(BF)
            sent_buf[half, head, 1] = value_total[at].astype(BF)
        pair_copy(head).start()
        return carry

    lax.fori_loop(0, heads, head_block, 0)
    for load in late_loads:
        load.wait()
    combine_kernel(*results, out_ref)

    def head_sum(head, carry):
        here = pl.ds(pl.multiple_of(head * HEAD_DIM, HEAD_DIM), HEAD_DIM)
        pair_copy(head).wait_recv()
        key = sent_buf[y, head, 0].astype(F32) + got_buf[head, 0].astype(F32)
        grads_buf[1, :, here] = (key * cos_ref[...] - half_turn(key) * sin_ref[...]).astype(BF)
        value = sent_buf[y, head, 1].astype(F32) + got_buf[head, 1].astype(F32)
        grads_buf[2, :, here] = value.astype(BF)
        return carry

    lax.fori_loop(0, heads, head_sum, 0)
    pick = pair_pick(side_ref[...], 1)
    notes = []
    heads_buf[...] = jnp.zeros_like(heads_buf)
    own_columns = pl.ds(pl.multiple_of(x * columns, columns), columns)
    for j in range(3):
        at = slice(j * PAIR, (j + 1) * PAIR)
        notes.append((dot_nt(grads_buf[j], second_ref[at]) * pick).astype(BF))
        heads_buf[at, own_columns] = dot_tn(lanes_ref[j], grads_buf[j]).astype(BF)
    notes_buf[...] = padded(jnp.concatenate(notes, axis=1)).reshape(notes_buf.shape)
    heads_mover = Mover(heads_plan, (heads_buf,), (heads_got,), heads_own, *heads_sems)
    heads_mover.take()
    heads_mover.start()
    for offset in (1, 3, 2):
        notes_copy(offset).start()
    mover.start()
    own_notes = pltpu.make_async_copy(notes_buf.at[x], notes_ref.at[x], own_sem.at[0])
    own_notes.start()
    for load in loads[3:]:
        load.wait()

    def own_parts():
        return pltpu.make_async_copy(parts_buf.at[x], parts_ref.at[x], own_sem.at[1])

    def row_block(number, carry):
        offset = x_step(lax.rem(number + 1, along))
        peer = lax.rem(x + offset, along)
        at = pl.ds(pl.multiple_of(peer * tokens, tokens), tokens)
        total = None
        for j in range(3):
            part = dot_nt(grads_buf[j, at], weight_buf[j].reshape(-1, columns))
            total = part if total is None else total + part
        parts_buf[peer] = total.astype(BF)

        @pl.when(number < along - 1)
        def send():
            parts_copy(offset).start()

        @pl.when(number == along - 1)
        def keep():
            own_parts().start()

        return carry

    lax.fori_loop(0, along, row_block, 0)
    mover.finish()
    heads_mover.finish()
    expert_mover.finish()
    own_notes.wait()
    own_parts().wait()

    def pairs_sent(head, carry):
        pair_copy(head).wait_send()
        return carry

    lax.fori_loop(0, heads, pairs_sent, 0)
    for offset in range(1, along):
        mixed_copy(offset).wait_send()
        parts_copy(offset).wait()
        notes_copy(offset).wait()
    early_got, shared_got, router_got = outputs
    got = (router_got, early_got, shared_got, heads_got, ends[5], expert_ref)
    finish_kernel(parts_ref, notes_ref, *ends[:5], *got, *end_outs, *end_scratch)


LATE = ((0, 0), (0, 3), (0, 4), (1, 0), (1, 1), (1, 2))
END_SCRATCH = 18 + 6 * 4 + 9


def attention_back(number, items, expert, mixed, query, pairs, weight, small, results, ends, columns_of):
    plan = tuple((kind, group) for kind, group, array in items)
    arrays = [array for kind, group, array in items]
    along = GROUP_SIZE["x"]
    tokens, width = mixed.shape
    columns = width // along
    heads = columns // HEAD_DIM
    rows_all = along * tokens
    heads_items = [("from_columns", "f", shape_of((3 * PAIR, width), BF))]
    vmem = pl.BlockSpec(memory_space=pltpu.VMEM)
    got = [exchanged_shape(kind, group, array.shape) for kind, group, array in items]
    got += [
        exchanged_shape("from_columns", "f", (3 * PAIR, width)),
        (along, tokens, width),
        (along, tokens, 128),
        expert.shape,
    ]
    late = [(results, ends)[group][place] for group, place in LATE]
    in_specs = [[vmem] * len(results), [vmem] * len(ends)]
    for group, place in LATE:
        in_specs[group][place] = HBM
    end_outs, end_scratch = finish_shapes(ends[0], ends[4], items, expert, columns_of)
    assert len(end_scratch) == END_SCRATCH
    dma = pltpu.SemaphoreType.DMA
    return pl.pallas_call(
        functools.partial(attention_back_kernel, plan, (("from_columns", "f"),)),
        out_shape=[shape_of((1, tokens, width), BF), *end_outs],
        in_specs=[HBM] * (len(items) + 5) + [vmem] * len(small) + in_specs[0] + in_specs[1],
        out_specs=[vmem] * (1 + len(end_outs)),
        scratch_shapes=[pltpu.VMEM(shape, BF) for shape in got]
        + [pltpu.VMEM(array.shape, array.dtype) for array in late]
        + [dma((len(LATE),))]
        + end_scratch
        + mover_scratch(items)
        + mover_scratch(heads_items)
        + mover_scratch([("rows", "x", expert)])
        + [
            pltpu.VMEM((along, tokens, columns), BF),
            pltpu.VMEM((rows_all, columns), BF),
            pltpu.VMEM(pairs.shape, BF),
            pltpu.VMEM((3, *weight.shape[:1], *weight.shape[2:]), BF),
            pltpu.VMEM((2, heads, 2, rows_all, HEAD_DIM), BF),
            pltpu.VMEM((heads, 2, rows_all, HEAD_DIM), BF),
            pltpu.VMEM((3, rows_all, columns), BF),
            pltpu.VMEM((3 * PAIR, width), BF),
            pltpu.VMEM((along, tokens, width), BF),
            pltpu.VMEM((along, tokens, 128), BF),
            dma((along,)),
            dma((along,)),
            dma((heads,)),
            dma((heads,)),
            dma((2, along)),
            dma((2, along)),
            dma((6,)),
            dma((2,)),
        ],
        compiler_params=pltpu.CompilerParams(
            collective_id=number, has_side_effects=True, vmem_limit_bytes=VMEM_LIMIT
        ),
        name="attention_back",
    )(*arrays, expert, mixed, query, pairs, weight, *small, *results, *ends)


def lane_expansion(ids_ref, group):
    ids = ids_ref[group][:, GROUP_SIZE["f"] : GROUP_SIZE["f"] + 1].astype(F32)
    lane = lane_index((PAIR, LANES))
    same = (lane // RANK).astype(F32) == ids
    return (same & (lane % RANK == row_index((PAIR, LANES)) % RANK)).astype(BF)


def expanded(expansions, got_ref, factor):
    total = None
    for group, expansion in enumerate(expansions):
        part = dot_tn(expansion, got_ref[group, factor * PAIR : (factor + 1) * PAIR, :])
        total = part if total is None else total + part
    return total.astype(BF)


FINISH = (
    (("from_columns", "f"),),
    (("from_columns", "f"),),
    (("rows", "c"), ("rows", "y")),
    (("gather", "c"), ("gather", "c"), ("gather", "c")),
    (("rows", "c"),),
    (("gather", "c"),),
)


def finish_kernel(*refs):
    parts_ref, notes_ref, rows_ref, normed_ref, residual_ref, gain_ref, first_ref = refs[:7]
    ids_ref, early_ref, shared_ref, heads_ref, column_ref, expert_ref = refs[7:13]
    grad_out, attn_in, attn_out, ffn_out, router_out, shared_out, shared_in_out = refs[13:20]
    expert_out, expert_in_out, down_out, expert_buf, refs = *refs[20:24], refs[24:]
    late_buf, late_got, early_buf, early_parts, shared_buf, shared_parts = refs[:6]
    expert_got, late_sum, early_row, shared_row, expert_sum = refs[6:11]
    late_all, early_all, shared_all, expert_all, late_parts, late_row, refs = *refs[11:17], refs[17:]
    ends = (
        ((expert_buf,), (expert_got,)),
        ((late_buf,), (late_got,)),
        ((early_buf, shared_buf), (early_parts, shared_parts)),
        ((early_row, shared_row, expert_sum), (early_all, shared_all, expert_all)),
        ((late_sum,), (late_parts,)),
        ((late_row,), (late_all,)),
    )
    movers = []
    for plan, (inputs, outputs) in zip(FINISH, ends):
        own, sems, refs = refs[: len(plan)], refs[len(plan) : len(plan) + 4], refs[len(plan) + 4 :]
        movers.append(Mover(plan, inputs, outputs, own, *sems))

    def begin(mover):
        mover.take()
        mover.start()

    lanes = sum(notes_ref[i].astype(F32) for i in range(notes_ref.shape[0]))[:, : 3 * PAIR]
    lanes = lanes.astype(BF)
    late_buf[...] = dot_tn(lanes, normed_ref[...]).astype(BF)
    begin(movers[1])
    count = expert_buf.shape[0]
    expert_buf[...] = sum(
        expert_ref[i * count : (i + 1) * count].astype(F32) for i in range(GROUP_SIZE["x"])
    ).astype(BF)
    begin(movers[0])

    groups = ids_ref.shape[0]
    expansions = [lane_expansion(ids_ref, group) for group in range(groups)]
    row = 0
    for got in (early_ref, heads_ref):
        for factor in range(got.shape[1] // PAIR):
            early_buf[row : row + LANES, :] = expanded(expansions, got, factor)
            row += LANES
    router = None
    for group in range(groups):
        part = dot_tn(expansions[group], ids_ref[group])
        router = part if router is None else router + part
    router = jnp.sum(router * column_ref[...].astype(F32), axis=1, keepdims=True)
    early_buf[row : row + LANES, :] = jnp.broadcast_to(router, (LANES, 128)).astype(BF)
    for factor in range(shared_ref.shape[1] // PAIR):
        shared_buf[factor * LANES : (factor + 1) * LANES, :] = expanded(
            expansions, shared_ref, factor
        )
    begin(movers[2])

    grad = sum(parts_ref[i].astype(F32) for i in range(parts_ref.shape[0]))
    grad = grad + dot(lanes, first_ref[...])
    total = residual_ref[...] + rms_backward(rows_ref[0].astype(F32), gain_ref[...], grad)
    grad_out[0] = total.astype(BF)

    movers[1].finish()
    for factor in range(late_got.shape[1] // PAIR):
        late_sum[factor * LANES : (factor + 1) * LANES, :] = expanded(expansions, late_got, factor)
    begin(movers[4])
    movers[0].finish()
    expert_sum[...] = sum(expert_got[i].astype(F32) for i in range(groups)).astype(BF)
    movers[2].finish()
    count = early_row.shape[0]
    early_row[...] = sum(
        early_parts[i * count : (i + 1) * count].astype(F32) for i in range(GROUP_SIZE["c"])
    ).astype(BF)
    count = shared_row.shape[0]
    shared_row[...] = (
        shared_parts[:count].astype(F32) + shared_parts[count:].astype(F32)
    ).astype(BF)
    begin(movers[3])
    movers[4].finish()
    count = late_row.shape[0]
    late_row[...] = sum(
        late_parts[i * count : (i + 1) * count].astype(F32) for i in range(GROUP_SIZE["c"])
    ).astype(BF)
    begin(movers[5])

    movers[3].finish()
    early = early_all[...].reshape(-1, 128).astype(F32)
    expert = jnp.concatenate(
        [
            expert_all[2 * i].astype(F32) + expert_all[2 * i + 1].astype(F32)
            for i in range(GROUP_SIZE["x"])
        ],
        axis=0,
    )
    factor = [early[i * LANES : (i + 1) * LANES] for i in range(early.shape[0] // LANES)]
    attn_in[3 * LANES :, :] = factor[5]
    attn_out[: 3 * LANES, :] = jnp.concatenate(factor[8:11], axis=0)
    attn_out[3 * LANES :, :] = factor[6]
    ffn_out[...] = jnp.concatenate(factor[:5], axis=0)
    router_out[...] = factor[11][:, : router_out.shape[1]]
    down_out[:LANES, :] = factor[7]
    down_out[LANES:, :] = expert[3 * LANES :]
    expert_out[...] = expert[: 2 * LANES, : expert_out.shape[1]]
    expert_in_out[...] = expert[2 * LANES : 3 * LANES, : expert_in_out.shape[1]]
    along = GROUP_SIZE["x"]
    columns = shared_out.shape[1] // along
    quarters = [
        shared_all[2 * i : 2 * i + 2].reshape(-1, 128)[:, :columns].astype(F32) for i in range(along)
    ]
    shared_rows = jnp.concatenate(quarters, axis=1)
    shared_out[...] = shared_rows[: 2 * LANES]
    shared_in_out[...] = shared_rows[2 * LANES :]
    movers[5].finish()
    attn_in[: 3 * LANES, :] = late_all[...].reshape(-1, 128).astype(F32)


def finish_shapes(rows, first, items, expert, columns_of):
    width = rows.shape[2]
    early, shared = items[0][2], items[1][2]
    shared_columns, expert_columns = columns_of
    groups, ctx = GROUP_SIZE["f"], GROUP_SIZE["c"]
    early_rows = ((early.shape[0] + first.shape[0]) // PAIR + 1) * LANES
    late_rows = first.shape[0] // PAIR * LANES
    shared_rows = shared.shape[0] // PAIR * LANES
    expert_rows = expert.shape[0] // GROUP_SIZE["x"]
    bufs = [
        first.shape,
        (groups, first.shape[0], 128),
        (early_rows, 128),
        (early_rows, 128),
        (shared_rows, 128),
        (shared_rows, 128),
        (groups, expert_rows, 128),
        (late_rows, 128),
        (early_rows // ctx, 128),
        (shared_rows // 2, 128),
        (expert_rows, 128),
        (ctx, late_rows // ctx, 128),
        (ctx, early_rows // ctx, 128),
        (ctx, shared_rows // 2, 128),
        (ctx, expert_rows, 128),
        (late_rows, 128),
        (late_rows // ctx, 128),
    ]
    sent = (((expert_rows, width),), (bufs[0],), (bufs[2], bufs[4]), (bufs[8], bufs[9], bufs[10]), (bufs[7],), (bufs[16],))
    scratch = [pltpu.VMEM(buf, BF) for buf in ((expert_rows, width), *bufs)]
    for plan, shapes in zip(FINISH, sent):
        scratch += mover_scratch(
            [(kind, group, shape_of(shape, BF)) for (kind, group), shape in zip(plan, shapes)]
        )
    outs = [
        shape_of(rows.shape, BF),
        shape_of((4 * LANES, 128), F32),
        shape_of((4 * LANES, 128), F32),
        shape_of((5 * LANES, 128), F32),
        shape_of((LANES, 1), F32),
        shape_of((2 * LANES, shared_columns), F32),
        shape_of((LANES, shared_columns), F32),
        shape_of((2 * LANES, expert_columns), F32),
        shape_of((LANES, expert_columns), F32),
        shape_of((2 * LANES, 128), F32),
    ]
    return outs, scratch


def deliver_kernel(*refs):
    amount = len(refs) // 2
    for source, target in zip(refs[:amount], refs[amount:]):
        target[...] = source[...]


def deliver(arrays):
    specs = [whole(array) for array in arrays]
    shapes = [shape_of(array.shape, array.dtype) for array in arrays]
    return stage(deliver_kernel, "deliver", shapes, specs, specs)(*arrays)


def combine_kernel(
    main_ref, rest_ref, routes_ref, residual_ref, parts_ref, side_ref, small_ref, picked_ref, out_ref
):
    experts = main_ref.shape[0] // MAIN
    unused, main_hot, rest_hot = routing(routes_ref[0], experts)
    mixture = slots_to_rows(main_hot, rest_hot, main_ref[...], rest_ref[...])
    shared = sum(parts_ref[i].astype(F32) for i in range(parts_ref.shape[0]))
    shared = shared + dot(side_ref[:, :PAIR], picked_ref[2 * PAIR :])
    mix = small_ref[:, 2 * PAIR + TOP : 2 * PAIR + TOP + 1]
    out_ref[0] = (residual_ref[...] + mixture + mix * shared).astype(BF)


def shards(
    layer_hidden_input,
    output_cotangent,
    sequence_pair_lengths,
    block_placement_order,
    sequence_adapter_index,
    token_expert_choices,
    attention_norm_gain,
    feedforward_norm_gain,
    query_key_value_weight,
    output_projection_weight,
    query_key_value_bias,
    router_weight_matrix,
    shared_gate_up_weight,
    shared_down_weight,
    shared_sigmoid_gate,
    routed_gate_up_weight,
    routed_down_weight,
    attention_adapter_first,
    attention_adapter_second,
    feedforward_adapter_first,
    router_adapter_second,
    shared_gate_adapter_second,
    shared_down_adapter_first,
    routed_gate_adapter_second,
    routed_down_adapter_first,
    down_adapter_second,
):
    tokens, width = layer_hidden_input.shape[1:]
    experts = router_weight_matrix.shape[1]
    capacity = tokens * TOP // experts * 9 // 8
    tail = capacity - MAIN
    ctx_count = lax.axis_size("ctx")
    group_rows = tokens * ctx_count
    along = ctx_count // 2
    rows_shared = tokens * along
    x_index = lax.axis_index("ctx") // 2
    y_index = lax.axis_index("ctx") % 2
    head_columns = width // along
    hidden = shared_down_weight.shape[0]
    quarter = hidden // along
    shards_of = lax.axis_size("fsdp")
    lengths = sequence_pair_lengths[0]
    order = block_placement_order[0]
    adapters = sequence_adapter_index[0]
    block_size = group_rows // order.shape[0]

    qkv_own = lax.dynamic_slice_in_dim(
        query_key_value_weight, x_index * head_columns, head_columns, 2
    ).reshape(-1, head_columns)
    out_weight = lax.all_gather(output_projection_weight, "fsdp", tiled=True)
    units = -(-quarter // 32) * 32
    own_up = jnp.swapaxes(
        lax.dynamic_slice_in_dim(shared_gate_up_weight, x_index * quarter, quarter, 2), 1, 2
    )
    own_down = lax.dynamic_slice_in_dim(shared_down_weight, x_index * quarter, quarter, 0)
    own_shared = jnp.pad(
        jnp.concatenate([own_up, own_down[None]]), ((0, 0), (0, units - quarter), (0, 0))
    ).reshape(3 * units, width)

    def of_group(factor):
        parts = [lax.dynamic_index_in_dim(factor, adapters[s], -3, keepdims=True) for s in range(2)]
        both = jnp.concatenate(parts, axis=-3)
        return both.reshape(both.shape[:-3] + (PAIR, both.shape[-1]))

    shared_second = jnp.concatenate(
        [
            of_group(shared_gate_adapter_second).reshape(2 * PAIR, hidden * shards_of),
            of_group(shared_down_adapter_first),
        ],
        axis=0,
    )
    shared_second = lax.dynamic_index_in_dim(
        shared_second.reshape(3 * PAIR, shards_of, along, quarter), x_index, 2, keepdims=False
    )
    shared_second = jnp.pad(shared_second, ((0, 0), (0, 0), (0, units - quarter)))
    shared_second = shared_second.reshape(3, PAIR, shards_of, units).transpose(0, 2, 3, 1)
    shared_second = jnp.stack(
        [
            jnp.pad(shared_second[i], ((0, 0), (0, 0), (before, 128 - PAIR - before)))
            for i, before in enumerate((0, PAIR, 0))
        ]
    )
    numbers = jnp.concatenate([adapters, x_index[None].astype(jnp.int32)])

    start = lengths[0]
    block_rows = jnp.arange(block_size, dtype=jnp.int32)
    blocks = order.reshape(along, 2, -1)
    key_places = (jnp.swapaxes(blocks, 0, 1).reshape(-1)[:, None] * block_size + block_rows).reshape(
        1, group_rows
    )
    own_blocks = lax.dynamic_index_in_dim(blocks, y_index, 1, keepdims=False).reshape(-1)
    places = own_blocks[:, None] * block_size + block_rows
    second = places >= start
    fractions = jnp.arange(0, HEAD_DIM, 2).astype(F32) / HEAD_DIM
    speeds = rope_theta ** (-fractions)
    bases = jnp.stack([own_blocks * block_size, own_blocks * block_size - start])
    base_angles = bases.astype(F32)[:, :, None, None] * speeds
    base_angles = jnp.concatenate([base_angles, base_angles], axis=3)
    base_cos, base_sin = jnp.cos(base_angles), jnp.sin(base_angles)
    base_cos = jnp.where(second[:, :, None], base_cos[1], base_cos[0])
    base_sin = jnp.where(second[:, :, None], base_sin[1], base_sin[0])
    row_angles = block_rows.astype(F32)[:, None] * speeds[None, :]
    row_angles = jnp.concatenate([row_angles, row_angles], axis=1)
    row_cos, row_sin = jnp.cos(row_angles), jnp.sin(row_angles)
    cosine = base_cos * row_cos - base_sin * row_sin
    sine = base_sin * row_cos + base_cos * row_sin
    sine = jnp.where(jnp.arange(HEAD_DIM) < HEAD_DIM // 2, -sine, sine)
    cosine, sine = cosine.reshape(rows_shared, HEAD_DIM), sine.reshape(rows_shared, HEAD_DIM)
    place_column = places.reshape(rows_shared, 1)
    start_column = jnp.where(second, start, 0).reshape(rows_shared, 1)
    side_shared = second.astype(F32).reshape(rows_shared, 1)
    side = lax.dynamic_slice_in_dim(side_shared, x_index * tokens, tokens)

    attention_gain = attention_norm_gain[None, :]
    feedforward_gain = feedforward_norm_gain[None, :]
    mix_weight = shared_sigmoid_gate[None, :]
    routed_second = routed_gate_adapter_second.reshape(2, LANES, -1)
    routed_first = routed_down_adapter_first.reshape(LANES, -1)
    ffn_flat = feedforward_adapter_first.reshape(-1, LANES, width)[3:]
    down_flat = down_adapter_second.reshape(2, LANES, width)

    normed_one, sent_grads_main, sent_grads_rest, picked, picked_first, picked_second = prologue(
        numbers,
        layer_hidden_input,
        output_cotangent,
        attention_gain,
        token_expert_choices,
        feedforward_adapter_first,
        down_adapter_second,
        attention_adapter_first,
        attention_adapter_second,
        experts,
        head_columns,
    )
    own_shared, normed_one = lax.optimization_barrier((own_shared, normed_one))
    shared_weight = lax.all_gather(own_shared, "fsdp")
    qkv, normed_shared = exchange(
        "gather_first", 0, ("share", "s", qkv_own), ("gather", "x", normed_one)
    )
    qkv = qkv.reshape(shards_of, 3, tokens, head_columns)
    projected, qkv_lanes = project(
        numbers,
        normed_shared.reshape(rows_shared, width),
        qkv,
        attention_adapter_first,
        attention_adapter_second,
        query_key_value_bias,
        side_shared,
        cosine,
        sine,
    )
    pairs, grads_shared = exchange(
        "keys", 1, ("gather", "y", projected[1:]), ("gather", "x", output_cotangent[0])
    )
    mixed_heads = attend(projected, pairs, place_column, start_column, key_places)
    (mixed,) = exchange(
        "mixed", 2, ("to_columns", "x", mixed_heads.reshape(along, tokens, head_columns))
    )
    residual, normed_two, small, sent_main, sent_rest, notes_main, notes_rest = after_attention(
        numbers,
        mixed,
        out_weight,
        layer_hidden_input,
        attention_adapter_first,
        attention_adapter_second,
        feedforward_gain,
        feedforward_adapter_first,
        router_weight_matrix,
        router_adapter_second,
        mix_weight,
        token_expert_choices,
        side,
    )
    *held, parts_rows, parts_lanes, value_part, shared_columns = shared_expert(
        3,
        normed_two,
        [
            ("rows", "f", sent_main),
            ("rows", "f", sent_rest),
            ("half", "f", sent_grads_main),
            ("half", "f", sent_grads_rest),
            ("rows", "f", notes_main),
            ("rows", "f", notes_rest),
        ],
        grads_shared,
        shared_weight,
        side_shared.reshape(along, tokens, 1),
        picked,
        shared_second,
        mix_weight,
    )
    (
        got_main,
        got_rest,
        got_notes_main,
        got_notes_rest,
        result_main,
        result_rest,
        value_parts,
        expert_columns,
    ) = routed_expert(
        4,
        held,
        (sent_grads_main, sent_grads_rest),
        value_part,
        ffn_flat,
        routed_second,
        routed_first,
        down_flat,
        routed_gate_up_weight,
        routed_down_weight,
    )
    grad_residual, grad_mixed, early_columns, router_rows, shared_side = after_experts(
        numbers,
        parts_rows,
        parts_lanes,
        got_main,
        got_rest,
        got_notes_main,
        got_notes_rest,
        output_cotangent,
        normed_two,
        residual,
        small,
        mixed,
        token_expert_choices,
        side,
        feedforward_adapter_first,
        router_weight_matrix,
        router_adapter_second,
        mix_weight,
        feedforward_gain,
        down_adapter_second,
        attention_adapter_first,
        attention_adapter_second,
        out_weight,
    )

    own_column = (jnp.arange(128) == lax.axis_index("fsdp")).astype(BF)[None, :]
    results = attention_back(
        5,
        [
            ("from_columns", "f", early_columns),
            ("from_columns", "f", shared_columns),
            ("gather", "f", router_rows),
        ],
        expert_columns,
        grad_mixed,
        projected,
        pairs,
        qkv,
        (
            place_column,
            start_column,
            key_places,
            cosine,
            sine,
            side_shared,
            qkv_lanes,
            picked_second,
        ),
        (
            result_main,
            result_rest,
            token_expert_choices,
            residual,
            value_parts,
            shared_side,
            small,
            picked,
        ),
        (
            layer_hidden_input,
            normed_one,
            grad_residual,
            attention_gain,
            picked_first,
            own_column,
        ),
        (along * quarter, routed_down_weight.shape[1] // shards_of),
    )

    output_value, *grads = deliver(results)

    def by_adapter(rows):
        parts = rows.reshape(-1, ADAPTER_COUNT, RANK, rows.shape[1])
        return parts[0] if parts.shape[0] == 1 else parts

    return (output_value, grads[0], *(by_adapter(rows) for rows in grads[1:]))


def solution(mesh):
    return jax.shard_map(
        shards,
        mesh=mesh,
        in_specs=(
            P("fsdp", "ctx", None),
            P("fsdp", "ctx", None),
            P("fsdp", None),
            P("fsdp", None),
            P("fsdp", None),
            P("fsdp", "ctx", None),
            P(),
            P(),
            P(None, "fsdp", None),
            P("fsdp", None),
            P(),
            P(),
            P(None, None, "fsdp"),
            P("fsdp", None),
            P(),
            P("fsdp", None, None, None),
            P("fsdp", None, None),
            P(),
            P(),
            P(),
            P(),
            P(),
            P(),
            P(),
            P(),
            P(),
        ),
        out_specs=(
            P("fsdp", "ctx", None),
            P("fsdp", "ctx", None),
            P(None, None, None, "fsdp"),
            P(None, None, None, "fsdp"),
            P(None, None, None, "fsdp"),
            P(None, None, "fsdp"),
            P(None, None, None, "fsdp"),
            P(None, None, "fsdp"),
            P(None, None, None, "fsdp"),
            P(None, None, "fsdp"),
            P(None, None, None, "fsdp"),
        ),
        check_vma=False,
    )
```

```python
import functools

import jax
import jax.numpy as jnp
from jax import lax
from jax.experimental import pallas as pl
from jax.experimental.pallas import tpu as pltpu
from jax.sharding import PartitionSpec as P

HEADS = 16
HEAD_DIM = 128
TOP = 4
ADAPTER_COUNT = 8
RANK = 16
LANES = ADAPTER_COUNT * RANK
PAIR = 2 * RANK
MAIN = 32

norm_eps = 1e-06
rope_theta = 1000000.0
masked_score = -1e30
highest = lax.Precision.HIGHEST
MESH = pl.DeviceIdType.MESH
BF = jnp.bfloat16
F32 = jnp.float32
VMEM_LIMIT = 56 * 2**20


def dot(left, right):
    return jnp.dot(left, right, preferred_element_type=F32)


def dot_nt(left, right):
    return lax.dot_general(left, right, (((1,), (1,)), ((), ())), preferred_element_type=F32)


def dot_tn(left, right):
    return lax.dot_general(left, right, (((0,), (0,)), ((), ())), preferred_element_type=F32)


GROUP_SIZE = {"x": 4, "y": 2, "c": 8, "f": 16}


def place_in(group):
    ctx, fsdp = lax.axis_index("ctx"), lax.axis_index("fsdp")
    return {"x": ctx // 2, "y": ctx % 2, "c": ctx, "f": fsdp}[group]


def device_of(group, index):
    ctx, fsdp = lax.axis_index("ctx"), lax.axis_index("fsdp")
    if group == "x":
        return (index * 2 + ctx % 2, fsdp)
    if group == "y":
        return ((ctx // 2) * 2 + index, fsdp)
    if group == "c":
        return (index, fsdp)
    return (ctx, index)


def chip():
    ctx, fsdp = lax.axis_index("ctx"), lax.axis_index("fsdp")
    return ctx % 2 * 2 + fsdp // 8, fsdp // 2 % 4, fsdp % 2


def device_at(y, z, core):
    return (lax.axis_index("ctx") // 2 * 2 + y // 2, y % 2 * 8 + z * 2 + core)


def shard_at(y, z, core):
    return y % 2 * 8 + z * 2 + core


def exchanged_shape(kind, group, shape):
    if kind == "share":
        return (GROUP_SIZE["f"],) + shape
    count = GROUP_SIZE[group]
    if kind == "gather":
        return (count,) + shape
    if kind in ("swap", "rows", "half"):
        return shape
    if kind == "from_columns":
        return (count, shape[0], shape[1] // count)
    return (shape[1], count * shape[2])


def own_shape(kind, group, shape):
    if kind in ("gather", "share"):
        return shape
    count = GROUP_SIZE[group]
    if kind in ("rows", "half"):
        return (shape[0] // count,) + shape[1:]
    if kind == "from_columns":
        return (shape[0], shape[1] // count)
    return shape[1:]


def copies_of(kind, group):
    return 23 if kind == "share" else GROUP_SIZE[group] - 1


def soon(offset):
    return offset % ROUTED_STEPS >= ROUTED_STEPS // 2


def block_of(ref, kind, count, index):
    if kind == "rows":
        depth = ref.shape[0] // count
        return ref.at[pl.ds(pl.multiple_of(index * depth, depth), depth)]
    if kind == "columns":
        width = ref.shape[1] // count
        return ref.at[:, pl.ds(pl.multiple_of(index * width, width), width)]
    return ref.at[index]


def source_of(kind, group, ref, index):
    if kind in ("gather", "share"):
        return ref
    cut = {"rows": "rows", "half": "rows", "from_columns": "columns"}.get(kind, "first")
    return block_of(ref, cut, GROUP_SIZE[group], index)


def target_of(kind, group, ref, index):
    cut = {"rows": "rows", "half": "rows", "to_columns": "columns"}.get(kind, "first")
    return block_of(ref, cut, GROUP_SIZE["f" if kind == "share" else group], index)


def remote(source, target, send, recv, device):
    return pltpu.make_async_remote_copy(
        src_ref=source,
        dst_ref=target,
        send_sem=send,
        recv_sem=recv,
        device_id=device,
        device_id_type=MESH,
    )


def greet(plan):
    barrier = pltpu.get_barrier_semaphore()
    count = 0
    for group in sorted({group for kind, group in plan}):
        if group == "s":
            y, z, core = chip()
            peers = [device_at(y, lax.rem(z + d, 4), core) for d in (1, 2, 3)]
            peers += [device_at(lax.rem(y + d, 4), z, core) for d in (1, 3)]
            peers += [device_at(y, z, 1 - core)]
        else:
            size = GROUP_SIZE[group]
            mine = place_in(group)
            peers = [device_of(group, lax.rem(mine + d, size)) for d in range(1, size)]
        for peer in peers:
            pl.semaphore_signal(barrier, inc=1, device_id=peer, device_id_type=MESH)
        count += len(peers)
    pl.semaphore_wait(barrier, count)


class Share:
    def __init__(self, source, target, send, recv, first):
        self.target = target
        self.sems = (send, recv, first)
        y, z, core = self.place = chip()
        self.order = (1, 3, 2)
        self.source = source
        self.along_z = [
            self.copy(source, shard_at(y, z, core), None, i, device_at(y, lax.rem(z + d, 4), core))
            for i, d in enumerate(self.order)
        ]
        self.along_y, self.across = [], []

    def copy(self, source, shard, half, number, device):
        send, recv, first = self.sems
        target = self.target.at[shard]
        if half is not None:
            target = target.at[half]
        return remote(source, target, send.at[first + number], recv.at[first + number], device)

    def halves(self):
        half = self.target.shape[1] // 2
        return pl.ds(0, half), pl.ds(half, half)

    def forward(self, number, source, z):
        y, unused, core = self.place
        unused, my_z, unused = self.place
        shard = shard_at(y, z, core)
        for i, (half, d) in enumerate(zip(self.halves(), (3, 1))):
            copy = self.copy(
                source.at[half], shard, half, 3 + 2 * number + i, device_at(lax.rem(y + d, 4), my_z, core)
            )
            copy.start()
            self.along_y.append(copy)
        copy = self.copy(source, shard, None, 11 + number, device_at(y, my_z, 1 - core))
        copy.start()
        self.across.append(copy)

    def start(self):
        for copy in self.along_z:
            copy.start()
        self.forward(0, self.source, self.place[1])

    def finish(self):
        y, z, core = self.place
        for i, d in enumerate(self.order):
            self.along_z[i].wait_recv()
            from_z = lax.rem(z + 4 - d, 4)
            self.forward(i + 1, self.target.at[shard_at(y, from_z, core)], from_z)
        for number in range(4):
            from_z = z if number == 0 else lax.rem(z + 4 - self.order[number - 1], 4)
            shard = shard_at(y + 1, from_z, core)
            for i, half in enumerate(self.halves()):
                self.along_y[2 * number + i].wait_recv()
                block = self.target.at[shard].at[half]
                copy = self.copy(block, shard, half, 15 + 2 * number + i, device_at(y, z, 1 - core))
                copy.start()
                self.across.append(copy)
        for copy in self.along_z + self.along_y:
            copy.wait_send()
        for copy in self.across:
            copy.wait()


class Mover:
    def __init__(self, plan, inputs, outputs, own, send, recv, in_sem, out_sem):
        self.plan, self.inputs, self.outputs, self.own = plan, inputs, outputs, own
        self.send, self.recv, self.in_sem, self.out_sem = send, recv, in_sem, out_sem
        self.taken, self.copies, self.shares = [], [], []

    def own_place(self, item):
        kind, group = self.plan[item]
        return shard_at(*chip()) if kind == "share" else place_in(group)

    def take(self):
        for item, (kind, group) in enumerate(self.plan):
            block = source_of(kind, group, self.inputs[item], self.own_place(item))
            copy = pltpu.make_async_copy(block, self.own[item], self.in_sem.at[item])
            copy.start()
            self.taken.append(copy)

    def start(self):
        slot = 0
        for item, (kind, group) in enumerate(self.plan):
            source, target = self.inputs[item], self.outputs[item]
            if kind == "share":
                share = Share(source, target, self.send, self.recv, slot)
                share.start()
                self.shares.append(share)
            else:
                count = GROUP_SIZE[group]
                mine = place_in(group)
                for offset in range(1, count):
                    if kind == "half" and not soon(offset):
                        continue
                    peer = lax.rem(mine + offset, count)
                    copy = remote(
                        source_of(kind, group, source, peer),
                        target_of(kind, group, target, mine),
                        self.send.at[slot + offset - 1],
                        self.recv.at[slot + offset - 1],
                        device_of(group, peer),
                    )
                    copy.start()
                    self.copies.append(copy)
            slot += copies_of(kind, group)
        for item, (kind, group) in enumerate(self.plan):
            self.taken[item].wait()
            block = target_of(kind, group, self.outputs[item], self.own_place(item))
            copy = pltpu.make_async_copy(self.own[item], block, self.out_sem.at[item])
            copy.start()
            self.copies.append(copy)

    def finish(self):
        for share in self.shares:
            share.finish()
        for copy in self.copies:
            copy.wait()


def exchange_kernel(plan, *refs):
    amount = len(plan)
    mover = Mover(
        plan, refs[:amount], refs[amount : 2 * amount], refs[2 * amount : 3 * amount], *refs[3 * amount :]
    )
    mover.take()
    greet(plan)
    mover.start()
    mover.finish()


def mover_scratch(items):
    plan = tuple((kind, group) for kind, group, array in items)
    slots = sum(copies_of(kind, group) for kind, group in plan)
    return [
        pltpu.VMEM(own_shape(kind, group, array.shape), array.dtype) for kind, group, array in items
    ] + [
        pltpu.SemaphoreType.DMA((slots,)),
        pltpu.SemaphoreType.DMA((slots,)),
        pltpu.SemaphoreType.DMA((len(items),)),
        pltpu.SemaphoreType.DMA((len(items),)),
    ]


def exchange(name, number, *items):
    plan = tuple((kind, group) for kind, group, array in items)
    arrays = [array for kind, group, array in items]
    return pl.pallas_call(
        functools.partial(exchange_kernel, plan),
        out_shape=[
            jax.ShapeDtypeStruct(exchanged_shape(kind, group, array.shape), array.dtype)
            for kind, group, array in items
        ],
        in_specs=[pl.BlockSpec(memory_space=pltpu.HBM)] * len(items),
        out_specs=[pl.BlockSpec(memory_space=pltpu.HBM)] * len(items),
        scratch_shapes=mover_scratch(items),
        compiler_params=pltpu.CompilerParams(
            collective_id=number, has_side_effects=True, vmem_limit_bytes=16 * 2**20
        ),
        name=name,
    )(*arrays)


def rms_forward(values, gain):
    mean_square = jnp.mean(values * values, axis=-1, keepdims=True)
    return values * lax.rsqrt(mean_square + norm_eps) * gain.astype(F32)


def rms_backward(values, gain, grad_result):
    scale = lax.rsqrt(jnp.mean(values * values, axis=-1, keepdims=True) + norm_eps)
    scaled = gain.astype(F32) * grad_result
    inner = jnp.mean(values * scaled, axis=-1, keepdims=True)
    return scale * scaled - values * (scale * scale * scale) * inner


def logistic(values):
    return 0.5 * jnp.tanh(0.5 * values) + 0.5


def swiglu(gate, upper):
    sigma = logistic(gate)
    silu = gate * sigma
    return (silu * upper).astype(BF), sigma, silu


def swiglu_backward(gate, upper, sigma, silu, grad_hidden):
    grad_gate = grad_hidden * upper * (sigma + silu * (1.0 - sigma))
    return (grad_gate.astype(BF), (grad_hidden * silu).astype(BF))


def two_parts(values):
    high = values.astype(BF)
    return high, (values - high.astype(F32)).astype(BF)


def lane_index(shape):
    return lax.broadcasted_iota(jnp.int32, shape, 1)


def row_index(shape):
    return lax.broadcasted_iota(jnp.int32, shape, 0)


def pair_pick(second, copies):
    shape = (second.shape[0], PAIR * copies)
    of_lane = (lane_index(shape) % PAIR >= RANK).astype(F32)
    return (of_lane == second).astype(F32)


def pair_of(first_ref, last_ref, index):
    return jnp.concatenate([first_ref[index, 0], last_ref[index, 0]], axis=0)


def padded(values):
    rest = 128 - values.shape[1]
    return jnp.concatenate([values, jnp.zeros((values.shape[0], rest), values.dtype)], axis=1)


def routing(routes, experts):
    tokens = routes.shape[0]
    expert_lane = lane_index((tokens, experts))
    expert_hot = [(routes[:, k : k + 1] == expert_lane).astype(F32) for k in range(TOP)]
    count = sum(expert_hot)
    below = (row_index((tokens, tokens)) > lane_index((tokens, tokens))).astype(BF)
    earlier = dot(below, count.astype(BF))
    rank = [jnp.sum(hot * earlier, axis=1, keepdims=True).astype(jnp.int32) for hot in expert_hot]
    main_lane = lane_index((tokens, experts * MAIN))
    rest_lane = lane_index((tokens, experts * 16))
    rest_code = (rest_lane // 16) * 4 + rest_lane % 4
    main_hot, rest_hot = [], []
    for k in range(TOP):
        expert = routes[:, k : k + 1]
        main_slot = jnp.where(rank[k] < MAIN, expert * MAIN + rank[k], -1)
        rest_slot = jnp.where(rank[k] < MAIN, -1, expert * 4 + rank[k] - MAIN)
        main_hot.append((main_lane == main_slot).astype(F32))
        rest_hot.append((rest_code == rest_slot).astype(F32))
    return expert_hot, main_hot, rest_hot


def quarter_mask(shape, quarter):
    return (lane_index(shape) % 16 // 4 == quarter).astype(F32)


def rows_to_slots(main_hot, rest_hot, rows):
    main = dot_tn(sum(main_hot).astype(BF), rows).astype(BF)
    rest_sum = sum(rest_hot)
    width = rows.shape[1] // 4
    rest = None
    for quarter in range(4):
        hot = (rest_sum * quarter_mask(rest_sum.shape, quarter)).astype(BF)
        part = dot_tn(hot, rows[:, quarter * width : (quarter + 1) * width])
        rest = part if rest is None else rest + part
    return main, rest.astype(BF)


def slots_to_rows(main_hot, rest_hot, main, rest):
    rest_sum = sum(rest_hot)
    parts = [
        dot((rest_sum * quarter_mask(rest_sum.shape, quarter)).astype(BF), rest)
        for quarter in range(4)
    ]
    return dot(sum(main_hot).astype(BF), main) + jnp.concatenate(parts, axis=1)


def rest_selectors(sources):
    shape = (4 * sources, 16 * sources)
    row, lane = row_index(shape), lane_index(shape)
    same = (lane // 16 == row // 4) & (lane % 4 == row % 4)
    return [(same & (lane % 16 // 4 == quarter)).astype(BF) for quarter in range(4)]


def rest_to_rows(selectors, rest):
    return jnp.concatenate([dot(selector, rest) for selector in selectors], axis=1).astype(BF)


def rows_to_rest(selectors, rows):
    width = rows.shape[1] // 4
    total = None
    for quarter in range(4):
        part = dot_tn(selectors[quarter], rows[:, quarter * width : (quarter + 1) * width])
        total = part if total is None else total + part
    return total.astype(BF)


def stage(kernel, name, out_shape, in_specs, out_specs, grid=(1,), scratch=(), prefetch=0):
    return pl.pallas_call(
        kernel,
        out_shape=out_shape,
        grid_spec=pltpu.PrefetchScalarGridSpec(
            num_scalar_prefetch=prefetch,
            grid=grid,
            in_specs=in_specs,
            out_specs=out_specs,
            scratch_shapes=list(scratch),
        ),
        compiler_params=pltpu.CompilerParams(vmem_limit_bytes=VMEM_LIMIT),
        name=name,
    )


def whole(array):
    zeros = (0,) * len(array.shape)
    return pl.BlockSpec(array.shape, lambda *unused: zeros)


def of_sequence(which, block):
    return pl.BlockSpec(block, lambda *at: (0, at[-1][which], 0, 0))


def shape_of(shape, kind):
    return jax.ShapeDtypeStruct(shape, kind)


HBM = pl.BlockSpec(memory_space=pltpu.HBM)


def prologue_kernel(
    numbers_ref,
    rows_ref,
    grads_ref,
    gain_ref,
    routes_ref,
    ffn_a_ref,
    ffn_b_ref,
    down_a_ref,
    down_b_ref,
    first_a_ref,
    first_b_ref,
    second_a_ref,
    second_b_ref,
    normed_ref,
    main_ref,
    rest_ref,
    picked_ref,
    first_ref,
    second_ref,
):
    normed_ref[...] = rms_forward(rows_ref[0].astype(F32), gain_ref[...]).astype(BF)
    experts = main_ref.shape[0] // MAIN
    unused, main_hot, rest_hot = routing(routes_ref[0], experts)
    main, rest = rows_to_slots(main_hot, rest_hot, grads_ref[0])
    main_ref[...] = main
    rest_ref[...] = rest
    picked_ref[...] = jnp.concatenate(
        [
            pair_of(ffn_a_ref, ffn_b_ref, 1),
            pair_of(ffn_a_ref, ffn_b_ref, 2),
            pair_of(down_a_ref, down_b_ref, 0),
        ],
        axis=0,
    )
    for j in range(3):
        first_ref[j * PAIR : (j + 1) * PAIR, :] = pair_of(first_a_ref, first_b_ref, j)
        second_ref[j * PAIR : (j + 1) * PAIR, :] = pair_of(second_a_ref, second_b_ref, j)


def prologue(
    numbers, rows, grads, gain, routes, ffn_first, down_second, first, second, experts, columns
):
    tokens, width = rows.shape[1:]
    heads = lambda which: pl.BlockSpec(
        (3, 1, RANK, columns), lambda n, a: (0, a[which], 0, a[2])
    )
    outs = [
        (tokens, width),
        (experts * MAIN, width),
        (experts * 16, width // 4),
        (3 * PAIR, width),
        (3 * PAIR, width),
        (3 * PAIR, columns),
    ]
    return stage(
        prologue_kernel,
        "prologue",
        [shape_of(shape, BF) for shape in outs],
        [
            whole(rows),
            whole(grads),
            whole(gain),
            whole(routes),
            of_sequence(0, (3, 1, RANK, width)),
            of_sequence(1, (3, 1, RANK, width)),
            of_sequence(0, (1, 1, RANK, width)),
            of_sequence(1, (1, 1, RANK, width)),
            of_sequence(0, (3, 1, RANK, width)),
            of_sequence(1, (3, 1, RANK, width)),
            heads(0),
            heads(1),
        ],
        [pl.BlockSpec(shape, lambda n, a: (0, 0)) for shape in outs],
        prefetch=1,
    )(
        numbers, rows, grads, gain, routes, ffn_first, ffn_first, down_second, down_second, first, first,
        second, second,
    )


def half_turn(values):
    parts = []
    for head in range(values.shape[1] // HEAD_DIM):
        part = values[:, head * HEAD_DIM : (head + 1) * HEAD_DIM]
        parts.append(jnp.concatenate([part[:, 64:], part[:, :64]], axis=1))
    return jnp.concatenate(parts, axis=1) if len(parts) > 1 else parts[0]


def project_kernel(
    numbers_ref,
    rows_ref,
    weight_ref,
    first_a_ref,
    first_b_ref,
    second_a_ref,
    second_b_ref,
    bias_ref,
    side_ref,
    cos_ref,
    sin_ref,
    out_ref,
    lanes_ref,
):
    which = pl.program_id(0)

    @pl.when(pl.program_id(1) == 0)
    def lanes():
        first = pair_of(first_a_ref, first_b_ref, 0)
        picked = dot_nt(rows_ref[...], first) * pair_pick(side_ref[...], 1)
        lanes_ref[0] = picked.astype(BF)

    weight = weight_ref[...].reshape(rows_ref.shape[1], weight_ref.shape[3])
    bias = bias_ref[...].astype(F32)
    bias = jnp.sum(jnp.where(row_index(bias.shape) == which, bias, 0.0), axis=0, keepdims=True)
    second = pair_of(second_a_ref, second_b_ref, 0)
    value = dot(rows_ref[...], weight) + bias + dot(lanes_ref[0], second)
    copies = value.shape[1] // HEAD_DIM
    cosine = jnp.concatenate([cos_ref[...]] * copies, axis=1)
    sine = jnp.concatenate([sin_ref[...]] * copies, axis=1)
    turned = value * cosine + half_turn(value) * sine
    out_ref[0] = jnp.where(which < 2, turned, value).astype(BF)


def project(numbers, rows, weight, first, second, bias, side, cosine, sine):
    tokens, width = rows.shape
    columns = weight.shape[3]
    step = 256
    steps = columns // step
    return stage(
        project_kernel,
        "project",
        [shape_of((3, tokens, columns), BF), shape_of((3, tokens, PAIR), BF)],
        [
            whole(rows),
            pl.BlockSpec((weight.shape[0], 1, weight.shape[2], step), lambda j, n, a: (0, j, 0, n)),
            pl.BlockSpec((1, 1, RANK, width), lambda j, n, a: (j, a[0], 0, 0)),
            pl.BlockSpec((1, 1, RANK, width), lambda j, n, a: (j, a[1], 0, 0)),
            pl.BlockSpec((1, 1, RANK, step), lambda j, n, a: (j, a[0], 0, a[2] * steps + n)),
            pl.BlockSpec((1, 1, RANK, step), lambda j, n, a: (j, a[1], 0, a[2] * steps + n)),
            pl.BlockSpec((3, step), lambda j, n, a: (0, a[2] * steps + n)),
            whole(side),
            whole(cosine),
            whole(sine),
        ],
        [
            pl.BlockSpec((1, tokens, step), lambda j, n, a: (j, 0, n)),
            pl.BlockSpec((1, tokens, PAIR), lambda j, n, a: (j, 0, 0)),
        ],
        grid=(3, steps),
        prefetch=1,
    )(numbers, rows, weight, first, first, second, second, bias, side, cosine, sine)


def probabilities(query, keys, query_place, query_start, key_place):
    scores = dot_nt(query, keys) * (HEAD_DIM**-0.5)
    allowed = (key_place <= query_place) & (key_place >= query_start)
    scores = jnp.where(allowed, scores, masked_score)
    top = jnp.max(scores, axis=1, keepdims=True)
    raised = jnp.exp(scores - top)
    return raised * (1.0 / jnp.sum(raised, axis=1, keepdims=True))


def attend_kernel(query_ref, key_ref, value_ref, place_ref, start_ref, key_place_ref, out_ref):
    keys = key_ref[...].reshape(-1, HEAD_DIM)
    values = value_ref[...].reshape(-1, HEAD_DIM)
    probs = probabilities(query_ref[0], keys, place_ref[...], start_ref[...], key_place_ref[...])
    out_ref[...] = dot(probs.astype(BF), values).astype(BF)


def attend(projected, pairs, place, start, key_place):
    tokens, columns = projected.shape[1:]
    step = 256
    keys = pairs.shape[0] * pairs.shape[2]
    half = pairs.shape[2]
    return pl.pallas_call(
        attend_kernel,
        grid=(columns // HEAD_DIM, tokens // step),
        out_shape=jax.ShapeDtypeStruct((tokens, columns), BF),
        in_specs=[
            pl.BlockSpec((1, step, HEAD_DIM), lambda h, i: (0, i, h)),
            pl.BlockSpec((2, 1, half, HEAD_DIM), lambda h, i: (0, 0, 0, h)),
            pl.BlockSpec((2, 1, half, HEAD_DIM), lambda h, i: (0, 1, 0, h)),
            pl.BlockSpec((step, 1), lambda h, i: (i, 0)),
            pl.BlockSpec((step, 1), lambda h, i: (i, 0)),
            pl.BlockSpec((1, keys), lambda h, i: (0, 0)),
        ],
        out_specs=pl.BlockSpec((step, HEAD_DIM), lambda h, i: (i, h)),
        compiler_params=pltpu.CompilerParams(vmem_limit_bytes=VMEM_LIMIT),
        name="attend",
    )(projected, pairs, pairs, place, start, key_place)


def after_attention_kernel(
    numbers_ref,
    mixed_ref,
    weight_ref,
    rows_ref,
    first_a_ref,
    first_b_ref,
    second_a_ref,
    second_b_ref,
    gain_ref,
    ffn_a_ref,
    ffn_b_ref,
    router_ref,
    router_a_ref,
    router_b_ref,
    mix_ref,
    routes_ref,
    side_ref,
    residual_ref,
    normed_ref,
    small_ref,
    main_ref,
    rest_ref,
    main_notes_ref,
    rest_notes_ref,
    lanes_ref,
):
    step = pl.program_id(0)
    side = side_ref[...]
    pick = pair_pick(side, 1)

    @pl.when(step == 0)
    def lanes():
        first = pair_of(first_a_ref, first_b_ref, 0)
        lanes_ref[...] = (dot_nt(mixed_ref[...], first) * pick).astype(BF)

    columns = weight_ref.shape[1]
    here = pl.ds(pl.multiple_of(step * columns, columns), columns)
    second = pair_of(second_a_ref, second_b_ref, 0)
    residual_ref[:, here] = rows_ref[0].astype(F32) + (
        dot(mixed_ref[...], weight_ref[...]) + dot(lanes_ref[...], second)
    )

    @pl.when(step == pl.num_programs(0) - 1)
    def last():
        tokens = residual_ref.shape[0]
        experts = router_ref.shape[1]
        normed = rms_forward(residual_ref[...], gain_ref[...]).astype(BF)
        normed_ref[...] = normed
        router_lanes = (dot_nt(normed, pair_of(ffn_a_ref, ffn_b_ref, 0)) * pick).astype(BF)
        router_second = jnp.concatenate([router_a_ref[0], router_b_ref[0]], axis=0)
        logits = dot(normed, router_ref[...]) + dot(router_lanes, router_second)
        expert_hot, main_hot, rest_hot = routing(routes_ref[0], experts)
        chosen = [jnp.sum(hot * logits, axis=1, keepdims=True) for hot in expert_hot]
        top = jnp.maximum(jnp.maximum(chosen[0], chosen[1]), jnp.maximum(chosen[2], chosen[3]))
        raised = [jnp.exp(value - top) for value in chosen]
        total = sum(raised)
        gates = [value / total for value in raised]
        mix = logistic(
            jnp.sum(normed.astype(F32) * mix_ref[...].astype(F32), axis=1, keepdims=True)
        )
        small_ref[...] = padded(
            jnp.concatenate(
                [lanes_ref[...].astype(F32), router_lanes.astype(F32), *gates, mix], axis=1
            )
        )
        main, rest = rows_to_slots(main_hot, rest_hot, normed)
        main_ref[...] = main
        rest_ref[...] = rest
        adapter = jnp.where(side > 0.5, numbers_ref[1], numbers_ref[0])
        lane = lane_index((tokens, 128))
        adapter_hot = (lane == adapter).astype(F32)
        main_notes, rest_notes = None, None
        for k in range(TOP):
            high, low = two_parts(gates[k])
            notes = jnp.where(
                lane == ADAPTER_COUNT,
                high.astype(F32),
                jnp.where(lane == ADAPTER_COUNT + 1, low.astype(F32), adapter_hot),
            ).astype(BF)
            main_part = dot_tn(main_hot[k].astype(BF), notes)
            rest_part = dot_tn(rest_hot[k].astype(BF), notes)
            main_notes = main_part if k == 0 else main_notes + main_part
            rest_notes = rest_part if k == 0 else rest_notes + rest_part
        main_notes_ref[...] = main_notes.astype(BF)
        rest_notes_ref[...] = rest_notes.astype(BF)


def after_attention(
    numbers, mixed, weight, rows, first, second, gain, ffn_first, router, router_second, mix, routes, side
):
    tokens, width = mixed.shape
    experts = router.shape[1]
    step = 512
    kept = lambda *shape: pl.BlockSpec(shape, lambda n, a: (0,) * len(shape))
    outs = [
        ((tokens, width), F32),
        ((tokens, width), BF),
        ((tokens, 128), F32),
        ((experts * MAIN, width), BF),
        ((experts * 16, width // 4), BF),
        ((experts * MAIN, 128), BF),
        ((experts * 16, 128), BF),
    ]
    return stage(
        after_attention_kernel,
        "after_attention",
        [shape_of(*out) for out in outs],
        [
            whole(mixed),
            pl.BlockSpec((width, step), lambda n, a: (0, n)),
            pl.BlockSpec((1, tokens, step), lambda n, a: (0, 0, n)),
            pl.BlockSpec((1, 1, RANK, width), lambda n, a: (3, a[0], 0, 0)),
            pl.BlockSpec((1, 1, RANK, width), lambda n, a: (3, a[1], 0, 0)),
            pl.BlockSpec((1, 1, RANK, step), lambda n, a: (3, a[0], 0, n)),
            pl.BlockSpec((1, 1, RANK, step), lambda n, a: (3, a[1], 0, n)),
            whole(gain),
            pl.BlockSpec((1, 1, RANK, width), lambda n, a: (0, a[0], 0, 0)),
            pl.BlockSpec((1, 1, RANK, width), lambda n, a: (0, a[1], 0, 0)),
            whole(router),
            pl.BlockSpec((1, RANK, experts), lambda n, a: (a[0], 0, 0)),
            pl.BlockSpec((1, RANK, experts), lambda n, a: (a[1], 0, 0)),
            whole(mix),
            whole(routes),
            whole(side),
        ],
        [kept(*shape) for shape, kind in outs],
        grid=(width // step,),
        scratch=[pltpu.VMEM((tokens, PAIR), BF)],
        prefetch=1,
    )(
        numbers, mixed, weight, rows, first, first, second, second, gain, ffn_first, ffn_first, router,
        router_second, router_second, mix, routes, side,
    )


def in_owner_columns(total, target, columns):
    count = total.shape[0]
    for owner in range(total.shape[1] // columns):
        part = total[:, owner * columns : (owner + 1) * columns].astype(BF)
        target[:count, owner * 128 : (owner + 1) * 128] = padded(part)


def x_step(step):
    return step + step // 2 * (1 - 2 * (step % 2))


SHARED_STEPS = 4


def shared_kernel(plan, *refs):
    amount = len(plan)
    inputs, refs = refs[:amount], refs[amount:]
    normed_ref, grads_hbm, weights_hbm, side_ref, picked_ref, first_ref, mix_ref = refs[:7]
    outputs, refs = refs[7 : 7 + amount], refs[7 + amount :]
    parts_refs, values_ref, adapter_ref, refs = refs[:2], refs[2], refs[3], refs[4:]
    own, move_sems, refs = refs[:amount], refs[amount : amount + 4], refs[amount + 4 :]
    rows_buf, grads_buf, gate_up_buf, down_buf = refs[:4]
    parts_buf, values_buf, total, refs = refs[4:6], refs[6], refs[7], refs[8:]
    rows_send, rows_recv, parts_send, parts_recv, load_sem, parts_sem = refs

    shards_of, units, wide = down_buf.shape
    along, tokens, width = rows_buf.shape
    hidden_units = shards_of * units
    me = place_in("x")
    loads = [
        pltpu.make_async_copy(normed_ref, rows_buf.at[me], load_sem.at[0]),
        pltpu.make_async_copy(grads_hbm, grads_buf, load_sem.at[1]),
    ]
    loads += [
        pltpu.make_async_copy(
            weights_hbm.at[:, pl.ds(i * units, units)],
            target.at[:, :, pl.ds(0, width)],
            load_sem.at[2 + i],
        )
        for i, target in enumerate((gate_up_buf.at[0], gate_up_buf.at[1], down_buf))
    ]
    for load in loads:
        load.start()
    mover = Mover(plan, inputs, outputs, own, *move_sems)
    mover.take()
    greet(plan + (("gather", "x"),))

    def rows_copy(offset):
        return remote(
            normed_ref,
            rows_buf.at[me],
            rows_send.at[offset],
            rows_recv.at[offset],
            device_of("x", lax.rem(me + offset, along)),
        )

    def parts_copy(kind, offset):
        peer = lax.rem(me + along - offset, along)
        return remote(
            parts_buf[kind].at[peer],
            parts_refs[kind].at[me],
            parts_send.at[kind, offset],
            parts_recv.at[kind, offset],
            device_of("x", peer),
        )

    def own_parts(kind):
        return pltpu.make_async_copy(
            parts_buf[kind].at[me], parts_refs[kind].at[me], parts_sem.at[kind]
        )

    for offset in (1, 3, 2):
        rows_copy(offset).start()
    mover.start()
    for i in range(2):
        gate_up_buf[i, :, :, width:] = first_ref[i]
    down_buf[:, :, width:] = first_ref[2]
    total[...] = jnp.zeros_like(total)
    for load in loads[:2]:
        load.wait()
    per_step = along // SHARED_STEPS

    def block(step, carry):
        offsets = [x_step(step * per_step + i) for i in range(per_step)]
        sources = [lax.rem(me + along - offset, along) for offset in offsets]
        for i, offset in enumerate(offsets):
            if i > 0:
                rows_copy(offset).wait_recv()
            else:

                @pl.when(step > 0)
                def arrived():
                    rows_copy(offset).wait_recv()

        rows = jnp.concatenate([rows_buf[source] for source in sources], axis=0)
        grads = jnp.concatenate([grads_buf[source] for source in sources], axis=0)
        side = jnp.concatenate([side_ref[source] for source in sources], axis=0)
        grads_f = grads.astype(F32)
        pick = pair_pick(side, 1)
        pick_both = pair_pick(side, 2)
        lanes = (dot_nt(rows, picked_ref[: 2 * PAIR]) * pick_both).astype(BF)
        mix = logistic(jnp.sum(rows.astype(F32) * mix_ref[...].astype(F32), axis=1, keepdims=True))
        grad_shared = (mix * grads_f).astype(BF)
        grad_side = (dot_nt(grad_shared, picked_ref[2 * PAIR :]) * pick).astype(BF)

        @pl.when(step == 0)
        def gate_up_loaded():
            for load in loads[2:4]:
                load.wait()

        both = dot_nt(jnp.concatenate([rows, padded(lanes)], axis=1), gate_up_buf[...].reshape(-1, wide))
        gate, upper = both[:, :hidden_units], both[:, hidden_units:]
        hidden, sigma, silu = swiglu(gate, upper)

        @pl.when(step == 0)
        def down_loaded():
            loads[4].wait()

        down = down_buf[...].reshape(hidden_units, wide)
        grad_hidden = dot_nt(jnp.concatenate([grad_shared, padded(grad_side)], axis=1), down)
        grad_gate, grad_upper = swiglu_backward(gate, upper, sigma, silu, grad_hidden)
        gate_up = gate_up_buf[...].reshape(2 * hidden_units, wide)
        back = dot(jnp.concatenate([grad_gate, grad_upper], axis=1), gate_up)
        grad_lanes = (back[:, width : width + 2 * PAIR] * pick_both).astype(BF)
        value = dot(hidden, down)
        side_lanes = (value[:, width : width + PAIR] * pick).astype(BF)
        value = value[:, :width]
        mix_sum = jnp.sum(grads_f * value, axis=1, keepdims=True)
        notes = padded(jnp.concatenate([side_lanes, grad_lanes, *two_parts(mix_sum)], axis=1))
        for i, source in enumerate(sources):
            at = slice(i * tokens, (i + 1) * tokens)
            parts_buf[0][source] = back[at, :width].astype(BF)
            parts_buf[1][source] = notes[at]
            values_buf[source] = value[at].astype(BF)

        for i, offset in enumerate(offsets):
            if i > 0:
                for kind in range(2):
                    parts_copy(kind, offset).start()
            else:

                @pl.when(step == 0)
                def keep():
                    for kind in range(2):
                        own_parts(kind).start()

                @pl.when(step > 0)
                def send():
                    for kind in range(2):
                        parts_copy(kind, offset).start()

        total[:PAIR] += dot_tn(lanes[:, :PAIR], grad_gate)
        total[PAIR : 2 * PAIR] += dot_tn(lanes[:, PAIR:], grad_upper)
        total[2 * PAIR :] += dot_tn(grad_side, hidden)
        return carry

    lax.fori_loop(0, SHARED_STEPS, block, 0)
    values_out = pltpu.make_async_copy(values_buf, values_ref, parts_sem.at[2])
    values_out.start()
    in_owner_columns(total, adapter_ref, units)
    mover.finish()
    for kind in range(2):
        own_parts(kind).wait()
    for offset in range(1, along):
        rows_copy(offset).wait_send()
        for kind in range(2):
            parts_copy(kind, offset).wait()
    values_out.wait()


def shared_expert(number, normed, items, grads, weights, side, picked, first, mix):
    tokens, width = normed.shape
    plan = tuple((kind, group) for kind, group, array in items)
    arrays = [array for kind, group, array in items]
    along = GROUP_SIZE["x"]
    shards_of, units = weights.shape[0], weights.shape[1] // 3
    hidden = shards_of * units
    vmem = pl.BlockSpec(memory_space=pltpu.VMEM)
    parts = [(along, tokens, width), (along, tokens, 128), (along, tokens, width)]
    return pl.pallas_call(
        functools.partial(shared_kernel, plan),
        out_shape=[shape_of(array.shape, BF) for array in arrays]
        + [shape_of(part, BF) for part in parts]
        + [shape_of((3 * PAIR, shards_of * 128), BF)],
        in_specs=[HBM] * (len(items) + 3) + [vmem] * 4,
        out_specs=[HBM] * (len(items) + 3) + [vmem],
        scratch_shapes=mover_scratch(items)
        + [pltpu.VMEM((along, tokens, width), BF)] * 2
        + [
            pltpu.VMEM((2, shards_of, units, width + 128), BF),
            pltpu.VMEM((shards_of, units, width + 128), BF),
        ]
        + [pltpu.VMEM(part, BF) for part in parts]
        + [pltpu.VMEM((3 * PAIR, hidden), F32)]
        + [
            pltpu.SemaphoreType.DMA((along,)),
            pltpu.SemaphoreType.DMA((along,)),
            pltpu.SemaphoreType.DMA((2, along)),
            pltpu.SemaphoreType.DMA((2, along)),
            pltpu.SemaphoreType.DMA((5,)),
            pltpu.SemaphoreType.DMA((3,)),
        ],
        compiler_params=pltpu.CompilerParams(
            collective_id=number, has_side_effects=True, vmem_limit_bytes=VMEM_LIMIT
        ),
        name="shared_expert",
    )(*arrays, normed, grads, weights, side, picked, first, mix)


BACK = 6
ROUTED_STEPS = 4


def routed_kernel(*refs):
    held_hbm, gate_up_hbm, down_hbm, values_hbm = refs[:6], refs[6], refs[7], refs[8]
    later_hbm, refs = refs[9:11], refs[2:]
    first_ref, second_ref, down_first_ref, down_second_ref = refs[9:13]
    back_refs, values_ref, refs = refs[13 : 13 + BACK], refs[13 + BACK], refs[14 + BACK :]
    adapter_ref = refs[0]
    own, move_sems, refs = refs[1:2], refs[2:6], refs[6:]
    held, back_buf, refs = refs[:6], refs[6 : 6 + BACK], refs[6 + BACK :]
    gate_up_buf, down_buf, total, total_down = refs[:4]
    send_sem, recv_sem, load_sem, own_sem, half_sem, later_send, later_recv = refs[4:]

    me = place_in("f")
    experts = GROUP_SIZE["f"]
    steps = ROUTED_STEPS
    loads = [
        pltpu.make_async_copy(held_hbm[i], held[i], load_sem.at[i]) for i in (0, 1, 4, 5)
    ]
    for offset in range(experts):
        if offset == 0 or soon(offset):
            source = lax.rem(me + experts - offset, experts)
            loads += [
                pltpu.make_async_copy(
                    block_of(held_hbm[2 + i], "rows", experts, source),
                    block_of(held[2 + i], "rows", experts, source),
                    half_sem.at[i, offset],
                )
                for i in range(2)
            ]
    loads += [
        pltpu.make_async_copy(gate_up_hbm.at[0, 0], gate_up_buf.at[0], load_sem.at[6]),
        pltpu.make_async_copy(gate_up_hbm.at[0, 1], gate_up_buf.at[1], load_sem.at[7]),
        pltpu.make_async_copy(down_hbm.at[0], down_buf, load_sem.at[8]),
    ]
    for load in loads:
        load.start()
    mover = Mover((("swap", "x"),), (values_hbm,), (values_ref,), own, *move_sems)
    mover.take()
    greet((("rows", "f"), ("swap", "x")))

    def later_copy(kind, offset):
        peer = lax.rem(me + offset, experts)
        return remote(
            block_of(later_hbm[kind], "rows", experts, peer),
            block_of(held[2 + kind], "rows", experts, me),
            later_send.at[kind, offset],
            later_recv.at[kind, offset],
            device_of("f", peer),
        )

    later = [offset for offset in range(1, experts) if not soon(offset)]
    for offset in sorted(later, key=lambda offset: -(offset % steps)):
        for kind in range(2):
            later_copy(kind, offset).start()
    mover.start()
    total[...] = jnp.zeros_like(total)
    total_down[...] = jnp.zeros_like(total_down)

    def back_copy(kind, peer, landing):
        return remote(
            block_of(back_buf[kind], "rows", experts, peer),
            block_of(back_refs[kind], "rows", experts, me),
            send_sem.at[kind, peer],
            recv_sem.at[kind, landing],
            device_of("f", peer),
        )

    def own_copy(kind):
        return pltpu.make_async_copy(
            block_of(back_buf[kind], "rows", experts, me),
            block_of(back_refs[kind], "rows", experts, me),
            own_sem.at[kind],
        )

    selectors = rest_selectors(experts // steps)
    spread = (row_index((128, LANES)) == lane_index((128, LANES)) // RANK).astype(BF)
    fold = (row_index((LANES, 128)) % RANK == lane_index((LANES, 128))).astype(BF)
    fold_later = (row_index((LANES, 128)) % RANK == lane_index((LANES, 128)) - RANK).astype(BF)
    for load in loads[:-3]:
        load.wait()
    count, rest_count = held[0].shape[0] // steps, held[1].shape[0] // steps

    def block(step, carry):
        number = lax.rem(me + 1 + step, steps)

        for turn in range(steps // 2):

            @pl.when(step == steps - 1 - turn)
            def arrived():
                for offset in later:
                    if offset % steps == turn:
                        for kind in range(2):
                            later_copy(kind, offset).wait_recv()

        peers = [number + steps * turn for turn in range(experts // steps)]

        def read(ref):
            depth = ref.shape[0] // experts
            blocks = [ref[pl.ds(pl.multiple_of(peer * depth, depth), depth)] for peer in peers]
            return jnp.concatenate(blocks, axis=0)

        def write(ref, value):
            depth = ref.shape[0] // experts
            for turn, peer in enumerate(peers):
                part = value[turn * depth : (turn + 1) * depth]
                ref[pl.ds(pl.multiple_of(peer * depth, depth), depth)] = part

        rows = jnp.concatenate([read(held[0]), rest_to_rows(selectors, read(held[1]))], axis=0)
        grads = jnp.concatenate([read(held[2]), rest_to_rows(selectors, read(held[3]))], axis=0)
        notes = jnp.concatenate(
            [read(held[4]), dot(selectors[0], read(held[5])).astype(BF)], axis=0
        )
        pick = dot(notes, spread)
        gate_of = (
            notes[:, ADAPTER_COUNT : ADAPTER_COUNT + 1].astype(F32)
            + notes[:, ADAPTER_COUNT + 1 : ADAPTER_COUNT + 2].astype(F32)
        )
        grads_f = grads.astype(F32)
        lanes_gate = (dot_nt(rows, first_ref[0]) * pick).astype(BF)
        lanes_up = (dot_nt(rows, first_ref[1]) * pick).astype(BF)
        grad_routed = (gate_of * grads_f).astype(BF)
        grad_side = (dot_nt(grads, down_second_ref[1]) * gate_of * pick).astype(BF)

        @pl.when(step == 0)
        def gate_up_loaded():
            for load in loads[-3:-1]:
                load.wait()

        gate = dot(rows, gate_up_buf[0]) + dot(lanes_gate, second_ref[0])
        upper = dot(rows, gate_up_buf[1]) + dot(lanes_up, second_ref[1])
        hidden, sigma, silu = swiglu(gate, upper)

        @pl.when(step == 0)
        def down_loaded():
            loads[-1].wait()

        grad_hidden = dot_nt(grad_routed, down_buf[...]) + dot(grad_side, down_first_ref[...])
        grad_gate, grad_upper = swiglu_backward(gate, upper, sigma, silu, grad_hidden)
        side = (dot_nt(hidden, down_first_ref[...]).astype(BF).astype(F32) * pick).astype(BF)
        value = dot(hidden, down_buf[...]) + dot(side, down_second_ref[1])
        gate_grad = jnp.sum(grads_f * value, axis=1, keepdims=True)
        result = (gate_of * value).astype(BF)
        write(back_buf[4], result[:count])
        write(back_buf[5], rows_to_rest(selectors, result[count:]))

        def dispatch(kinds):
            for peer in peers:

                @pl.when(peer == me)
                def keep():
                    for kind in kinds:
                        own_copy(kind).start()

                @pl.when(peer != me)
                def send():
                    for kind in kinds:
                        back_copy(kind, peer, me).start()

        dispatch(range(4, BACK))
        back = (dot_nt(grad_gate, gate_up_buf[0]) + dot_nt(grad_upper, gate_up_buf[1])).astype(BF)
        back_gate = (dot_nt(grad_gate, second_ref[0]) * pick).astype(BF)
        back_up = (dot_nt(grad_upper, second_ref[1]) * pick).astype(BF)
        high, low = two_parts(gate_grad)
        lane = lane_index((count + rest_count // 4, 128))
        back_notes = jnp.where(
            lane == PAIR,
            high.astype(F32),
            jnp.where(
                lane == PAIR + 1, low.astype(F32), dot(back_gate, fold) + dot(back_up, fold_later)
            ),
        ).astype(BF)
        write(back_buf[0], back[:count])
        write(back_buf[1], rows_to_rest(selectors, back[count:]))
        write(back_buf[2], back_notes[:count])
        write(back_buf[3], dot_tn(selectors[0], back_notes[count:]).astype(BF))
        dispatch(range(4))
        total[:LANES] += dot_tn(lanes_gate, grad_gate)
        total[LANES : 2 * LANES] += dot_tn(lanes_up, grad_upper)
        total[2 * LANES :] += dot_tn(grad_side, hidden)
        total_down[...] += dot_tn(side, grad_routed)
        return carry

    lax.fori_loop(0, steps, block, 0)
    in_owner_columns(total, adapter_ref, total.shape[1] // experts)
    adapter_ref[3 * LANES :, :] = total_down[...].astype(BF)
    mover.finish()
    for offset in later:
        for kind in range(2):
            later_copy(kind, offset).wait_send()
    for kind in range(BACK):
        own_copy(kind).wait()

    def settle(offset, carry):
        peer = lax.rem(me + offset, experts)
        for kind in range(BACK):
            copy = back_copy(kind, peer, peer)
            copy.wait_send()
            copy.wait_recv()
        return carry

    lax.fori_loop(1, experts, settle, 0)


def routed_expert(number, held, later, values, first, second, down_first, down_second, gate_up, down):
    width, hidden = gate_up.shape[2:]
    experts = GROUP_SIZE["f"]
    vmem = pl.BlockSpec(memory_space=pltpu.VMEM)
    back = [held[0], held[1], held[4], held[5], held[0], held[1]]
    items = [("swap", "x", values)]
    return pl.pallas_call(
        routed_kernel,
        out_shape=[shape_of(array.shape, BF) for array in (*back, values)]
        + [shape_of((4 * LANES, experts * 128), BF)],
        in_specs=[HBM] * 11 + [vmem] * 4,
        out_specs=[HBM] * (BACK + 1) + [vmem],
        scratch_shapes=mover_scratch(items)
        + [pltpu.VMEM(array.shape, BF) for array in held]
        + [pltpu.VMEM(array.shape, BF) for array in back]
        + [
            pltpu.VMEM((2, width, hidden), BF),
            pltpu.VMEM((hidden, width), BF),
            pltpu.VMEM((3 * LANES, hidden), F32),
            pltpu.VMEM((LANES, width), F32),
            pltpu.SemaphoreType.DMA((BACK, experts)),
            pltpu.SemaphoreType.DMA((BACK, experts)),
            pltpu.SemaphoreType.DMA((9,)),
            pltpu.SemaphoreType.DMA((BACK,)),
            pltpu.SemaphoreType.DMA((2, experts)),
            pltpu.SemaphoreType.DMA((2, experts)),
            pltpu.SemaphoreType.DMA((2, experts)),
        ],
        compiler_params=pltpu.CompilerParams(
            collective_id=number, has_side_effects=True, vmem_limit_bytes=VMEM_LIMIT
        ),
        name="routed_expert",
    )(*held, gate_up, down, values, *later, first, second, down_first, down_second)


def after_experts_kernel(
    numbers_ref,
    parts_ref,
    part_notes_ref,
    main_ref,
    rest_ref,
    main_notes_ref,
    rest_notes_ref,
    grads_ref,
    normed_ref,
    residual_ref,
    small_ref,
    mixed_ref,
    routes_ref,
    side_ref,
    ffn_a_ref,
    ffn_b_ref,
    router_ref,
    router_a_ref,
    router_b_ref,
    mix_ref,
    gain_ref,
    down_a_ref,
    down_b_ref,
    first_a_ref,
    first_b_ref,
    second_a_ref,
    second_b_ref,
    weight_hbm,
    grad_residual_ref,
    grad_mixed_ref,
    adapter_ref,
    router_grad_ref,
    shared_side_ref,
    weight_ref,
    sem,
):
    load = pltpu.make_async_copy(weight_hbm, weight_ref, sem)
    load.start()
    experts = router_ref.shape[1]
    side = side_ref[...]
    pick = pair_pick(side, 1)
    grads = grads_ref[0]
    grads_f = grads.astype(F32)
    normed = normed_ref[...]
    out_lanes = small_ref[:, :PAIR].astype(BF)
    router_lanes = small_ref[:, PAIR : 2 * PAIR].astype(BF)
    gates = [small_ref[:, 2 * PAIR + k : 2 * PAIR + k + 1] for k in range(TOP)]
    mix = small_ref[:, 2 * PAIR + TOP : 2 * PAIR + TOP + 1]
    notes = sum(part_notes_ref[i].astype(F32) for i in range(part_notes_ref.shape[0]))
    shared_side = notes[:, :PAIR].astype(BF)
    shared_side_ref[...] = padded(shared_side)
    down_second = pair_of(down_a_ref, down_b_ref, 0)
    mix_total = (
        notes[:, 3 * PAIR : 3 * PAIR + 1]
        + notes[:, 3 * PAIR + 1 : 3 * PAIR + 2]
        + jnp.sum(shared_side.astype(F32) * dot_nt(grads, down_second), axis=1, keepdims=True)
    )
    grad_mix = mix_total * mix * (1.0 - mix)
    grad_shared = (mix * grads_f).astype(BF)
    expert_hot, main_hot, rest_hot = routing(routes_ref[0], experts)
    grad_gates = []
    mask = quarter_mask(rest_hot[0].shape, 0)
    token_notes = None
    for k in range(TOP):
        mine = dot(main_hot[k].astype(BF), main_notes_ref[...]) + dot(
            (rest_hot[k] * mask).astype(BF), rest_notes_ref[...]
        )
        grad_gates.append(mine[:, PAIR : PAIR + 1] + mine[:, PAIR + 1 : PAIR + 2])
        token_notes = mine if k == 0 else token_notes + mine
    inner = sum(gate * grad for gate, grad in zip(gates, grad_gates))
    grad_logits = sum(
        hot * (gate * (grad - inner)) for hot, gate, grad in zip(expert_hot, gates, grad_gates)
    )
    logits_high, logits_low = two_parts(grad_logits)
    router_second = jnp.concatenate([router_a_ref[0], router_b_ref[0]], axis=0)
    grad_router_lanes = dot_nt(logits_high, router_second) + dot_nt(logits_low, router_second)
    router_grad = dot_tn(router_lanes, logits_high) + dot_tn(router_lanes, logits_low)
    of_row = jnp.where(row_index((PAIR, 128)) < RANK, numbers_ref[0], numbers_ref[1]).astype(F32)
    router_grad_ref[...] = jnp.where(
        lane_index((PAIR, 128)) == experts, of_row, padded(router_grad)
    ).astype(BF)
    lane_grads = (
        jnp.concatenate(
            [
                grad_router_lanes,
                notes[:, PAIR : 3 * PAIR],
                token_notes[:, :RANK],
                token_notes[:, :RANK],
                token_notes[:, RANK:PAIR],
                token_notes[:, RANK:PAIR],
            ],
            axis=1,
        )
        * pair_pick(side, 5)
    ).astype(BF)
    factors = ffn_a_ref.shape[0]
    ffn_first = jnp.concatenate([pair_of(ffn_a_ref, ffn_b_ref, i) for i in range(factors)], axis=0)
    grad_second = (
        grad_mix * mix_ref[...].astype(F32)
        + dot_nt(logits_high, router_ref[...])
        + dot_nt(logits_low, router_ref[...])
        + sum(parts_ref[i].astype(F32) for i in range(parts_ref.shape[0]))
        + slots_to_rows(main_hot, rest_hot, main_ref[...], rest_ref[...])
        + dot(lane_grads, ffn_first)
    )
    grad_residual = grads_f + rms_backward(residual_ref[...], gain_ref[...], grad_second)
    grad_residual_ref[...] = grad_residual
    grad_attended = grad_residual.astype(BF)
    first, second = pair_of(first_a_ref, first_b_ref, 0), pair_of(second_a_ref, second_b_ref, 0)
    grad_out_lanes = (dot_nt(grad_attended, second) * pick).astype(BF)
    adapter_ref[...] = jnp.concatenate(
        [
            dot_tn(lane_grads, normed),
            dot_tn(grad_out_lanes, mixed_ref[...]),
            dot_tn(out_lanes, grad_attended),
            dot_tn(shared_side, grad_shared),
        ],
        axis=0,
    ).astype(BF)
    load.wait()
    grad_mixed_ref[...] = (
        dot_nt(grad_attended, weight_ref[...]) + dot(grad_out_lanes, first)
    ).astype(BF)


def after_experts(
    numbers, parts, part_notes, main, rest, main_notes, rest_notes, grads, normed, residual, small, mixed,
    routes, side, ffn_first, router, router_second, mix, gain, down_second, first, second, weight,
):
    tokens, width = normed.shape
    experts = router.shape[1]
    factors = ffn_first.shape[0]
    last = lambda which: pl.BlockSpec((1, 1, RANK, width), lambda n, a: (3, a[which], 0, 0))
    outs = [
        ((tokens, width), F32),
        ((tokens, width), BF),
        (((factors + 3) * PAIR, width), BF),
        ((PAIR, 128), BF),
        ((tokens, 128), BF),
    ]
    plain = (
        parts, part_notes, main, rest, main_notes, rest_notes, grads, normed, residual, small, mixed, routes,
        side,
    )
    return stage(
        after_experts_kernel,
        "after_experts",
        [shape_of(*out) for out in outs],
        [whole(array) for array in plain]
        + [
            of_sequence(0, (factors, 1, RANK, width)),
            of_sequence(1, (factors, 1, RANK, width)),
            whole(router),
            pl.BlockSpec((1, RANK, experts), lambda n, a: (a[0], 0, 0)),
            pl.BlockSpec((1, RANK, experts), lambda n, a: (a[1], 0, 0)),
            whole(mix),
            whole(gain),
            of_sequence(0, (1, 1, RANK, width)),
            of_sequence(1, (1, 1, RANK, width)),
            last(0),
            last(1),
            last(0),
            last(1),
            HBM,
        ],
        [pl.BlockSpec(shape, lambda n, a: (0, 0)) for shape, kind in outs],
        scratch=[pltpu.VMEM(weight.shape, BF), pltpu.SemaphoreType.DMA],
        prefetch=1,
    )(
        numbers, *plain, ffn_first, ffn_first, router, router_second, router_second, mix, gain, down_second,
        down_second, first, first, second, second, weight,
    )


def attention_back_kernel(plan, heads_plan, *refs):
    amount = len(plan)
    inputs, expert_hbm, refs = refs[:amount], refs[amount], refs[amount + 1 :]
    mixed_hbm, query_hbm, pairs_hbm, weight_hbm = refs[:4]
    place_ref, start_ref, key_place_ref, cos_ref, sin_ref, side_ref, lanes_ref, second_ref = refs[4:12]
    results, ends, refs = list(refs[12:20]), list(refs[20:26]), refs[26:]
    out_ref, end_outs, refs = refs[0], refs[1:11], refs[11:]
    outputs, refs = refs[:amount], refs[amount:]
    heads_got, parts_ref, notes_ref, expert_ref, refs = *refs[:4], refs[4:]
    late_bufs, late_sem, refs = refs[:6], refs[6], refs[7:]
    end_scratch, refs = refs[:END_SCRATCH], refs[END_SCRATCH:]
    own, move_sems, refs = refs[:amount], refs[amount : amount + 4], refs[amount + 4 :]
    heads_own, heads_sems, refs = refs[:1], refs[1:5], refs[5:]
    expert_own, expert_sems, refs = refs[:1], refs[1:5], refs[5:]
    mixed_buf, query_buf, pairs_buf, weight_buf = refs[:4]
    sent_buf, got_buf, grads_buf, heads_buf, parts_buf, notes_buf = refs[4:10]
    mixed_send, mixed_recv, pair_send, pair_recv, parts_send, parts_recv, load_sem, own_sem = refs[10:]

    x, y = place_in("x"), place_in("y")
    along, tokens, columns = mixed_buf.shape
    rows_all = along * tokens
    heads = columns // HEAD_DIM
    loads = [
        pltpu.make_async_copy(block_of(mixed_hbm, "columns", along, x), mixed_buf.at[x], load_sem.at[0]),
        pltpu.make_async_copy(query_hbm.at[0], query_buf, load_sem.at[1]),
        pltpu.make_async_copy(pairs_hbm, pairs_buf, load_sem.at[2]),
    ]
    loads += [
        pltpu.make_async_copy(weight_hbm.at[:, j], weight_buf.at[j], load_sem.at[3 + j])
        for j in range(3)
    ]
    for load in loads:
        load.start()
    late_loads = []
    for i, (group, place) in enumerate(LATE):
        refs_of = (results, ends)[group]
        late_loads.append(pltpu.make_async_copy(refs_of[place], late_bufs[i], late_sem.at[i]))
        refs_of[place] = late_bufs[i]
    for load in late_loads:
        load.start()
    mover = Mover(plan, inputs, outputs, own, *move_sems)
    mover.take()
    expert_mover = Mover((("rows", "x"),), (expert_hbm,), (expert_ref,), expert_own, *expert_sems)
    expert_mover.take()
    greet((("rows", "f"), ("swap", "x"), ("swap", "y"), ("rows", "c")))

    def mixed_copy(offset):
        peer = lax.rem(x + offset, along)
        return remote(
            block_of(mixed_hbm, "columns", along, peer),
            mixed_buf.at[x],
            mixed_send.at[offset],
            mixed_recv.at[offset],
            device_of("x", peer),
        )

    def pair_copy(head):
        return remote(
            sent_buf.at[1 - y, head],
            got_buf.at[head],
            pair_send.at[head],
            pair_recv.at[head],
            device_of("y", 1 - y),
        )

    def parts_copy(offset):
        peer = lax.rem(x + offset, along)
        return remote(
            parts_buf.at[peer],
            parts_ref.at[x],
            parts_send.at[0, offset],
            parts_recv.at[0, offset],
            device_of("x", peer),
        )

    def notes_copy(offset):
        peer = lax.rem(x + offset, along)
        return remote(
            notes_buf.at[peer],
            notes_ref.at[x],
            parts_send.at[1, offset],
            parts_recv.at[1, offset],
            device_of("x", peer),
        )

    for offset in (2, 1, 3):
        mixed_copy(offset).start()
    for load in loads[:3]:
        load.wait()
    for offset in (1, 3, 2):
        mixed_copy(offset).wait_recv()
    expert_mover.start()

    step = rows_all // 2

    def head_block(head, carry):
        here = pl.ds(pl.multiple_of(head * HEAD_DIM, HEAD_DIM), HEAD_DIM)
        keys = pairs_buf[:, 0, :, here].reshape(-1, HEAD_DIM)
        values = pairs_buf[:, 1, :, here].reshape(-1, HEAD_DIM)
        key_total, value_total = None, None
        for i in range(2):
            at = slice(i * step, (i + 1) * step)
            query = query_buf[at, here]
            blocks = along // 2
            grad = mixed_buf[i * blocks : (i + 1) * blocks, :, here].reshape(step, HEAD_DIM)
            probs = probabilities(query, keys, place_ref[at], start_ref[at], key_place_ref[...])
            grad_probs = dot_nt(grad, values)
            mean = jnp.sum(probs * grad_probs, axis=1, keepdims=True)
            grad_scores = (probs * (grad_probs - mean)).astype(BF)
            grad_query = dot(grad_scores, keys) * (HEAD_DIM**-0.5)
            grads_buf[0, at, here] = (
                grad_query * cos_ref[at] - half_turn(grad_query) * sin_ref[at]
            ).astype(BF)
            grad_keys = dot_tn(grad_scores, query) * (HEAD_DIM**-0.5)
            grad_values = dot_tn(probs.astype(BF), grad)
            key_total = grad_keys if i == 0 else key_total + grad_keys
            value_total = grad_values if i == 0 else value_total + grad_values
        for half in range(2):
            at = slice(half * rows_all, (half + 1) * rows_all)
            sent_buf[half, head, 0] = key_total[at].astype(BF)
            sent_buf[half, head, 1] = value_total[at].astype(BF)
        pair_copy(head).start()
        return carry

    lax.fori_loop(0, heads, head_block, 0)
    for load in late_loads:
        load.wait()
    combine_kernel(*results, out_ref)

    def head_sum(head, carry):
        here = pl.ds(pl.multiple_of(head * HEAD_DIM, HEAD_DIM), HEAD_DIM)
        pair_copy(head).wait_recv()
        key = sent_buf[y, head, 0].astype(F32) + got_buf[head, 0].astype(F32)
        grads_buf[1, :, here] = (key * cos_ref[...] - half_turn(key) * sin_ref[...]).astype(BF)
        value = sent_buf[y, head, 1].astype(F32) + got_buf[head, 1].astype(F32)
        grads_buf[2, :, here] = value.astype(BF)
        return carry

    lax.fori_loop(0, heads, head_sum, 0)
    pick = pair_pick(side_ref[...], 1)
    notes = []
    heads_buf[...] = jnp.zeros_like(heads_buf)
    own_columns = pl.ds(pl.multiple_of(x * columns, columns), columns)
    for j in range(3):
        at = slice(j * PAIR, (j + 1) * PAIR)
        notes.append((dot_nt(grads_buf[j], second_ref[at]) * pick).astype(BF))
        heads_buf[at, own_columns] = dot_tn(lanes_ref[j], grads_buf[j]).astype(BF)
    notes_buf[...] = padded(jnp.concatenate(notes, axis=1)).reshape(notes_buf.shape)
    heads_mover = Mover(heads_plan, (heads_buf,), (heads_got,), heads_own, *heads_sems)
    heads_mover.take()
    heads_mover.start()
    for offset in (1, 3, 2):
        notes_copy(offset).start()
    mover.start()
    own_notes = pltpu.make_async_copy(notes_buf.at[x], notes_ref.at[x], own_sem.at[0])
    own_notes.start()
    for load in loads[3:]:
        load.wait()

    def own_parts():
        return pltpu.make_async_copy(parts_buf.at[x], parts_ref.at[x], own_sem.at[1])

    def row_block(number, carry):
        offset = x_step(lax.rem(number + 1, along))
        peer = lax.rem(x + offset, along)
        at = pl.ds(pl.multiple_of(peer * tokens, tokens), tokens)
        total = None
        for j in range(3):
            part = dot_nt(grads_buf[j, at], weight_buf[j].reshape(-1, columns))
            total = part if total is None else total + part
        parts_buf[peer] = total.astype(BF)

        @pl.when(number < along - 1)
        def send():
            parts_copy(offset).start()

        @pl.when(number == along - 1)
        def keep():
            own_parts().start()

        return carry

    lax.fori_loop(0, along, row_block, 0)
    mover.finish()
    heads_mover.finish()
    expert_mover.finish()
    own_notes.wait()
    own_parts().wait()

    def pairs_sent(head, carry):
        pair_copy(head).wait_send()
        return carry

    lax.fori_loop(0, heads, pairs_sent, 0)
    for offset in range(1, along):
        mixed_copy(offset).wait_send()
        parts_copy(offset).wait()
        notes_copy(offset).wait()
    early_got, shared_got, router_got = outputs
    got = (router_got, early_got, shared_got, heads_got, ends[5], expert_ref)
    finish_kernel(parts_ref, notes_ref, *ends[:5], *got, *end_outs, *end_scratch)


LATE = ((0, 0), (0, 3), (0, 4), (1, 0), (1, 1), (1, 2))
END_SCRATCH = 18 + 6 * 4 + 9


def attention_back(number, items, expert, mixed, query, pairs, weight, small, results, ends, columns_of):
    plan = tuple((kind, group) for kind, group, array in items)
    arrays = [array for kind, group, array in items]
    along = GROUP_SIZE["x"]
    tokens, width = mixed.shape
    columns = width // along
    heads = columns // HEAD_DIM
    rows_all = along * tokens
    heads_items = [("from_columns", "f", shape_of((3 * PAIR, width), BF))]
    vmem = pl.BlockSpec(memory_space=pltpu.VMEM)
    got = [exchanged_shape(kind, group, array.shape) for kind, group, array in items]
    got += [
        exchanged_shape("from_columns", "f", (3 * PAIR, width)),
        (along, tokens, width),
        (along, tokens, 128),
        expert.shape,
    ]
    late = [(results, ends)[group][place] for group, place in LATE]
    in_specs = [[vmem] * len(results), [vmem] * len(ends)]
    for group, place in LATE:
        in_specs[group][place] = HBM
    end_outs, end_scratch = finish_shapes(ends[0], ends[4], items, expert, columns_of)
    assert len(end_scratch) == END_SCRATCH
    dma = pltpu.SemaphoreType.DMA
    return pl.pallas_call(
        functools.partial(attention_back_kernel, plan, (("from_columns", "f"),)),
        out_shape=[shape_of((1, tokens, width), BF), *end_outs],
        in_specs=[HBM] * (len(items) + 5) + [vmem] * len(small) + in_specs[0] + in_specs[1],
        out_specs=[vmem] * (1 + len(end_outs)),
        scratch_shapes=[pltpu.VMEM(shape, BF) for shape in got]
        + [pltpu.VMEM(array.shape, array.dtype) for array in late]
        + [dma((len(LATE),))]
        + end_scratch
        + mover_scratch(items)
        + mover_scratch(heads_items)
        + mover_scratch([("rows", "x", expert)])
        + [
            pltpu.VMEM((along, tokens, columns), BF),
            pltpu.VMEM((rows_all, columns), BF),
            pltpu.VMEM(pairs.shape, BF),
            pltpu.VMEM((3, *weight.shape[:1], *weight.shape[2:]), BF),
            pltpu.VMEM((2, heads, 2, rows_all, HEAD_DIM), BF),
            pltpu.VMEM((heads, 2, rows_all, HEAD_DIM), BF),
            pltpu.VMEM((3, rows_all, columns), BF),
            pltpu.VMEM((3 * PAIR, width), BF),
            pltpu.VMEM((along, tokens, width), BF),
            pltpu.VMEM((along, tokens, 128), BF),
            dma((along,)),
            dma((along,)),
            dma((heads,)),
            dma((heads,)),
            dma((2, along)),
            dma((2, along)),
            dma((6,)),
            dma((2,)),
        ],
        compiler_params=pltpu.CompilerParams(
            collective_id=number, has_side_effects=True, vmem_limit_bytes=VMEM_LIMIT
        ),
        name="attention_back",
    )(*arrays, expert, mixed, query, pairs, weight, *small, *results, *ends)


def lane_expansion(ids_ref, group):
    ids = ids_ref[group][:, GROUP_SIZE["f"] : GROUP_SIZE["f"] + 1].astype(F32)
    lane = lane_index((PAIR, LANES))
    same = (lane // RANK).astype(F32) == ids
    return (same & (lane % RANK == row_index((PAIR, LANES)) % RANK)).astype(BF)


def expanded(expansions, got_ref, factor):
    total = None
    for group, expansion in enumerate(expansions):
        part = dot_tn(expansion, got_ref[group, factor * PAIR : (factor + 1) * PAIR, :])
        total = part if total is None else total + part
    return total.astype(BF)


FINISH = (
    (("from_columns", "f"),),
    (("from_columns", "f"),),
    (("rows", "c"), ("rows", "y")),
    (("gather", "c"), ("gather", "c"), ("gather", "c")),
    (("rows", "c"),),
    (("gather", "c"),),
)


def finish_kernel(*refs):
    parts_ref, notes_ref, rows_ref, normed_ref, residual_ref, gain_ref, first_ref = refs[:7]
    ids_ref, early_ref, shared_ref, heads_ref, column_ref, expert_ref = refs[7:13]
    grad_out, attn_in, attn_out, ffn_out, router_out, shared_out, shared_in_out = refs[13:20]
    expert_out, expert_in_out, down_out, expert_buf, refs = *refs[20:24], refs[24:]
    late_buf, late_got, early_buf, early_parts, shared_buf, shared_parts = refs[:6]
    expert_got, late_sum, early_row, shared_row, expert_sum = refs[6:11]
    late_all, early_all, shared_all, expert_all, late_parts, late_row, refs = *refs[11:17], refs[17:]
    ends = (
        ((expert_buf,), (expert_got,)),
        ((late_buf,), (late_got,)),
        ((early_buf, shared_buf), (early_parts, shared_parts)),
        ((early_row, shared_row, expert_sum), (early_all, shared_all, expert_all)),
        ((late_sum,), (late_parts,)),
        ((late_row,), (late_all,)),
    )
    movers = []
    for plan, (inputs, outputs) in zip(FINISH, ends):
        own, sems, refs = refs[: len(plan)], refs[len(plan) : len(plan) + 4], refs[len(plan) + 4 :]
        movers.append(Mover(plan, inputs, outputs, own, *sems))

    def begin(mover):
        mover.take()
        mover.start()

    lanes = sum(notes_ref[i].astype(F32) for i in range(notes_ref.shape[0]))[:, : 3 * PAIR]
    lanes = lanes.astype(BF)
    late_buf[...] = dot_tn(lanes, normed_ref[...]).astype(BF)
    begin(movers[1])
    count = expert_buf.shape[0]
    expert_buf[...] = sum(
        expert_ref[i * count : (i + 1) * count].astype(F32) for i in range(GROUP_SIZE["x"])
    ).astype(BF)
    begin(movers[0])

    groups = ids_ref.shape[0]
    expansions = [lane_expansion(ids_ref, group) for group in range(groups)]
    row = 0
    for got in (early_ref, heads_ref):
        for factor in range(got.shape[1] // PAIR):
            early_buf[row : row + LANES, :] = expanded(expansions, got, factor)
            row += LANES
    router = None
    for group in range(groups):
        part = dot_tn(expansions[group], ids_ref[group])
        router = part if router is None else router + part
    router = jnp.sum(router * column_ref[...].astype(F32), axis=1, keepdims=True)
    early_buf[row : row + LANES, :] = jnp.broadcast_to(router, (LANES, 128)).astype(BF)
    for factor in range(shared_ref.shape[1] // PAIR):
        shared_buf[factor * LANES : (factor + 1) * LANES, :] = expanded(
            expansions, shared_ref, factor
        )
    begin(movers[2])

    grad = sum(parts_ref[i].astype(F32) for i in range(parts_ref.shape[0]))
    grad = grad + dot(lanes, first_ref[...])
    total = residual_ref[...] + rms_backward(rows_ref[0].astype(F32), gain_ref[...], grad)
    grad_out[0] = total.astype(BF)

    movers[1].finish()
    for factor in range(late_got.shape[1] // PAIR):
        late_sum[factor * LANES : (factor + 1) * LANES, :] = expanded(expansions, late_got, factor)
    begin(movers[4])
    movers[0].finish()
    expert_sum[...] = sum(expert_got[i].astype(F32) for i in range(groups)).astype(BF)
    movers[2].finish()
    count = early_row.shape[0]
    early_row[...] = sum(
        early_parts[i * count : (i + 1) * count].astype(F32) for i in range(GROUP_SIZE["c"])
    ).astype(BF)
    count = shared_row.shape[0]
    shared_row[...] = (
        shared_parts[:count].astype(F32) + shared_parts[count:].astype(F32)
    ).astype(BF)
    begin(movers[3])
    movers[4].finish()
    count = late_row.shape[0]
    late_row[...] = sum(
        late_parts[i * count : (i + 1) * count].astype(F32) for i in range(GROUP_SIZE["c"])
    ).astype(BF)
    begin(movers[5])

    movers[3].finish()
    early = early_all[...].reshape(-1, 128).astype(F32)
    expert = jnp.concatenate(
        [
            expert_all[2 * i].astype(F32) + expert_all[2 * i + 1].astype(F32)
            for i in range(GROUP_SIZE["x"])
        ],
        axis=0,
    )
    factor = [early[i * LANES : (i + 1) * LANES] for i in range(early.shape[0] // LANES)]
    attn_in[3 * LANES :, :] = factor[5]
    attn_out[: 3 * LANES, :] = jnp.concatenate(factor[8:11], axis=0)
    attn_out[3 * LANES :, :] = factor[6]
    ffn_out[...] = jnp.concatenate(factor[:5], axis=0)
    router_out[...] = factor[11][:, : router_out.shape[1]]
    down_out[:LANES, :] = factor[7]
    down_out[LANES:, :] = expert[3 * LANES :]
    expert_out[...] = expert[: 2 * LANES, : expert_out.shape[1]]
    expert_in_out[...] = expert[2 * LANES : 3 * LANES, : expert_in_out.shape[1]]
    along = GROUP_SIZE["x"]
    columns = shared_out.shape[1] // along
    quarters = [
        shared_all[2 * i : 2 * i + 2].reshape(-1, 128)[:, :columns].astype(F32) for i in range(along)
    ]
    shared_rows = jnp.concatenate(quarters, axis=1)
    shared_out[...] = shared_rows[: 2 * LANES]
    shared_in_out[...] = shared_rows[2 * LANES :]
    movers[5].finish()
    attn_in[: 3 * LANES, :] = late_all[...].reshape(-1, 128).astype(F32)


def finish_shapes(rows, first, items, expert, columns_of):
    width = rows.shape[2]
    early, shared = items[0][2], items[1][2]
    shared_columns, expert_columns = columns_of
    groups, ctx = GROUP_SIZE["f"], GROUP_SIZE["c"]
    early_rows = ((early.shape[0] + first.shape[0]) // PAIR + 1) * LANES
    late_rows = first.shape[0] // PAIR * LANES
    shared_rows = shared.shape[0] // PAIR * LANES
    expert_rows = expert.shape[0] // GROUP_SIZE["x"]
    bufs = [
        first.shape,
        (groups, first.shape[0], 128),
        (early_rows, 128),
        (early_rows, 128),
        (shared_rows, 128),
        (shared_rows, 128),
        (groups, expert_rows, 128),
        (late_rows, 128),
        (early_rows // ctx, 128),
        (shared_rows // 2, 128),
        (expert_rows, 128),
        (ctx, late_rows // ctx, 128),
        (ctx, early_rows // ctx, 128),
        (ctx, shared_rows // 2, 128),
        (ctx, expert_rows, 128),
        (late_rows, 128),
        (late_rows // ctx, 128),
    ]
    sent = (((expert_rows, width),), (bufs[0],), (bufs[2], bufs[4]), (bufs[8], bufs[9], bufs[10]), (bufs[7],), (bufs[16],))
    scratch = [pltpu.VMEM(buf, BF) for buf in ((expert_rows, width), *bufs)]
    for plan, shapes in zip(FINISH, sent):
        scratch += mover_scratch(
            [(kind, group, shape_of(shape, BF)) for (kind, group), shape in zip(plan, shapes)]
        )
    outs = [
        shape_of(rows.shape, BF),
        shape_of((4 * LANES, 128), F32),
        shape_of((4 * LANES, 128), F32),
        shape_of((5 * LANES, 128), F32),
        shape_of((LANES, 1), F32),
        shape_of((2 * LANES, shared_columns), F32),
        shape_of((LANES, shared_columns), F32),
        shape_of((2 * LANES, expert_columns), F32),
        shape_of((LANES, expert_columns), F32),
        shape_of((2 * LANES, 128), F32),
    ]
    return outs, scratch


def deliver_kernel(*refs):
    amount = len(refs) // 2
    for source, target in zip(refs[:amount], refs[amount:]):
        target[...] = source[...]


def deliver(arrays):
    specs = [whole(array) for array in arrays]
    shapes = [shape_of(array.shape, array.dtype) for array in arrays]
    return stage(deliver_kernel, "deliver", shapes, specs, specs)(*arrays)


def combine_kernel(
    main_ref, rest_ref, routes_ref, residual_ref, parts_ref, side_ref, small_ref, picked_ref, out_ref
):
    experts = main_ref.shape[0] // MAIN
    unused, main_hot, rest_hot = routing(routes_ref[0], experts)
    mixture = slots_to_rows(main_hot, rest_hot, main_ref[...], rest_ref[...])
    shared = sum(parts_ref[i].astype(F32) for i in range(parts_ref.shape[0]))
    shared = shared + dot(side_ref[:, :PAIR], picked_ref[2 * PAIR :])
    mix = small_ref[:, 2 * PAIR + TOP : 2 * PAIR + TOP + 1]
    out_ref[0] = (residual_ref[...] + mixture + mix * shared).astype(BF)


def shards(
    layer_hidden_input,
    output_cotangent,
    sequence_pair_lengths,
    block_placement_order,
    sequence_adapter_index,
    token_expert_choices,
    attention_norm_gain,
    feedforward_norm_gain,
    query_key_value_weight,
    output_projection_weight,
    query_key_value_bias,
    router_weight_matrix,
    shared_gate_up_weight,
    shared_down_weight,
    shared_sigmoid_gate,
    routed_gate_up_weight,
    routed_down_weight,
    attention_adapter_first,
    attention_adapter_second,
    feedforward_adapter_first,
    router_adapter_second,
    shared_gate_adapter_second,
    shared_down_adapter_first,
    routed_gate_adapter_second,
    routed_down_adapter_first,
    down_adapter_second,
):
    tokens, width = layer_hidden_input.shape[1:]
    experts = router_weight_matrix.shape[1]
    capacity = tokens * TOP // experts * 9 // 8
    tail = capacity - MAIN
    ctx_count = lax.axis_size("ctx")
    group_rows = tokens * ctx_count
    along = ctx_count // 2
    rows_shared = tokens * along
    x_index = lax.axis_index("ctx") // 2
    y_index = lax.axis_index("ctx") % 2
    head_columns = width // along
    hidden = shared_down_weight.shape[0]
    quarter = hidden // along
    shards_of = lax.axis_size("fsdp")
    lengths = sequence_pair_lengths[0]
    order = block_placement_order[0]
    adapters = sequence_adapter_index[0]
    block_size = group_rows // order.shape[0]

    qkv_own = lax.dynamic_slice_in_dim(
        query_key_value_weight, x_index * head_columns, head_columns, 2
    ).reshape(-1, head_columns)
    out_weight = lax.all_gather(output_projection_weight, "fsdp", tiled=True)
    units = -(-quarter // 32) * 32
    own_up = jnp.swapaxes(
        lax.dynamic_slice_in_dim(shared_gate_up_weight, x_index * quarter, quarter, 2), 1, 2
    )
    own_down = lax.dynamic_slice_in_dim(shared_down_weight, x_index * quarter, quarter, 0)
    own_shared = jnp.pad(
        jnp.concatenate([own_up, own_down[None]]), ((0, 0), (0, units - quarter), (0, 0))
    ).reshape(3 * units, width)

    def of_group(factor):
        parts = [lax.dynamic_index_in_dim(factor, adapters[s], -3, keepdims=True) for s in range(2)]
        both = jnp.concatenate(parts, axis=-3)
        return both.reshape(both.shape[:-3] + (PAIR, both.shape[-1]))

    shared_second = jnp.concatenate(
        [
            of_group(shared_gate_adapter_second).reshape(2 * PAIR, hidden * shards_of),
            of_group(shared_down_adapter_first),
        ],
        axis=0,
    )
    shared_second = lax.dynamic_index_in_dim(
        shared_second.reshape(3 * PAIR, shards_of, along, quarter), x_index, 2, keepdims=False
    )
    shared_second = jnp.pad(shared_second, ((0, 0), (0, 0), (0, units - quarter)))
    shared_second = shared_second.reshape(3, PAIR, shards_of, units).transpose(0, 2, 3, 1)
    shared_second = jnp.stack(
        [
            jnp.pad(shared_second[i], ((0, 0), (0, 0), (before, 128 - PAIR - before)))
            for i, before in enumerate((0, PAIR, 0))
        ]
    )
    numbers = jnp.concatenate([adapters, x_index[None].astype(jnp.int32)])

    start = lengths[0]
    block_rows = jnp.arange(block_size, dtype=jnp.int32)
    blocks = order.reshape(along, 2, -1)
    key_places = (jnp.swapaxes(blocks, 0, 1).reshape(-1)[:, None] * block_size + block_rows).reshape(
        1, group_rows
    )
    own_blocks = lax.dynamic_index_in_dim(blocks, y_index, 1, keepdims=False).reshape(-1)
    places = own_blocks[:, None] * block_size + block_rows
    second = places >= start
    fractions = jnp.arange(0, HEAD_DIM, 2).astype(F32) / HEAD_DIM
    speeds = rope_theta ** (-fractions)
    bases = jnp.stack([own_blocks * block_size, own_blocks * block_size - start])
    base_angles = bases.astype(F32)[:, :, None, None] * speeds
    base_angles = jnp.concatenate([base_angles, base_angles], axis=3)
    base_cos, base_sin = jnp.cos(base_angles), jnp.sin(base_angles)
    base_cos = jnp.where(second[:, :, None], base_cos[1], base_cos[0])
    base_sin = jnp.where(second[:, :, None], base_sin[1], base_sin[0])
    row_angles = block_rows.astype(F32)[:, None] * speeds[None, :]
    row_angles = jnp.concatenate([row_angles, row_angles], axis=1)
    row_cos, row_sin = jnp.cos(row_angles), jnp.sin(row_angles)
    cosine = base_cos * row_cos - base_sin * row_sin
    sine = base_sin * row_cos + base_cos * row_sin
    sine = jnp.where(jnp.arange(HEAD_DIM) < HEAD_DIM // 2, -sine, sine)
    cosine, sine = cosine.reshape(rows_shared, HEAD_DIM), sine.reshape(rows_shared, HEAD_DIM)
    place_column = places.reshape(rows_shared, 1)
    start_column = jnp.where(second, start, 0).reshape(rows_shared, 1)
    side_shared = second.astype(F32).reshape(rows_shared, 1)
    side = lax.dynamic_slice_in_dim(side_shared, x_index * tokens, tokens)

    attention_gain = attention_norm_gain[None, :]
    feedforward_gain = feedforward_norm_gain[None, :]
    mix_weight = shared_sigmoid_gate[None, :]
    routed_second = routed_gate_adapter_second.reshape(2, LANES, -1)
    routed_first = routed_down_adapter_first.reshape(LANES, -1)
    ffn_flat = feedforward_adapter_first.reshape(-1, LANES, width)[3:]
    down_flat = down_adapter_second.reshape(2, LANES, width)

    normed_one, sent_grads_main, sent_grads_rest, picked, picked_first, picked_second = prologue(
        numbers,
        layer_hidden_input,
        output_cotangent,
        attention_gain,
        token_expert_choices,
        feedforward_adapter_first,
        down_adapter_second,
        attention_adapter_first,
        attention_adapter_second,
        experts,
        head_columns,
    )
    own_shared, normed_one = lax.optimization_barrier((own_shared, normed_one))
    shared_weight = lax.all_gather(own_shared, "fsdp")
    qkv, normed_shared = exchange(
        "gather_first", 0, ("share", "s", qkv_own), ("gather", "x", normed_one)
    )
    qkv = qkv.reshape(shards_of, 3, tokens, head_columns)
    projected, qkv_lanes = project(
        numbers,
        normed_shared.reshape(rows_shared, width),
        qkv,
        attention_adapter_first,
        attention_adapter_second,
        query_key_value_bias,
        side_shared,
        cosine,
        sine,
    )
    pairs, grads_shared = exchange(
        "keys", 1, ("gather", "y", projected[1:]), ("gather", "x", output_cotangent[0])
    )
    mixed_heads = attend(projected, pairs, place_column, start_column, key_places)
    (mixed,) = exchange(
        "mixed", 2, ("to_columns", "x", mixed_heads.reshape(along, tokens, head_columns))
    )
    residual, normed_two, small, sent_main, sent_rest, notes_main, notes_rest = after_attention(
        numbers,
        mixed,
        out_weight,
        layer_hidden_input,
        attention_adapter_first,
        attention_adapter_second,
        feedforward_gain,
        feedforward_adapter_first,
        router_weight_matrix,
        router_adapter_second,
        mix_weight,
        token_expert_choices,
        side,
    )
    *held, parts_rows, parts_lanes, value_part, shared_columns = shared_expert(
        3,
        normed_two,
        [
            ("rows", "f", sent_main),
            ("rows", "f", sent_rest),
            ("half", "f", sent_grads_main),
            ("half", "f", sent_grads_rest),
            ("rows", "f", notes_main),
            ("rows", "f", notes_rest),
        ],
        grads_shared,
        shared_weight,
        side_shared.reshape(along, tokens, 1),
        picked,
        shared_second,
        mix_weight,
    )
    (
        got_main,
        got_rest,
        got_notes_main,
        got_notes_rest,
        result_main,
        result_rest,
        value_parts,
        expert_columns,
    ) = routed_expert(
        4,
        held,
        (sent_grads_main, sent_grads_rest),
        value_part,
        ffn_flat,
        routed_second,
        routed_first,
        down_flat,
        routed_gate_up_weight,
        routed_down_weight,
    )
    grad_residual, grad_mixed, early_columns, router_rows, shared_side = after_experts(
        numbers,
        parts_rows,
        parts_lanes,
        got_main,
        got_rest,
        got_notes_main,
        got_notes_rest,
        output_cotangent,
        normed_two,
        residual,
        small,
        mixed,
        token_expert_choices,
        side,
        feedforward_adapter_first,
        router_weight_matrix,
        router_adapter_second,
        mix_weight,
        feedforward_gain,
        down_adapter_second,
        attention_adapter_first,
        attention_adapter_second,
        out_weight,
    )

    own_column = (jnp.arange(128) == lax.axis_index("fsdp")).astype(BF)[None, :]
    results = attention_back(
        5,
        [
            ("from_columns", "f", early_columns),
            ("from_columns", "f", shared_columns),
            ("gather", "f", router_rows),
        ],
        expert_columns,
        grad_mixed,
        projected,
        pairs,
        qkv,
        (
            place_column,
            start_column,
            key_places,
            cosine,
            sine,
            side_shared,
            qkv_lanes,
            picked_second,
        ),
        (
            result_main,
            result_rest,
            token_expert_choices,
            residual,
            value_parts,
            shared_side,
            small,
            picked,
        ),
        (
            layer_hidden_input,
            normed_one,
            grad_residual,
            attention_gain,
            picked_first,
            own_column,
        ),
        (along * quarter, routed_down_weight.shape[1] // shards_of),
    )

    output_value, *grads = deliver(results)

    def by_adapter(rows):
        parts = rows.reshape(-1, ADAPTER_COUNT, RANK, rows.shape[1])
        return parts[0] if parts.shape[0] == 1 else parts

    return (output_value, grads[0], *(by_adapter(rows) for rows in grads[1:]))


def solution(mesh):
    return jax.shard_map(
        shards,
        mesh=mesh,
        in_specs=(
            P("fsdp", "ctx", None),
            P("fsdp", "ctx", None),
            P("fsdp", None),
            P("fsdp", None),
            P("fsdp", None),
            P("fsdp", "ctx", None),
            P(),
            P(),
            P(None, "fsdp", None),
            P("fsdp", None),
            P(),
            P(),
            P(None, None, "fsdp"),
            P("fsdp", None),
            P(),
            P("fsdp", None, None, None),
            P("fsdp", None, None),
            P(),
            P(),
            P(),
            P(),
            P(),
            P(),
            P(),
            P(),
            P(),
        ),
        out_specs=(
            P("fsdp", "ctx", None),
            P("fsdp", "ctx", None),
            P(None, None, None, "fsdp"),
            P(None, None, None, "fsdp"),
            P(None, None, None, "fsdp"),
            P(None, None, "fsdp"),
            P(None, None, None, "fsdp"),
            P(None, None, "fsdp"),
            P(None, None, None, "fsdp"),
            P(None, None, "fsdp"),
            P(None, None, None, "fsdp"),
        ),
        check_vma=False,
    )
```
